32 devices in a mesh: gz: 8 (over z, y), gy: 4 (over x, core).
Axes of the slice: x: 2, y: 2, z: 4, core: 2. Of those that a mesh axis runs over, the one named last changes fastest.
Arguments:
- features: bfloat16 [64, 16, 32, 128], P(None, 'gz', 'gy'), may hold values from -6 to 6
- conv_weight: bfloat16 [3, 3, 64, 192], replicated, may hold values from -0.15625 to 0.15625
- down_weight: bfloat16 [2, 2, 128, 128], replicated, may hold values from -0.25 to 0.25
- cotangent: bfloat16 [128, 8, 1024], P(None, 'gz', 'gy'), may hold values from -6 to 6
Outputs:
- section_out: bfloat16 [128, 8, 1024], P(None, 'gz', 'gy')
- grad_field: float32 [64, 16, 32, 128], P(None, 'gz', 'gy')
- grad_conv: float32 [3, 3, 64, 192], replicated
- grad_down: float32 [2, 2, 128, 128], replicated
The draws below stay inside these ranges and needn't reach their ends.
All inputs are finite; a program needn't handle non-finite values.
Results may differ from the reference program's by a relative error of at most 0.005.
Values may be sent and summed in bfloat16 or wider, within the bound.
No kernel may reach another device: no remote copies, remote signals or barrier semaphores. Data moves between devices by JAX's collectives and lax.ppermute only.
A program may use at most 64 MiB of HBM per device.

```python
import math
import jax
import jax.numpy as jnp

C = 64
COUT = 128
NX = 128
NZ = 16
NY = 32


def steps_of(stream_key, shape, shards, smallest, high):
    loudness, own = 1.0, jax.random.fold_in(stream_key, 6)
    for position, blocks in shards:
        draws = jnp.exp(jax.random.uniform(jax.random.fold_in(own, position), (blocks,), jnp.float32, smallest / len(shards), high / len(shards)))
        loudness = loudness * jnp.repeat(draws, shape[position] // blocks).reshape([-1 if axis == position else 1 for axis in range(len(shape))])
    return loudness


def noise(key, dims, width, bound, shards=(), dtype=jnp.bfloat16):
    values = jax.random.normal(key, dims, jnp.float32) * width
    if len(shards) > 0:
        values = steps_of(key, dims, shards, -0.22, 0.18) * values
    return jnp.clip(values, min=-bound, max=bound).astype(dtype)


def setup_inputs(seed: int = 0) -> dict:
    key_list = jax.random.split(jax.random.key(seed), 5)
    return {
        "features": noise(key_list[0], (C, NZ, NY, NX), 1.0, 6.0, ((1, 8), (2, 4))),
        "conv_weight": noise(key_list[1], (3, 3, C, 3 * C), (27 * C) ** -0.5, 0.15625),
        "down_weight": noise(key_list[2], (2, 2, COUT, 2 * C), (8 * C) ** -0.5, 0.25),
        "cotangent": noise(key_list[3], (COUT, NZ // 2, (NY // 2) * (NX // 2)), 1.0, 6.0, ((1, 8), (2, 4))),
    }


def reference(features, conv_weight, down_weight, cotangent):
    channels = features.shape[0]
    out_channels = down_weight.shape[2]
    grad_scale = 1.0 / math.sqrt(NZ * NY * NX)
    source = features.astype(jnp.float32)
    preact = jnp.zeros(features.shape, jnp.float32)
    for tap_z in range(3):
        for tap_y in range(3):
            for tap_x in range(3):
                shifted = jnp.roll(source, (1 - tap_z, 1 - tap_y, 1 - tap_x), axis=(1, 2, 3))
                tap_block = conv_weight[tap_z, tap_y][:, tap_x * channels:(tap_x + 1) * channels].astype(jnp.float32)
                preact = preact + jnp.einsum('oi,izyx->ozyx', tap_block, shifted)
    hidden = jax.nn.silu(preact).astype(jnp.bfloat16)
    blocks = hidden.astype(jnp.float32).reshape(channels, NZ // 2, 2, NY // 2, 2, NX // 2, 2)
    down_split = down_weight.astype(jnp.float32).reshape(2, 2, out_channels, 2, channels)
    coarse = jnp.einsum('aboei,iZaYbXe->oZYX', down_split, blocks)
    section_out = coarse.reshape(out_channels, NZ // 2, NY // 2 * (NX // 2)).astype(jnp.bfloat16)
    coarse_cot = cotangent.astype(jnp.float32).reshape(out_channels, NZ // 2, NY // 2, NX // 2)
    hidden_grad = jnp.einsum('aboei,oZYX->iZaYbXe', down_split, coarse_cot).reshape(channels, NZ, NY, NX)
    grad_down = jnp.einsum('oZYX,iZaYbXe->aboei', coarse_cot, blocks).reshape(2, 2, out_channels, 2 * channels) * grad_scale
    gate_sig = jax.nn.sigmoid(preact)
    gate_grad = (hidden_grad * gate_sig * (1.0 + preact * (1.0 - gate_sig))).astype(jnp.bfloat16)
    gate_wide = gate_grad.astype(jnp.float32)
    grad_field = jnp.zeros(features.shape, jnp.float32)
    kernel_rows = []
    for tap_z in range(3):
        row_list = []
        for tap_y in range(3):
            pieces = []
            for tap_x in range(3):
                shifted = jnp.roll(source, (1 - tap_z, 1 - tap_y, 1 - tap_x), axis=(1, 2, 3))
                pieces.append(jnp.einsum('ozyx,izyx->oi', gate_wide, shifted))
                tap_block = conv_weight[tap_z, tap_y][:, tap_x * channels:(tap_x + 1) * channels].astype(jnp.float32)
                contrib = jnp.einsum('oi,ozyx->izyx', tap_block, gate_wide)
                grad_field = grad_field + jnp.roll(contrib, (tap_z - 1, tap_y - 1, tap_x - 1), axis=(1, 2, 3))
            row_list.append(jnp.concatenate(pieces, axis=1))
        kernel_rows.append(jnp.stack(row_list, axis=0))
    grad_conv = jnp.stack(kernel_rows, axis=0) * grad_scale
    return (section_out, grad_field, grad_conv, grad_down)
```

```python
import math

import jax
import jax.numpy as jnp
from jax import lax
from jax.sharding import PartitionSpec as P


def extended(cells, sides, width):
    for axis, dim in sides:
        count = lax.axis_size(axis)
        head = lax.slice_in_dim(cells, 0, width, axis=dim)
        tail = lax.slice_in_dim(cells, cells.shape[dim] - width, cells.shape[dim], axis=dim)
        cells = jnp.concatenate(
            [
                lax.ppermute(tail, axis, [(i, (i + 1) % count) for i in range(count)]),
                cells,
                lax.ppermute(head, axis, [((i + 1) % count, i) for i in range(count)]),
            ],
            axis=dim,
        )
    return cells


def widen(framed):
    return jnp.concatenate([jnp.roll(framed, 1 - tap_x, axis=3) for tap_x in range(3)], axis=0)


def fold_along(spread, channels):
    result = jnp.roll(spread[0:channels], -1, axis=3)
    result = result + spread[channels : 2 * channels]
    result = result + jnp.roll(spread[2 * channels : 3 * channels], 1, axis=3)
    return result


def summed_over_devices(local_conv, local_down):
    axes = ("gz", "gy")
    count = lax.axis_size("gz") * lax.axis_size("gy")
    flat = jnp.concatenate([local_conv.reshape(-1, 128), local_down.reshape(-1, 128)], axis=0)
    rows = flat.shape[0]
    share = -(-rows // (16 * count)) * 16
    flat = jnp.pad(flat, ((0, share * count - rows), (0, 0))).astype(jnp.bfloat16)
    terms = lax.all_to_all(flat.reshape(count, share, 128), axes, 0, 0, tiled=True)
    mine = jnp.sum(terms.astype(jnp.float32), axis=0).astype(jnp.bfloat16)
    copies = jnp.broadcast_to(mine[None], (count, share, 128))
    sums = lax.all_to_all(copies, axes, 0, 0, tiled=True).reshape(count * share, 128).astype(jnp.float32)
    split = local_conv.size // 128
    return sums[:split].reshape(local_conv.shape), sums[split:rows].reshape(local_down.shape)


def body(features, conv_weight, down_weight, cotangent):
    channels, plane_count, row_count, breadth = features.shape
    out_channels = down_weight.shape[2]
    cell_count = plane_count * row_count * breadth * lax.axis_size("gz") * lax.axis_size("gy")
    grad_scale = 1.0 / math.sqrt(cell_count)
    framed = extended(features, (("gz", 1), ("gy", 2)), 1)
    columns = widen(framed)
    preact = jnp.zeros((channels, plane_count, row_count, breadth), jnp.float32)
    for tap_z in range(3):
        for tap_y in range(3):
            window = columns[:, tap_z : tap_z + plane_count, tap_y : tap_y + row_count]
            preact = preact + jnp.einsum(
                "oj,jzyx->ozyx",
                conv_weight[tap_z, tap_y],
                window,
                preferred_element_type=jnp.float32,
            )
    hidden = jax.nn.silu(preact).astype(jnp.bfloat16)
    blocks = hidden.reshape(channels, plane_count // 2, 2, row_count // 2, 2, breadth // 2, 2)
    down_split = down_weight.reshape(2, 2, out_channels, 2, channels)
    coarse = jnp.einsum(
        "aboei,iZaYbXe->oZYX", down_split, blocks, preferred_element_type=jnp.float32
    )
    section_out = coarse.reshape(out_channels, plane_count // 2, -1).astype(jnp.bfloat16)
    coarse_cot = cotangent.reshape(out_channels, plane_count // 2, row_count // 2, breadth // 2)
    hidden_grad = jnp.einsum(
        "aboei,oZYX->iZaYbXe", down_split, coarse_cot, preferred_element_type=jnp.float32
    )
    hidden_grad = hidden_grad.reshape(channels, plane_count, row_count, breadth)
    local_down = jnp.einsum(
        "oZYX,iZaYbXe->aboei", coarse_cot, blocks, preferred_element_type=jnp.float32
    )
    local_down = local_down.reshape(2, 2, out_channels, 2 * channels)
    gate_sig = jax.nn.sigmoid(preact)
    gate_grad = (hidden_grad * gate_sig * (1.0 + preact * (1.0 - gate_sig))).astype(jnp.bfloat16)
    kernel_rows = []
    for tap_z in range(3):
        row_list = []
        for tap_y in range(3):
            window = columns[:, tap_z : tap_z + plane_count, tap_y : tap_y + row_count]
            row_list.append(
                jnp.einsum("ozyx,jzyx->oj", gate_grad, window, preferred_element_type=jnp.float32)
            )
        kernel_rows.append(jnp.stack(row_list, axis=0))
    local_conv = jnp.stack(kernel_rows, axis=0)
    spread = jnp.zeros((3 * channels, plane_count + 2, row_count + 2, breadth), jnp.float32)
    for tap_z in range(3):
        for tap_y in range(3):
            term = jnp.einsum(
                "oj,ozyx->jzyx",
                conv_weight[tap_z, tap_y],
                gate_grad,
                preferred_element_type=jnp.float32,
            )
            spread = spread.at[:, tap_z : tap_z + plane_count, tap_y : tap_y + row_count].add(term)
    folded = fold_along(spread, channels)
    bordered = extended(folded.astype(jnp.bfloat16), (("gz", 1), ("gy", 2)), 1).astype(folded.dtype)
    plane_fold = bordered[:, 2 : plane_count + 2]
    plane_fold = plane_fold.at[:, 0].add(bordered[:, 0])
    plane_fold = plane_fold.at[:, plane_count - 1].add(bordered[:, plane_count + 3])
    row_fold = plane_fold[:, :, 2 : row_count + 2]
    row_fold = row_fold.at[:, :, 0].add(plane_fold[:, :, 0])
    row_fold = row_fold.at[:, :, row_count - 1].add(plane_fold[:, :, row_count + 3])
    summed_conv, summed_down = summed_over_devices(local_conv, local_down)
    grad_conv = summed_conv * grad_scale
    grad_down = summed_down * grad_scale
    return (section_out, row_fold, grad_conv, grad_down)


def solution(mesh):
    return jax.shard_map(
        body,
        mesh=mesh,
        in_specs=(P(None, "gz", "gy", None), P(), P(), P(None, "gz", "gy")),
        out_specs=(P(None, "gz", "gy"), P(None, "gz", "gy", None), P(), P()),
        check_vma=False,
    )
```

```python
import functools
import math

import jax
import jax.numpy as jnp
from jax import lax
from jax.experimental import pallas as pl
from jax.experimental.pallas import tpu as pltpu
from jax.sharding import PartitionSpec as P

F32 = jnp.float32
BF16 = jnp.bfloat16
PARAMS = pltpu.CompilerParams(vmem_limit_bytes=24 * 1024 * 1024)


def call(kernel, outs, scratch, flops, operands):
    moved = sum(x.size * x.dtype.itemsize for x in operands)
    moved += sum(math.prod(s) * jnp.dtype(d).itemsize for s, d in outs)
    return pl.pallas_call(
        kernel,
        out_shape=[jax.ShapeDtypeStruct(s, d) for s, d in outs],
        in_specs=[pl.BlockSpec(memory_space=pltpu.VMEM)] * len(operands),
        out_specs=[pl.BlockSpec(memory_space=pltpu.VMEM)] * len(outs),
        scratch_shapes=[pltpu.VMEM(s, d) for s, d in scratch],
        compiler_params=PARAMS,
        cost_estimate=pl.CostEstimate(flops=flops, bytes_accessed=moved, transcendentals=0),
    )(*operands)


def lines_kernel(f_ref, f0_ref, f1_ref, first_ref, last_ref, wide):
    channels, planes, rows, breadth = f_ref.shape
    wide[...] = f_ref[...].astype(F32).reshape(channels * planes * rows, breadth)
    for z, plane_ref in enumerate((f0_ref, f1_ref)):
        for y in range(rows):
            line = wide[pl.ds(z * rows + y, channels, stride=planes * rows), :].astype(BF16)
            plane_ref[y] = line
            if y == 0:
                first_ref[z] = line
            if y == rows - 1:
                last_ref[z] = line


def fill_columns(cols, planes, sides, corners, turn):
    rows, channels, _ = planes[0].shape

    def put(p, q, line):
        wide = line.astype(F32)
        cols[p, q, 0:channels] = pltpu.roll(wide, turn % 128, 1).astype(BF16)
        cols[p, q, channels : 2 * channels] = line
        cols[p, q, 2 * channels : 3 * channels] = pltpu.roll(wide, -turn % 128, 1).astype(BF16)

    for p in range(4):
        def step(y, carry, p=p):
            put(p, y + 1, planes[p][y])
            return carry

        lax.fori_loop(0, rows, step, 0, unroll=2)
    low, high = sides
    for z in range(2):
        put(z + 1, 0, low[z])
        put(z + 1, rows + 1, high[z])
    for p, corner in zip((0, 3), corners):
        put(p, 0, corner[0])
        put(p, rows + 1, corner[1])


def convolve(cols, w_ref, y):
    channels = w_ref.shape[0] // 3
    depth = w_ref.shape[1]
    breadth = cols.shape[3]

    def window(p):
        pair = [cols[p, pl.ds(y + s, 3)].reshape(depth, breadth) for s in range(2)]
        return jnp.concatenate(pair, axis=1)

    dot = functools.partial(jnp.dot, preferred_element_type=F32)
    acc = dot(w_ref[0 : 2 * channels], window(1)) + dot(w_ref[channels : 3 * channels], window(2))
    upper = acc[0:channels] + dot(w_ref[2 * channels : 3 * channels], window(3))
    lower = acc[channels : 2 * channels] + dot(w_ref[0:channels], window(0))
    return lower, upper


def forward_kernel(
    zlo, f0, f1, zhi, ylo, yhi, clo, chi, w_ref, dt_ref, cot_ref,
    cols, g0_ref, g1_ref, first_ref, last_ref, h_ref, up,
):
    rows, channels, breadth = f0.shape
    half = breadth // 2
    fill_columns(cols, (zlo, f0, f1, zhi), (ylo, yhi), (clo, chi), 1)
    source = lax.broadcasted_iota(jnp.int32, (breadth, 2 * breadth), 0)
    target = lax.broadcasted_iota(jnp.int32, (breadth, 2 * breadth), 1)
    spread = jnp.where(source == target // 2, 1.0, 0.0).astype(BF16)
    for pair in range(rows // 4):
        both = jnp.dot(cot_ref[:, pair * breadth : (pair + 1) * breadth], spread, preferred_element_type=F32)
        up[2 * pair] = both[:, 0:breadth].astype(BF16)
        up[2 * pair + 1] = both[:, breadth : 2 * breadth].astype(BF16)
    lane = lax.broadcasted_iota(jnp.int32, (channels, breadth), 1)
    even = lane % 2 == 0

    def step(t, carry):
        y = 2 * t
        preacts = convolve(cols, w_ref, y)
        for z, plane_ref in enumerate((g0_ref, g1_ref)):
            for b in range(2):
                preact = preacts[z][:, b * breadth : (b + 1) * breadth]
                sig = 1.0 / (1.0 + jnp.exp(-preact))
                h_ref[z, y + b] = (preact * sig).astype(BF16)
                terms = jnp.dot(dt_ref[z, b], up[t], preferred_element_type=F32)
                grad = jnp.where(even, terms[0:channels], terms[channels : 2 * channels])
                plane_ref[y + b] = (grad * sig * (1.0 + preact * (1.0 - sig))).astype(BF16)
        return carry

    lax.fori_loop(0, rows // 2, step, 0)
    for z, plane_ref in enumerate((g0_ref, g1_ref)):
        first_ref[z] = plane_ref[0]
        last_ref[z] = plane_ref[rows - 1]


def weight_grad_kernel(cols, g0_ref, g1_ref, h_ref, d_ref, cot_ref, out_ref, packed):
    rows, channels, breadth = g0_ref.shape
    across = (((1,), (1,)), ((), ()))
    flat = lambda ref, rows_of: jnp.concatenate([ref[r] for r in rows_of], axis=1)
    gates = jnp.concatenate([flat(g0_ref, range(rows)), flat(g1_ref, range(rows))], axis=0)
    lane = lax.broadcasted_iota(jnp.int32, (channels // 2, breadth), 1)
    for b in range(3):
        parts = []
        for p in range(4):
            window = jnp.concatenate([cols[p, y + b] for y in range(rows)], axis=1)
            lhs = gates[0:channels] if p == 0 else gates[channels:] if p == 3 else gates
            parts.append(lax.dot_general(lhs, window, across, preferred_element_type=F32))
        for a in range(3):
            low = parts[a][0:channels]
            high = parts[a + 1] if a == 2 else parts[a + 1][channels:]
            total = low + high
            base = (a * 3 + b) * 3 * channels // 2
            packed[base : base + channels] = total[:, 0:breadth].astype(BF16)
            rest = jnp.concatenate([total[:, breadth:], total[:, breadth:]], axis=1)
            mix = jnp.where(lane < channels, rest[0 : channels // 2], rest[channels // 2 :])
            packed[base + channels : base + 3 * channels // 2] = mix.astype(BF16)
    base = 9 * 3 * channels // 2
    source = lax.broadcasted_iota(jnp.int32, (2 * breadth, 2 * breadth), 0)
    target = lax.broadcasted_iota(jnp.int32, (2 * breadth, 2 * breadth), 1)
    wanted = 2 * (target % breadth) + target // breadth
    pick = jnp.where(source == wanted, 1.0, 0.0).astype(BF16)
    coarse = None
    for a in range(2):
        for b in range(2):
            pairs = []
            for pair in range(rows // 4):
                both = jnp.concatenate([h_ref[a, 4 * pair + b], h_ref[a, 4 * pair + 2 + b]], axis=1)
                pairs.append(jnp.dot(both, pick, preferred_element_type=F32).astype(BF16))
            hidden = jnp.concatenate(
                [jnp.concatenate([x[:, e * breadth : (e + 1) * breadth] for x in pairs], axis=1) for e in range(2)],
                axis=0,
            )
            term = jnp.dot(d_ref[a, b], hidden, preferred_element_type=F32)
            coarse = term if coarse is None else coarse + term
            down = lax.dot_general(cot_ref[...], hidden, across, preferred_element_type=F32)
            at = base + (2 * a + b) * d_ref.shape[2]
            packed[at : at + d_ref.shape[2]] = down.astype(BF16)
    out_ref[...] = coarse.astype(BF16)
    end = base + 4 * d_ref.shape[2]
    if end < packed.shape[0]:
        packed[end:] = jnp.zeros((packed.shape[0] - end, packed.shape[1]), BF16)


def field_kernel(zlo, g0, g1, zhi, ylo, yhi, clo, chi, w_ref, out_ref, cols):
    rows, channels, breadth = g0.shape
    fill_columns(cols, (zlo, g0, g1, zhi), (ylo, yhi), (clo, chi), 1)

    def step(t, carry):
        y = 2 * t
        lines = convolve(cols, w_ref, y)
        for z in range(2):
            for b in range(2):
                part = lines[z][:, b * breadth : (b + 1) * breadth]
                out_ref[pl.ds(z * rows + y + b, channels, stride=2 * rows), :] = part
        return carry

    lax.fori_loop(0, rows // 2, step, 0)


def unpack_kernel(sums_ref, conv_ref, down_ref, *, scale):
    channels = conv_ref.shape[2]
    for a in range(3):
        for b in range(3):
            base = (a * 3 + b) * 3 * channels // 2
            conv_ref[a, b, :, 0 : 2 * channels] = sums_ref[base : base + channels].astype(F32) * scale
            rest = sums_ref[base + channels : base + 3 * channels // 2].astype(F32) * scale
            conv_ref[a, b, 0 : channels // 2, 2 * channels :] = rest[:, 0:channels]
            conv_ref[a, b, channels // 2 :, 2 * channels :] = rest[:, channels:]
    base = 9 * 3 * channels // 2
    height = down_ref.shape[2]
    for a in range(2):
        for b in range(2):
            at = base + (2 * a + b) * height
            down_ref[a, b] = sums_ref[at : at + height].astype(F32) * scale


def shifted(cells, axis, step):
    count = lax.axis_size(axis)
    return lax.ppermute(cells, axis, [(i, (i + step) % count) for i in range(count)])


def halos(plane0, plane1, first, last):
    zlo, zhi = shifted(plane1, "gz", 1), shifted(plane0, "gz", -1)
    ylo, yhi = shifted(last, "gy", 1), shifted(first, "gy", -1)
    clo = shifted(jnp.stack([ylo[1], yhi[1]]), "gz", 1)
    chi = shifted(jnp.stack([ylo[0], yhi[0]]), "gz", -1)
    return zlo, zhi, ylo, yhi, clo, chi


def summed_over_devices(packed, count):
    axes = ("gz", "gy")
    share = packed.shape[0] // count
    terms = lax.all_to_all(packed.reshape(count, share, 128), axes, 0, 0, tiled=True)
    mine = jnp.sum(terms.astype(F32), axis=0).astype(BF16)
    copies = jnp.broadcast_to(mine[None], (count, share, 128))
    return lax.all_to_all(copies, axes, 0, 0, tiled=True).reshape(count * share, 128)


def body(features, conv_weight, down_weight, cotangent):
    channels, plane_count, row_count, breadth = features.shape
    out_channels = down_weight.shape[2]
    count = lax.axis_size("gz") * lax.axis_size("gy")
    grad_scale = 1.0 / math.sqrt(plane_count * row_count * breadth * count)
    depth = 9 * channels
    weight_fwd = conv_weight.transpose(0, 2, 1, 3).reshape(3 * channels, depth)
    taps = conv_weight.reshape(3, 3, channels, 3, channels)[::-1, ::-1, :, ::-1]
    weight_bwd = taps.transpose(0, 4, 1, 3, 2).reshape(3 * channels, depth)
    down_turned = down_weight.transpose(0, 1, 3, 2)
    cot = cotangent.reshape(out_channels, -1)
    plane = ((row_count, channels, breadth), BF16)
    edge = ((plane_count, channels, breadth), BF16)
    cols = ((4, row_count + 2, 3 * channels, breadth), BF16)
    conv_flops = 2 * 27 * channels * channels * plane_count * row_count * breadth

    f0, f1, first, last = call(
        lines_kernel, [plane, plane, edge, edge],
        [((channels * plane_count * row_count, breadth), F32)], 0, (features,),
    )
    zlo, zhi, ylo, yhi, clo, chi = halos(f0, f1, first, last)
    columns, g0, g1, gate_first, gate_last, hidden = call(
        forward_kernel,
        [cols, plane, plane, edge, edge, ((plane_count, row_count, channels, breadth), BF16)],
        [((row_count // 2, out_channels, breadth), BF16)],
        conv_flops,
        (zlo, f0, f1, zhi, ylo, yhi, clo, chi, weight_fwd, down_turned, cot),
    )
    gate_halos = halos(g0, g1, gate_first, gate_last)
    used = 27 * channels // 2 * channels // 64 + 4 * out_channels
    share = -(-used // (16 * count)) * 16
    section_out, packed = call(
        weight_grad_kernel,
        [((out_channels, cot.shape[1]), BF16), ((share * count, 128), BF16)],
        [], conv_flops, (columns, g0, g1, hidden, down_weight, cot),
    )
    sums = summed_over_devices(packed, count)
    zlo, zhi, ylo, yhi, clo, chi = gate_halos
    (field,) = call(
        field_kernel, [((channels * plane_count * row_count, breadth), F32)], [cols], conv_flops,
        (zlo, g0, g1, zhi, ylo, yhi, clo, chi, weight_bwd),
    )
    grad_conv, grad_down = call(
        functools.partial(unpack_kernel, scale=grad_scale),
        [(conv_weight.shape, F32), (down_weight.shape, F32)], [], 0, (sums,),
    )
    section_out = section_out.reshape(out_channels, plane_count // 2, -1)
    return (section_out, field.reshape(features.shape), grad_conv, grad_down)


def solution(mesh):
    return jax.shard_map(
        body,
        mesh=mesh,
        in_specs=(P(None, "gz", "gy", None), P(), P(), P(None, "gz", "gy")),
        out_specs=(P(None, "gz", "gy"), P(None, "gz", "gy", None), P(), P()),
        check_vma=False,
    )
```

```python
import functools
import math

import jax
import jax.numpy as jnp
from jax import lax
from jax.experimental import pallas as pl
from jax.experimental.pallas import tpu as pltpu
from jax.sharding import PartitionSpec as P

F32 = jnp.float32
BF16 = jnp.bfloat16
PARAMS = pltpu.CompilerParams(vmem_limit_bytes=24 * 1024 * 1024)


def call(kernel, outs, scratch, flops, scalars, operands):
    moved = sum(x.size * x.dtype.itemsize for x in operands)
    moved += sum(math.prod(s) * jnp.dtype(d).itemsize for s, d in outs)
    vmem = pl.BlockSpec(memory_space=pltpu.VMEM)
    return pl.pallas_call(
        kernel,
        out_shape=[jax.ShapeDtypeStruct(s, d) for s, d in outs],
        in_specs=[pl.BlockSpec(memory_space=pltpu.SMEM)] * len(scalars) + [vmem] * len(operands),
        out_specs=[vmem] * len(outs),
        scratch_shapes=[pltpu.VMEM(s, d) for s, d in scratch],
        compiler_params=PARAMS,
        cost_estimate=pl.CostEstimate(flops=flops, bytes_accessed=moved, transcendentals=0),
    )(*scalars, *operands)


def choose(cond, yes, no):
    return jnp.where(jnp.broadcast_to(cond, yes.shape), yes, no)


def lines_kernel(place, f_ref, f0_ref, f1_ref, near_ref, far_ref, wide):
    channels, planes, rows, breadth = f_ref.shape
    wide[...] = f_ref[...].astype(F32).reshape(channels * planes * rows, breadth)

    def line(z, y):
        return wide[pl.ds(z * rows + y, channels, stride=planes * rows), :].astype(BF16)

    even = place[1] == 0
    for z, plane_ref in enumerate((f0_ref, f1_ref)):
        first, last = line(z, 0), line(z, rows - 1)
        near_ref[z] = choose(even, last, first)
        far_ref[z] = choose(even, first, last)
        plane_ref[0] = first
        plane_ref[rows - 1] = last
        for y in range(1, rows - 1):
            plane_ref[y] = line(z, y)


def faces_kernel(place, p0, p1, near, far, near_ref, far_ref):
    rows = p0.shape[0]
    even_z, even_y = place[0] == 0, place[1] == 0

    def put(q, low, high):
        near_ref[q] = choose(even_z, high, low)
        far_ref[q] = choose(even_z, low, high)

    put(0, choose(even_y, far[0], near[0]), choose(even_y, far[1], near[1]))
    for y in range(rows):
        put(y + 1, p0[y], p1[y])
    put(rows + 1, choose(even_y, near[0], far[0]), choose(even_y, near[1], far[1]))


def put_columns(cols, p, q, line):
    channels = line.shape[0]
    wide = line.astype(F32)
    cols[p, q, 0:channels] = pltpu.roll(wide, 1, 1).astype(BF16)
    cols[p, q, channels : 2 * channels] = line
    cols[p, q, 2 * channels : 3 * channels] = pltpu.roll(wide, line.shape[1] - 1, 1).astype(BF16)


def fill_columns(cols, near, far, near_first):
    def step(q, carry):
        put_columns(cols, 0, q, choose(near_first, near[q], far[q]))
        put_columns(cols, 1, q, choose(near_first, far[q], near[q]))
        return carry

    lax.fori_loop(0, near.shape[0], step, 0, unroll=2)


def window(cols, p, q):
    return jnp.concatenate([cols[p, q], cols[p, q + 1]], axis=1)


def inner_terms(cols, taps, y):
    acc = None
    for b in range(3):
        w = taps(b)
        count = w.shape[0] // 3
        for p in range(2):
            term = jnp.dot(w[p * count : (p + 2) * count], window(cols, p, y + b), preferred_element_type=F32)
            acc = term if acc is None else acc + term
    half = acc.shape[0] // 2
    return acc[half:], acc[:half]


def outer_terms(cols, taps, y):
    lower = upper = None
    for b in range(3):
        w = taps(b)
        count = w.shape[0] // 3
        low = jnp.dot(w[0:count], window(cols, 0, y + b), preferred_element_type=F32)
        high = jnp.dot(w[2 * count :], window(cols, 1, y + b), preferred_element_type=F32)
        lower = low if lower is None else lower + low
        upper = high if upper is None else upper + high
    return lower, upper


def stacked(w_ref):
    return lambda b: jnp.concatenate([w_ref[a, b] for a in range(3)], axis=0)


def inner_kernel(place, near, far, w_ref, d_ref, cot_ref, cols, acc_ref, grad_ref, up):
    channels, breadth = near.shape[1:]
    rows = near.shape[0] - 2
    fill_columns(cols, near, far, place[0] == 1)
    source = lax.broadcasted_iota(jnp.int32, (breadth, 2 * breadth), 0)
    target = lax.broadcasted_iota(jnp.int32, (breadth, 2 * breadth), 1)
    spread = jnp.where(source == target // 2, 1.0, 0.0).astype(BF16)
    for pair in range(rows // 4):
        both = jnp.dot(cot_ref[:, pair * breadth : (pair + 1) * breadth], spread, preferred_element_type=F32)
        up[:, 2 * pair * breadth : 2 * (pair + 1) * breadth] = both.astype(BF16)
    even = lax.broadcasted_iota(jnp.int32, (channels, breadth), 1) % 2 == 0
    for a in range(2):
        for b in range(2):
            terms = lax.dot_general(d_ref[a, b], up[...], (((0,), (0,)), ((), ())), preferred_element_type=F32)
            for t in range(rows // 2):
                part = terms[:, t * breadth : (t + 1) * breadth]
                grad_ref[a, 2 * t + b] = jnp.where(even, part[0:channels], part[channels:])

    def step(t, carry):
        y = 2 * t
        for z, lines in enumerate(inner_terms(cols, stacked(w_ref), y)):
            for b in range(2):
                acc_ref[z, y + b] = lines[:, b * breadth : (b + 1) * breadth]
        return carry

    lax.fori_loop(0, rows // 2, step, 0)


def gate_kernel(place, near, far, acc_ref, grad_ref, w_ref, cols, g0_ref, g1_ref, near_ref, far_ref, h_ref):
    channels, breadth = near.shape[1:]
    rows = near.shape[0] - 2
    fill_columns(cols, near, far, place[0] == 1)

    def step(t, carry):
        y = 2 * t
        outer = outer_terms(cols, stacked(w_ref), y)
        for z, plane_ref in enumerate((g0_ref, g1_ref)):
            for b in range(2):
                preact = acc_ref[z, y + b] + outer[z][:, b * breadth : (b + 1) * breadth]
                sig = 1.0 / (1.0 + jnp.exp(-preact))
                h_ref[z, y + b] = (preact * sig).astype(BF16)
                plane_ref[y + b] = (grad_ref[z, y + b] * sig * (1.0 + preact * (1.0 - sig))).astype(BF16)
        return carry

    lax.fori_loop(0, rows // 2, step, 0)
    even = place[1] == 0
    for z, plane_ref in enumerate((g0_ref, g1_ref)):
        near_ref[z] = choose(even, plane_ref[rows - 1], plane_ref[0])
        far_ref[z] = choose(even, plane_ref[0], plane_ref[rows - 1])


def weight_grad_kernel(place, inner, outer, g0_ref, g1_ref, h_ref, d_ref, cot_ref, out_ref, keep, send, packed):
    rows, channels, breadth = g0_ref.shape
    across = (((1,), (1,)), ((), ()))
    flat = lambda ref, rows_of: jnp.concatenate([ref[r] for r in rows_of], axis=1)
    gates = jnp.concatenate([flat(g0_ref, range(rows)), flat(g1_ref, range(rows))], axis=0)
    lane = lax.broadcasted_iota(jnp.int32, (channels // 2, breadth), 1)
    for b in range(3):
        parts = []
        for p in range(4):
            cols, at = (inner, p - 1) if p in (1, 2) else (outer, p // 3)
            window = jnp.concatenate([cols[at, y + b] for y in range(rows)], axis=1)
            lhs = gates[0:channels] if p == 0 else gates[channels:] if p == 3 else gates
            parts.append(lax.dot_general(lhs, window, across, preferred_element_type=F32))
        for a in range(3):
            low = parts[a][0:channels]
            high = parts[a + 1] if a == 2 else parts[a + 1][channels:]
            total = low + high
            base = (a * 3 + b) * 3 * channels // 2
            packed[base : base + channels] = total[:, 0:breadth].astype(BF16)
            rest = jnp.concatenate([total[:, breadth:], total[:, breadth:]], axis=1)
            mix = jnp.where(lane < channels, rest[0 : channels // 2], rest[channels // 2 :])
            packed[base + channels : base + 3 * channels // 2] = mix.astype(BF16)
    base = 9 * 3 * channels // 2
    source = lax.broadcasted_iota(jnp.int32, (2 * breadth, 2 * breadth), 0)
    target = lax.broadcasted_iota(jnp.int32, (2 * breadth, 2 * breadth), 1)
    wanted = 2 * (target % breadth) + target // breadth
    pick = jnp.where(source == wanted, 1.0, 0.0).astype(BF16)
    coarse = None
    for a in range(2):
        for b in range(2):
            pairs = []
            for pair in range(rows // 4):
                both = jnp.concatenate([h_ref[a, 4 * pair + b], h_ref[a, 4 * pair + 2 + b]], axis=1)
                pairs.append(jnp.dot(both, pick, preferred_element_type=F32).astype(BF16))
            hidden = jnp.concatenate(
                [jnp.concatenate([x[:, e * breadth : (e + 1) * breadth] for x in pairs], axis=1) for e in range(2)],
                axis=0,
            )
            term = jnp.dot(d_ref[a, b], hidden, preferred_element_type=F32)
            coarse = term if coarse is None else coarse + term
            down = lax.dot_general(cot_ref[...], hidden, across, preferred_element_type=F32)
            at = base + (2 * a + b) * d_ref.shape[2]
            packed[at : at + d_ref.shape[2]] = down.astype(BF16)
    out_ref[...] = coarse.astype(BF16)
    end = base + 4 * d_ref.shape[2]
    if end < packed.shape[0]:
        packed[end:] = jnp.zeros((packed.shape[0] - end, packed.shape[1]), BF16)
    half = packed.shape[0] // 2
    keep[...] = packed[pl.ds(pl.multiple_of(place[2] * half, 16), half)]
    send[...] = packed[pl.ds(pl.multiple_of((1 - place[2]) * half, 16), half)]


def add_kernel(x, y, out):
    out[...] = (x[...].astype(F32) + y[...].astype(F32)).astype(BF16)


def total_kernel(terms, out):
    total = jnp.sum(terms[...].astype(F32), axis=0).astype(BF16)
    for member in range(out.shape[0]):
        out[member] = total


def field_kernel(place, near, far, near_in, far_in, w_ref, out_ref, inner, outer):
    channels, breadth = near.shape[1:]
    rows = near.shape[0] - 2
    fill_columns(inner, near, far, place[0] == 1)
    fill_columns(outer, near_in, far_in, place[0] == 1)

    def step(t, carry):
        y = 2 * t
        own = inner_terms(inner, stacked(w_ref), y)
        rest = outer_terms(outer, stacked(w_ref), y)
        for z in range(2):
            total = own[z] + rest[z]
            for b in range(2):
                part = total[:, b * breadth : (b + 1) * breadth]
                out_ref[pl.ds(z * rows + y + b, channels, stride=2 * rows), :] = part
        return carry

    lax.fori_loop(0, rows // 2, step, 0)


def unpack_kernel(place, mine, other, conv_ref, down_ref, sums_ref, *, scale):
    half = mine.shape[0]
    sums_ref[pl.ds(pl.multiple_of(place[2] * half, 16), half)] = mine[...]
    sums_ref[pl.ds(pl.multiple_of((1 - place[2]) * half, 16), half)] = other[...]
    channels = conv_ref.shape[2]
    for a in range(3):
        for b in range(3):
            base = (a * 3 + b) * 3 * channels // 2
            conv_ref[a, b, :, 0 : 2 * channels] = sums_ref[base : base + channels].astype(F32) * scale
            rest = sums_ref[base + channels : base + 3 * channels // 2].astype(F32) * scale
            conv_ref[a, b, 0 : channels // 2, 2 * channels :] = rest[:, 0:channels]
            conv_ref[a, b, channels // 2 :, 2 * channels :] = rest[:, channels:]
    base = 9 * 3 * channels // 2
    height = down_ref.shape[2]
    for a in range(2):
        for b in range(2):
            at = base + (2 * a + b) * height
            down_ref[a, b] = sums_ref[at : at + height].astype(F32) * scale


def swap(cells, axis, low):
    count = lax.axis_size(axis)
    pairs = [(i % count, (i + 1) % count) for i in range(low, low + count, 2)]
    return lax.ppermute(cells, axis, pairs + [(b, a) for a, b in pairs])


def swapped(near, far, axis):
    return swap(near, axis, 0), swap(far, axis, 1)


def body(features, conv_weight, down_weight, cotangent):
    channels, plane_count, row_count, breadth = features.shape
    out_channels = down_weight.shape[2]
    count = lax.axis_size("gz") * lax.axis_size("gy")
    grad_scale = 1.0 / math.sqrt(plane_count * row_count * breadth * count)
    taps = conv_weight.reshape(3, 3, channels, 3, channels)[::-1, ::-1, :, ::-1]
    weight_bwd = taps.transpose(0, 1, 4, 3, 2).reshape(3, 3, channels, 3 * channels)
    cot = cotangent.reshape(out_channels, -1)
    along_z, along_y = lax.axis_index("gz"), lax.axis_index("gy")
    place = jnp.stack([along_z % 2, along_y % 2, along_y % 2]).astype(jnp.int32)
    plane = ((row_count, channels, breadth), BF16)
    edge = ((plane_count, channels, breadth), BF16)
    face = ((row_count + 2, channels, breadth), BF16)
    cols = ((2, row_count + 2, 3 * channels, breadth), BF16)
    lines = (plane_count, row_count, channels, breadth)
    conv_flops = 2 * 27 * channels * channels * plane_count * row_count * breadth

    f0, f1, near, far = call(
        lines_kernel, [plane, plane, edge, edge],
        [((channels * plane_count * row_count, breadth), F32)], 0, (place,), (features,),
    )
    near, far = swapped(near, far, "gy")
    near_own, far_own = call(faces_kernel, [face, face], [], 0, (place,), (f0, f1, near, far))
    near_face, far_face = swapped(near_own, far_own, "gz")
    inner, partial, hidden_grad = call(
        inner_kernel, [cols, (lines, F32), (lines, F32)],
        [((out_channels, row_count // 2 * breadth), BF16)],
        2 * conv_flops // 3, (place,), (near_own, far_own, conv_weight, down_weight, cot),
    )
    outer, g0, g1, near, far, hidden = call(
        gate_kernel, [cols, plane, plane, edge, edge, (lines, BF16)], [],
        conv_flops // 3, (place,), (near_face, far_face, partial, hidden_grad, conv_weight),
    )
    near, far = swapped(near, far, "gy")
    near_own, far_own = call(faces_kernel, [face, face], [], 0, (place,), (g0, g1, near, far))
    near_face, far_face = swapped(near_own, far_own, "gz")

    chips = count // 2
    used = 27 * channels * channels // 128 + 4 * out_channels
    share = -(-used // (16 * count)) * 16
    half = ((chips * share, 128), BF16)
    section_out, keep, send = call(
        weight_grad_kernel, [((out_channels, cot.shape[1]), BF16), half, half],
        [((share * count, 128), BF16)], conv_flops, (place,),
        (inner, outer, g0, g1, hidden, down_weight, cot),
    )
    (terms,) = call(add_kernel, [half], [], 0, (), (keep, swap(send, "gy", 0)))
    groups = [list(range(core, count, 2)) for core in range(2)]
    exchange = functools.partial(
        lax.all_to_all, axis_name=("gz", "gy"), split_axis=0, concat_axis=0, axis_index_groups=groups, tiled=True
    )
    parts = ((chips, share, 128), BF16)
    (mine,) = call(total_kernel, [parts], [], 0, (), (exchange(terms.reshape(parts[0])),))
    sums = exchange(mine).reshape(half[0])
    other = swap(sums, "gy", 0)

    (field,) = call(
        field_kernel, [((channels * plane_count * row_count, breadth), F32)], [cols, cols], conv_flops,
        (place,), (near_own, far_own, near_face, far_face, weight_bwd),
    )
    grad_conv, grad_down = call(
        functools.partial(unpack_kernel, scale=grad_scale),
        [(conv_weight.shape, F32), (down_weight.shape, F32)], [((share * count, 128), BF16)], 0,
        (place,), (sums, other),
    )
    section_out = section_out.reshape(out_channels, plane_count // 2, -1)
    return (section_out, field.reshape(features.shape), grad_conv, grad_down)


def solution(mesh):
    return jax.shard_map(
        body,
        mesh=mesh,
        in_specs=(P(None, "gz", "gy", None), P(), P(), P(None, "gz", "gy")),
        out_specs=(P(None, "gz", "gy"), P(None, "gz", "gy", None), P(), P()),
        check_vma=False,
    )
```

```python
import functools
import math

import jax
import jax.numpy as jnp
from jax import lax
from jax.experimental import pallas as pl
from jax.experimental.pallas import tpu as pltpu
from jax.sharding import PartitionSpec as P

F32 = jnp.float32
BF16 = jnp.bfloat16
PARAMS = pltpu.CompilerParams(vmem_limit_bytes=24 * 1024 * 1024)


def call(kernel, outs, scratch, flops, operands):
    moved = sum(x.size * x.dtype.itemsize for x in operands)
    moved += sum(math.prod(s) * jnp.dtype(d).itemsize for s, d in outs)
    vmem = pl.BlockSpec(memory_space=pltpu.VMEM)
    return pl.pallas_call(
        kernel,
        out_shape=[jax.ShapeDtypeStruct(s, d) for s, d in outs],
        in_specs=[vmem] * len(operands),
        out_specs=[vmem] * len(outs),
        scratch_shapes=[pltpu.VMEM(s, d) for s, d in scratch],
        compiler_params=PARAMS,
        cost_estimate=pl.CostEstimate(flops=flops, bytes_accessed=moved, transcendentals=0),
    )(*operands)


def is_even(axis):
    return lax.rem(lax.axis_index(axis), 2) == 0


def choose(cond, yes, no):
    return jnp.where(jnp.broadcast_to(cond, yes.shape), yes, no)


def lines_kernel(f_ref, near_ref, far_ref, wide):
    channels, planes, rows, breadth = f_ref.shape
    wide[...] = f_ref[...].astype(F32).reshape(channels * planes * rows, breadth)
    even = is_even("gz")
    for y in range(rows):
        low, high = (
            wide[pl.ds(z * rows + y, channels, stride=planes * rows), :].astype(BF16) for z in range(2)
        )
        near_ref[y] = choose(even, high, low)
        far_ref[y] = choose(even, low, high)


def edges_kernel(near, far, near_in, far_in, near_ref, far_ref):
    rows = near.shape[0]
    even_z, even_y = is_even("gz"), is_even("gy")

    def put(p, one, other):
        first = choose(even_z, one[0], other[0])
        last = choose(even_z, one[rows - 1], other[rows - 1])
        near_ref[p] = choose(even_y, last, first)
        far_ref[p] = choose(even_y, first, last)

    put(0, far_in, near_in)
    put(1, far, near)
    put(2, near, far)
    put(3, near_in, far_in)


def put_columns(cols, p, q, line):
    channels = line.shape[0]
    wide = line.astype(F32)
    cols[p, q, 0:channels] = pltpu.roll(wide, 1, 1).astype(BF16)
    cols[p, q, channels : 2 * channels] = line
    cols[p, q, 2 * channels : 3 * channels] = pltpu.roll(wide, line.shape[1] - 1, 1).astype(BF16)


def fill_columns(cols, near, far):
    rows = near.shape[0]
    even = is_even("gz")

    def step(y, carry):
        put_columns(cols, 0, y + 1, choose(even, far[y], near[y]))
        put_columns(cols, 1, y + 1, choose(even, near[y], far[y]))
        return carry

    lax.fori_loop(0, rows, step, 0, unroll=2)
    for p in range(2):
        for q in (0, rows + 1):
            cols[p, q] = jnp.zeros(cols.shape[2:], BF16)


def fill_edges(cols, near, far):
    even = is_even("gy")
    for p in range(4):
        put_columns(cols, p, 0, choose(even, far[p], near[p]))
        put_columns(cols, p, 1, choose(even, near[p], far[p]))


def dot(lhs, rhs):
    return jnp.dot(lhs, rhs, preferred_element_type=F32)


def taps(w_ref, b, first, last):
    return jnp.concatenate([w_ref[a, b] for a in range(first, last)], axis=0)


def window(cols, p, q):
    return jnp.concatenate([cols[p, q], cols[p, q + 1]], axis=1)


def inner_terms(cols, w_ref, y):
    acc = None
    for b in range(3):
        for p in range(2):
            term = dot(taps(w_ref, b, p, p + 2), window(cols, p, y + b))
            acc = term if acc is None else acc + term
    half = acc.shape[0] // 2
    return acc[half:], acc[:half]


def outer_terms(cols, w_ref, y):
    lower = upper = None
    for b in range(3):
        low, high = dot(w_ref[0, b], window(cols, 0, y + b)), dot(w_ref[2, b], window(cols, 1, y + b))
        lower = low if lower is None else lower + low
        upper = high if upper is None else upper + high
    return lower, upper


def edge_terms(edges, w_ref, side):
    b = 2 * side
    half = w_ref.shape[2]
    acc = dot(taps(w_ref, b, 0, 2), edges[1, side]) + dot(taps(w_ref, b, 1, 3), edges[2, side])
    return acc[half:] + dot(w_ref[0, b], edges[0, side]), acc[:half] + dot(w_ref[2, b], edges[3, side])


def inner_kernel(near, far, w_ref, d_ref, cot_ref, cols, acc_ref, grad_ref, up):
    rows, channels, breadth = near.shape
    fill_columns(cols, near, far)
    source = lax.broadcasted_iota(jnp.int32, (breadth, 2 * breadth), 0)
    target = lax.broadcasted_iota(jnp.int32, (breadth, 2 * breadth), 1)
    spread = jnp.where(source == target // 2, 1.0, 0.0).astype(BF16)
    for pair in range(rows // 4):
        both = dot(cot_ref[:, pair * breadth : (pair + 1) * breadth], spread)
        up[:, 2 * pair * breadth : 2 * (pair + 1) * breadth] = both.astype(BF16)
    even = lax.broadcasted_iota(jnp.int32, (channels, breadth), 1) % 2 == 0
    for a in range(2):
        for b in range(2):
            terms = lax.dot_general(d_ref[a, b], up[...], (((0,), (0,)), ((), ())), preferred_element_type=F32)
            for t in range(rows // 2):
                part = terms[:, t * breadth : (t + 1) * breadth]
                grad_ref[a, 2 * t + b] = jnp.where(even, part[0:channels], part[channels:])

    def step(t, carry):
        y = 2 * t
        for z, lines in enumerate(inner_terms(cols, w_ref, y)):
            for b in range(2):
                acc_ref[z, y + b] = lines[:, b * breadth : (b + 1) * breadth]
        return carry

    lax.fori_loop(0, rows // 2, step, 0)


def outer_kernel(near, far, w_ref, acc_ref, cols, out_ref):
    rows, channels, breadth = near.shape
    fill_columns(cols, near, far)

    def step(t, carry):
        y = 2 * t
        for z, lines in enumerate(outer_terms(cols, w_ref, y)):
            for b in range(2):
                out_ref[z, y + b] = acc_ref[z, y + b] + lines[:, b * breadth : (b + 1) * breadth]
        return carry

    lax.fori_loop(0, rows // 2, step, 0)


def gate_kernel(near, far, acc_ref, grad_ref, w_ref, edges, near_ref, far_ref, h_ref):
    rows, channels, breadth = acc_ref.shape[1:]
    fill_edges(edges, near, far)
    sides = [edge_terms(edges, w_ref, side) for side in range(2)]
    even = is_even("gz")

    def gate(y, extra):
        found = []
        for z in range(2):
            preact = acc_ref[z, y] if extra is None else acc_ref[z, y] + extra[z]
            sig = 1.0 / (1.0 + jnp.exp(-preact))
            h_ref[z, y] = (preact * sig).astype(BF16)
            found.append((grad_ref[z, y] * sig * (1.0 + preact * (1.0 - sig))).astype(BF16))
        near_ref[y] = choose(even, found[1], found[0])
        far_ref[y] = choose(even, found[0], found[1])

    gate(0, sides[0])
    for y in range(1, rows - 1):
        gate(y, None)
    gate(rows - 1, sides[1])


def weight_grad_kernel(inner, outer, edges, near, far, h_ref, d_ref, cot_ref, out_ref, keep, send, packed):
    rows, channels, breadth = near.shape
    across = (((1,), (1,)), ((), ()))
    even = is_even("gz")
    low = [choose(even, far[y], near[y]) for y in range(rows)]
    high = [choose(even, near[y], far[y]) for y in range(rows)]
    gates = jnp.concatenate([jnp.concatenate(low, axis=1), jnp.concatenate(high, axis=1)], axis=0)

    def columns(p, q):
        if q in (0, rows + 1):
            return edges[p, 0 if q == 0 else 1]
        return inner[p - 1, q] if p in (1, 2) else outer[p // 3, q]

    lane = lax.broadcasted_iota(jnp.int32, (channels // 2, breadth), 1)
    for b in range(3):
        parts = []
        for p in range(4):
            across_rows = jnp.concatenate([columns(p, y + b) for y in range(rows)], axis=1)
            lhs = gates[0:channels] if p == 0 else gates[channels:] if p == 3 else gates
            parts.append(lax.dot_general(lhs, across_rows, across, preferred_element_type=F32))
        for a in range(3):
            low = parts[a][0:channels]
            high = parts[a + 1] if a == 2 else parts[a + 1][channels:]
            total = low + high
            base = (a * 3 + b) * 3 * channels // 2
            packed[base : base + channels] = total[:, 0:breadth].astype(BF16)
            rest = jnp.concatenate([total[:, breadth:], total[:, breadth:]], axis=1)
            mix = jnp.where(lane < channels, rest[0 : channels // 2], rest[channels // 2 :])
            packed[base + channels : base + 3 * channels // 2] = mix.astype(BF16)
    base = 9 * 3 * channels // 2
    source = lax.broadcasted_iota(jnp.int32, (2 * breadth, 2 * breadth), 0)
    target = lax.broadcasted_iota(jnp.int32, (2 * breadth, 2 * breadth), 1)
    wanted = 2 * (target % breadth) + target // breadth
    pick = jnp.where(source == wanted, 1.0, 0.0).astype(BF16)
    coarse = None
    for a in range(2):
        for b in range(2):
            pairs = []
            for pair in range(rows // 4):
                both = jnp.concatenate([h_ref[a, 4 * pair + b], h_ref[a, 4 * pair + 2 + b]], axis=1)
                pairs.append(jnp.dot(both, pick, preferred_element_type=F32).astype(BF16))
            hidden = jnp.concatenate(
                [jnp.concatenate([x[:, e * breadth : (e + 1) * breadth] for x in pairs], axis=1) for e in range(2)],
                axis=0,
            )
            term = jnp.dot(d_ref[a, b], hidden, preferred_element_type=F32)
            coarse = term if coarse is None else coarse + term
            down = lax.dot_general(cot_ref[...], hidden, across, preferred_element_type=F32)
            at = base + (2 * a + b) * d_ref.shape[2]
            packed[at : at + d_ref.shape[2]] = down.astype(BF16)
    out_ref[...] = coarse.astype(BF16)
    end = base + 4 * d_ref.shape[2]
    if end < packed.shape[0]:
        packed[end:] = jnp.zeros((packed.shape[0] - end, packed.shape[1]), BF16)
    half = packed.shape[0] // 2
    core = lax.rem(lax.axis_index("gy"), 2)
    keep[...] = packed[pl.ds(pl.multiple_of(core * half, 16), half)]
    send[...] = packed[pl.ds(pl.multiple_of((1 - core) * half, 16), half)]


def add_kernel(x, y, out):
    out[...] = (x[...].astype(F32) + y[...].astype(F32)).astype(BF16)


def total_kernel(terms, out):
    total = jnp.sum(terms[...].astype(F32), axis=0).astype(BF16)
    for member in range(out.shape[0]):
        out[member] = total


def field_kernel(near, far, near_in, far_in, w_ref, acc_ref, inner, outer):
    rows, channels, breadth = near.shape
    fill_columns(inner, near, far)
    fill_columns(outer, near_in, far_in)

    def step(t, carry):
        y = 2 * t
        own = inner_terms(inner, w_ref, y)
        rest = outer_terms(outer, w_ref, y)
        for z in range(2):
            total = own[z] + rest[z]
            for b in range(2):
                acc_ref[z, y + b] = total[:, b * breadth : (b + 1) * breadth]
        return carry

    lax.fori_loop(0, rows // 2, step, 0)


def field_edges_kernel(near, far, acc_ref, w_ref, out_ref, edges):
    rows, channels, breadth = acc_ref.shape[1:]
    fill_edges(edges, near, far)
    sides = [edge_terms(edges, w_ref, side) for side in range(2)]
    for z in range(2):
        for y in range(rows):
            line = acc_ref[z, y]
            if y in (0, rows - 1):
                line = line + sides[0 if y == 0 else 1][z]
            out_ref[pl.ds(z * rows + y, channels, stride=2 * rows), :] = line


def unpack_kernel(mine, other, conv_ref, down_ref, sums_ref, *, scale):
    half = mine.shape[0]
    core = lax.rem(lax.axis_index("gy"), 2)
    sums_ref[pl.ds(pl.multiple_of(core * half, 16), half)] = mine[...]
    sums_ref[pl.ds(pl.multiple_of((1 - core) * half, 16), half)] = other[...]
    channels = conv_ref.shape[2]
    for a in range(3):
        for b in range(3):
            base = (a * 3 + b) * 3 * channels // 2
            conv_ref[a, b, :, 0 : 2 * channels] = sums_ref[base : base + channels].astype(F32) * scale
            rest = sums_ref[base + channels : base + 3 * channels // 2].astype(F32) * scale
            conv_ref[a, b, 0 : channels // 2, 2 * channels :] = rest[:, 0:channels]
            conv_ref[a, b, channels // 2 :, 2 * channels :] = rest[:, channels:]
    base = 9 * 3 * channels // 2
    height = down_ref.shape[2]
    for a in range(2):
        for b in range(2):
            at = base + (2 * a + b) * height
            down_ref[a, b] = sums_ref[at : at + height].astype(F32) * scale


def swap(cells, axis, low):
    count = lax.axis_size(axis)
    pairs = [(i % count, (i + 1) % count) for i in range(low, low + count, 2)]
    return lax.ppermute(cells, axis, pairs + [(b, a) for a, b in pairs])


def swapped(near, far, axis):
    return swap(near, axis, 0), swap(far, axis, 1)


def body(features, conv_weight, down_weight, cotangent):
    channels, plane_count, row_count, breadth = features.shape
    out_channels = down_weight.shape[2]
    count = lax.axis_size("gz") * lax.axis_size("gy")
    grad_scale = 1.0 / math.sqrt(plane_count * row_count * breadth * count)
    turned = conv_weight.reshape(3, 3, channels, 3, channels)[::-1, ::-1, :, ::-1]
    weight_bwd = turned.transpose(0, 1, 4, 3, 2).reshape(3, 3, channels, 3 * channels)
    cot = cotangent.reshape(out_channels, -1)
    plane = ((row_count, channels, breadth), BF16)
    edge = ((plane_count + 2, channels, breadth), BF16)
    cols = ((plane_count, row_count + 2, 3 * channels, breadth), BF16)
    edge_cols = ((plane_count + 2, 2, 3 * channels, breadth), BF16)
    lines = (plane_count, row_count, channels, breadth)
    conv_flops = 2 * 27 * channels * channels * plane_count * row_count * breadth

    own = call(
        lines_kernel, [plane, plane], [((channels * plane_count * row_count, breadth), F32)], 0, (features,)
    )
    outside = swapped(*own, "gz")
    inner, acc, hidden_grad = call(
        inner_kernel, [cols, (lines, F32), (lines, F32)],
        [((out_channels, row_count // 2 * breadth), BF16)],
        2 * conv_flops // 3, (*own, conv_weight, down_weight, cot),
    )
    near, far, acc = lax.optimization_barrier((*outside, acc))
    outside = (near, far)
    beside = swapped(*call(edges_kernel, [edge, edge], [], 0, (*own, *outside)), "gy")
    outer, acc = call(
        outer_kernel, [cols, (lines, F32)], [], conv_flops // 3, (*outside, conv_weight, acc)
    )
    edges, near, far, hidden = call(
        gate_kernel, [edge_cols, plane, plane, (lines, BF16)], [], conv_flops // 10,
        (*beside, acc, hidden_grad, conv_weight),
    )
    gates = (near, far)

    chips = count // 2
    used = 27 * channels * channels // 128 + 4 * out_channels
    share = -(-used // (16 * count)) * 16
    half = ((chips * share, 128), BF16)
    section_out, keep, send = call(
        weight_grad_kernel, [((out_channels, cot.shape[1]), BF16), half, half],
        [((share * count, 128), BF16)], conv_flops,
        (inner, outer, edges, *gates, hidden, down_weight, cot),
    )
    (terms,) = call(add_kernel, [half], [], 0, (keep, swap(send, "gy", 0)))
    groups = [list(range(core, count, 2)) for core in range(2)]
    exchange = functools.partial(
        lax.all_to_all, axis_name=("gz", "gy"), split_axis=0, concat_axis=0, axis_index_groups=groups, tiled=True
    )
    parts = ((chips, share, 128), BF16)
    terms, near, far = lax.optimization_barrier((terms, *gates))
    gates = (near, far)
    terms = exchange(terms.reshape(parts[0]))
    outside = swapped(*gates, "gz")
    terms, near, far = lax.optimization_barrier((terms, *outside))
    outside = (near, far)
    (mine,) = call(total_kernel, [parts], [], 0, (terms,))
    sends = call(edges_kernel, [edge, edge], [], 0, (*gates, *outside))
    mine, near, far = lax.optimization_barrier((mine, *sends))
    sums = exchange(mine).reshape(half[0])
    beside = swapped(near, far, "gy")
    (acc,) = call(
        field_kernel, [(lines, F32)], [cols, cols], conv_flops, (*gates, *outside, weight_bwd)
    )
    (field,) = call(
        field_edges_kernel, [((channels * plane_count * row_count, breadth), F32)], [edge_cols],
        conv_flops // 10, (*beside, acc, weight_bwd),
    )
    sums, field = lax.optimization_barrier((sums, field))
    grad_conv, grad_down = call(
        functools.partial(unpack_kernel, scale=grad_scale),
        [(conv_weight.shape, F32), (down_weight.shape, F32)], [((share * count, 128), BF16)], 0,
        (sums, swap(sums, "gy", 0)),
    )
    section_out = section_out.reshape(out_channels, plane_count // 2, -1)
    return (section_out, field.reshape(features.shape), grad_conv, grad_down)


def solution(mesh):
    return jax.shard_map(
        body,
        mesh=mesh,
        in_specs=(P(None, "gz", "gy", None), P(), P(), P(None, "gz", "gy")),
        out_specs=(P(None, "gz", "gy"), P(None, "gz", "gy", None), P(), P()),
        check_vma=False,
    )
```

```python
import functools
import math

import jax
import jax.numpy as jnp
from jax import lax
from jax.experimental import pallas as pl
from jax.experimental.pallas import tpu as pltpu
from jax.sharding import PartitionSpec as P

F32 = jnp.float32
BF16 = jnp.bfloat16
PARAMS = pltpu.CompilerParams(vmem_limit_bytes=24 * 1024 * 1024)


def call(kernel, outs, scratch, flops, operands):
    moved = sum(x.size * x.dtype.itemsize for x in operands)
    moved += sum(math.prod(s) * jnp.dtype(d).itemsize for s, d in outs)
    vmem = pl.BlockSpec(memory_space=pltpu.VMEM)
    return pl.pallas_call(
        kernel,
        out_shape=[jax.ShapeDtypeStruct(s, d) for s, d in outs],
        in_specs=[vmem] * len(operands),
        out_specs=[vmem] * len(outs),
        scratch_shapes=[pltpu.VMEM(s, d) for s, d in scratch],
        compiler_params=PARAMS,
        cost_estimate=pl.CostEstimate(flops=flops, bytes_accessed=moved, transcendentals=0),
    )(*operands)


def is_even(axis):
    return lax.rem(lax.axis_index(axis), 2) == 0


def choose(cond, yes, no):
    return jnp.where(jnp.broadcast_to(cond, yes.shape), yes, no)


def lines_kernel(f_ref, near_ref, far_ref, wide):
    channels, planes, rows, breadth = f_ref.shape
    wide[...] = f_ref[...].astype(F32).reshape(channels * planes * rows, breadth)
    even = is_even("gz")
    for y in range(rows):
        low, high = (
            wide[pl.ds(z * rows + y, channels, stride=planes * rows), :].astype(BF16) for z in range(2)
        )
        near_ref[y] = choose(even, high, low)
        far_ref[y] = choose(even, low, high)


def edges_kernel(near, far, near_in, far_in, near_ref, far_ref):
    rows = near.shape[0]
    even_z, even_y = is_even("gz"), is_even("gy")

    def put(p, one, other):
        first = choose(even_z, one[0], other[0])
        last = choose(even_z, one[rows - 1], other[rows - 1])
        near_ref[p] = choose(even_y, last, first)
        far_ref[p] = choose(even_y, first, last)

    put(0, far_in, near_in)
    put(1, far, near)
    put(2, near, far)
    put(3, near_in, far_in)


def put_columns(cols, p, q, line):
    channels = line.shape[0]
    wide = line.astype(F32)
    cols[p, q, 0:channels] = pltpu.roll(wide, 1, 1).astype(BF16)
    cols[p, q, channels : 2 * channels] = line
    cols[p, q, 2 * channels : 3 * channels] = pltpu.roll(wide, line.shape[1] - 1, 1).astype(BF16)


def fill_columns(cols, near, far):
    rows = near.shape[0]
    even = is_even("gz")

    def step(y, carry):
        put_columns(cols, 0, y + 1, choose(even, far[y], near[y]))
        put_columns(cols, 1, y + 1, choose(even, near[y], far[y]))
        return carry

    lax.fori_loop(0, rows, step, 0, unroll=2)
    for p in range(2):
        for q in (0, rows + 1):
            cols[p, q] = jnp.zeros(cols.shape[2:], BF16)


def fill_edges(cols, near, far):
    even = is_even("gy")
    for p in range(4):
        put_columns(cols, p, 0, choose(even, far[p], near[p]))
        put_columns(cols, p, 1, choose(even, near[p], far[p]))


def dot(lhs, rhs):
    return jnp.dot(lhs, rhs, preferred_element_type=F32)


def taps(w_ref, b, first, last):
    return jnp.concatenate([w_ref[a, b] for a in range(first, last)], axis=0)


def window(cols, p, q):
    return jnp.concatenate([cols[p, q], cols[p, q + 1]], axis=1)


def inner_terms(cols, w_ref, y):
    acc = None
    for b in range(3):
        for p in range(2):
            term = dot(taps(w_ref, b, p, p + 2), window(cols, p, y + b))
            acc = term if acc is None else acc + term
    half = acc.shape[0] // 2
    return acc[half:], acc[:half]


def outer_terms(cols, w_ref, y):
    lower = upper = None
    for b in range(3):
        low, high = dot(w_ref[0, b], window(cols, 0, y + b)), dot(w_ref[2, b], window(cols, 1, y + b))
        lower = low if lower is None else lower + low
        upper = high if upper is None else upper + high
    return lower, upper


def edge_terms(edges, w_ref, side):
    b = 2 * side
    half = w_ref.shape[2]
    acc = dot(taps(w_ref, b, 0, 2), edges[1, side]) + dot(taps(w_ref, b, 1, 3), edges[2, side])
    return acc[half:] + dot(w_ref[0, b], edges[0, side]), acc[:half] + dot(w_ref[2, b], edges[3, side])


def inner_kernel(near, far, w_ref, d_ref, cot_ref, cols, acc_ref, grad_ref, up):
    rows, channels, breadth = near.shape
    fill_columns(cols, near, far)
    source = lax.broadcasted_iota(jnp.int32, (breadth, 2 * breadth), 0)
    target = lax.broadcasted_iota(jnp.int32, (breadth, 2 * breadth), 1)
    spread = jnp.where(source == target // 2, 1.0, 0.0).astype(BF16)
    for pair in range(rows // 4):
        both = dot(cot_ref[:, pair * breadth : (pair + 1) * breadth], spread)
        up[:, 2 * pair * breadth : 2 * (pair + 1) * breadth] = both.astype(BF16)
    even = lax.broadcasted_iota(jnp.int32, (channels, breadth), 1) % 2 == 0
    for a in range(2):
        for b in range(2):
            terms = lax.dot_general(d_ref[a, b], up[...], (((0,), (0,)), ((), ())), preferred_element_type=F32)
            for t in range(rows // 2):
                part = terms[:, t * breadth : (t + 1) * breadth]
                grad_ref[a, 2 * t + b] = jnp.where(even, part[0:channels], part[channels:])

    def step(t, carry):
        y = 2 * t
        for z, lines in enumerate(inner_terms(cols, w_ref, y)):
            for b in range(2):
                acc_ref[z, y + b] = lines[:, b * breadth : (b + 1) * breadth]
        return carry

    lax.fori_loop(0, rows // 2, step, 0)


def outer_kernel(near, far, w_ref, acc_ref, cols, out_ref):
    rows, channels, breadth = near.shape
    fill_columns(cols, near, far)

    def step(t, carry):
        y = 2 * t
        for z, lines in enumerate(outer_terms(cols, w_ref, y)):
            for b in range(2):
                out_ref[z, y + b] = acc_ref[z, y + b] + lines[:, b * breadth : (b + 1) * breadth]
        return carry

    lax.fori_loop(0, rows // 2, step, 0)


def gate_kernel(near, far, acc_ref, grad_ref, w_ref, edges, near_ref, far_ref, h_ref):
    rows, channels, breadth = acc_ref.shape[1:]
    fill_edges(edges, near, far)
    sides = [edge_terms(edges, w_ref, side) for side in range(2)]
    even = is_even("gz")

    def gate(y, extra):
        found = []
        for z in range(2):
            preact = acc_ref[z, y] if extra is None else acc_ref[z, y] + extra[z]
            sig = 1.0 / (1.0 + jnp.exp(-preact))
            h_ref[z, y] = (preact * sig).astype(BF16)
            found.append((grad_ref[z, y] * sig * (1.0 + preact * (1.0 - sig))).astype(BF16))
        near_ref[y] = choose(even, found[1], found[0])
        far_ref[y] = choose(even, found[0], found[1])

    gate(0, sides[0])
    for y in range(1, rows - 1):
        gate(y, None)
    gate(rows - 1, sides[1])


def weight_grad_kernel(inner, outer, edges, near, far, h_ref, d_ref, cot_ref, out_ref, keep, send, packed):
    rows, channels, breadth = near.shape
    across = (((1,), (1,)), ((), ()))
    even = is_even("gz")
    low = [choose(even, far[y], near[y]) for y in range(rows)]
    high = [choose(even, near[y], far[y]) for y in range(rows)]
    gates = jnp.concatenate([jnp.concatenate(low, axis=1), jnp.concatenate(high, axis=1)], axis=0)

    def columns(p, q):
        if q in (0, rows + 1):
            return edges[p, 0 if q == 0 else 1]
        return inner[p - 1, q] if p in (1, 2) else outer[p // 3, q]

    lane = lax.broadcasted_iota(jnp.int32, (channels // 2, breadth), 1)
    for b in range(3):
        parts = []
        for p in range(4):
            across_rows = jnp.concatenate([columns(p, y + b) for y in range(rows)], axis=1)
            lhs = gates[0:channels] if p == 0 else gates[channels:] if p == 3 else gates
            parts.append(lax.dot_general(lhs, across_rows, across, preferred_element_type=F32))
        for a in range(3):
            low = parts[a][0:channels]
            high = parts[a + 1] if a == 2 else parts[a + 1][channels:]
            total = low + high
            base = (a * 3 + b) * 3 * channels // 2
            packed[base : base + channels] = total[:, 0:breadth]
            rest = jnp.concatenate([total[:, breadth:], total[:, breadth:]], axis=1)
            mix = jnp.where(lane < channels, rest[0 : channels // 2], rest[channels // 2 :])
            packed[base + channels : base + 3 * channels // 2] = mix
    base = 9 * 3 * channels // 2
    source = lax.broadcasted_iota(jnp.int32, (2 * breadth, 2 * breadth), 0)
    target = lax.broadcasted_iota(jnp.int32, (2 * breadth, 2 * breadth), 1)
    wanted = 2 * (target % breadth) + target // breadth
    pick = jnp.where(source == wanted, 1.0, 0.0).astype(BF16)
    coarse = None
    for a in range(2):
        for b in range(2):
            pairs = []
            for pair in range(rows // 4):
                both = jnp.concatenate([h_ref[a, 4 * pair + b], h_ref[a, 4 * pair + 2 + b]], axis=1)
                pairs.append(jnp.dot(both, pick, preferred_element_type=F32).astype(BF16))
            hidden = jnp.concatenate(
                [jnp.concatenate([x[:, e * breadth : (e + 1) * breadth] for x in pairs], axis=1) for e in range(2)],
                axis=0,
            )
            term = jnp.dot(d_ref[a, b], hidden, preferred_element_type=F32)
            coarse = term if coarse is None else coarse + term
            down = lax.dot_general(cot_ref[...], hidden, across, preferred_element_type=F32)
            at = base + (2 * a + b) * d_ref.shape[2]
            packed[at : at + d_ref.shape[2]] = down
    out_ref[...] = coarse.astype(BF16)
    end = base + 4 * d_ref.shape[2]
    if end < packed.shape[0]:
        packed[end:] = jnp.zeros((packed.shape[0] - end, packed.shape[1]), F32)
    half = packed.shape[0] // 2
    split(packed, keep, send, half, "gy", 1)


def side_of(axis, bit):
    return lax.rem(lax.axis_index(axis) // bit, 2)


def part(side, rows):
    return pl.ds(pl.multiple_of(side * rows, 16), rows)


def split(packed, keep, send, half, axis, bit):
    side = side_of(axis, bit)
    keep[...] = packed[part(side, half)]
    send[...] = packed[part(1 - side, half)].astype(BF16)


def halve_kernel(mine, other, keep, send, total, *, axis, bit):
    total[...] = mine[...] + other[...].astype(F32)
    split(total, keep, send, total.shape[0] // 2, axis, bit)


def add_kernel(x, y, out):
    out[...] = (x[...].astype(F32) + y[...].astype(F32)).astype(BF16)


def join_kernel(mine, other, out, *, axis, bit):
    rows = mine.shape[0]
    side = side_of(axis, bit)
    out[part(side, rows)] = mine[...]
    out[part(1 - side, rows)] = other[...]


def field_kernel(near, far, near_in, far_in, w_ref, acc_ref, inner, outer):
    rows, channels, breadth = near.shape
    fill_columns(inner, near, far)
    fill_columns(outer, near_in, far_in)

    def step(t, carry):
        y = 2 * t
        own = inner_terms(inner, w_ref, y)
        rest = outer_terms(outer, w_ref, y)
        for z in range(2):
            total = own[z] + rest[z]
            for b in range(2):
                acc_ref[z, y + b] = total[:, b * breadth : (b + 1) * breadth]
        return carry

    lax.fori_loop(0, rows // 2, step, 0)


def field_edges_kernel(near, far, acc_ref, w_ref, out_ref, edges):
    rows, channels, breadth = acc_ref.shape[1:]
    fill_edges(edges, near, far)
    sides = [edge_terms(edges, w_ref, side) for side in range(2)]
    for z in range(2):
        for y in range(rows):
            line = acc_ref[z, y]
            if y in (0, rows - 1):
                line = line + sides[0 if y == 0 else 1][z]
            out_ref[pl.ds(z * rows + y, channels, stride=2 * rows), :] = line


def unpack_kernel(mine, other, conv_ref, down_ref, sums_ref, *, scale):
    join_kernel(mine, other, sums_ref, axis="gy", bit=1)
    channels = conv_ref.shape[2]
    for a in range(3):
        for b in range(3):
            base = (a * 3 + b) * 3 * channels // 2
            conv_ref[a, b, :, 0 : 2 * channels] = sums_ref[base : base + channels].astype(F32) * scale
            rest = sums_ref[base + channels : base + 3 * channels // 2].astype(F32) * scale
            conv_ref[a, b, 0 : channels // 2, 2 * channels :] = rest[:, 0:channels]
            conv_ref[a, b, channels // 2 :, 2 * channels :] = rest[:, channels:]
    base = 9 * 3 * channels // 2
    height = down_ref.shape[2]
    for a in range(2):
        for b in range(2):
            at = base + (2 * a + b) * height
            down_ref[a, b] = sums_ref[at : at + height].astype(F32) * scale


def swap(cells, axis, low):
    count = lax.axis_size(axis)
    pairs = [(i % count, (i + 1) % count) for i in range(low, low + count, 2)]
    return lax.ppermute(cells, axis, pairs + [(b, a) for a, b in pairs])


def flip(cells, axis, bit):
    return lax.ppermute(cells, axis, [(i, i ^ bit) for i in range(lax.axis_size(axis))])


def tied(first, *others):
    found = lax.optimization_barrier((first, *others))
    return found[0], tuple(found[1:])


def swapped(near, far, axis):
    return swap(near, axis, 0), swap(far, axis, 1)


def body(features, conv_weight, down_weight, cotangent):
    channels, plane_count, row_count, breadth = features.shape
    out_channels = down_weight.shape[2]
    count = lax.axis_size("gz") * lax.axis_size("gy")
    grad_scale = 1.0 / math.sqrt(plane_count * row_count * breadth * count)
    turned = conv_weight.reshape(3, 3, channels, 3, channels)[::-1, ::-1, :, ::-1]
    weight_bwd = turned.transpose(0, 1, 4, 3, 2).reshape(3, 3, channels, 3 * channels)
    cot = cotangent.reshape(out_channels, -1)
    plane = ((row_count, channels, breadth), BF16)
    edge = ((plane_count + 2, channels, breadth), BF16)
    cols = ((plane_count, row_count + 2, 3 * channels, breadth), BF16)
    edge_cols = ((plane_count + 2, 2, 3 * channels, breadth), BF16)
    lines = (plane_count, row_count, channels, breadth)
    conv_flops = 2 * 27 * channels * channels * plane_count * row_count * breadth

    own = call(
        lines_kernel, [plane, plane], [((channels * plane_count * row_count, breadth), F32)], 0, (features,)
    )
    outside = swapped(*own, "gz")
    inner, acc, hidden_grad = call(
        inner_kernel, [cols, (lines, F32), (lines, F32)],
        [((out_channels, row_count // 2 * breadth), BF16)],
        2 * conv_flops // 3, (*own, conv_weight, down_weight, cot),
    )
    near, far, acc = lax.optimization_barrier((*outside, acc))
    outside = (near, far)
    beside = swapped(*call(edges_kernel, [edge, edge], [], 0, (*own, *outside)), "gy")
    outer, acc = call(
        outer_kernel, [cols, (lines, F32)], [], conv_flops // 3, (*outside, conv_weight, acc)
    )
    edges, near, far, hidden = call(
        gate_kernel, [edge_cols, plane, plane, (lines, BF16)], [], conv_flops // 10,
        (*beside, acc, hidden_grad, conv_weight),
    )
    gates = (near, far)

    used = 27 * channels * channels // 128 + 4 * out_channels
    rows = -(-used // 128) * 128
    section_out, keep, send = call(
        weight_grad_kernel,
        [((out_channels, cot.shape[1]), BF16), ((rows // 2, 128), F32), ((rows // 2, 128), BF16)],
        [((rows, 128), F32)], conv_flops,
        (inner, outer, edges, *gates, hidden, down_weight, cot),
    )
    keep, gates = tied(keep, *gates)
    near, far = gates
    near_in = swap(near, "gz", 0)
    for level, (axis, bit) in enumerate((("gy", 2), ("gz", 1))):
        size = rows >> (level + 2)
        mine, got = keep, flip(send, *(("gy", 1), ("gy", 2))[level])
        keep, send = call(
            functools.partial(halve_kernel, axis=axis, bit=bit),
            [((size, 128), F32), ((size, 128), BF16)], [((2 * size, 128), F32)], 0, (mine, got),
        )
        if level == 0:
            keep, (far,) = tied(keep, far)
            far_in = swap(far, "gz", 1)
    shard = ((rows // 8, 128), BF16)
    (sums,) = call(add_kernel, [shard], [], 0, (keep, flip(send, "gz", 1)))
    sums, outside = tied(sums, near_in, far_in)
    sends = call(edges_kernel, [edge, edge], [], 0, (*gates, *outside))
    beside = swapped(*sends, "gy")
    (acc,) = call(
        field_kernel, [(lines, F32)], [cols, cols], conv_flops, (*gates, *outside, weight_bwd)
    )
    wide = [("gy", 1 << k) for k in range(2, lax.axis_size("gy").bit_length() - 1)]
    wide += [("gz", 1 << k) for k in range(1, lax.axis_size("gz").bit_length() - 1)]
    for axis, bit in wide:
        (sums,) = call(add_kernel, [shard], [], 0, (sums, flip(sums, axis, bit)))
    sums, beside = tied(sums, *beside)
    (sums,) = call(
        functools.partial(join_kernel, axis="gz", bit=1), [((rows // 4, 128), BF16)], [], 0,
        (sums, flip(sums, "gz", 1)),
    )
    sums, (acc,) = tied(sums, acc)
    (field,) = call(
        field_edges_kernel, [((channels * plane_count * row_count, breadth), F32)], [edge_cols],
        conv_flops // 10, (*beside, acc, weight_bwd),
    )
    (sums,) = call(
        functools.partial(join_kernel, axis="gy", bit=2), [((rows // 2, 128), BF16)], [], 0,
        (sums, flip(sums, "gy", 2)),
    )
    sums, (field,) = tied(sums, field)
    grad_conv, grad_down = call(
        functools.partial(unpack_kernel, scale=grad_scale),
        [(conv_weight.shape, F32), (down_weight.shape, F32)], [((rows, 128), BF16)], 0,
        (sums, flip(sums, "gy", 1)),
    )
    section_out = section_out.reshape(out_channels, plane_count // 2, -1)
    return (section_out, field.reshape(features.shape), grad_conv, grad_down)


def solution(mesh):
    return jax.shard_map(
        body,
        mesh=mesh,
        in_specs=(P(None, "gz", "gy", None), P(), P(), P(None, "gz", "gy")),
        out_specs=(P(None, "gz", "gy"), P(None, "gz", "gy", None), P(), P()),
        check_vma=False,
    )
```

```python
import functools
import math

import jax
import jax.numpy as jnp
from jax import lax
from jax.experimental import pallas as pl
from jax.experimental.pallas import tpu as pltpu
from jax.sharding import PartitionSpec as P

F32 = jnp.float32
BF16 = jnp.bfloat16
PARAMS = pltpu.CompilerParams(vmem_limit_bytes=24 * 1024 * 1024)


def call(kernel, outs, scratch, flops, operands):
    moved = sum(x.size * x.dtype.itemsize for x in operands)
    moved += sum(math.prod(s) * jnp.dtype(d).itemsize for s, d in outs)
    vmem = pl.BlockSpec(memory_space=pltpu.VMEM)
    return pl.pallas_call(
        kernel,
        out_shape=[jax.ShapeDtypeStruct(s, d) for s, d in outs],
        in_specs=[vmem] * len(operands),
        out_specs=[vmem] * len(outs),
        scratch_shapes=[pltpu.VMEM(s, d) for s, d in scratch],
        compiler_params=PARAMS,
        cost_estimate=pl.CostEstimate(flops=flops, bytes_accessed=moved, transcendentals=0),
    )(*operands)


def is_even(axis):
    return lax.rem(lax.axis_index(axis), 2) == 0


def choose(cond, yes, no):
    return jnp.where(jnp.broadcast_to(cond, yes.shape), yes, no)


def lines_kernel(f_ref, near_ref, far_ref, near_row, far_row, wide):
    channels, planes, rows, breadth = f_ref.shape
    wide[...] = f_ref[...].astype(F32).reshape(channels * planes * rows, breadth)
    even, even_y = is_even("gz"), is_even("gy")
    ends = {}
    for y in (0, rows - 1, *range(1, rows - 1)):
        low, high = ends[y] = [
            wide[pl.ds(z * rows + y, channels, stride=planes * rows), :].astype(BF16) for z in range(2)
        ]
        near_ref[y] = choose(even, high, low)
        far_ref[y] = choose(even, low, high)
    for z in range(2):
        near_row[z] = choose(even_y, ends[rows - 1][z], ends[0][z])
        far_row[z] = choose(even_y, ends[0][z], ends[rows - 1][z])


def corners_kernel(near, far, near_ref, far_ref):
    even_z, even_y = is_even("gz"), is_even("gy")
    for side in range(2):
        below, above = (choose(even_y, *((far[z], near[z]) if side == 0 else (near[z], far[z]))) for z in range(2))
        near_ref[side] = choose(even_z, above, below)
        far_ref[side] = choose(even_z, below, above)


def edges_kernel(near, far, near_in, far_in, near_ref, far_ref):
    rows = near.shape[0]
    even_z, even_y = is_even("gz"), is_even("gy")

    def put(p, one, other):
        first = choose(even_z, one[0], other[0])
        last = choose(even_z, one[rows - 1], other[rows - 1])
        near_ref[p] = choose(even_y, last, first)
        far_ref[p] = choose(even_y, first, last)

    put(0, far_in, near_in)
    put(1, far, near)
    put(2, near, far)
    put(3, near_in, far_in)


def put_columns(cols, p, q, line):
    channels = line.shape[0]
    wide = line.astype(F32)
    cols[p, q, 0:channels] = pltpu.roll(wide, 1, 1).astype(BF16)
    cols[p, q, channels : 2 * channels] = line
    cols[p, q, 2 * channels : 3 * channels] = pltpu.roll(wide, line.shape[1] - 1, 1).astype(BF16)


def fill_columns(cols, near, far):
    rows = near.shape[0]
    even = is_even("gz")

    def step(y, carry):
        put_columns(cols, 0, y + 1, choose(even, far[y], near[y]))
        put_columns(cols, 1, y + 1, choose(even, near[y], far[y]))
        return carry

    lax.fori_loop(0, rows, step, 0, unroll=2)
    for p in range(2):
        for q in (0, rows + 1):
            cols[p, q] = jnp.zeros(cols.shape[2:], BF16)


def fill_edges(cols, near, far):
    even = is_even("gy")
    for p in range(4):
        put_columns(cols, p, 0, choose(even, far[p], near[p]))
        put_columns(cols, p, 1, choose(even, near[p], far[p]))


def fill_edges_and_corners(cols, near, far, near_corner, far_corner):
    even_z, even_y = is_even("gz"), is_even("gy")
    for side in range(2):
        put_columns(cols, 0, side, choose(even_z, far_corner[side], near_corner[side]))
        put_columns(cols, 3, side, choose(even_z, near_corner[side], far_corner[side]))
        for z in range(2):
            pair = (far[z], near[z]) if side == 0 else (near[z], far[z])
            put_columns(cols, z + 1, side, choose(even_y, *pair))


def dot(lhs, rhs):
    return jnp.dot(lhs, rhs, preferred_element_type=F32)


def taps(w_ref, b, first, last):
    return jnp.concatenate([w_ref[a, b] for a in range(first, last)], axis=0)


def window(cols, p, q):
    return jnp.concatenate([cols[p, q], cols[p, q + 1]], axis=1)


def inner_terms(cols, w_ref, y):
    acc = None
    for b in range(3):
        for p in range(2):
            term = dot(taps(w_ref, b, p, p + 2), window(cols, p, y + b))
            acc = term if acc is None else acc + term
    half = acc.shape[0] // 2
    return acc[half:], acc[:half]


def outer_terms(cols, w_ref, y):
    lower = upper = None
    for b in range(3):
        low, high = dot(w_ref[0, b], window(cols, 0, y + b)), dot(w_ref[2, b], window(cols, 1, y + b))
        lower = low if lower is None else lower + low
        upper = high if upper is None else upper + high
    return lower, upper


def edge_terms(edges, w_ref, side):
    b = 2 * side
    half = w_ref.shape[2]
    acc = dot(taps(w_ref, b, 0, 2), edges[1, side]) + dot(taps(w_ref, b, 1, 3), edges[2, side])
    return acc[half:] + dot(w_ref[0, b], edges[0, side]), acc[:half] + dot(w_ref[2, b], edges[3, side])


def inner_kernel(near, far, w_ref, d_ref, cot_ref, cols, acc_ref, grad_ref, up):
    rows, channels, breadth = near.shape
    fill_columns(cols, near, far)
    source = lax.broadcasted_iota(jnp.int32, (breadth, 2 * breadth), 0)
    target = lax.broadcasted_iota(jnp.int32, (breadth, 2 * breadth), 1)
    spread = jnp.where(source == target // 2, 1.0, 0.0).astype(BF16)
    for pair in range(rows // 4):
        both = dot(cot_ref[:, pair * breadth : (pair + 1) * breadth], spread)
        up[:, 2 * pair * breadth : 2 * (pair + 1) * breadth] = both.astype(BF16)
    even = lax.broadcasted_iota(jnp.int32, (channels, breadth), 1) % 2 == 0
    for a in range(2):
        for b in range(2):
            terms = lax.dot_general(d_ref[a, b], up[...], (((0,), (0,)), ((), ())), preferred_element_type=F32)
            for t in range(rows // 2):
                part = terms[:, t * breadth : (t + 1) * breadth]
                grad_ref[a, 2 * t + b] = jnp.where(even, part[0:channels], part[channels:])

    def step(t, carry):
        y = 2 * t
        for z, lines in enumerate(inner_terms(cols, w_ref, y)):
            for b in range(2):
                acc_ref[z, y + b] = lines[:, b * breadth : (b + 1) * breadth]
        return carry

    lax.fori_loop(0, rows // 2, step, 0)


def outer_kernel(near, far, w_ref, acc_ref, cols, out_ref):
    rows, channels, breadth = near.shape
    fill_columns(cols, near, far)

    def step(t, carry):
        y = 2 * t
        for z, lines in enumerate(outer_terms(cols, w_ref, y)):
            for b in range(2):
                out_ref[z, y + b] = acc_ref[z, y + b] + lines[:, b * breadth : (b + 1) * breadth]
        return carry

    lax.fori_loop(0, rows // 2, step, 0)


def gate_kernel(near, far, near_corner, far_corner, acc_ref, grad_ref, w_ref, edges, near_ref, far_ref, h_ref):
    rows, channels, breadth = acc_ref.shape[1:]
    fill_edges_and_corners(edges, near, far, near_corner, far_corner)
    sides = [edge_terms(edges, w_ref, side) for side in range(2)]
    even = is_even("gz")

    def gate(y, extra):
        found = []
        for z in range(2):
            preact = acc_ref[z, y] if extra is None else acc_ref[z, y] + extra[z]
            sig = 1.0 / (1.0 + jnp.exp(-preact))
            h_ref[z, y] = (preact * sig).astype(BF16)
            found.append((grad_ref[z, y] * sig * (1.0 + preact * (1.0 - sig))).astype(BF16))
        near_ref[y] = choose(even, found[1], found[0])
        far_ref[y] = choose(even, found[0], found[1])

    gate(0, sides[0])
    for y in range(1, rows - 1):
        gate(y, None)
    gate(rows - 1, sides[1])


def weight_grad_kernel(inner, outer, edges, near, far, h_ref, d_ref, cot_ref, out_ref, keep, send, packed):
    rows, channels, breadth = near.shape
    across = (((1,), (1,)), ((), ()))
    even = is_even("gz")
    low = [choose(even, far[y], near[y]) for y in range(rows)]
    high = [choose(even, near[y], far[y]) for y in range(rows)]
    gates = jnp.concatenate([jnp.concatenate(low, axis=1), jnp.concatenate(high, axis=1)], axis=0)

    def columns(p, q):
        if q in (0, rows + 1):
            return edges[p, 0 if q == 0 else 1]
        return inner[p - 1, q] if p in (1, 2) else outer[p // 3, q]

    lane = lax.broadcasted_iota(jnp.int32, (channels // 2, breadth), 1)
    for b in range(3):
        parts = []
        for p in range(4):
            across_rows = jnp.concatenate([columns(p, y + b) for y in range(rows)], axis=1)
            lhs = gates[0:channels] if p == 0 else gates[channels:] if p == 3 else gates
            parts.append(lax.dot_general(lhs, across_rows, across, preferred_element_type=F32))
        for a in range(3):
            low = parts[a][0:channels]
            high = parts[a + 1] if a == 2 else parts[a + 1][channels:]
            total = low + high
            base = (a * 3 + b) * 3 * channels // 2
            packed[base : base + channels] = total[:, 0:breadth]
            rest = jnp.concatenate([total[:, breadth:], total[:, breadth:]], axis=1)
            mix = jnp.where(lane < channels, rest[0 : channels // 2], rest[channels // 2 :])
            packed[base + channels : base + 3 * channels // 2] = mix
    base = 9 * 3 * channels // 2
    source = lax.broadcasted_iota(jnp.int32, (2 * breadth, 2 * breadth), 0)
    target = lax.broadcasted_iota(jnp.int32, (2 * breadth, 2 * breadth), 1)
    wanted = 2 * (target % breadth) + target // breadth
    pick = jnp.where(source == wanted, 1.0, 0.0).astype(BF16)
    coarse = None
    for a in range(2):
        for b in range(2):
            pairs = []
            for pair in range(rows // 4):
                both = jnp.concatenate([h_ref[a, 4 * pair + b], h_ref[a, 4 * pair + 2 + b]], axis=1)
                pairs.append(jnp.dot(both, pick, preferred_element_type=F32).astype(BF16))
            hidden = jnp.concatenate(
                [jnp.concatenate([x[:, e * breadth : (e + 1) * breadth] for x in pairs], axis=1) for e in range(2)],
                axis=0,
            )
            term = jnp.dot(d_ref[a, b], hidden, preferred_element_type=F32)
            coarse = term if coarse is None else coarse + term
            down = lax.dot_general(cot_ref[...], hidden, across, preferred_element_type=F32)
            at = base + (2 * a + b) * d_ref.shape[2]
            packed[at : at + d_ref.shape[2]] = down
    out_ref[...] = coarse.astype(BF16)
    end = base + 4 * d_ref.shape[2]
    if end < packed.shape[0]:
        packed[end:] = jnp.zeros((packed.shape[0] - end, packed.shape[1]), F32)
    half = packed.shape[0] // 2
    split(packed, keep, send, half, "gy", 1)


def side_of(axis, bit):
    return lax.rem(lax.axis_index(axis) // bit, 2)


def part(side, rows):
    return pl.ds(pl.multiple_of(side * rows, 16), rows)


def split(packed, keep, send, half, axis, bit):
    side = side_of(axis, bit)
    keep[...] = packed[part(side, half)]
    send[...] = packed[part(1 - side, half)].astype(BF16)


def quarter(flips=0):
    x, y = side_of("gy", 2), side_of("gz", 1)
    return 2 * (1 - x if flips & 2 else x) + (1 - y if flips & 1 else y)


def quarter_kernel(mine, other, keep, to_x, to_y, to_both, total):
    total[...] = mine[...] + other[...].astype(F32)
    rows = keep.shape[0]
    keep[...] = total[part(quarter(), rows)]
    for flips, send in ((2, to_x), (1, to_y), (3, to_both)):
        send[...] = total[part(quarter(flips), rows)].astype(BF16)


def add_kernel(own, x, y, both, out):
    found = [ref[...].astype(F32) for ref in (own, x, y, both)]
    out[...] = ((found[0] + found[1]) + (found[2] + found[3])).astype(BF16)


def add_two_kernel(own, other, out):
    out[...] = (own[...].astype(F32) + other[...].astype(F32)).astype(BF16)


def gather_kernel(own, x, y, both, out):
    rows = own.shape[0]
    for flips, ref in ((0, own), (2, x), (1, y), (3, both)):
        out[part(quarter(flips), rows)] = ref[...]


def join_kernel(mine, other, out, *, axis, bit):
    rows = mine.shape[0]
    side = side_of(axis, bit)
    out[part(side, rows)] = mine[...]
    out[part(1 - side, rows)] = other[...]


def field_kernel(near, far, near_in, far_in, w_ref, acc_ref, inner, outer):
    rows, channels, breadth = near.shape
    fill_columns(inner, near, far)
    fill_columns(outer, near_in, far_in)

    def step(t, carry):
        y = 2 * t
        own = inner_terms(inner, w_ref, y)
        rest = outer_terms(outer, w_ref, y)
        for z in range(2):
            total = own[z] + rest[z]
            for b in range(2):
                acc_ref[z, y + b] = total[:, b * breadth : (b + 1) * breadth]
        return carry

    lax.fori_loop(0, rows // 2, step, 0)


def field_edges_kernel(near, far, acc_ref, w_ref, out_ref, edges):
    rows, channels, breadth = acc_ref.shape[1:]
    fill_edges(edges, near, far)
    sides = [edge_terms(edges, w_ref, side) for side in range(2)]
    for z in range(2):
        for y in range(rows):
            line = acc_ref[z, y]
            if y in (0, rows - 1):
                line = line + sides[0 if y == 0 else 1][z]
            out_ref[pl.ds(z * rows + y, channels, stride=2 * rows), :] = line


def unpack_kernel(mine, other, conv_ref, down_ref, sums_ref, *, scale):
    join_kernel(mine, other, sums_ref, axis="gy", bit=1)
    channels = conv_ref.shape[2]
    for a in range(3):
        for b in range(3):
            base = (a * 3 + b) * 3 * channels // 2
            conv_ref[a, b, :, 0 : 2 * channels] = sums_ref[base : base + channels].astype(F32) * scale
            rest = sums_ref[base + channels : base + 3 * channels // 2].astype(F32) * scale
            conv_ref[a, b, 0 : channels // 2, 2 * channels :] = rest[:, 0:channels]
            conv_ref[a, b, channels // 2 :, 2 * channels :] = rest[:, channels:]
    base = 9 * 3 * channels // 2
    height = down_ref.shape[2]
    for a in range(2):
        for b in range(2):
            at = base + (2 * a + b) * height
            down_ref[a, b] = sums_ref[at : at + height].astype(F32) * scale


def swap(cells, axis, low):
    count = lax.axis_size(axis)
    pairs = [(i % count, (i + 1) % count) for i in range(low, low + count, 2)]
    return lax.ppermute(cells, axis, pairs + [(b, a) for a, b in pairs])


def flip(cells, z_bits, y_bits):
    row = lax.axis_size("gy")
    count = lax.axis_size("gz") * row
    mask = z_bits * row + y_bits
    return lax.ppermute(cells, ("gz", "gy"), [(i, i ^ mask) for i in range(count)])


def tied(first, *others):
    found = lax.optimization_barrier((first, *others))
    return found[0], tuple(found[1:])


def swapped(near, far, axis):
    return swap(near, axis, 0), swap(far, axis, 1)


def body(features, conv_weight, down_weight, cotangent):
    channels, plane_count, row_count, breadth = features.shape
    out_channels = down_weight.shape[2]
    count = lax.axis_size("gz") * lax.axis_size("gy")
    grad_scale = 1.0 / math.sqrt(plane_count * row_count * breadth * count)
    turned = conv_weight.reshape(3, 3, channels, 3, channels)[::-1, ::-1, :, ::-1]
    weight_bwd = turned.transpose(0, 1, 4, 3, 2).reshape(3, 3, channels, 3 * channels)
    cot = cotangent.reshape(out_channels, -1)
    plane = ((row_count, channels, breadth), BF16)
    edge = ((plane_count + 2, channels, breadth), BF16)
    cols = ((plane_count, row_count + 2, 3 * channels, breadth), BF16)
    edge_cols = ((plane_count + 2, 2, 3 * channels, breadth), BF16)
    lines = (plane_count, row_count, channels, breadth)
    conv_flops = 2 * 27 * channels * channels * plane_count * row_count * breadth

    pair = ((2, channels, breadth), BF16)
    *own, near_row, far_row = call(
        lines_kernel, [plane, plane, pair, pair],
        [((channels * plane_count * row_count, breadth), F32)], 0, (features,),
    )
    beside = swapped(near_row, far_row, "gy")
    outside = swapped(*own, "gz")
    corners = call(corners_kernel, [pair, pair], [], 0, beside)
    near, far, *corners = lax.optimization_barrier((*own, *corners))
    own = (near, far)
    corners = swapped(*corners, "gz")
    inner, acc, hidden_grad = call(
        inner_kernel, [cols, (lines, F32), (lines, F32)],
        [((out_channels, row_count // 2 * breadth), BF16)],
        2 * conv_flops // 3, (*own, conv_weight, down_weight, cot),
    )
    near, far, acc = lax.optimization_barrier((*outside, acc))
    outside = (near, far)
    outer, acc = call(
        outer_kernel, [cols, (lines, F32)], [], conv_flops // 3, (*outside, conv_weight, acc)
    )
    edges, near, far, hidden = call(
        gate_kernel, [edge_cols, plane, plane, (lines, BF16)], [], conv_flops // 10,
        (*beside, *corners, acc, hidden_grad, conv_weight),
    )
    gates = (near, far)

    used = 27 * channels * channels // 128 + 4 * out_channels
    rows = -(-used // 128) * 128
    section_out, keep, send = call(
        weight_grad_kernel,
        [((out_channels, cot.shape[1]), BF16), ((rows // 2, 128), F32), ((rows // 2, 128), BF16)],
        [((rows, 128), F32)], conv_flops,
        (inner, outer, edges, *gates, hidden, down_weight, cot),
    )
    near, far = gates
    near_in = swap(near, "gz", 0)
    other, (near_in,) = tied(flip(send, 0, 1), near_in)
    shard = ((rows // 8, 128), BF16)
    keep, to_x, to_y, to_both = call(
        quarter_kernel, [((rows // 8, 128), F32), shard, shard, shard], [((rows // 2, 128), F32)], 0,
        (keep, other),
    )
    keep, (far,) = tied(keep, far)
    found = flip(to_both, 1, 2), flip(to_x, 0, 2), flip(to_y, 1, 0)
    far_in = swap(far, "gz", 1)
    (sums,) = call(add_kernel, [shard], [], 0, (keep, found[1], found[2], found[0]))
    sums, outside = tied(sums, near_in, far_in)
    sends = call(edges_kernel, [edge, edge], [], 0, (*gates, *outside))
    beside = swapped(*sends, "gy")
    (acc,) = call(
        field_kernel, [(lines, F32)], [cols, cols], conv_flops, (*gates, *outside, weight_bwd)
    )
    bits = [(0, 1 << k) for k in range(2, lax.axis_size("gy").bit_length() - 1)]
    bits += [(1 << k, 0) for k in range(1, lax.axis_size("gz").bit_length() - 1)]
    while bits:
        (z, y), *bits = bits
        if bits:
            (z2, y2), *bits = bits
            found = flip(sums, z, y), flip(sums, z2, y2), flip(sums, z | z2, y | y2)
            (sums,) = call(add_kernel, [shard], [], 0, (sums, *found))
        else:
            (sums,) = call(add_two_kernel, [shard], [], 0, (sums, flip(sums, z, y)))
    sums, beside = tied(sums, *beside)
    found = flip(sums, 1, 2), flip(sums, 0, 2), flip(sums, 1, 0)
    sums, (acc,) = tied(sums, acc)
    (sums,) = call(
        gather_kernel, [((rows // 2, 128), BF16)], [], 0, (sums, found[1], found[2], found[0])
    )
    (field,) = call(
        field_edges_kernel, [((channels * plane_count * row_count, breadth), F32)], [edge_cols],
        conv_flops // 10, (*beside, acc, weight_bwd),
    )
    other, (field,) = tied(flip(sums, 0, 1), field)
    grad_conv, grad_down = call(
        functools.partial(unpack_kernel, scale=grad_scale),
        [(conv_weight.shape, F32), (down_weight.shape, F32)], [((rows, 128), BF16)], 0,
        (sums, other),
    )
    section_out = section_out.reshape(out_channels, plane_count // 2, -1)
    return (section_out, field.reshape(features.shape), grad_conv, grad_down)


def solution(mesh):
    return jax.shard_map(
        body,
        mesh=mesh,
        in_specs=(P(None, "gz", "gy", None), P(), P(), P(None, "gz", "gy")),
        out_specs=(P(None, "gz", "gy"), P(None, "gz", "gy", None), P(), P()),
        check_vma=False,
    )
```

```python
import functools
import math

import jax
import jax.numpy as jnp
from jax import lax
from jax.experimental import pallas as pl
from jax.experimental.pallas import tpu as pltpu
from jax.sharding import PartitionSpec as P

F32 = jnp.float32
BF16 = jnp.bfloat16
PARAMS = pltpu.CompilerParams(vmem_limit_bytes=24 * 1024 * 1024)


def call(kernel, outs, scratch, flops, operands):
    moved = sum(x.size * x.dtype.itemsize for x in operands)
    moved += sum(math.prod(s) * jnp.dtype(d).itemsize for s, d in outs)
    vmem = pl.BlockSpec(memory_space=pltpu.VMEM)
    return pl.pallas_call(
        kernel,
        out_shape=[jax.ShapeDtypeStruct(s, d) for s, d in outs],
        in_specs=[vmem] * len(operands),
        out_specs=[vmem] * len(outs),
        scratch_shapes=[pltpu.VMEM(s, d) for s, d in scratch],
        compiler_params=PARAMS,
        cost_estimate=pl.CostEstimate(flops=flops, bytes_accessed=moved, transcendentals=0),
    )(*operands)


def is_even(axis):
    return lax.rem(lax.axis_index(axis), 2) == 0


def choose(cond, yes, no):
    return jnp.where(jnp.broadcast_to(cond, yes.shape), yes, no)


def lines_kernel(f_ref, near_ref, far_ref, wide):
    channels, planes, rows, breadth = f_ref.shape
    wide[...] = f_ref[...].astype(F32).reshape(channels * planes * rows, breadth)
    even = is_even("gz")
    for y in range(rows):
        low, high = (
            wide[pl.ds(z * rows + y, channels, stride=planes * rows), :].astype(BF16) for z in range(2)
        )
        near_ref[y] = choose(even, high, low)
        far_ref[y] = choose(even, low, high)


def edges_kernel(near, far, near_in, far_in, near_ref, far_ref):
    rows = near.shape[0]
    even_z, even_y = is_even("gz"), is_even("gy")

    def put(p, one, other):
        first = choose(even_z, one[0], other[0])
        last = choose(even_z, one[rows - 1], other[rows - 1])
        near_ref[p] = choose(even_y, last, first)
        far_ref[p] = choose(even_y, first, last)

    put(0, far_in, near_in)
    put(1, far, near)
    put(2, near, far)
    put(3, near_in, far_in)


def put_columns(cols, p, q, line):
    channels = line.shape[0]
    wide = line.astype(F32)
    cols[p, q, 0:channels] = pltpu.roll(wide, 1, 1).astype(BF16)
    cols[p, q, channels : 2 * channels] = line
    cols[p, q, 2 * channels : 3 * channels] = pltpu.roll(wide, line.shape[1] - 1, 1).astype(BF16)


def fill_columns(cols, near, far):
    rows = near.shape[0]
    even = is_even("gz")

    def step(y, carry):
        put_columns(cols, 0, y + 1, choose(even, far[y], near[y]))
        put_columns(cols, 1, y + 1, choose(even, near[y], far[y]))
        return carry

    lax.fori_loop(0, rows, step, 0, unroll=2)
    for p in range(2):
        for q in (0, rows + 1):
            cols[p, q] = jnp.zeros(cols.shape[2:], BF16)


def fill_edges(cols, near, far):
    even = is_even("gy")
    for p in range(4):
        put_columns(cols, p, 0, choose(even, far[p], near[p]))
        put_columns(cols, p, 1, choose(even, near[p], far[p]))


def dot(lhs, rhs):
    return jnp.dot(lhs, rhs, preferred_element_type=F32)


def taps(w_ref, b, first, last):
    return jnp.concatenate([w_ref[a, b] for a in range(first, last)], axis=0)


def window(cols, p, q):
    return jnp.concatenate([cols[p, q], cols[p, q + 1]], axis=1)


def inner_terms(cols, w_ref, y):
    acc = None
    for b in range(3):
        for p in range(2):
            term = dot(taps(w_ref, b, p, p + 2), window(cols, p, y + b))
            acc = term if acc is None else acc + term
    half = acc.shape[0] // 2
    return acc[half:], acc[:half]


def outer_terms(cols, w_ref, y):
    lower = upper = None
    for b in range(3):
        low, high = dot(w_ref[0, b], window(cols, 0, y + b)), dot(w_ref[2, b], window(cols, 1, y + b))
        lower = low if lower is None else lower + low
        upper = high if upper is None else upper + high
    return lower, upper


def edge_terms(edges, w_ref, side):
    b = 2 * side
    half = w_ref.shape[2]
    acc = dot(taps(w_ref, b, 0, 2), edges[1, side]) + dot(taps(w_ref, b, 1, 3), edges[2, side])
    return acc[half:] + dot(w_ref[0, b], edges[0, side]), acc[:half] + dot(w_ref[2, b], edges[3, side])


def inner_kernel(near, far, w_ref, d_ref, cot_ref, cols, acc_ref, grad_ref, up):
    rows, channels, breadth = near.shape
    fill_columns(cols, near, far)
    source = lax.broadcasted_iota(jnp.int32, (breadth, 2 * breadth), 0)
    target = lax.broadcasted_iota(jnp.int32, (breadth, 2 * breadth), 1)
    spread = jnp.where(source == target // 2, 1.0, 0.0).astype(BF16)
    for pair in range(rows // 4):
        both = dot(cot_ref[:, pair * breadth : (pair + 1) * breadth], spread)
        up[:, 2 * pair * breadth : 2 * (pair + 1) * breadth] = both.astype(BF16)
    even = lax.broadcasted_iota(jnp.int32, (channels, breadth), 1) % 2 == 0
    for a in range(2):
        for b in range(2):
            terms = lax.dot_general(d_ref[a, b], up[...], (((0,), (0,)), ((), ())), preferred_element_type=F32)
            for t in range(rows // 2):
                part = terms[:, t * breadth : (t + 1) * breadth]
                grad_ref[a, 2 * t + b] = jnp.where(even, part[0:channels], part[channels:])

    def step(t, carry):
        y = 2 * t
        for z, lines in enumerate(inner_terms(cols, w_ref, y)):
            for b in range(2):
                acc_ref[z, y + b] = lines[:, b * breadth : (b + 1) * breadth]
        return carry

    lax.fori_loop(0, rows // 2, step, 0)


def outer_kernel(near, far, w_ref, acc_ref, cols, out_ref):
    rows, channels, breadth = near.shape
    fill_columns(cols, near, far)

    def step(t, carry):
        y = 2 * t
        for z, lines in enumerate(outer_terms(cols, w_ref, y)):
            for b in range(2):
                out_ref[z, y + b] = acc_ref[z, y + b] + lines[:, b * breadth : (b + 1) * breadth]
        return carry

    lax.fori_loop(0, rows // 2, step, 0)


def gate_kernel(near, far, acc_ref, grad_ref, w_ref, edges, near_ref, far_ref, h_ref):
    rows, channels, breadth = acc_ref.shape[1:]
    fill_edges(edges, near, far)
    sides = [edge_terms(edges, w_ref, side) for side in range(2)]
    even = is_even("gz")

    def gate(y, extra):
        found = []
        for z in range(2):
            preact = acc_ref[z, y] if extra is None else acc_ref[z, y] + extra[z]
            sig = 1.0 / (1.0 + jnp.exp(-preact))
            h_ref[z, y] = (preact * sig).astype(BF16)
            found.append((grad_ref[z, y] * sig * (1.0 + preact * (1.0 - sig))).astype(BF16))
        near_ref[y] = choose(even, found[1], found[0])
        far_ref[y] = choose(even, found[0], found[1])

    gate(0, sides[0])
    for y in range(1, rows - 1):
        gate(y, None)
    gate(rows - 1, sides[1])


def coarse_hidden(h_ref, a, b):
    rows, channels, breadth = h_ref.shape[1:]
    source = lax.broadcasted_iota(jnp.int32, (2 * breadth, 2 * breadth), 0)
    target = lax.broadcasted_iota(jnp.int32, (2 * breadth, 2 * breadth), 1)
    wanted = 2 * (target % breadth) + target // breadth
    pick = jnp.where(source == wanted, 1.0, 0.0).astype(BF16)
    pairs = []
    for pair in range(rows // 4):
        both = jnp.concatenate([h_ref[a, 4 * pair + b], h_ref[a, 4 * pair + 2 + b]], axis=1)
        pairs.append(dot(both, pick).astype(BF16))
    return jnp.concatenate(
        [jnp.concatenate([x[:, e * breadth : (e + 1) * breadth] for x in pairs], axis=1) for e in range(2)],
        axis=0,
    )


def section_kernel(h_ref, d_ref, out_ref):
    coarse = None
    for a in range(2):
        for b in range(2):
            term = dot(d_ref[a, b], coarse_hidden(h_ref, a, b))
            coarse = term if coarse is None else coarse + term
    out_ref[...] = coarse.astype(BF16)


def weight_grad_kernel(inner, outer, edges, near, far, h_ref, cot_ref, keep, send, packed):
    rows, channels, breadth = near.shape
    across = (((1,), (1,)), ((), ()))
    even = is_even("gz")
    low = [choose(even, far[y], near[y]) for y in range(rows)]
    high = [choose(even, near[y], far[y]) for y in range(rows)]
    gates = jnp.concatenate([jnp.concatenate(low, axis=1), jnp.concatenate(high, axis=1)], axis=0)

    def columns(p, q):
        if q in (0, rows + 1):
            return edges[p, 0 if q == 0 else 1]
        return inner[p - 1, q] if p in (1, 2) else outer[p // 3, q]

    lane = lax.broadcasted_iota(jnp.int32, (channels // 2, breadth), 1)
    for b in range(3):
        parts = []
        for p in range(4):
            across_rows = jnp.concatenate([columns(p, y + b) for y in range(rows)], axis=1)
            lhs = gates[0:channels] if p == 0 else gates[channels:] if p == 3 else gates
            parts.append(lax.dot_general(lhs, across_rows, across, preferred_element_type=F32))
        for a in range(3):
            low = parts[a][0:channels]
            high = parts[a + 1] if a == 2 else parts[a + 1][channels:]
            total = low + high
            base = (a * 3 + b) * 3 * channels // 2
            packed[base : base + channels] = total[:, 0:breadth]
            rest = jnp.concatenate([total[:, breadth:], total[:, breadth:]], axis=1)
            mix = jnp.where(lane < channels, rest[0 : channels // 2], rest[channels // 2 :])
            packed[base + channels : base + 3 * channels // 2] = mix
    base = 9 * 3 * channels // 2
    height = cot_ref.shape[0]
    for a in range(2):
        for b in range(2):
            down = lax.dot_general(cot_ref[...], coarse_hidden(h_ref, a, b), across, preferred_element_type=F32)
            at = base + (2 * a + b) * height
            packed[at : at + height] = down
    end = base + 4 * height
    if end < packed.shape[0]:
        packed[end:] = jnp.zeros((packed.shape[0] - end, packed.shape[1]), F32)
    half = packed.shape[0] // 2
    split(packed, keep, send, half, "gy", 1)


def side_of(axis, bit):
    return lax.rem(lax.axis_index(axis) // bit, 2)


def part(side, rows):
    return pl.ds(pl.multiple_of(side * rows, 16), rows)


def split(packed, keep, send, half, axis, bit):
    side = side_of(axis, bit)
    keep[...] = packed[part(side, half)]
    send[...] = packed[part(1 - side, half)].astype(BF16)


def add_kernel(mine, other, out):
    total = mine[...] + other[...].astype(F32)
    out[...] = total.reshape(out.shape).astype(BF16)


def total_kernel(terms, out):
    count = terms.shape[0]
    for core in range(2):
        total = None
        for s in range(core, count, 2):
            term = terms[s].astype(F32)
            total = term if total is None else total + term
        total = total.astype(BF16)
        for s in range(core, count, 2):
            out[s] = total


def field_kernel(near, far, near_in, far_in, w_ref, acc_ref, inner, outer):
    rows, channels, breadth = near.shape
    fill_columns(inner, near, far)
    fill_columns(outer, near_in, far_in)

    def step(t, carry):
        y = 2 * t
        own = inner_terms(inner, w_ref, y)
        rest = outer_terms(outer, w_ref, y)
        for z in range(2):
            total = own[z] + rest[z]
            for b in range(2):
                acc_ref[z, y + b] = total[:, b * breadth : (b + 1) * breadth]
        return carry

    lax.fori_loop(0, rows // 2, step, 0)


def field_edges_kernel(near, far, acc_ref, w_ref, out_ref, edges):
    rows, channels, breadth = acc_ref.shape[1:]
    fill_edges(edges, near, far)
    sides = [edge_terms(edges, w_ref, side) for side in range(2)]
    for z in range(2):
        for y in range(rows):
            line = acc_ref[z, y]
            if y in (0, rows - 1):
                line = line + sides[0 if y == 0 else 1][z]
            out_ref[pl.ds(z * rows + y, channels, stride=2 * rows), :] = line


def unpack_kernel(mine, other, conv_ref, down_ref, sums_ref, *, scale):
    half = sums_ref.shape[0] // 2
    side = side_of("gy", 1)
    sums_ref[part(side, half)] = mine[...].astype(F32).reshape(half, sums_ref.shape[1])
    sums_ref[part(1 - side, half)] = other[...].astype(F32).reshape(half, sums_ref.shape[1])
    channels = conv_ref.shape[2]
    for a in range(3):
        for b in range(3):
            base = (a * 3 + b) * 3 * channels // 2
            conv_ref[a, b, :, 0 : 2 * channels] = sums_ref[base : base + channels]* scale
            rest = sums_ref[base + channels : base + 3 * channels // 2]* scale
            conv_ref[a, b, 0 : channels // 2, 2 * channels :] = rest[:, 0:channels]
            conv_ref[a, b, channels // 2 :, 2 * channels :] = rest[:, channels:]
    base = 9 * 3 * channels // 2
    height = down_ref.shape[2]
    for a in range(2):
        for b in range(2):
            at = base + (2 * a + b) * height
            down_ref[a, b] = sums_ref[at : at + height]* scale


def swap(cells, axis, low):
    count = lax.axis_size(axis)
    pairs = [(i % count, (i + 1) % count) for i in range(low, low + count, 2)]
    return lax.ppermute(cells, axis, pairs + [(b, a) for a, b in pairs])


def flip(cells, axis, bit):
    return lax.ppermute(cells, axis, [(i, i ^ bit) for i in range(lax.axis_size(axis))])


def tied(first, *others):
    found = lax.optimization_barrier((first, *others))
    return found[0], tuple(found[1:])


def swapped(near, far, axis):
    return swap(near, axis, 0), swap(far, axis, 1)


def body(features, conv_weight, down_weight, cotangent):
    channels, plane_count, row_count, breadth = features.shape
    out_channels = down_weight.shape[2]
    count = lax.axis_size("gz") * lax.axis_size("gy")
    grad_scale = 1.0 / math.sqrt(plane_count * row_count * breadth * count)
    turned = conv_weight.reshape(3, 3, channels, 3, channels)[::-1, ::-1, :, ::-1]
    weight_bwd = turned.transpose(0, 1, 4, 3, 2).reshape(3, 3, channels, 3 * channels)
    cot = cotangent.reshape(out_channels, -1)
    plane = ((row_count, channels, breadth), BF16)
    edge = ((plane_count + 2, channels, breadth), BF16)
    cols = ((plane_count, row_count + 2, 3 * channels, breadth), BF16)
    edge_cols = ((plane_count + 2, 2, 3 * channels, breadth), BF16)
    lines = (plane_count, row_count, channels, breadth)
    conv_flops = 2 * 27 * channels * channels * plane_count * row_count * breadth

    own = call(
        lines_kernel, [plane, plane], [((channels * plane_count * row_count, breadth), F32)], 0, (features,)
    )
    outside = swapped(*own, "gz")
    inner, acc, hidden_grad = call(
        inner_kernel, [cols, (lines, F32), (lines, F32)],
        [((out_channels, row_count // 2 * breadth), BF16)],
        2 * conv_flops // 3, (*own, conv_weight, down_weight, cot),
    )
    near, far, acc = lax.optimization_barrier((*outside, acc))
    outside = (near, far)
    beside = swapped(*call(edges_kernel, [edge, edge], [], 0, (*own, *outside)), "gy")
    outer, acc = call(
        outer_kernel, [cols, (lines, F32)], [], conv_flops // 3, (*outside, conv_weight, acc)
    )
    edges, near, far, hidden = call(
        gate_kernel, [edge_cols, plane, plane, (lines, BF16)], [], conv_flops // 10,
        (*beside, acc, hidden_grad, conv_weight),
    )
    gates = (near, far)

    used = 27 * channels * channels // 128 + 4 * out_channels
    share = -(-used // (16 * count)) * 8
    half = share * count
    parts = ((count, share, 128), BF16)
    keep, send = call(
        weight_grad_kernel, [((half, 128), F32), ((half, 128), BF16)], [((2 * half, 128), F32)], conv_flops,
        (inner, outer, edges, *gates, hidden, cot),
    )
    exchange = functools.partial(
        lax.all_to_all, axis_name=("gz", "gy"), split_axis=0, concat_axis=0, tiled=True
    )
    keep, gates = tied(keep, *gates)
    near, far = gates
    outside = swap(near, "gz", 0), swap(far, "gz", 1)
    (terms,) = call(add_kernel, [parts], [], 0, (keep, flip(send, "gy", 1)))
    terms, (hidden,) = tied(terms, hidden)
    (section_out,) = call(
        section_kernel, [((out_channels, cot.shape[1]), BF16)], [], conv_flops // 10, (hidden, down_weight)
    )
    beside = swapped(*call(edges_kernel, [edge, edge], [], 0, (*gates, *outside)), "gy")
    terms, beside = tied(exchange(terms), *beside)
    (sums,) = call(total_kernel, [parts], [], 0, (terms,))
    (acc,) = call(
        field_kernel, [(lines, F32)], [cols, cols], conv_flops, (*gates, *outside, weight_bwd)
    )
    (field,) = call(
        field_edges_kernel, [((channels * plane_count * row_count, breadth), F32)], [edge_cols],
        conv_flops // 10, (*beside, acc, weight_bwd),
    )
    sums, (field,) = tied(exchange(sums), field)
    grad_conv, grad_down = call(
        functools.partial(unpack_kernel, scale=grad_scale),
        [(conv_weight.shape, F32), (down_weight.shape, F32)], [((2 * half, 128), F32)], 0,
        (sums, flip(sums, "gy", 1)),
    )
    section_out = section_out.reshape(out_channels, plane_count // 2, -1)
    return (section_out, field.reshape(features.shape), grad_conv, grad_down)


def solution(mesh):
    return jax.shard_map(
        body,
        mesh=mesh,
        in_specs=(P(None, "gz", "gy", None), P(), P(), P(None, "gz", "gy")),
        out_specs=(P(None, "gz", "gy"), P(None, "gz", "gy", None), P(), P()),
        check_vma=False,
    )
```

```python
import functools
import math

import jax
import jax.numpy as jnp
from jax import lax
from jax.experimental import pallas as pl
from jax.experimental.pallas import tpu as pltpu
from jax.sharding import PartitionSpec as P

F32 = jnp.float32
BF16 = jnp.bfloat16
PARAMS = pltpu.CompilerParams(vmem_limit_bytes=24 * 1024 * 1024)


def call(kernel, outs, scratch, flops, operands):
    moved = sum(x.size * x.dtype.itemsize for x in operands)
    moved += sum(math.prod(s) * jnp.dtype(d).itemsize for s, d in outs)
    vmem = pl.BlockSpec(memory_space=pltpu.VMEM)
    return pl.pallas_call(
        kernel,
        out_shape=[jax.ShapeDtypeStruct(s, d) for s, d in outs],
        in_specs=[vmem] * len(operands),
        out_specs=[vmem] * len(outs),
        scratch_shapes=[pltpu.VMEM(s, d) for s, d in scratch],
        compiler_params=PARAMS,
        cost_estimate=pl.CostEstimate(flops=flops, bytes_accessed=moved, transcendentals=0),
    )(*operands)


def is_even(axis):
    return lax.rem(lax.axis_index(axis), 2) == 0


def choose(cond, yes, no):
    return jnp.where(jnp.broadcast_to(cond, yes.shape), yes, no)


def lines_kernel(f_ref, near_ref, far_ref, wide):
    channels, planes, rows, breadth = f_ref.shape
    wide[...] = f_ref[...].astype(F32).reshape(channels * planes * rows, breadth)
    even = is_even("gz")
    for y in range(rows):
        low, high = (
            wide[pl.ds(z * rows + y, channels, stride=planes * rows), :].astype(BF16) for z in range(2)
        )
        near_ref[y] = choose(even, high, low)
        far_ref[y] = choose(even, low, high)


def edges_kernel(near, far, near_in, far_in, near_ref, far_ref):
    rows = near.shape[0]
    even_z, even_y = is_even("gz"), is_even("gy")

    def put(p, one, other):
        first = choose(even_z, one[0], other[0])
        last = choose(even_z, one[rows - 1], other[rows - 1])
        near_ref[p] = choose(even_y, last, first)
        far_ref[p] = choose(even_y, first, last)

    put(0, far_in, near_in)
    put(1, far, near)
    put(2, near, far)
    put(3, near_in, far_in)


def put_columns(cols, p, q, line):
    channels = line.shape[0]
    wide = line.astype(F32)
    cols[p, q, 0:channels] = pltpu.roll(wide, 1, 1).astype(BF16)
    cols[p, q, channels : 2 * channels] = line
    cols[p, q, 2 * channels : 3 * channels] = pltpu.roll(wide, line.shape[1] - 1, 1).astype(BF16)


def fill_columns(cols, near, far):
    rows = near.shape[0]
    even = is_even("gz")

    def step(y, carry):
        put_columns(cols, 0, y + 1, choose(even, far[y], near[y]))
        put_columns(cols, 1, y + 1, choose(even, near[y], far[y]))
        return carry

    lax.fori_loop(0, rows, step, 0, unroll=2)
    for p in range(2):
        for q in (0, rows + 1):
            cols[p, q] = jnp.zeros(cols.shape[2:], BF16)


def fill_edges(cols, near, far):
    even = is_even("gy")
    for p in range(4):
        put_columns(cols, p, 0, choose(even, far[p], near[p]))
        put_columns(cols, p, 1, choose(even, near[p], far[p]))


def dot(lhs, rhs):
    return jnp.dot(lhs, rhs, preferred_element_type=F32)


def taps(w_ref, b, first, last):
    return jnp.concatenate([w_ref[a, b] for a in range(first, last)], axis=0)


def window(cols, p, q):
    return jnp.concatenate([cols[p, q], cols[p, q + 1]], axis=1)


def inner_terms(cols, w_ref, y):
    acc = None
    for b in range(3):
        for p in range(2):
            term = dot(taps(w_ref, b, p, p + 2), window(cols, p, y + b))
            acc = term if acc is None else acc + term
    half = acc.shape[0] // 2
    return acc[half:], acc[:half]


def outer_terms(cols, w_ref, y):
    lower = upper = None
    for b in range(3):
        low, high = dot(w_ref[0, b], window(cols, 0, y + b)), dot(w_ref[2, b], window(cols, 1, y + b))
        lower = low if lower is None else lower + low
        upper = high if upper is None else upper + high
    return lower, upper


def edge_terms(edges, w_ref, side):
    b = 2 * side
    half = w_ref.shape[2]
    acc = dot(taps(w_ref, b, 0, 2), edges[1, side]) + dot(taps(w_ref, b, 1, 3), edges[2, side])
    return acc[half:] + dot(w_ref[0, b], edges[0, side]), acc[:half] + dot(w_ref[2, b], edges[3, side])


def inner_kernel(near, far, w_ref, d_ref, cot_ref, cols, acc_ref, grad_ref, up):
    rows, channels, breadth = near.shape
    fill_columns(cols, near, far)
    source = lax.broadcasted_iota(jnp.int32, (breadth, 2 * breadth), 0)
    target = lax.broadcasted_iota(jnp.int32, (breadth, 2 * breadth), 1)
    spread = jnp.where(source == target // 2, 1.0, 0.0).astype(BF16)
    for pair in range(rows // 4):
        both = dot(cot_ref[:, pair * breadth : (pair + 1) * breadth], spread)
        up[:, 2 * pair * breadth : 2 * (pair + 1) * breadth] = both.astype(BF16)
    even = lax.broadcasted_iota(jnp.int32, (channels, breadth), 1) % 2 == 0
    for a in range(2):
        for b in range(2):
            terms = lax.dot_general(d_ref[a, b], up[...], (((0,), (0,)), ((), ())), preferred_element_type=F32)
            for t in range(rows // 2):
                part = terms[:, t * breadth : (t + 1) * breadth]
                grad_ref[a, 2 * t + b] = jnp.where(even, part[0:channels], part[channels:])

    def step(t, carry):
        y = 2 * t
        for z, lines in enumerate(inner_terms(cols, w_ref, y)):
            for b in range(2):
                acc_ref[z, y + b] = lines[:, b * breadth : (b + 1) * breadth]
        return carry

    lax.fori_loop(0, rows // 2, step, 0)


def outer_kernel(near, far, w_ref, acc_ref, cols, out_ref):
    rows, channels, breadth = near.shape
    fill_columns(cols, near, far)

    def step(t, carry):
        y = 2 * t
        for z, lines in enumerate(outer_terms(cols, w_ref, y)):
            for b in range(2):
                out_ref[z, y + b] = acc_ref[z, y + b] + lines[:, b * breadth : (b + 1) * breadth]
        return carry

    lax.fori_loop(0, rows // 2, step, 0)


def gate_kernel(near, far, acc_ref, grad_ref, w_ref, edges, near_ref, far_ref, h_ref):
    rows, channels, breadth = acc_ref.shape[1:]
    fill_edges(edges, near, far)
    sides = [edge_terms(edges, w_ref, side) for side in range(2)]
    even = is_even("gz")

    def gate(y, extra):
        found = []
        for z in range(2):
            preact = acc_ref[z, y] if extra is None else acc_ref[z, y] + extra[z]
            sig = 1.0 / (1.0 + jnp.exp(-preact))
            h_ref[z, y] = (preact * sig).astype(BF16)
            found.append((grad_ref[z, y] * sig * (1.0 + preact * (1.0 - sig))).astype(BF16))
        near_ref[y] = choose(even, found[1], found[0])
        far_ref[y] = choose(even, found[0], found[1])

    gate(0, sides[0])
    for y in range(1, rows - 1):
        gate(y, None)
    gate(rows - 1, sides[1])


def coarse_hidden(h_ref, a, b):
    rows, channels, breadth = h_ref.shape[1:]
    source = lax.broadcasted_iota(jnp.int32, (2 * breadth, 2 * breadth), 0)
    target = lax.broadcasted_iota(jnp.int32, (2 * breadth, 2 * breadth), 1)
    wanted = 2 * (target % breadth) + target // breadth
    pick = jnp.where(source == wanted, 1.0, 0.0).astype(BF16)
    pairs = []
    for pair in range(rows // 4):
        both = jnp.concatenate([h_ref[a, 4 * pair + b], h_ref[a, 4 * pair + 2 + b]], axis=1)
        pairs.append(dot(both, pick).astype(BF16))
    return jnp.concatenate(
        [jnp.concatenate([x[:, e * breadth : (e + 1) * breadth] for x in pairs], axis=1) for e in range(2)],
        axis=0,
    )


def section_kernel(h_ref, d_ref, out_ref):
    coarse = None
    for a in range(2):
        for b in range(2):
            term = dot(d_ref[a, b], coarse_hidden(h_ref, a, b))
            coarse = term if coarse is None else coarse + term
    out_ref[...] = coarse.astype(BF16)


def weight_grad_kernel(inner, outer, edges, near, far, h_ref, cot_ref, keep0, keep1, send0, send1, packed):
    rows, channels, breadth = near.shape
    across = (((1,), (1,)), ((), ()))
    even = is_even("gz")
    low = [choose(even, far[y], near[y]) for y in range(rows)]
    high = [choose(even, near[y], far[y]) for y in range(rows)]
    gates = jnp.concatenate([jnp.concatenate(low, axis=1), jnp.concatenate(high, axis=1)], axis=0)

    def columns(p, q):
        if q in (0, rows + 1):
            return edges[p, 0 if q == 0 else 1]
        return inner[p - 1, q] if p in (1, 2) else outer[p // 3, q]

    lane = lax.broadcasted_iota(jnp.int32, (channels // 2, breadth), 1)
    for b in range(3):
        parts = []
        for p in range(4):
            across_rows = jnp.concatenate([columns(p, y + b) for y in range(rows)], axis=1)
            lhs = gates[0:channels] if p == 0 else gates[channels:] if p == 3 else gates
            parts.append(lax.dot_general(lhs, across_rows, across, preferred_element_type=F32))
        for a in range(3):
            low = parts[a][0:channels]
            high = parts[a + 1] if a == 2 else parts[a + 1][channels:]
            total = low + high
            base = (a * 3 + b) * 3 * channels // 2
            packed[base : base + channels] = total[:, 0:breadth]
            rest = jnp.concatenate([total[:, breadth:], total[:, breadth:]], axis=1)
            mix = jnp.where(lane < channels, rest[0 : channels // 2], rest[channels // 2 :])
            packed[base + channels : base + 3 * channels // 2] = mix
    base = 9 * 3 * channels // 2
    height = cot_ref.shape[0]
    for a in range(2):
        for b in range(2):
            down = lax.dot_general(cot_ref[...], coarse_hidden(h_ref, a, b), across, preferred_element_type=F32)
            at = base + (2 * a + b) * height
            packed[at : at + height] = down
    end = base + 4 * height
    if end < packed.shape[0]:
        packed[end:] = jnp.zeros((packed.shape[0] - end, packed.shape[1]), F32)
    rows0 = keep0.shape[0]
    for keep, send, at in ((keep0, send0, slice(0, rows0)), (keep1, send1, slice(rows0, None))):
        keep[...] = packed[at]
        send[...] = packed[at].astype(BF16)


def side_of(axis, bit):
    return lax.rem(lax.axis_index(axis) // bit, 2)


def part(side, rows):
    return pl.ds(pl.multiple_of(side * rows, 16), rows)


def halve_kernel(mine0, mine1, got0, got1, keep0, keep1, send0, send1, total0, total1, *, axis, bit):
    side = side_of(axis, bit)
    for mine, got, keep, send, total in (
        (mine0, got0, keep0, send0, total0), (mine1, got1, keep1, send1, total1)
    ):
        total[...] = mine[...] + got[...].astype(F32)
        half = keep.shape[0]
        keep[...] = total[part(side, half)]
        send[...] = total[part(1 - side, half)].astype(BF16)


def add_kernel(mine0, mine1, got0, got1, out0, out1):
    out0[...] = (mine0[...].astype(F32) + got0[...].astype(F32)).astype(BF16)
    out1[...] = (mine1[...].astype(F32) + got1[...].astype(F32)).astype(BF16)


def join_kernel(mine0, mine1, got0, got1, out0, out1, *, axis, bit):
    side = side_of(axis, bit)
    for mine, got, out in ((mine0, got0, out0), (mine1, got1, out1)):
        rows = mine.shape[0]
        out[part(side, rows)] = mine[...]
        out[part(1 - side, rows)] = got[...]


def field_kernel(near, far, near_in, far_in, w_ref, acc_ref, inner, outer):
    rows, channels, breadth = near.shape
    fill_columns(inner, near, far)
    fill_columns(outer, near_in, far_in)

    def step(t, carry):
        y = 2 * t
        own = inner_terms(inner, w_ref, y)
        rest = outer_terms(outer, w_ref, y)
        for z in range(2):
            total = own[z] + rest[z]
            for b in range(2):
                acc_ref[z, y + b] = total[:, b * breadth : (b + 1) * breadth]
        return carry

    lax.fori_loop(0, rows // 2, step, 0)


def field_edges_kernel(near, far, acc_ref, w_ref, out_ref, edges):
    rows, channels, breadth = acc_ref.shape[1:]
    fill_edges(edges, near, far)
    sides = [edge_terms(edges, w_ref, side) for side in range(2)]
    for z in range(2):
        for y in range(rows):
            line = acc_ref[z, y]
            if y in (0, rows - 1):
                line = line + sides[0 if y == 0 else 1][z]
            out_ref[pl.ds(z * rows + y, channels, stride=2 * rows), :] = line


def unpack_kernel(mine0, mine1, got0, got1, conv_ref, down_ref, sums_ref, *, scale):
    even = is_even("gy")
    rows0 = mine0.shape[0]
    sums_ref[0:rows0] = choose(even, mine0[...], got0[...])
    sums_ref[rows0:] = choose(even, got1[...], mine1[...])
    channels = conv_ref.shape[2]
    for a in range(3):
        for b in range(3):
            base = (a * 3 + b) * 3 * channels // 2
            conv_ref[a, b, :, 0 : 2 * channels] = sums_ref[base : base + channels].astype(F32) * scale
            rest = sums_ref[base + channels : base + 3 * channels // 2].astype(F32) * scale
            conv_ref[a, b, 0 : channels // 2, 2 * channels :] = rest[:, 0:channels]
            conv_ref[a, b, channels // 2 :, 2 * channels :] = rest[:, channels:]
    base = 9 * 3 * channels // 2
    height = down_ref.shape[2]
    for a in range(2):
        for b in range(2):
            at = base + (2 * a + b) * height
            down_ref[a, b] = sums_ref[at : at + height].astype(F32) * scale


def swap(cells, axis, low):
    count = lax.axis_size(axis)
    pairs = [(i % count, (i + 1) % count) for i in range(low, low + count, 2)]
    return lax.ppermute(cells, axis, pairs + [(b, a) for a, b in pairs])


def flip(pair, axis, bit):
    row = lax.axis_size("gy")
    mask = bit * row if axis == "gz" else bit
    found = []
    for core, cells in enumerate(pair):
        devices = [i for i in range(lax.axis_size("gz") * row) if i % 2 == core]
        found.append(lax.ppermute(cells, ("gz", "gy"), [(i, i ^ mask) for i in devices]))
    return found


def across(pair, sources):
    count = lax.axis_size("gy")
    return [
        lax.ppermute(cells, "gy", [(i, i ^ 1) for i in range(count) if i % 2 == core])
        for core, cells in zip(sources, pair)
    ]


def tied(first, *others):
    found = lax.optimization_barrier((first, *others))
    return found[0], tuple(found[1:])


def swapped(near, far, axis):
    return swap(near, axis, 0), swap(far, axis, 1)


def body(features, conv_weight, down_weight, cotangent):
    channels, plane_count, row_count, breadth = features.shape
    out_channels = down_weight.shape[2]
    count = lax.axis_size("gz") * lax.axis_size("gy")
    grad_scale = 1.0 / math.sqrt(plane_count * row_count * breadth * count)
    turned = conv_weight.reshape(3, 3, channels, 3, channels)[::-1, ::-1, :, ::-1]
    weight_bwd = turned.transpose(0, 1, 4, 3, 2).reshape(3, 3, channels, 3 * channels)
    cot = cotangent.reshape(out_channels, -1)
    plane = ((row_count, channels, breadth), BF16)
    edge = ((plane_count + 2, channels, breadth), BF16)
    cols = ((plane_count, row_count + 2, 3 * channels, breadth), BF16)
    edge_cols = ((plane_count + 2, 2, 3 * channels, breadth), BF16)
    lines = (plane_count, row_count, channels, breadth)
    conv_flops = 2 * 27 * channels * channels * plane_count * row_count * breadth

    own = call(
        lines_kernel, [plane, plane], [((channels * plane_count * row_count, breadth), F32)], 0, (features,)
    )
    outside = swapped(*own, "gz")
    inner, acc, hidden_grad = call(
        inner_kernel, [cols, (lines, F32), (lines, F32)],
        [((out_channels, row_count // 2 * breadth), BF16)],
        2 * conv_flops // 3, (*own, conv_weight, down_weight, cot),
    )
    near, far, acc = lax.optimization_barrier((*outside, acc))
    outside = (near, far)
    beside = swapped(*call(edges_kernel, [edge, edge], [], 0, (*own, *outside)), "gy")
    outer, acc = call(
        outer_kernel, [cols, (lines, F32)], [], conv_flops // 3, (*outside, conv_weight, acc)
    )
    edges, near, far, hidden = call(
        gate_kernel, [edge_cols, plane, plane, (lines, BF16)], [], conv_flops // 10,
        (*beside, acc, hidden_grad, conv_weight),
    )
    gates = (near, far)

    used = 27 * channels * channels // 128 + 4 * out_channels
    total = -(-used // 64)
    sizes = [64 * (total // 3), 64 * (total - total // 3)]

    def both(shrink, kind):
        return [((size // shrink, 128), kind) for size in sizes]

    found = call(
        weight_grad_kernel, [*both(1, F32), *both(1, BF16)], [((sum(sizes), 128), F32)], conv_flops,
        (inner, outer, edges, *gates, hidden, cot),
    )
    keep, send = list(found[:2]), found[2:]
    keep[0], (hidden, *gates) = tied(keep[0], hidden, *gates)
    near, far = gates
    near_in = swap(near, "gz", 0)
    got = across(send, (1, 0))
    for level, (axis, bit) in enumerate((("gy", 2), ("gz", 2))):
        shrink = 2 << level
        found = call(
            functools.partial(halve_kernel, axis=axis, bit=bit),
            [*both(shrink, F32), *both(shrink, BF16)], both(shrink // 2, F32), 0, (*keep, *got),
        )
        keep, send = list(found[:2]), found[2:]
        if level == 0:
            keep[0], (far,) = tied(keep[0], far)
            far_in = swap(far, "gz", 1)
            (section_out,) = call(
                section_kernel, [((out_channels, cot.shape[1]), BF16)], [], conv_flops // 10,
                (hidden, down_weight),
            )
        got = flip(send, axis, bit)
    sums = list(call(add_kernel, both(4, BF16), [], 0, (*keep, *got)))
    sums[0], outside = tied(sums[0], near_in, far_in)
    sends = call(edges_kernel, [edge, edge], [], 0, (*gates, *outside))
    beside = swapped(*sends, "gy")
    (acc,) = call(
        field_kernel, [(lines, F32)], [cols, cols], conv_flops, (*gates, *outside, weight_bwd)
    )
    bits = [("gz", 1)]
    bits += [("gy", 1 << k) for k in range(2, lax.axis_size("gy").bit_length() - 1)]
    bits += [("gz", 1 << k) for k in range(2, lax.axis_size("gz").bit_length() - 1)]
    for axis, bit in bits:
        sums = list(call(add_kernel, both(4, BF16), [], 0, (*sums, *flip(sums, axis, bit))))
    sums[0], (*beside, section_out) = tied(sums[0], *beside, section_out)
    sums = list(
        call(
            functools.partial(join_kernel, axis="gz", bit=2), both(2, BF16), [], 0,
            (*sums, *flip(sums, "gz", 2)),
        )
    )
    sums[0], (acc,) = tied(sums[0], acc)
    (field,) = call(
        field_edges_kernel, [((channels * plane_count * row_count, breadth), F32)], [edge_cols],
        conv_flops // 10, (*beside, acc, weight_bwd),
    )
    sums = call(
        functools.partial(join_kernel, axis="gy", bit=2), both(1, BF16), [], 0,
        (*sums, *flip(sums, "gy", 2)),
    )
    got = across(sums, (0, 1))
    got[0], (field,) = tied(got[0], field)
    grad_conv, grad_down = call(
        functools.partial(unpack_kernel, scale=grad_scale),
        [(conv_weight.shape, F32), (down_weight.shape, F32)], [((sum(sizes), 128), BF16)], 0,
        (*sums, *got),
    )
    section_out = section_out.reshape(out_channels, plane_count // 2, -1)
    return (section_out, field.reshape(features.shape), grad_conv, grad_down)


def solution(mesh):
    return jax.shard_map(
        body,
        mesh=mesh,
        in_specs=(P(None, "gz", "gy", None), P(), P(), P(None, "gz", "gy")),
        out_specs=(P(None, "gz", "gy"), P(None, "gz", "gy", None), P(), P()),
        check_vma=False,
    )
```

```python
import functools
import math

import jax
import jax.numpy as jnp
from jax import lax
from jax.experimental import pallas as pl
from jax.experimental.pallas import tpu as pltpu
from jax.sharding import PartitionSpec as P

F32 = jnp.float32
BF16 = jnp.bfloat16
PARAMS = pltpu.CompilerParams(vmem_limit_bytes=24 * 1024 * 1024)


def call(kernel, outs, scratch, flops, operands):
    moved = sum(x.size * x.dtype.itemsize for x in operands)
    moved += sum(math.prod(s) * jnp.dtype(d).itemsize for s, d in outs)
    vmem = pl.BlockSpec(memory_space=pltpu.VMEM)
    return pl.pallas_call(
        kernel,
        out_shape=[jax.ShapeDtypeStruct(s, d) for s, d in outs],
        in_specs=[vmem] * len(operands),
        out_specs=[vmem] * len(outs),
        scratch_shapes=[pltpu.VMEM(s, d) for s, d in scratch],
        compiler_params=PARAMS,
        cost_estimate=pl.CostEstimate(flops=flops, bytes_accessed=moved, transcendentals=0),
    )(*operands)


def is_even(axis):
    return lax.rem(lax.axis_index(axis), 2) == 0


def choose(cond, yes, no):
    return jnp.where(jnp.broadcast_to(cond, yes.shape), yes, no)


def lines_kernel(f_ref, near_ref, far_ref, wide):
    channels, planes, rows, breadth = f_ref.shape
    wide[...] = f_ref[...].astype(F32).reshape(channels * planes * rows, breadth)
    even = is_even("gz")
    for y in range(rows):
        low, high = (
            wide[pl.ds(z * rows + y, channels, stride=planes * rows), :].astype(BF16) for z in range(2)
        )
        near_ref[y] = choose(even, high, low)
        far_ref[y] = choose(even, low, high)


def edges_kernel(near, far, near_in, far_in, near_ref, far_ref):
    rows = near.shape[0]
    even_z, even_y = is_even("gz"), is_even("gy")

    def put(p, one, other):
        first = choose(even_z, one[0], other[0])
        last = choose(even_z, one[rows - 1], other[rows - 1])
        near_ref[p] = choose(even_y, last, first)
        far_ref[p] = choose(even_y, first, last)

    put(0, far_in, near_in)
    put(1, far, near)
    put(2, near, far)
    put(3, near_in, far_in)


def put_columns(cols, p, q, line):
    channels = line.shape[0]
    wide = line.astype(F32)
    cols[p, q, 0:channels] = pltpu.roll(wide, 1, 1).astype(BF16)
    cols[p, q, channels : 2 * channels] = line
    cols[p, q, 2 * channels : 3 * channels] = pltpu.roll(wide, line.shape[1] - 1, 1).astype(BF16)


def fill_columns(cols, near, far):
    rows = near.shape[0]
    even = is_even("gz")

    def step(y, carry):
        put_columns(cols, 0, y + 1, choose(even, far[y], near[y]))
        put_columns(cols, 1, y + 1, choose(even, near[y], far[y]))
        return carry

    lax.fori_loop(0, rows, step, 0, unroll=2)
    for p in range(2):
        for q in (0, rows + 1):
            cols[p, q] = jnp.zeros(cols.shape[2:], BF16)


def fill_edges(cols, near, far):
    even = is_even("gy")
    for p in range(4):
        put_columns(cols, p, 0, choose(even, far[p], near[p]))
        put_columns(cols, p, 1, choose(even, near[p], far[p]))


def dot(lhs, rhs):
    return jnp.dot(lhs, rhs, preferred_element_type=F32)


def taps(w_ref, b, first, last):
    return jnp.concatenate([w_ref[a, b] for a in range(first, last)], axis=0)


def window(cols, p, q):
    return jnp.concatenate([cols[p, q], cols[p, q + 1]], axis=1)


def inner_terms(cols, w_ref, y):
    acc = None
    for b in range(3):
        for p in range(2):
            term = dot(taps(w_ref, b, p, p + 2), window(cols, p, y + b))
            acc = term if acc is None else acc + term
    half = acc.shape[0] // 2
    return acc[half:], acc[:half]


def outer_terms(cols, w_ref, y):
    lower = upper = None
    for b in range(3):
        low, high = dot(w_ref[0, b], window(cols, 0, y + b)), dot(w_ref[2, b], window(cols, 1, y + b))
        lower = low if lower is None else lower + low
        upper = high if upper is None else upper + high
    return lower, upper


def edge_terms(edges, w_ref, side):
    b = 2 * side
    half = w_ref.shape[2]
    acc = dot(taps(w_ref, b, 0, 2), edges[1, side]) + dot(taps(w_ref, b, 1, 3), edges[2, side])
    return acc[half:] + dot(w_ref[0, b], edges[0, side]), acc[:half] + dot(w_ref[2, b], edges[3, side])


def inner_kernel(near, far, w_ref, d_ref, cot_ref, cols, acc_ref, grad_ref, up):
    rows, channels, breadth = near.shape
    fill_columns(cols, near, far)
    source = lax.broadcasted_iota(jnp.int32, (breadth, 2 * breadth), 0)
    target = lax.broadcasted_iota(jnp.int32, (breadth, 2 * breadth), 1)
    spread = jnp.where(source == target // 2, 1.0, 0.0).astype(BF16)
    for pair in range(rows // 4):
        both = dot(cot_ref[:, pair * breadth : (pair + 1) * breadth], spread)
        up[:, 2 * pair * breadth : 2 * (pair + 1) * breadth] = both.astype(BF16)
    even = lax.broadcasted_iota(jnp.int32, (channels, breadth), 1) % 2 == 0
    for a in range(2):
        for b in range(2):
            terms = lax.dot_general(d_ref[a, b], up[...], (((0,), (0,)), ((), ())), preferred_element_type=F32)
            for t in range(rows // 2):
                part = terms[:, t * breadth : (t + 1) * breadth]
                grad_ref[a, 2 * t + b] = jnp.where(even, part[0:channels], part[channels:])

    def step(t, carry):
        y = 2 * t
        for z, lines in enumerate(inner_terms(cols, w_ref, y)):
            for b in range(2):
                acc_ref[z, y + b] = lines[:, b * breadth : (b + 1) * breadth]
        return carry

    lax.fori_loop(0, rows // 2, step, 0)


def outer_kernel(near, far, w_ref, acc_ref, cols, out_ref):
    rows, channels, breadth = near.shape
    fill_columns(cols, near, far)

    def step(t, carry):
        y = 2 * t
        for z, lines in enumerate(outer_terms(cols, w_ref, y)):
            for b in range(2):
                out_ref[z, y + b] = acc_ref[z, y + b] + lines[:, b * breadth : (b + 1) * breadth]
        return carry

    lax.fori_loop(0, rows // 2, step, 0)


def gate_kernel(near, far, acc_ref, grad_ref, w_ref, edges, near_ref, far_ref, h_ref):
    rows, channels, breadth = acc_ref.shape[1:]
    fill_edges(edges, near, far)
    sides = [edge_terms(edges, w_ref, side) for side in range(2)]
    even = is_even("gz")

    def gate(y, extra):
        found = []
        for z in range(2):
            preact = acc_ref[z, y] if extra is None else acc_ref[z, y] + extra[z]
            sig = 1.0 / (1.0 + jnp.exp(-preact))
            h_ref[z, y] = (preact * sig).astype(BF16)
            found.append((grad_ref[z, y] * sig * (1.0 + preact * (1.0 - sig))).astype(BF16))
        near_ref[y] = choose(even, found[1], found[0])
        far_ref[y] = choose(even, found[0], found[1])

    gate(0, sides[0])
    for y in range(1, rows - 1):
        gate(y, None)
    gate(rows - 1, sides[1])


def coarse_hidden(h_ref, a, b):
    rows, channels, breadth = h_ref.shape[1:]
    source = lax.broadcasted_iota(jnp.int32, (2 * breadth, 2 * breadth), 0)
    target = lax.broadcasted_iota(jnp.int32, (2 * breadth, 2 * breadth), 1)
    wanted = 2 * (target % breadth) + target // breadth
    pick = jnp.where(source == wanted, 1.0, 0.0).astype(BF16)
    pairs = []
    for pair in range(rows // 4):
        both = jnp.concatenate([h_ref[a, 4 * pair + b], h_ref[a, 4 * pair + 2 + b]], axis=1)
        pairs.append(dot(both, pick).astype(BF16))
    return jnp.concatenate(
        [jnp.concatenate([x[:, e * breadth : (e + 1) * breadth] for x in pairs], axis=1) for e in range(2)],
        axis=0,
    )


def section_kernel(h_ref, d_ref, out_ref):
    coarse = None
    for a in range(2):
        for b in range(2):
            term = dot(d_ref[a, b], coarse_hidden(h_ref, a, b))
            coarse = term if coarse is None else coarse + term
    out_ref[...] = coarse.astype(BF16)


def weight_grad_kernel(inner, outer, edges, near, far, h_ref, cot_ref, keep, send, packed):
    rows, channels, breadth = near.shape
    across = (((1,), (1,)), ((), ()))
    even = is_even("gz")
    low = [choose(even, far[y], near[y]) for y in range(rows)]
    high = [choose(even, near[y], far[y]) for y in range(rows)]
    gates = jnp.concatenate([jnp.concatenate(low, axis=1), jnp.concatenate(high, axis=1)], axis=0)

    def columns(p, q):
        if q in (0, rows + 1):
            return edges[p, 0 if q == 0 else 1]
        return inner[p - 1, q] if p in (1, 2) else outer[p // 3, q]

    lane = lax.broadcasted_iota(jnp.int32, (channels // 2, breadth), 1)
    for b in range(3):
        parts = []
        for p in range(4):
            across_rows = jnp.concatenate([columns(p, y + b) for y in range(rows)], axis=1)
            lhs = gates[0:channels] if p == 0 else gates[channels:] if p == 3 else gates
            parts.append(lax.dot_general(lhs, across_rows, across, preferred_element_type=F32))
        for a in range(3):
            low = parts[a][0:channels]
            high = parts[a + 1] if a == 2 else parts[a + 1][channels:]
            total = low + high
            base = (a * 3 + b) * 3 * channels // 2
            packed[base : base + channels] = total[:, 0:breadth]
            rest = jnp.concatenate([total[:, breadth:], total[:, breadth:]], axis=1)
            mix = jnp.where(lane < channels, rest[0 : channels // 2], rest[channels // 2 :])
            packed[base + channels : base + 3 * channels // 2] = mix
    base = 9 * 3 * channels // 2
    height = cot_ref.shape[0]
    for a in range(2):
        for b in range(2):
            down = lax.dot_general(cot_ref[...], coarse_hidden(h_ref, a, b), across, preferred_element_type=F32)
            at = base + (2 * a + b) * height
            packed[at : at + height] = down
    end = base + 4 * height
    if end < packed.shape[0]:
        packed[end:] = jnp.zeros((packed.shape[0] - end, packed.shape[1]), F32)
    half = packed.shape[0] // 2
    split(packed, keep, send, half, "gy", 1)


def side_of(axis, bit):
    return lax.rem(lax.axis_index(axis) // bit, 2)


def part(side, rows):
    return pl.ds(pl.multiple_of(side * rows, 16), rows)


def split(packed, keep, send, half, axis, bit):
    side = side_of(axis, bit)
    keep[...] = packed[part(side, half)]
    send[...] = packed[part(1 - side, half)].astype(BF16)


def halve_kernel(mine, other, keep, send, total, *, axis, bit):
    total[...] = mine[...] + other[...].astype(F32)
    split(total, keep, send, total.shape[0] // 2, axis, bit)


def add_kernel(x, y, out):
    out[...] = (x[...].astype(F32) + y[...].astype(F32)).astype(BF16)


def join_kernel(mine, other, out, *, axis, bit):
    rows = mine.shape[0]
    side = side_of(axis, bit)
    out[part(side, rows)] = mine[...]
    out[part(1 - side, rows)] = other[...]


def field_kernel(near, far, near_in, far_in, w_ref, acc_ref, inner, outer):
    rows, channels, breadth = near.shape
    fill_columns(inner, near, far)
    fill_columns(outer, near_in, far_in)

    def step(t, carry):
        y = 2 * t
        own = inner_terms(inner, w_ref, y)
        rest = outer_terms(outer, w_ref, y)
        for z in range(2):
            total = own[z] + rest[z]
            for b in range(2):
                acc_ref[z, y + b] = total[:, b * breadth : (b + 1) * breadth]
        return carry

    lax.fori_loop(0, rows // 2, step, 0)


def field_edges_kernel(near, far, acc_ref, w_ref, out_ref, edges):
    rows, channels, breadth = acc_ref.shape[1:]
    fill_edges(edges, near, far)
    sides = [edge_terms(edges, w_ref, side) for side in range(2)]
    for z in range(2):
        for y in range(rows):
            line = acc_ref[z, y]
            if y in (0, rows - 1):
                line = line + sides[0 if y == 0 else 1][z]
            out_ref[pl.ds(z * rows + y, channels, stride=2 * rows), :] = line


def unpack_kernel(mine, other, conv_ref, down_ref, sums_ref, *, scale):
    join_kernel(mine, other, sums_ref, axis="gy", bit=1)
    channels = conv_ref.shape[2]
    for a in range(3):
        for b in range(3):
            base = (a * 3 + b) * 3 * channels // 2
            conv_ref[a, b, :, 0 : 2 * channels] = sums_ref[base : base + channels].astype(F32) * scale
            rest = sums_ref[base + channels : base + 3 * channels // 2].astype(F32) * scale
            conv_ref[a, b, 0 : channels // 2, 2 * channels :] = rest[:, 0:channels]
            conv_ref[a, b, channels // 2 :, 2 * channels :] = rest[:, channels:]
    base = 9 * 3 * channels // 2
    height = down_ref.shape[2]
    for a in range(2):
        for b in range(2):
            at = base + (2 * a + b) * height
            down_ref[a, b] = sums_ref[at : at + height].astype(F32) * scale


def swap(cells, axis, low):
    count = lax.axis_size(axis)
    pairs = [(i % count, (i + 1) % count) for i in range(low, low + count, 2)]
    return lax.ppermute(cells, axis, pairs + [(b, a) for a, b in pairs])


def flip(cells, axis, bit):
    return lax.ppermute(cells, axis, [(i, i ^ bit) for i in range(lax.axis_size(axis))])


def tied(first, *others):
    found = lax.optimization_barrier((first, *others))
    return found[0], tuple(found[1:])


def swapped(near, far, axis):
    return swap(near, axis, 0), swap(far, axis, 1)


def body(features, conv_weight, down_weight, cotangent):
    channels, plane_count, row_count, breadth = features.shape
    out_channels = down_weight.shape[2]
    count = lax.axis_size("gz") * lax.axis_size("gy")
    grad_scale = 1.0 / math.sqrt(plane_count * row_count * breadth * count)
    turned = conv_weight.reshape(3, 3, channels, 3, channels)[::-1, ::-1, :, ::-1]
    weight_bwd = turned.transpose(0, 1, 4, 3, 2).reshape(3, 3, channels, 3 * channels)
    cot = cotangent.reshape(out_channels, -1)
    plane = ((row_count, channels, breadth), BF16)
    edge = ((plane_count + 2, channels, breadth), BF16)
    cols = ((plane_count, row_count + 2, 3 * channels, breadth), BF16)
    edge_cols = ((plane_count + 2, 2, 3 * channels, breadth), BF16)
    lines = (plane_count, row_count, channels, breadth)
    conv_flops = 2 * 27 * channels * channels * plane_count * row_count * breadth

    own = call(
        lines_kernel, [plane, plane], [((channels * plane_count * row_count, breadth), F32)], 0, (features,)
    )
    outside = swapped(*own, "gz")
    inner, acc, hidden_grad = call(
        inner_kernel, [cols, (lines, F32), (lines, F32)],
        [((out_channels, row_count // 2 * breadth), BF16)],
        2 * conv_flops // 3, (*own, conv_weight, down_weight, cot),
    )
    near, far, acc = lax.optimization_barrier((*outside, acc))
    outside = (near, far)
    beside = swapped(*call(edges_kernel, [edge, edge], [], 0, (*own, *outside)), "gy")
    outer, acc = call(
        outer_kernel, [cols, (lines, F32)], [], conv_flops // 3, (*outside, conv_weight, acc)
    )
    edges, near, far, hidden = call(
        gate_kernel, [edge_cols, plane, plane, (lines, BF16)], [], conv_flops // 10,
        (*beside, acc, hidden_grad, conv_weight),
    )
    gates = (near, far)

    used = 27 * channels * channels // 128 + 4 * out_channels
    rows = -(-used // 128) * 128
    keep, send = call(
        weight_grad_kernel, [((rows // 2, 128), F32), ((rows // 2, 128), BF16)], [((rows, 128), F32)],
        conv_flops, (inner, outer, edges, *gates, hidden, cot),
    )
    keep, gates = tied(keep, *gates)
    near, far = gates
    near_in = swap(near, "gz", 0)
    for level, (axis, bit) in enumerate((("gy", 2), ("gz", 2))):
        size = rows >> (level + 2)
        mine, got = keep, flip(send, *(("gy", 1), ("gy", 2))[level])
        keep, send = call(
            functools.partial(halve_kernel, axis=axis, bit=bit),
            [((size, 128), F32), ((size, 128), BF16)], [((2 * size, 128), F32)], 0, (mine, got),
        )
        if level == 0:
            keep, (far, hidden) = tied(keep, far, hidden)
            far_in = swap(far, "gz", 1)
            (section_out,) = call(
                section_kernel, [((out_channels, cot.shape[1]), BF16)], [], conv_flops // 10,
                (hidden, down_weight),
            )
    shard = ((rows // 8, 128), BF16)
    (sums,) = call(add_kernel, [shard], [], 0, (keep, flip(send, "gz", 2)))
    (sums,) = call(add_kernel, [shard], [], 0, (sums, flip(sums, "gz", 1)))
    sums, outside = tied(sums, near_in, far_in)
    sends = call(edges_kernel, [edge, edge], [], 0, (*gates, *outside))
    beside = swapped(*sends, "gy")
    (acc,) = call(
        field_kernel, [(lines, F32)], [cols, cols], conv_flops, (*gates, *outside, weight_bwd)
    )
    wide = [("gy", 1 << k) for k in range(2, lax.axis_size("gy").bit_length() - 1)]
    wide += [("gz", 1 << k) for k in range(2, lax.axis_size("gz").bit_length() - 1)]
    for axis, bit in wide:
        (sums,) = call(add_kernel, [shard], [], 0, (sums, flip(sums, axis, bit)))
    sums, (section_out,) = tied(sums, section_out)
    (sums,) = call(
        functools.partial(join_kernel, axis="gz", bit=2), [((rows // 4, 128), BF16)], [], 0,
        (sums, flip(sums, "gz", 2)),
    )
    sums, (acc, *beside) = tied(sums, acc, *beside)
    (field,) = call(
        field_edges_kernel, [((channels * plane_count * row_count, breadth), F32)], [edge_cols],
        conv_flops // 10, (*beside, acc, weight_bwd),
    )
    (sums,) = call(
        functools.partial(join_kernel, axis="gy", bit=2), [((rows // 2, 128), BF16)], [], 0,
        (sums, flip(sums, "gy", 2)),
    )
    sums, (field,) = tied(sums, field)
    grad_conv, grad_down = call(
        functools.partial(unpack_kernel, scale=grad_scale),
        [(conv_weight.shape, F32), (down_weight.shape, F32)], [((rows, 128), BF16)], 0,
        (sums, flip(sums, "gy", 1)),
    )
    section_out = section_out.reshape(out_channels, plane_count // 2, -1)
    return (section_out, field.reshape(features.shape), grad_conv, grad_down)


def solution(mesh):
    return jax.shard_map(
        body,
        mesh=mesh,
        in_specs=(P(None, "gz", "gy", None), P(), P(), P(None, "gz", "gy")),
        out_specs=(P(None, "gz", "gy"), P(None, "gz", "gy", None), P(), P()),
        check_vma=False,
    )
```

```python
import functools
import math

import jax
import jax.numpy as jnp
from jax import lax
from jax.experimental import pallas as pl
from jax.experimental.pallas import tpu as pltpu
from jax.sharding import PartitionSpec as P

F32 = jnp.float32
BF16 = jnp.bfloat16
PARAMS = pltpu.CompilerParams(vmem_limit_bytes=24 * 1024 * 1024)


def call(kernel, outs, scratch, flops, operands):
    moved = sum(x.size * x.dtype.itemsize for x in operands)
    moved += sum(math.prod(s) * jnp.dtype(d).itemsize for s, d in outs)
    vmem = pl.BlockSpec(memory_space=pltpu.VMEM)
    return pl.pallas_call(
        kernel,
        out_shape=[jax.ShapeDtypeStruct(s, d) for s, d in outs],
        in_specs=[vmem] * len(operands),
        out_specs=[vmem] * len(outs),
        scratch_shapes=[pltpu.VMEM(s, d) for s, d in scratch],
        compiler_params=PARAMS,
        cost_estimate=pl.CostEstimate(flops=flops, bytes_accessed=moved, transcendentals=0),
    )(*operands)


def is_even(axis):
    return lax.rem(lax.axis_index(axis), 2) == 0


def choose(cond, yes, no):
    return jnp.where(jnp.broadcast_to(cond, yes.shape), yes, no)


def lines_kernel(f_ref, near_ref, far_ref, wide):
    channels, planes, rows, breadth = f_ref.shape
    wide[...] = f_ref[...].astype(F32).reshape(channels * planes * rows, breadth)
    even = is_even("gz")
    for y in range(rows):
        low, high = (
            wide[pl.ds(z * rows + y, channels, stride=planes * rows), :].astype(BF16) for z in range(2)
        )
        near_ref[y] = choose(even, high, low)
        far_ref[y] = choose(even, low, high)


def edges_kernel(near, far, near_in, far_in, near_ref, far_ref):
    rows = near.shape[0]
    even_z, even_y = is_even("gz"), is_even("gy")

    def put(p, one, other):
        first = choose(even_z, one[0], other[0])
        last = choose(even_z, one[rows - 1], other[rows - 1])
        near_ref[p] = choose(even_y, last, first)
        far_ref[p] = choose(even_y, first, last)

    put(0, far_in, near_in)
    put(1, far, near)
    put(2, near, far)
    put(3, near_in, far_in)


def put_columns(cols, p, q, line):
    channels = line.shape[0]
    wide = line.astype(F32)
    cols[p, q, 0:channels] = pltpu.roll(wide, 1, 1).astype(BF16)
    cols[p, q, channels : 2 * channels] = line
    cols[p, q, 2 * channels : 3 * channels] = pltpu.roll(wide, line.shape[1] - 1, 1).astype(BF16)


def fill_columns(cols, near, far):
    rows = near.shape[0]
    even = is_even("gz")

    def step(y, carry):
        put_columns(cols, 0, y + 1, choose(even, far[y], near[y]))
        put_columns(cols, 1, y + 1, choose(even, near[y], far[y]))
        return carry

    lax.fori_loop(0, rows, step, 0, unroll=2)
    for p in range(2):
        for q in (0, rows + 1):
            cols[p, q] = jnp.zeros(cols.shape[2:], BF16)


def fill_edges(cols, near, far):
    even = is_even("gy")
    for p in range(4):
        put_columns(cols, p, 0, choose(even, far[p], near[p]))
        put_columns(cols, p, 1, choose(even, near[p], far[p]))


def dot(lhs, rhs):
    return jnp.dot(lhs, rhs, preferred_element_type=F32)


def taps(w_ref, b, first, last):
    return jnp.concatenate([w_ref[a, b] for a in range(first, last)], axis=0)


def window(cols, p, q):
    return jnp.concatenate([cols[p, q], cols[p, q + 1]], axis=1)


def inner_terms(cols, w_ref, y):
    acc = None
    for b in range(3):
        for p in range(2):
            term = dot(taps(w_ref, b, p, p + 2), window(cols, p, y + b))
            acc = term if acc is None else acc + term
    half = acc.shape[0] // 2
    return acc[half:], acc[:half]


def outer_terms(cols, w_ref, y):
    lower = upper = None
    for b in range(3):
        low, high = dot(w_ref[0, b], window(cols, 0, y + b)), dot(w_ref[2, b], window(cols, 1, y + b))
        lower = low if lower is None else lower + low
        upper = high if upper is None else upper + high
    return lower, upper


def edge_terms(edges, w_ref, side):
    b = 2 * side
    half = w_ref.shape[2]
    acc = dot(taps(w_ref, b, 0, 2), edges[1, side]) + dot(taps(w_ref, b, 1, 3), edges[2, side])
    return acc[half:] + dot(w_ref[0, b], edges[0, side]), acc[:half] + dot(w_ref[2, b], edges[3, side])


def inner_kernel(near, far, w_ref, d_ref, cot_ref, cols, acc_ref, grad_ref, up):
    rows, channels, breadth = near.shape
    fill_columns(cols, near, far)
    source = lax.broadcasted_iota(jnp.int32, (breadth, 2 * breadth), 0)
    target = lax.broadcasted_iota(jnp.int32, (breadth, 2 * breadth), 1)
    spread = jnp.where(source == target // 2, 1.0, 0.0).astype(BF16)
    for pair in range(rows // 4):
        both = dot(cot_ref[:, pair * breadth : (pair + 1) * breadth], spread)
        up[:, 2 * pair * breadth : 2 * (pair + 1) * breadth] = both.astype(BF16)
    even = lax.broadcasted_iota(jnp.int32, (channels, breadth), 1) % 2 == 0
    for a in range(2):
        for b in range(2):
            terms = lax.dot_general(d_ref[a, b], up[...], (((0,), (0,)), ((), ())), preferred_element_type=F32)
            for t in range(rows // 2):
                part = terms[:, t * breadth : (t + 1) * breadth]
                grad_ref[a, 2 * t + b] = jnp.where(even, part[0:channels], part[channels:])

    def step(t, carry):
        y = 2 * t
        for z, lines in enumerate(inner_terms(cols, w_ref, y)):
            for b in range(2):
                acc_ref[z, y + b] = lines[:, b * breadth : (b + 1) * breadth]
        return carry

    lax.fori_loop(0, rows // 2, step, 0)


def outer_kernel(near, far, w_ref, acc_ref, cols, out_ref):
    rows, channels, breadth = near.shape
    fill_columns(cols, near, far)

    def step(t, carry):
        y = 2 * t
        for z, lines in enumerate(outer_terms(cols, w_ref, y)):
            for b in range(2):
                out_ref[z, y + b] = acc_ref[z, y + b] + lines[:, b * breadth : (b + 1) * breadth]
        return carry

    lax.fori_loop(0, rows // 2, step, 0)


def gate_kernel(near, far, acc_ref, grad_ref, w_ref, edges, near_ref, far_ref, h_ref):
    rows, channels, breadth = acc_ref.shape[1:]
    fill_edges(edges, near, far)
    sides = [edge_terms(edges, w_ref, side) for side in range(2)]
    even = is_even("gz")

    def gate(y, extra):
        found = []
        for z in range(2):
            preact = acc_ref[z, y] if extra is None else acc_ref[z, y] + extra[z]
            sig = 1.0 / (1.0 + jnp.exp(-preact))
            h_ref[z, y] = (preact * sig).astype(BF16)
            found.append((grad_ref[z, y] * sig * (1.0 + preact * (1.0 - sig))).astype(BF16))
        near_ref[y] = choose(even, found[1], found[0])
        far_ref[y] = choose(even, found[0], found[1])

    gate(0, sides[0])
    for y in range(1, rows - 1):
        gate(y, None)
    gate(rows - 1, sides[1])


def coarse_hidden(h_ref, a, b):
    rows, channels, breadth = h_ref.shape[1:]
    source = lax.broadcasted_iota(jnp.int32, (2 * breadth, 2 * breadth), 0)
    target = lax.broadcasted_iota(jnp.int32, (2 * breadth, 2 * breadth), 1)
    wanted = 2 * (target % breadth) + target // breadth
    pick = jnp.where(source == wanted, 1.0, 0.0).astype(BF16)
    pairs = []
    for pair in range(rows // 4):
        both = jnp.concatenate([h_ref[a, 4 * pair + b], h_ref[a, 4 * pair + 2 + b]], axis=1)
        pairs.append(dot(both, pick).astype(BF16))
    return jnp.concatenate(
        [jnp.concatenate([x[:, e * breadth : (e + 1) * breadth] for x in pairs], axis=1) for e in range(2)],
        axis=0,
    )


def section_kernel(h_ref, d_ref, out_ref):
    coarse = None
    for a in range(2):
        for b in range(2):
            term = dot(d_ref[a, b], coarse_hidden(h_ref, a, b))
            coarse = term if coarse is None else coarse + term
    out_ref[...] = coarse.astype(BF16)


def weight_grad_kernel(inner, outer, edges, near, far, h_ref, cot_ref, keep, send, packed):
    rows, channels, breadth = near.shape
    across = (((1,), (1,)), ((), ()))
    even = is_even("gz")
    low = [choose(even, far[y], near[y]) for y in range(rows)]
    high = [choose(even, near[y], far[y]) for y in range(rows)]
    gates = jnp.concatenate([jnp.concatenate(low, axis=1), jnp.concatenate(high, axis=1)], axis=0)

    def columns(p, q):
        if q in (0, rows + 1):
            return edges[p, 0 if q == 0 else 1]
        return inner[p - 1, q] if p in (1, 2) else outer[p // 3, q]

    lane = lax.broadcasted_iota(jnp.int32, (channels // 2, breadth), 1)
    for b in range(3):
        parts = []
        for p in range(4):
            across_rows = jnp.concatenate([columns(p, y + b) for y in range(rows)], axis=1)
            lhs = gates[0:channels] if p == 0 else gates[channels:] if p == 3 else gates
            parts.append(lax.dot_general(lhs, across_rows, across, preferred_element_type=F32))
        for a in range(3):
            low = parts[a][0:channels]
            high = parts[a + 1] if a == 2 else parts[a + 1][channels:]
            total = low + high
            base = (a * 3 + b) * 3 * channels // 2
            packed[base : base + channels] = total[:, 0:breadth]
            rest = jnp.concatenate([total[:, breadth:], total[:, breadth:]], axis=1)
            mix = jnp.where(lane < channels, rest[0 : channels // 2], rest[channels // 2 :])
            packed[base + channels : base + 3 * channels // 2] = mix
    base = 9 * 3 * channels // 2
    height = cot_ref.shape[0]
    for a in range(2):
        for b in range(2):
            down = lax.dot_general(cot_ref[...], coarse_hidden(h_ref, a, b), across, preferred_element_type=F32)
            at = base + (2 * a + b) * height
            packed[at : at + height] = down
    end = base + 4 * height
    if end < packed.shape[0]:
        packed[end:] = jnp.zeros((packed.shape[0] - end, packed.shape[1]), F32)
    split(packed, keep, send, owned_half())


def side_of(axis, bit):
    return lax.rem(lax.axis_index(axis) // bit, 2)


def owned_half():
    total = 0
    for axis in ("gz", "gy"):
        for k in range(lax.axis_size(axis).bit_length() - 1):
            total = total + side_of(axis, 1 << k)
    return lax.rem(total, 2)


def part(side, rows):
    return pl.ds(pl.multiple_of(side * rows, 16), rows)


def split(packed, keep, send, side):
    half = keep.shape[0]
    keep[...] = packed[part(side, half)]
    send[...] = packed[part(1 - side, half)].astype(BF16)


def halve_kernel(mine, other, keep, send, total, *, axis, bit):
    total[...] = mine[...] + other[...].astype(F32)
    split(total, keep, send, side_of(axis, bit))


def add_kernel(x, y, out):
    out[...] = (x[...].astype(F32) + y[...].astype(F32)).astype(BF16)


def join_kernel(mine, other, out, *, axis, bit):
    join(mine, other, out, side_of(axis, bit))


def join(mine, other, out, side):
    rows = mine.shape[0]
    out[part(side, rows)] = mine[...]
    out[part(1 - side, rows)] = other[...]


def field_kernel(near, far, near_in, far_in, w_ref, acc_ref, inner, outer):
    rows, channels, breadth = near.shape
    fill_columns(inner, near, far)
    fill_columns(outer, near_in, far_in)

    def step(t, carry):
        y = 2 * t
        own = inner_terms(inner, w_ref, y)
        rest = outer_terms(outer, w_ref, y)
        for z in range(2):
            total = own[z] + rest[z]
            for b in range(2):
                acc_ref[z, y + b] = total[:, b * breadth : (b + 1) * breadth]
        return carry

    lax.fori_loop(0, rows // 2, step, 0)


def field_edges_kernel(near, far, acc_ref, w_ref, out_ref, edges):
    rows, channels, breadth = acc_ref.shape[1:]
    fill_edges(edges, near, far)
    sides = [edge_terms(edges, w_ref, side) for side in range(2)]
    for z in range(2):
        for y in range(rows):
            line = acc_ref[z, y]
            if y in (0, rows - 1):
                line = line + sides[0 if y == 0 else 1][z]
            out_ref[pl.ds(z * rows + y, channels, stride=2 * rows), :] = line


def unpack_kernel(mine, other, conv_ref, down_ref, sums_ref, *, scale):
    join(mine, other, sums_ref, owned_half())
    channels = conv_ref.shape[2]
    for a in range(3):
        for b in range(3):
            base = (a * 3 + b) * 3 * channels // 2
            conv_ref[a, b, :, 0 : 2 * channels] = sums_ref[base : base + channels].astype(F32) * scale
            rest = sums_ref[base + channels : base + 3 * channels // 2].astype(F32) * scale
            conv_ref[a, b, 0 : channels // 2, 2 * channels :] = rest[:, 0:channels]
            conv_ref[a, b, channels // 2 :, 2 * channels :] = rest[:, channels:]
    base = 9 * 3 * channels // 2
    height = down_ref.shape[2]
    for a in range(2):
        for b in range(2):
            at = base + (2 * a + b) * height
            down_ref[a, b] = sums_ref[at : at + height].astype(F32) * scale


def swap(cells, axis, low):
    count = lax.axis_size(axis)
    pairs = [(i % count, (i + 1) % count) for i in range(low, low + count, 2)]
    return lax.ppermute(cells, axis, pairs + [(b, a) for a, b in pairs])


def flip(cells, axis, bit):
    row = lax.axis_size("gy")
    mask = bit * row | 1 if axis == "gz" else bit | 1
    return lax.ppermute(cells, ("gz", "gy"), [(i, i ^ mask) for i in range(lax.axis_size("gz") * row)])


def tied(first, *others):
    found = lax.optimization_barrier((first, *others))
    return found[0], tuple(found[1:])


def swapped(near, far, axis):
    return swap(near, axis, 0), swap(far, axis, 1)


def body(features, conv_weight, down_weight, cotangent):
    channels, plane_count, row_count, breadth = features.shape
    out_channels = down_weight.shape[2]
    count = lax.axis_size("gz") * lax.axis_size("gy")
    grad_scale = 1.0 / math.sqrt(plane_count * row_count * breadth * count)
    turned = conv_weight.reshape(3, 3, channels, 3, channels)[::-1, ::-1, :, ::-1]
    weight_bwd = turned.transpose(0, 1, 4, 3, 2).reshape(3, 3, channels, 3 * channels)
    cot = cotangent.reshape(out_channels, -1)
    plane = ((row_count, channels, breadth), BF16)
    edge = ((plane_count + 2, channels, breadth), BF16)
    cols = ((plane_count, row_count + 2, 3 * channels, breadth), BF16)
    edge_cols = ((plane_count + 2, 2, 3 * channels, breadth), BF16)
    lines = (plane_count, row_count, channels, breadth)
    conv_flops = 2 * 27 * channels * channels * plane_count * row_count * breadth

    own = call(
        lines_kernel, [plane, plane], [((channels * plane_count * row_count, breadth), F32)], 0, (features,)
    )
    outside = swapped(*own, "gz")
    inner, acc, hidden_grad = call(
        inner_kernel, [cols, (lines, F32), (lines, F32)],
        [((out_channels, row_count // 2 * breadth), BF16)],
        2 * conv_flops // 3, (*own, conv_weight, down_weight, cot),
    )
    near, far, acc = lax.optimization_barrier((*outside, acc))
    outside = (near, far)
    beside = swapped(*call(edges_kernel, [edge, edge], [], 0, (*own, *outside)), "gy")
    outer, acc = call(
        outer_kernel, [cols, (lines, F32)], [], conv_flops // 3, (*outside, conv_weight, acc)
    )
    edges, near, far, hidden = call(
        gate_kernel, [edge_cols, plane, plane, (lines, BF16)], [], conv_flops // 10,
        (*beside, acc, hidden_grad, conv_weight),
    )
    gates = (near, far)

    used = 27 * channels * channels // 128 + 4 * out_channels
    rows = -(-used // 128) * 128
    keep, send = call(
        weight_grad_kernel, [((rows // 2, 128), F32), ((rows // 2, 128), BF16)], [((rows, 128), F32)],
        conv_flops, (inner, outer, edges, *gates, hidden, cot),
    )
    keep, gates = tied(keep, *gates)
    near, far = gates
    near_in = swap(near, "gz", 0)
    for level, (axis, bit) in enumerate((("gy", 2), ("gz", 2))):
        size = rows >> (level + 2)
        mine, got = keep, flip(send, *(("gy", 1), ("gy", 2))[level])
        keep, send = call(
            functools.partial(halve_kernel, axis=axis, bit=bit),
            [((size, 128), F32), ((size, 128), BF16)], [((2 * size, 128), F32)], 0, (mine, got),
        )
        if level == 0:
            keep, (far, hidden) = tied(keep, far, hidden)
            far_in = swap(far, "gz", 1)
            (section_out,) = call(
                section_kernel, [((out_channels, cot.shape[1]), BF16)], [], conv_flops // 10,
                (hidden, down_weight),
            )
    shard = ((rows // 8, 128), BF16)
    (sums,) = call(add_kernel, [shard], [], 0, (keep, flip(send, "gz", 2)))
    (sums,) = call(add_kernel, [shard], [], 0, (sums, flip(sums, "gz", 1)))
    sums, outside = tied(sums, near_in, far_in)
    sends = call(edges_kernel, [edge, edge], [], 0, (*gates, *outside))
    beside = swapped(*sends, "gy")
    (acc,) = call(
        field_kernel, [(lines, F32)], [cols, cols], conv_flops, (*gates, *outside, weight_bwd)
    )
    wide = [("gy", 1 << k) for k in range(2, lax.axis_size("gy").bit_length() - 1)]
    wide += [("gz", 1 << k) for k in range(2, lax.axis_size("gz").bit_length() - 1)]
    for axis, bit in wide:
        (sums,) = call(add_kernel, [shard], [], 0, (sums, flip(sums, axis, bit)))
    sums, (section_out,) = tied(sums, section_out)
    (sums,) = call(
        functools.partial(join_kernel, axis="gz", bit=2), [((rows // 4, 128), BF16)], [], 0,
        (sums, flip(sums, "gz", 2)),
    )
    sums, (acc, *beside) = tied(sums, acc, *beside)
    (field,) = call(
        field_edges_kernel, [((channels * plane_count * row_count, breadth), F32)], [edge_cols],
        conv_flops // 10, (*beside, acc, weight_bwd),
    )
    (sums,) = call(
        functools.partial(join_kernel, axis="gy", bit=2), [((rows // 2, 128), BF16)], [], 0,
        (sums, flip(sums, "gy", 2)),
    )
    sums, (field,) = tied(sums, field)
    grad_conv, grad_down = call(
        functools.partial(unpack_kernel, scale=grad_scale),
        [(conv_weight.shape, F32), (down_weight.shape, F32)], [((rows, 128), BF16)], 0,
        (sums, flip(sums, "gy", 1)),
    )
    section_out = section_out.reshape(out_channels, plane_count // 2, -1)
    return (section_out, field.reshape(features.shape), grad_conv, grad_down)


def solution(mesh):
    return jax.shard_map(
        body,
        mesh=mesh,
        in_specs=(P(None, "gz", "gy", None), P(), P(), P(None, "gz", "gy")),
        out_specs=(P(None, "gz", "gy"), P(None, "gz", "gy", None), P(), P()),
        check_vma=False,
    )
```

```python
import functools
import math

import jax
import jax.numpy as jnp
from jax import lax
from jax.experimental import pallas as pl
from jax.experimental.pallas import tpu as pltpu
from jax.sharding import PartitionSpec as P

F32 = jnp.float32
BF16 = jnp.bfloat16
PARAMS = pltpu.CompilerParams(vmem_limit_bytes=24 * 1024 * 1024)


def call(kernel, outs, scratch, flops, operands):
    moved = sum(x.size * x.dtype.itemsize for x in operands)
    moved += sum(math.prod(s) * jnp.dtype(d).itemsize for s, d in outs)
    vmem = pl.BlockSpec(memory_space=pltpu.VMEM)
    return pl.pallas_call(
        kernel,
        out_shape=[jax.ShapeDtypeStruct(s, d) for s, d in outs],
        in_specs=[vmem] * len(operands),
        out_specs=[vmem] * len(outs),
        scratch_shapes=[pltpu.VMEM(s, d) for s, d in scratch],
        compiler_params=PARAMS,
        cost_estimate=pl.CostEstimate(flops=flops, bytes_accessed=moved, transcendentals=0),
    )(*operands)


def is_even(axis):
    return lax.rem(lax.axis_index(axis), 2) == 0


def choose(cond, yes, no):
    return jnp.where(jnp.broadcast_to(cond, yes.shape), yes, no)


def lines_kernel(f_ref, near_ref, far_ref, wide):
    channels, planes, rows, breadth = f_ref.shape
    wide[...] = f_ref[...].astype(F32).reshape(channels * planes * rows, breadth)
    even = is_even("gz")
    for y in range(rows):
        low, high = (
            wide[pl.ds(z * rows + y, channels, stride=planes * rows), :].astype(BF16) for z in range(2)
        )
        near_ref[y] = choose(even, high, low)
        far_ref[y] = choose(even, low, high)


def edges_kernel(near, far, near_in, far_in, near_ref, far_ref):
    rows = near.shape[0]
    even_z, even_y = is_even("gz"), is_even("gy")

    def put(p, one, other):
        first = choose(even_z, one[0], other[0])
        last = choose(even_z, one[rows - 1], other[rows - 1])
        near_ref[p] = choose(even_y, last, first)
        far_ref[p] = choose(even_y, first, last)

    put(0, far_in, near_in)
    put(1, far, near)
    put(2, near, far)
    put(3, near_in, far_in)


def put_columns(cols, p, q, line):
    channels = line.shape[0]
    wide = line.astype(F32)
    cols[p, q, 0:channels] = pltpu.roll(wide, 1, 1).astype(BF16)
    cols[p, q, channels : 2 * channels] = line
    cols[p, q, 2 * channels : 3 * channels] = pltpu.roll(wide, line.shape[1] - 1, 1).astype(BF16)


def fill_columns(cols, near, far):
    rows = near.shape[0]
    even = is_even("gz")

    def step(y, carry):
        put_columns(cols, 0, y + 1, choose(even, far[y], near[y]))
        put_columns(cols, 1, y + 1, choose(even, near[y], far[y]))
        return carry

    lax.fori_loop(0, rows, step, 0, unroll=2)
    for p in range(2):
        for q in (0, rows + 1):
            cols[p, q] = jnp.zeros(cols.shape[2:], BF16)


def fill_edges(cols, near, far):
    even = is_even("gy")
    for p in range(4):
        put_columns(cols, p, 0, choose(even, far[p], near[p]))
        put_columns(cols, p, 1, choose(even, near[p], far[p]))


def dot(lhs, rhs):
    return jnp.dot(lhs, rhs, preferred_element_type=F32)


def taps(w_ref, b, first, last):
    return jnp.concatenate([w_ref[a, b] for a in range(first, last)], axis=0)


def window(cols, p, q):
    return jnp.concatenate([cols[p, q], cols[p, q + 1]], axis=1)


def inner_terms(cols, w_ref, y):
    acc = None
    for b in range(3):
        for p in range(2):
            term = dot(taps(w_ref, b, p, p + 2), window(cols, p, y + b))
            acc = term if acc is None else acc + term
    half = acc.shape[0] // 2
    return acc[half:], acc[:half]


def outer_terms(cols, w_ref, y):
    lower = upper = None
    for b in range(3):
        low, high = dot(w_ref[0, b], window(cols, 0, y + b)), dot(w_ref[2, b], window(cols, 1, y + b))
        lower = low if lower is None else lower + low
        upper = high if upper is None else upper + high
    return lower, upper


def edge_terms(edges, w_ref, side):
    b = 2 * side
    half = w_ref.shape[2]
    acc = dot(taps(w_ref, b, 0, 2), edges[1, side]) + dot(taps(w_ref, b, 1, 3), edges[2, side])
    return acc[half:] + dot(w_ref[0, b], edges[0, side]), acc[:half] + dot(w_ref[2, b], edges[3, side])


def inner_kernel(near, far, w_ref, d_ref, cot_ref, cols, acc_ref, grad_ref, up):
    rows, channels, breadth = near.shape
    fill_columns(cols, near, far)
    source = lax.broadcasted_iota(jnp.int32, (breadth, 2 * breadth), 0)
    target = lax.broadcasted_iota(jnp.int32, (breadth, 2 * breadth), 1)
    spread = jnp.where(source == target // 2, 1.0, 0.0).astype(BF16)
    for pair in range(rows // 4):
        both = dot(cot_ref[:, pair * breadth : (pair + 1) * breadth], spread)
        up[:, 2 * pair * breadth : 2 * (pair + 1) * breadth] = both.astype(BF16)
    even = lax.broadcasted_iota(jnp.int32, (channels, breadth), 1) % 2 == 0
    for a in range(2):
        for b in range(2):
            terms = lax.dot_general(d_ref[a, b], up[...], (((0,), (0,)), ((), ())), preferred_element_type=F32)
            for t in range(rows // 2):
                part = terms[:, t * breadth : (t + 1) * breadth]
                grad_ref[a, 2 * t + b] = jnp.where(even, part[0:channels], part[channels:])

    def step(t, carry):
        y = 2 * t
        for z, lines in enumerate(inner_terms(cols, w_ref, y)):
            for b in range(2):
                acc_ref[z, y + b] = lines[:, b * breadth : (b + 1) * breadth]
        return carry

    lax.fori_loop(0, rows // 2, step, 0)


def outer_kernel(near, far, w_ref, acc_ref, cols, out_ref):
    rows, channels, breadth = near.shape
    fill_columns(cols, near, far)

    def step(t, carry):
        y = 2 * t
        for z, lines in enumerate(outer_terms(cols, w_ref, y)):
            for b in range(2):
                out_ref[z, y + b] = acc_ref[z, y + b] + lines[:, b * breadth : (b + 1) * breadth]
        return carry

    lax.fori_loop(0, rows // 2, step, 0)


def gate_kernel(near, far, acc_ref, grad_ref, w_ref, edges, near_ref, far_ref, h_ref):
    rows, channels, breadth = acc_ref.shape[1:]
    fill_edges(edges, near, far)
    sides = [edge_terms(edges, w_ref, side) for side in range(2)]
    even = is_even("gz")

    def gate(y, extra):
        found = []
        for z in range(2):
            preact = acc_ref[z, y] if extra is None else acc_ref[z, y] + extra[z]
            sig = 1.0 / (1.0 + jnp.exp(-preact))
            h_ref[z, y] = (preact * sig).astype(BF16)
            found.append((grad_ref[z, y] * sig * (1.0 + preact * (1.0 - sig))).astype(BF16))
        near_ref[y] = choose(even, found[1], found[0])
        far_ref[y] = choose(even, found[0], found[1])

    gate(0, sides[0])
    for y in range(1, rows - 1):
        gate(y, None)
    gate(rows - 1, sides[1])


def coarse_hidden(h_ref, a, b):
    rows, channels, breadth = h_ref.shape[1:]
    source = lax.broadcasted_iota(jnp.int32, (2 * breadth, 2 * breadth), 0)
    target = lax.broadcasted_iota(jnp.int32, (2 * breadth, 2 * breadth), 1)
    wanted = 2 * (target % breadth) + target // breadth
    pick = jnp.where(source == wanted, 1.0, 0.0).astype(BF16)
    pairs = []
    for pair in range(rows // 4):
        both = jnp.concatenate([h_ref[a, 4 * pair + b], h_ref[a, 4 * pair + 2 + b]], axis=1)
        pairs.append(dot(both, pick).astype(BF16))
    return jnp.concatenate(
        [jnp.concatenate([x[:, e * breadth : (e + 1) * breadth] for x in pairs], axis=1) for e in range(2)],
        axis=0,
    )


def section_kernel(h_ref, d_ref, out_ref):
    coarse = None
    for a in range(2):
        for b in range(2):
            term = dot(d_ref[a, b], coarse_hidden(h_ref, a, b))
            coarse = term if coarse is None else coarse + term
    out_ref[...] = coarse.astype(BF16)


def weight_grad_kernel(inner, outer, edges, near, far, h_ref, cot_ref, keep, send, packed):
    rows, channels, breadth = near.shape
    across = (((1,), (1,)), ((), ()))
    even = is_even("gz")
    low = [choose(even, far[y], near[y]) for y in range(rows)]
    high = [choose(even, near[y], far[y]) for y in range(rows)]
    gates = jnp.concatenate([jnp.concatenate(low, axis=1), jnp.concatenate(high, axis=1)], axis=0)

    def columns(p, q):
        if q in (0, rows + 1):
            return edges[p, 0 if q == 0 else 1]
        return inner[p - 1, q] if p in (1, 2) else outer[p // 3, q]

    lane = lax.broadcasted_iota(jnp.int32, (channels // 2, breadth), 1)
    for b in range(3):
        parts = []
        for p in range(4):
            across_rows = jnp.concatenate([columns(p, y + b) for y in range(rows)], axis=1)
            lhs = gates[0:channels] if p == 0 else gates[channels:] if p == 3 else gates
            parts.append(lax.dot_general(lhs, across_rows, across, preferred_element_type=F32))
        for a in range(3):
            low = parts[a][0:channels]
            high = parts[a + 1] if a == 2 else parts[a + 1][channels:]
            total = low + high
            base = (a * 3 + b) * 3 * channels // 2
            packed[base : base + channels] = total[:, 0:breadth]
            rest = jnp.concatenate([total[:, breadth:], total[:, breadth:]], axis=1)
            mix = jnp.where(lane < channels, rest[0 : channels // 2], rest[channels // 2 :])
            packed[base + channels : base + 3 * channels // 2] = mix
    base = 9 * 3 * channels // 2
    height = cot_ref.shape[0]
    for a in range(2):
        for b in range(2):
            down = lax.dot_general(cot_ref[...], coarse_hidden(h_ref, a, b), across, preferred_element_type=F32)
            at = base + (2 * a + b) * height
            packed[at : at + height] = down
    end = base + 4 * height
    if end < packed.shape[0]:
        packed[end:] = jnp.zeros((packed.shape[0] - end, packed.shape[1]), F32)
    split(packed, keep, send, owned_half())


def side_of(axis, bit):
    return lax.rem(lax.axis_index(axis) // bit, 2)


def owned_half():
    total = 0
    for axis in ("gz", "gy"):
        for k in range(lax.axis_size(axis).bit_length() - 1):
            total = total + side_of(axis, 1 << k)
    return lax.rem(total, 2)


def part(side, rows):
    return pl.ds(pl.multiple_of(side * rows, 16), rows)


def split(packed, keep, send, side):
    half = keep.shape[0]
    keep[...] = packed[part(side, half)]
    send[...] = packed[part(1 - side, half)].astype(BF16)


def halve_kernel(mine, other, keep, send, total, *, axis, bit):
    total[...] = mine[...] + other[...].astype(F32)
    split(total, keep, send, side_of(axis, bit))


def add_kernel(x, y, out):
    out[...] = (x[...].astype(F32) + y[...].astype(F32)).astype(BF16)


def join_kernel(mine, other, out, *, axis, bit):
    join(mine, other, out, side_of(axis, bit))


def join(mine, other, out, side):
    rows = mine.shape[0]
    out[part(side, rows)] = mine[...]
    out[part(1 - side, rows)] = other[...]


def field_kernel(near, far, near_in, far_in, w_ref, acc_ref, inner, outer):
    rows, channels, breadth = near.shape
    fill_columns(inner, near, far)
    fill_columns(outer, near_in, far_in)

    def step(t, carry):
        y = 2 * t
        own = inner_terms(inner, w_ref, y)
        rest = outer_terms(outer, w_ref, y)
        for z in range(2):
            total = own[z] + rest[z]
            for b in range(2):
                acc_ref[z, y + b] = total[:, b * breadth : (b + 1) * breadth]
        return carry

    lax.fori_loop(0, rows // 2, step, 0)


def field_edges_kernel(near, far, acc_ref, w_ref, out_ref, edges):
    rows, channels, breadth = acc_ref.shape[1:]
    fill_edges(edges, near, far)
    sides = [edge_terms(edges, w_ref, side) for side in range(2)]
    for z in range(2):
        for y in range(rows):
            line = acc_ref[z, y]
            if y in (0, rows - 1):
                line = line + sides[0 if y == 0 else 1][z]
            out_ref[pl.ds(z * rows + y, channels, stride=2 * rows), :] = line


def unpack_kernel(mine, other, conv_ref, down_ref, sums_ref, *, scale):
    join(mine, other, sums_ref, owned_half())
    channels = conv_ref.shape[2]
    for a in range(3):
        for b in range(3):
            base = (a * 3 + b) * 3 * channels // 2
            conv_ref[a, b, :, 0 : 2 * channels] = sums_ref[base : base + channels].astype(F32) * scale
            rest = sums_ref[base + channels : base + 3 * channels // 2].astype(F32) * scale
            conv_ref[a, b, 0 : channels // 2, 2 * channels :] = rest[:, 0:channels]
            conv_ref[a, b, channels // 2 :, 2 * channels :] = rest[:, channels:]
    base = 9 * 3 * channels // 2
    height = down_ref.shape[2]
    for a in range(2):
        for b in range(2):
            at = base + (2 * a + b) * height
            down_ref[a, b] = sums_ref[at : at + height].astype(F32) * scale


def swap(cells, axis, low):
    count = lax.axis_size(axis)
    pairs = [(i % count, (i + 1) % count) for i in range(low, low + count, 2)]
    return lax.ppermute(cells, axis, pairs + [(b, a) for a, b in pairs])


def flip(cells, axis, bit):
    row = lax.axis_size("gy")
    mask = bit * row | 1 if axis == "gz" else bit | 1
    return lax.ppermute(cells, ("gz", "gy"), [(i, i ^ mask) for i in range(lax.axis_size("gz") * row)])


def tied(first, *others):
    found = lax.optimization_barrier((first, *others))
    return found[0], tuple(found[1:])


def swapped(near, far, axis):
    return swap(near, axis, 0), swap(far, axis, 1)


def body(features, conv_weight, down_weight, cotangent):
    channels, plane_count, row_count, breadth = features.shape
    out_channels = down_weight.shape[2]
    count = lax.axis_size("gz") * lax.axis_size("gy")
    grad_scale = 1.0 / math.sqrt(plane_count * row_count * breadth * count)
    turned = conv_weight.reshape(3, 3, channels, 3, channels)[::-1, ::-1, :, ::-1]
    weight_bwd = turned.transpose(0, 1, 4, 3, 2).reshape(3, 3, channels, 3 * channels)
    cot = cotangent.reshape(out_channels, -1)
    plane = ((row_count, channels, breadth), BF16)
    edge = ((plane_count + 2, channels, breadth), BF16)
    cols = ((plane_count, row_count + 2, 3 * channels, breadth), BF16)
    edge_cols = ((plane_count + 2, 2, 3 * channels, breadth), BF16)
    lines = (plane_count, row_count, channels, breadth)
    conv_flops = 2 * 27 * channels * channels * plane_count * row_count * breadth

    own = call(
        lines_kernel, [plane, plane], [((channels * plane_count * row_count, breadth), F32)], 0, (features,)
    )
    outside = swapped(*own, "gz")
    inner, acc, hidden_grad = call(
        inner_kernel, [cols, (lines, F32), (lines, F32)],
        [((out_channels, row_count // 2 * breadth), BF16)],
        2 * conv_flops // 3, (*own, conv_weight, down_weight, cot),
    )
    near, far, acc = lax.optimization_barrier((*outside, acc))
    outside = (near, far)
    beside = swapped(*call(edges_kernel, [edge, edge], [], 0, (*own, *outside)), "gy")
    outer, acc = call(
        outer_kernel, [cols, (lines, F32)], [], conv_flops // 3, (*outside, conv_weight, acc)
    )
    edges, near, far, hidden = call(
        gate_kernel, [edge_cols, plane, plane, (lines, BF16)], [], conv_flops // 10,
        (*beside, acc, hidden_grad, conv_weight),
    )
    gates = (near, far)

    used = 27 * channels * channels // 128 + 4 * out_channels
    rows = -(-used // 128) * 128
    keep, send = call(
        weight_grad_kernel, [((rows // 2, 128), F32), ((rows // 2, 128), BF16)], [((rows, 128), F32)],
        conv_flops, (inner, outer, edges, *gates, hidden, cot),
    )
    keep, gates = tied(keep, *gates)
    near, far = gates
    near_in, far_in = swap(near, "gz", 0), swap(far, "gz", 1)
    for level, (axis, bit) in enumerate((("gy", 2), ("gz", 2))):
        size = rows >> (level + 2)
        mine, got = keep, flip(send, *(("gy", 1), ("gy", 2))[level])
        keep, send = call(
            functools.partial(halve_kernel, axis=axis, bit=bit),
            [((size, 128), F32), ((size, 128), BF16)], [((2 * size, 128), F32)], 0, (mine, got),
        )
        if level == 0:
            keep, (hidden,) = tied(keep, hidden)
            (section_out,) = call(
                section_kernel, [((out_channels, cot.shape[1]), BF16)], [], conv_flops // 10,
                (hidden, down_weight),
            )
    shard = ((rows // 8, 128), BF16)
    send, outside = tied(send, near_in, far_in)
    (sums,) = call(add_kernel, [shard], [], 0, (keep, flip(send, "gz", 2)))
    (sums,) = call(add_kernel, [shard], [], 0, (sums, flip(sums, "gz", 1)))
    sends = call(edges_kernel, [edge, edge], [], 0, (*gates, *outside))
    beside = swapped(*sends, "gy")
    (acc,) = call(
        field_kernel, [(lines, F32)], [cols, cols], conv_flops, (*gates, *outside, weight_bwd)
    )
    wide = [("gy", 1 << k) for k in range(2, lax.axis_size("gy").bit_length() - 1)]
    wide += [("gz", 1 << k) for k in range(2, lax.axis_size("gz").bit_length() - 1)]
    for axis, bit in wide:
        (sums,) = call(add_kernel, [shard], [], 0, (sums, flip(sums, axis, bit)))
    sums, (section_out,) = tied(sums, section_out)
    (sums,) = call(
        functools.partial(join_kernel, axis="gz", bit=2), [((rows // 4, 128), BF16)], [], 0,
        (sums, flip(sums, "gz", 2)),
    )
    sums, (acc, *beside) = tied(sums, acc, *beside)
    (field,) = call(
        field_edges_kernel, [((channels * plane_count * row_count, breadth), F32)], [edge_cols],
        conv_flops // 10, (*beside, acc, weight_bwd),
    )
    (sums,) = call(
        functools.partial(join_kernel, axis="gy", bit=2), [((rows // 2, 128), BF16)], [], 0,
        (sums, flip(sums, "gy", 2)),
    )
    sums, (field,) = tied(sums, field)
    grad_conv, grad_down = call(
        functools.partial(unpack_kernel, scale=grad_scale),
        [(conv_weight.shape, F32), (down_weight.shape, F32)], [((rows, 128), BF16)], 0,
        (sums, flip(sums, "gy", 1)),
    )
    section_out = section_out.reshape(out_channels, plane_count // 2, -1)
    return (section_out, field.reshape(features.shape), grad_conv, grad_down)


def solution(mesh):
    return jax.shard_map(
        body,
        mesh=mesh,
        in_specs=(P(None, "gz", "gy", None), P(), P(), P(None, "gz", "gy")),
        out_specs=(P(None, "gz", "gy"), P(None, "gz", "gy", None), P(), P()),
        check_vma=False,
    )
```

```python
import functools
import math

import jax
import jax.numpy as jnp
from jax import lax
from jax.experimental import pallas as pl
from jax.experimental.pallas import tpu as pltpu
from jax.sharding import PartitionSpec as P

F32 = jnp.float32
BF16 = jnp.bfloat16
PARAMS = pltpu.CompilerParams(vmem_limit_bytes=24 * 1024 * 1024)


def call(kernel, outs, scratch, flops, operands):
    moved = sum(x.size * x.dtype.itemsize for x in operands)
    moved += sum(math.prod(s) * jnp.dtype(d).itemsize for s, d in outs)
    vmem = pl.BlockSpec(memory_space=pltpu.VMEM)
    return pl.pallas_call(
        kernel,
        out_shape=[jax.ShapeDtypeStruct(s, d) for s, d in outs],
        in_specs=[vmem] * len(operands),
        out_specs=[vmem] * len(outs),
        scratch_shapes=[pltpu.VMEM(s, d) for s, d in scratch],
        compiler_params=PARAMS,
        cost_estimate=pl.CostEstimate(flops=flops, bytes_accessed=moved, transcendentals=0),
    )(*operands)


def is_even(axis):
    return lax.rem(lax.axis_index(axis), 2) == 0


def choose(cond, yes, no):
    return jnp.where(jnp.broadcast_to(cond, yes.shape), yes, no)


def lines_kernel(f_ref, near_ref, far_ref, wide):
    channels, planes, rows, breadth = f_ref.shape
    wide[...] = f_ref[...].astype(F32).reshape(channels * planes * rows, breadth)
    even = is_even("gz")
    for y in range(rows):
        low, high = (
            wide[pl.ds(z * rows + y, channels, stride=planes * rows), :].astype(BF16) for z in range(2)
        )
        near_ref[y] = choose(even, high, low)
        far_ref[y] = choose(even, low, high)


def edges_kernel(near, far, near_in, far_in, near_ref, far_ref):
    rows = near.shape[0]
    even_z, even_y = is_even("gz"), is_even("gy")

    def put(p, one, other):
        first = choose(even_z, one[0], other[0])
        last = choose(even_z, one[rows - 1], other[rows - 1])
        near_ref[p] = choose(even_y, last, first)
        far_ref[p] = choose(even_y, first, last)

    put(0, far_in, near_in)
    put(1, far, near)
    put(2, near, far)
    put(3, near_in, far_in)


def put_columns(cols, p, q, line):
    channels = line.shape[0]
    wide = line.astype(F32)
    cols[p, q, 0:channels] = pltpu.roll(wide, 1, 1).astype(BF16)
    cols[p, q, channels : 2 * channels] = line
    cols[p, q, 2 * channels : 3 * channels] = pltpu.roll(wide, line.shape[1] - 1, 1).astype(BF16)


def fill_columns(cols, near, far):
    rows = near.shape[0]
    even = is_even("gz")

    def step(y, carry):
        put_columns(cols, 0, y + 1, choose(even, far[y], near[y]))
        put_columns(cols, 1, y + 1, choose(even, near[y], far[y]))
        return carry

    lax.fori_loop(0, rows, step, 0, unroll=2)
    for p in range(2):
        for q in (0, rows + 1):
            cols[p, q] = jnp.zeros(cols.shape[2:], BF16)


def fill_edges(cols, near, far):
    even = is_even("gy")
    for p in range(4):
        put_columns(cols, p, 0, choose(even, far[p], near[p]))
        put_columns(cols, p, 1, choose(even, near[p], far[p]))


def dot(lhs, rhs):
    return jnp.dot(lhs, rhs, preferred_element_type=F32)


def taps(w_ref, b, first, last):
    return jnp.concatenate([w_ref[a, b] for a in range(first, last)], axis=0)


def window(cols, p, q):
    return jnp.concatenate([cols[p, q], cols[p, q + 1]], axis=1)


def inner_terms(cols, w_ref, y):
    acc = None
    for b in range(3):
        for p in range(2):
            term = dot(taps(w_ref, b, p, p + 2), window(cols, p, y + b))
            acc = term if acc is None else acc + term
    half = acc.shape[0] // 2
    return acc[half:], acc[:half]


def outer_terms(cols, w_ref, y):
    lower = upper = None
    for b in range(3):
        low, high = dot(w_ref[0, b], window(cols, 0, y + b)), dot(w_ref[2, b], window(cols, 1, y + b))
        lower = low if lower is None else lower + low
        upper = high if upper is None else upper + high
    return lower, upper


def edge_terms(edges, w_ref, side):
    b = 2 * side
    half = w_ref.shape[2]
    acc = dot(taps(w_ref, b, 0, 2), edges[1, side]) + dot(taps(w_ref, b, 1, 3), edges[2, side])
    return acc[half:] + dot(w_ref[0, b], edges[0, side]), acc[:half] + dot(w_ref[2, b], edges[3, side])


def inner_kernel(near, far, w_ref, d_ref, cot_ref, cols, acc_ref, grad_ref, up):
    rows, channels, breadth = near.shape
    fill_columns(cols, near, far)
    source = lax.broadcasted_iota(jnp.int32, (breadth, 2 * breadth), 0)
    target = lax.broadcasted_iota(jnp.int32, (breadth, 2 * breadth), 1)
    spread = jnp.where(source == target // 2, 1.0, 0.0).astype(BF16)
    for pair in range(rows // 4):
        both = dot(cot_ref[:, pair * breadth : (pair + 1) * breadth], spread)
        up[:, 2 * pair * breadth : 2 * (pair + 1) * breadth] = both.astype(BF16)
    even = lax.broadcasted_iota(jnp.int32, (channels, breadth), 1) % 2 == 0
    for a in range(2):
        for b in range(2):
            terms = lax.dot_general(d_ref[a, b], up[...], (((0,), (0,)), ((), ())), preferred_element_type=F32)
            for t in range(rows // 2):
                part = terms[:, t * breadth : (t + 1) * breadth]
                grad_ref[a, 2 * t + b] = jnp.where(even, part[0:channels], part[channels:])

    def step(t, carry):
        y = 2 * t
        for z, lines in enumerate(inner_terms(cols, w_ref, y)):
            for b in range(2):
                acc_ref[z, y + b] = lines[:, b * breadth : (b + 1) * breadth]
        return carry

    lax.fori_loop(0, rows // 2, step, 0)


def outer_kernel(near, far, w_ref, acc_ref, cols, out_ref):
    rows, channels, breadth = near.shape
    fill_columns(cols, near, far)

    def step(t, carry):
        y = 2 * t
        for z, lines in enumerate(outer_terms(cols, w_ref, y)):
            for b in range(2):
                out_ref[z, y + b] = acc_ref[z, y + b] + lines[:, b * breadth : (b + 1) * breadth]
        return carry

    lax.fori_loop(0, rows // 2, step, 0)


def gate_kernel(near, far, acc_ref, grad_ref, w_ref, edges, near_ref, far_ref, h_ref):
    rows, channels, breadth = acc_ref.shape[1:]
    fill_edges(edges, near, far)
    sides = [edge_terms(edges, w_ref, side) for side in range(2)]
    even = is_even("gz")

    def gate(y, extra):
        found = []
        for z in range(2):
            preact = acc_ref[z, y] if extra is None else acc_ref[z, y] + extra[z]
            sig = 1.0 / (1.0 + jnp.exp(-preact))
            h_ref[z, y] = (preact * sig).astype(BF16)
            found.append((grad_ref[z, y] * sig * (1.0 + preact * (1.0 - sig))).astype(BF16))
        near_ref[y] = choose(even, found[1], found[0])
        far_ref[y] = choose(even, found[0], found[1])

    gate(0, sides[0])
    for y in range(1, rows - 1):
        gate(y, None)
    gate(rows - 1, sides[1])


def coarse_hidden(h_ref, a, b):
    rows, channels, breadth = h_ref.shape[1:]
    source = lax.broadcasted_iota(jnp.int32, (2 * breadth, 2 * breadth), 0)
    target = lax.broadcasted_iota(jnp.int32, (2 * breadth, 2 * breadth), 1)
    wanted = 2 * (target % breadth) + target // breadth
    pick = jnp.where(source == wanted, 1.0, 0.0).astype(BF16)
    pairs = []
    for pair in range(rows // 4):
        both = jnp.concatenate([h_ref[a, 4 * pair + b], h_ref[a, 4 * pair + 2 + b]], axis=1)
        pairs.append(dot(both, pick).astype(BF16))
    return jnp.concatenate(
        [jnp.concatenate([x[:, e * breadth : (e + 1) * breadth] for x in pairs], axis=1) for e in range(2)],
        axis=0,
    )


def section_kernel(h_ref, d_ref, out_ref):
    coarse = None
    for a in range(2):
        for b in range(2):
            term = dot(d_ref[a, b], coarse_hidden(h_ref, a, b))
            coarse = term if coarse is None else coarse + term
    out_ref[...] = coarse.astype(BF16)


def weight_grad_kernel(inner, outer, edges, near, far, h_ref, cot_ref, keep, send, packed):
    rows, channels, breadth = near.shape
    across = (((1,), (1,)), ((), ()))
    even = is_even("gz")
    low = [choose(even, far[y], near[y]) for y in range(rows)]
    high = [choose(even, near[y], far[y]) for y in range(rows)]
    gates = jnp.concatenate([jnp.concatenate(low, axis=1), jnp.concatenate(high, axis=1)], axis=0)

    def columns(p, q):
        if q in (0, rows + 1):
            return edges[p, 0 if q == 0 else 1]
        return inner[p - 1, q] if p in (1, 2) else outer[p // 3, q]

    lane = lax.broadcasted_iota(jnp.int32, (channels // 2, breadth), 1)
    for b in range(3):
        parts = []
        for p in range(4):
            across_rows = jnp.concatenate([columns(p, y + b) for y in range(rows)], axis=1)
            lhs = gates[0:channels] if p == 0 else gates[channels:] if p == 3 else gates
            parts.append(lax.dot_general(lhs, across_rows, across, preferred_element_type=F32))
        for a in range(3):
            low = parts[a][0:channels]
            high = parts[a + 1] if a == 2 else parts[a + 1][channels:]
            total = low + high
            base = (a * 3 + b) * 3 * channels // 2
            packed[base : base + channels] = total[:, 0:breadth]
            rest = jnp.concatenate([total[:, breadth:], total[:, breadth:]], axis=1)
            mix = jnp.where(lane < channels, rest[0 : channels // 2], rest[channels // 2 :])
            packed[base + channels : base + 3 * channels // 2] = mix
    base = 9 * 3 * channels // 2
    height = cot_ref.shape[0]
    for a in range(2):
        for b in range(2):
            down = lax.dot_general(cot_ref[...], coarse_hidden(h_ref, a, b), across, preferred_element_type=F32)
            at = base + (2 * a + b) * height
            packed[at : at + height] = down
    end = base + 4 * height
    if end < packed.shape[0]:
        packed[end:] = jnp.zeros((packed.shape[0] - end, packed.shape[1]), F32)
    split(packed, keep, send, owned_half())


def side_of(axis, bit):
    return lax.rem(lax.axis_index(axis) // bit, 2)


def owned_half():
    total = 0
    for axis in ("gz", "gy"):
        for k in range(lax.axis_size(axis).bit_length() - 1):
            total = total + side_of(axis, 1 << k)
    return lax.rem(total, 2)


def part(side, rows):
    return pl.ds(pl.multiple_of(side * rows, 16), rows)


def split(packed, keep, send, side):
    half = keep.shape[0]
    keep[...] = packed[part(side, half)]
    send[...] = packed[part(1 - side, half)].astype(BF16)


def halve_kernel(mine, other, keep, send, total, *, axis, bit):
    total[...] = mine[...] + other[...].astype(F32)
    split(total, keep, send, side_of(axis, bit))


def add_kernel(x, y, out):
    out[...] = (x[...].astype(F32) + y[...].astype(F32)).astype(BF16)


def join_kernel(mine, other, out, *, axis, bit):
    join(mine, other, out, side_of(axis, bit))


def join(mine, other, out, side):
    rows = mine.shape[0]
    out[part(side, rows)] = mine[...]
    out[part(1 - side, rows)] = other[...]


def field_kernel(near, far, near_in, far_in, w_ref, acc_ref, inner, outer):
    rows, channels, breadth = near.shape
    fill_columns(inner, near, far)
    fill_columns(outer, near_in, far_in)

    def step(t, carry):
        y = 2 * t
        own = inner_terms(inner, w_ref, y)
        rest = outer_terms(outer, w_ref, y)
        for z in range(2):
            total = own[z] + rest[z]
            for b in range(2):
                acc_ref[z, y + b] = total[:, b * breadth : (b + 1) * breadth]
        return carry

    lax.fori_loop(0, rows // 2, step, 0)


def field_edges_kernel(near, far, acc_ref, w_ref, out_ref, edges):
    rows, channels, breadth = acc_ref.shape[1:]
    fill_edges(edges, near, far)
    sides = [edge_terms(edges, w_ref, side) for side in range(2)]
    for z in range(2):
        for y in range(rows):
            line = acc_ref[z, y]
            if y in (0, rows - 1):
                line = line + sides[0 if y == 0 else 1][z]
            out_ref[pl.ds(z * rows + y, channels, stride=2 * rows), :] = line


def unpack_kernel(mine, other, conv_ref, down_ref, sums_ref, *, scale):
    join(mine, other, sums_ref, owned_half())
    channels = conv_ref.shape[2]
    for a in range(3):
        for b in range(3):
            base = (a * 3 + b) * 3 * channels // 2
            conv_ref[a, b, :, 0 : 2 * channels] = sums_ref[base : base + channels].astype(F32) * scale
            rest = sums_ref[base + channels : base + 3 * channels // 2].astype(F32) * scale
            conv_ref[a, b, 0 : channels // 2, 2 * channels :] = rest[:, 0:channels]
            conv_ref[a, b, channels // 2 :, 2 * channels :] = rest[:, channels:]
    base = 9 * 3 * channels // 2
    height = down_ref.shape[2]
    for a in range(2):
        for b in range(2):
            at = base + (2 * a + b) * height
            down_ref[a, b] = sums_ref[at : at + height].astype(F32) * scale


def swap(cells, axis, low):
    count = lax.axis_size(axis)
    pairs = [(i % count, (i + 1) % count) for i in range(low, low + count, 2)]
    return lax.ppermute(cells, axis, pairs + [(b, a) for a, b in pairs])


def flip(cells, axis, bit):
    row = lax.axis_size("gy")
    mask = bit * row | 1 if axis == "gz" else bit | 1
    return lax.ppermute(cells, ("gz", "gy"), [(i, i ^ mask) for i in range(lax.axis_size("gz") * row)])


def tied(first, *others):
    found = lax.optimization_barrier((first, *others))
    return found[0], tuple(found[1:])


def swapped(near, far, axis):
    return swap(near, axis, 0), swap(far, axis, 1)


def body(features, conv_weight, down_weight, cotangent):
    channels, plane_count, row_count, breadth = features.shape
    out_channels = down_weight.shape[2]
    count = lax.axis_size("gz") * lax.axis_size("gy")
    grad_scale = 1.0 / math.sqrt(plane_count * row_count * breadth * count)
    turned = conv_weight.reshape(3, 3, channels, 3, channels)[::-1, ::-1, :, ::-1]
    weight_bwd = turned.transpose(0, 1, 4, 3, 2).reshape(3, 3, channels, 3 * channels)
    cot = cotangent.reshape(out_channels, -1)
    plane = ((row_count, channels, breadth), BF16)
    edge = ((plane_count + 2, channels, breadth), BF16)
    cols = ((plane_count, row_count + 2, 3 * channels, breadth), BF16)
    edge_cols = ((plane_count + 2, 2, 3 * channels, breadth), BF16)
    lines = (plane_count, row_count, channels, breadth)
    conv_flops = 2 * 27 * channels * channels * plane_count * row_count * breadth

    own = call(
        lines_kernel, [plane, plane], [((channels * plane_count * row_count, breadth), F32)], 0, (features,)
    )
    outside = swapped(*own, "gz")
    inner, acc, hidden_grad = call(
        inner_kernel, [cols, (lines, F32), (lines, F32)],
        [((out_channels, row_count // 2 * breadth), BF16)],
        2 * conv_flops // 3, (*own, conv_weight, down_weight, cot),
    )
    near, far, acc = lax.optimization_barrier((*outside, acc))
    outside = (near, far)
    beside = swapped(*call(edges_kernel, [edge, edge], [], 0, (*own, *outside)), "gy")
    outer, acc = call(
        outer_kernel, [cols, (lines, F32)], [], conv_flops // 3, (*outside, conv_weight, acc)
    )
    edges, near, far, hidden = call(
        gate_kernel, [edge_cols, plane, plane, (lines, BF16)], [], conv_flops // 10,
        (*beside, acc, hidden_grad, conv_weight),
    )
    gates = (near, far)

    used = 27 * channels * channels // 128 + 4 * out_channels
    rows = -(-used // 128) * 128
    keep, send = call(
        weight_grad_kernel, [((rows // 2, 128), F32), ((rows // 2, 128), BF16)], [((rows, 128), F32)],
        conv_flops, (inner, outer, edges, *gates, hidden, cot),
    )
    for level, (axis, bit) in enumerate((("gy", 2), ("gz", 2))):
        size = rows >> (level + 2)
        mine, got = keep, flip(send, *(("gy", 1), ("gy", 2))[level])
        keep, send = call(
            functools.partial(halve_kernel, axis=axis, bit=bit),
            [((size, 128), F32), ((size, 128), BF16)], [((2 * size, 128), F32)], 0, (mine, got),
        )
        if level == 0:
            keep, (hidden, *gates) = tied(keep, hidden, *gates)
            (section_out,) = call(
                section_kernel, [((out_channels, cot.shape[1]), BF16)], [], conv_flops // 10,
                (hidden, down_weight),
            )
    shard = ((rows // 8, 128), BF16)
    (sums,) = call(add_kernel, [shard], [], 0, (keep, flip(send, "gz", 2)))
    sums, (section_out, *gates) = tied(sums, section_out, *gates)
    outside = swapped(*gates, "gz")
    (sums,) = call(add_kernel, [shard], [], 0, (sums, flip(sums, "gz", 1)))
    wide = [("gy", 1 << k) for k in range(2, lax.axis_size("gy").bit_length() - 1)]
    wide += [("gz", 1 << k) for k in range(2, lax.axis_size("gz").bit_length() - 1)]
    for axis, bit in wide:
        (sums,) = call(add_kernel, [shard], [], 0, (sums, flip(sums, axis, bit)))
    (sums,) = call(
        functools.partial(join_kernel, axis="gz", bit=2), [((rows // 4, 128), BF16)], [], 0,
        (sums, flip(sums, "gz", 2)),
    )
    sums, outside = tied(sums, *outside)
    beside = swapped(*call(edges_kernel, [edge, edge], [], 0, (*gates, *outside)), "gy")
    (acc,) = call(
        field_kernel, [(lines, F32)], [cols, cols], conv_flops, (*gates, *outside, weight_bwd)
    )
    (sums,) = call(
        functools.partial(join_kernel, axis="gy", bit=2), [((rows // 2, 128), BF16)], [], 0,
        (sums, flip(sums, "gy", 2)),
    )
    sums, (acc, *beside) = tied(sums, acc, *beside)
    (field,) = call(
        field_edges_kernel, [((channels * plane_count * row_count, breadth), F32)], [edge_cols],
        conv_flops // 10, (*beside, acc, weight_bwd),
    )
    other, (field,) = tied(flip(sums, "gy", 1), field)
    grad_conv, grad_down = call(
        functools.partial(unpack_kernel, scale=grad_scale),
        [(conv_weight.shape, F32), (down_weight.shape, F32)], [((rows, 128), BF16)], 0,
        (sums, other),
    )
    section_out = section_out.reshape(out_channels, plane_count // 2, -1)
    return (section_out, field.reshape(features.shape), grad_conv, grad_down)


def solution(mesh):
    return jax.shard_map(
        body,
        mesh=mesh,
        in_specs=(P(None, "gz", "gy", None), P(), P(), P(None, "gz", "gy")),
        out_specs=(P(None, "gz", "gy"), P(None, "gz", "gy", None), P(), P()),
        check_vma=False,
    )
```

```python
import functools
import math

import jax
import jax.numpy as jnp
from jax import lax
from jax.experimental import pallas as pl
from jax.experimental.pallas import tpu as pltpu
from jax.sharding import PartitionSpec as P

F32 = jnp.float32
BF16 = jnp.bfloat16
PARAMS = pltpu.CompilerParams(vmem_limit_bytes=24 * 1024 * 1024)


def call(kernel, outs, scratch, flops, operands):
    moved = sum(x.size * x.dtype.itemsize for x in operands)
    moved += sum(math.prod(s) * jnp.dtype(d).itemsize for s, d in outs)
    vmem = pl.BlockSpec(memory_space=pltpu.VMEM)
    return pl.pallas_call(
        kernel,
        out_shape=[jax.ShapeDtypeStruct(s, d) for s, d in outs],
        in_specs=[vmem] * len(operands),
        out_specs=[vmem] * len(outs),
        scratch_shapes=[pltpu.VMEM(s, d) for s, d in scratch],
        compiler_params=PARAMS,
        cost_estimate=pl.CostEstimate(flops=flops, bytes_accessed=moved, transcendentals=0),
    )(*operands)


def is_even(axis):
    return lax.rem(lax.axis_index(axis), 2) == 0


def choose(cond, yes, no):
    return jnp.where(jnp.broadcast_to(cond, yes.shape), yes, no)


def lines_kernel(f_ref, near_ref, far_ref, wide):
    channels, planes, rows, breadth = f_ref.shape
    wide[...] = f_ref[...].astype(F32).reshape(channels * planes * rows, breadth)
    even = is_even("gz")
    for y in range(rows):
        low, high = (
            wide[pl.ds(z * rows + y, channels, stride=planes * rows), :].astype(BF16) for z in range(2)
        )
        near_ref[y] = choose(even, high, low)
        far_ref[y] = choose(even, low, high)


def edges_kernel(near, far, near_in, far_in, near_ref, far_ref):
    rows = near.shape[0]
    even_z, even_y = is_even("gz"), is_even("gy")

    def put(p, one, other):
        first = choose(even_z, one[0], other[0])
        last = choose(even_z, one[rows - 1], other[rows - 1])
        near_ref[p] = choose(even_y, last, first)
        far_ref[p] = choose(even_y, first, last)

    put(0, far_in, near_in)
    put(1, far, near)
    put(2, near, far)
    put(3, near_in, far_in)


def put_columns(cols, p, q, line):
    channels = line.shape[0]
    wide = line.astype(F32)
    cols[p, q, 0:channels] = pltpu.roll(wide, 1, 1).astype(BF16)
    cols[p, q, channels : 2 * channels] = line
    cols[p, q, 2 * channels : 3 * channels] = pltpu.roll(wide, line.shape[1] - 1, 1).astype(BF16)


def fill_columns(cols, near, far):
    rows = near.shape[0]
    even = is_even("gz")

    def step(y, carry):
        put_columns(cols, 0, y + 1, choose(even, far[y], near[y]))
        put_columns(cols, 1, y + 1, choose(even, near[y], far[y]))
        return carry

    lax.fori_loop(0, rows, step, 0, unroll=2)
    for p in range(2):
        for q in (0, rows + 1):
            cols[p, q] = jnp.zeros(cols.shape[2:], BF16)


def fill_edges(cols, near, far):
    even = is_even("gy")
    for p in range(4):
        put_columns(cols, p, 0, choose(even, far[p], near[p]))
        put_columns(cols, p, 1, choose(even, near[p], far[p]))


def dot(lhs, rhs):
    return jnp.dot(lhs, rhs, preferred_element_type=F32)


def taps(w_ref, b, first, last):
    return jnp.concatenate([w_ref[a, b] for a in range(first, last)], axis=0)


def window(cols, p, q):
    return jnp.concatenate([cols[p, q], cols[p, q + 1]], axis=1)


def inner_terms(cols, w_ref, y):
    acc = None
    for b in range(3):
        for p in range(2):
            term = dot(taps(w_ref, b, p, p + 2), window(cols, p, y + b))
            acc = term if acc is None else acc + term
    half = acc.shape[0] // 2
    return acc[half:], acc[:half]


def outer_terms(cols, w_ref, y):
    lower = upper = None
    for b in range(3):
        low, high = dot(w_ref[0, b], window(cols, 0, y + b)), dot(w_ref[2, b], window(cols, 1, y + b))
        lower = low if lower is None else lower + low
        upper = high if upper is None else upper + high
    return lower, upper


def edge_terms(edges, w_ref, side):
    b = 2 * side
    half = w_ref.shape[2]
    acc = dot(taps(w_ref, b, 0, 2), edges[1, side]) + dot(taps(w_ref, b, 1, 3), edges[2, side])
    return acc[half:] + dot(w_ref[0, b], edges[0, side]), acc[:half] + dot(w_ref[2, b], edges[3, side])


def inner_kernel(near, far, w_ref, d_ref, cot_ref, cols, acc_ref, grad_ref, up):
    rows, channels, breadth = near.shape
    fill_columns(cols, near, far)
    source = lax.broadcasted_iota(jnp.int32, (breadth, 2 * breadth), 0)
    target = lax.broadcasted_iota(jnp.int32, (breadth, 2 * breadth), 1)
    spread = jnp.where(source == target // 2, 1.0, 0.0).astype(BF16)
    for pair in range(rows // 4):
        both = dot(cot_ref[:, pair * breadth : (pair + 1) * breadth], spread)
        up[:, 2 * pair * breadth : 2 * (pair + 1) * breadth] = both.astype(BF16)
    even = lax.broadcasted_iota(jnp.int32, (channels, breadth), 1) % 2 == 0
    for a in range(2):
        for b in range(2):
            terms = lax.dot_general(d_ref[a, b], up[...], (((0,), (0,)), ((), ())), preferred_element_type=F32)
            for t in range(rows // 2):
                part = terms[:, t * breadth : (t + 1) * breadth]
                grad_ref[a, 2 * t + b] = jnp.where(even, part[0:channels], part[channels:])

    def step(t, carry):
        y = 2 * t
        for z, lines in enumerate(inner_terms(cols, w_ref, y)):
            for b in range(2):
                acc_ref[z, y + b] = lines[:, b * breadth : (b + 1) * breadth]
        return carry

    lax.fori_loop(0, rows // 2, step, 0)


def outer_kernel(near, far, w_ref, acc_ref, cols, out_ref):
    rows, channels, breadth = near.shape
    fill_columns(cols, near, far)

    def step(t, carry):
        y = 2 * t
        for z, lines in enumerate(outer_terms(cols, w_ref, y)):
            for b in range(2):
                out_ref[z, y + b] = acc_ref[z, y + b] + lines[:, b * breadth : (b + 1) * breadth]
        return carry

    lax.fori_loop(0, rows // 2, step, 0)


def gate_kernel(near, far, acc_ref, grad_ref, w_ref, edges, near_ref, far_ref, h_ref):
    rows, channels, breadth = acc_ref.shape[1:]
    fill_edges(edges, near, far)
    sides = [edge_terms(edges, w_ref, side) for side in range(2)]
    even = is_even("gz")

    def gate(y, extra):
        found = []
        for z in range(2):
            preact = acc_ref[z, y] if extra is None else acc_ref[z, y] + extra[z]
            sig = 1.0 / (1.0 + jnp.exp(-preact))
            h_ref[z, y] = (preact * sig).astype(BF16)
            found.append((grad_ref[z, y] * sig * (1.0 + preact * (1.0 - sig))).astype(BF16))
        near_ref[y] = choose(even, found[1], found[0])
        far_ref[y] = choose(even, found[0], found[1])

    gate(0, sides[0])
    for y in range(1, rows - 1):
        gate(y, None)
    gate(rows - 1, sides[1])


def coarse_hidden(h_ref, a, b):
    rows, channels, breadth = h_ref.shape[1:]
    source = lax.broadcasted_iota(jnp.int32, (2 * breadth, 2 * breadth), 0)
    target = lax.broadcasted_iota(jnp.int32, (2 * breadth, 2 * breadth), 1)
    wanted = 2 * (target % breadth) + target // breadth
    pick = jnp.where(source == wanted, 1.0, 0.0).astype(BF16)
    pairs = []
    for pair in range(rows // 4):
        both = jnp.concatenate([h_ref[a, 4 * pair + b], h_ref[a, 4 * pair + 2 + b]], axis=1)
        pairs.append(dot(both, pick).astype(BF16))
    return jnp.concatenate(
        [jnp.concatenate([x[:, e * breadth : (e + 1) * breadth] for x in pairs], axis=1) for e in range(2)],
        axis=0,
    )


def section_kernel(h_ref, d_ref, out_ref):
    coarse = None
    for a in range(2):
        for b in range(2):
            term = dot(d_ref[a, b], coarse_hidden(h_ref, a, b))
            coarse = term if coarse is None else coarse + term
    out_ref[...] = coarse.astype(BF16)


def weight_grad_kernel(inner, outer, edges, near, far, h_ref, cot_ref, keep, send, packed):
    rows, channels, breadth = near.shape
    across = (((1,), (1,)), ((), ()))
    even = is_even("gz")
    low = [choose(even, far[y], near[y]) for y in range(rows)]
    high = [choose(even, near[y], far[y]) for y in range(rows)]
    gates = jnp.concatenate([jnp.concatenate(low, axis=1), jnp.concatenate(high, axis=1)], axis=0)

    def columns(p, q):
        if q in (0, rows + 1):
            return edges[p, 0 if q == 0 else 1]
        return inner[p - 1, q] if p in (1, 2) else outer[p // 3, q]

    lane = lax.broadcasted_iota(jnp.int32, (channels // 2, breadth), 1)
    for b in range(3):
        parts = []
        for p in range(4):
            across_rows = jnp.concatenate([columns(p, y + b) for y in range(rows)], axis=1)
            lhs = gates[0:channels] if p == 0 else gates[channels:] if p == 3 else gates
            parts.append(lax.dot_general(lhs, across_rows, across, preferred_element_type=F32))
        for a in range(3):
            low = parts[a][0:channels]
            high = parts[a + 1] if a == 2 else parts[a + 1][channels:]
            total = low + high
            base = (a * 3 + b) * 3 * channels // 2
            packed[base : base + channels] = total[:, 0:breadth]
            rest = jnp.concatenate([total[:, breadth:], total[:, breadth:]], axis=1)
            mix = jnp.where(lane < channels, rest[0 : channels // 2], rest[channels // 2 :])
            packed[base + channels : base + 3 * channels // 2] = mix
    base = 9 * 3 * channels // 2
    height = cot_ref.shape[0]
    for a in range(2):
        for b in range(2):
            down = lax.dot_general(cot_ref[...], coarse_hidden(h_ref, a, b), across, preferred_element_type=F32)
            at = base + (2 * a + b) * height
            packed[at : at + height] = down
    end = base + 4 * height
    if end < packed.shape[0]:
        packed[end:] = jnp.zeros((packed.shape[0] - end, packed.shape[1]), F32)
    split(packed, keep, send, owned_half())


def side_of(axis, bit):
    return lax.rem(lax.axis_index(axis) // bit, 2)


def owned_half():
    total = 0
    for axis in ("gz", "gy"):
        for k in range(lax.axis_size(axis).bit_length() - 1):
            total = total + side_of(axis, 1 << k)
    return lax.rem(total, 2)


def part(side, rows):
    return pl.ds(pl.multiple_of(side * rows, 16), rows)


def split(packed, keep, send, side):
    half = keep.shape[0]
    keep[...] = packed[part(side, half)]
    send[...] = packed[part(1 - side, half)].astype(BF16)


def halve_kernel(mine, other, keep, send, total, *, axis, bit):
    total[...] = mine[...] + other[...].astype(F32)
    split(total, keep, send, side_of(axis, bit))


def add_kernel(x, y, out):
    out[...] = (x[...].astype(F32) + y[...].astype(F32)).astype(BF16)


def join_kernel(mine, other, out, *, axis, bit):
    join(mine, other, out, side_of(axis, bit))


def join(mine, other, out, side):
    rows = mine.shape[0]
    out[part(side, rows)] = mine[...]
    out[part(1 - side, rows)] = other[...]


def field_kernel(near, far, near_in, far_in, w_ref, acc_ref, inner, outer):
    rows, channels, breadth = near.shape
    fill_columns(inner, near, far)
    fill_columns(outer, near_in, far_in)

    def step(t, carry):
        y = 2 * t
        own = inner_terms(inner, w_ref, y)
        rest = outer_terms(outer, w_ref, y)
        for z in range(2):
            total = own[z] + rest[z]
            for b in range(2):
                acc_ref[z, y + b] = total[:, b * breadth : (b + 1) * breadth]
        return carry

    lax.fori_loop(0, rows // 2, step, 0)


def field_edges_kernel(near, far, acc_ref, w_ref, out_ref, edges):
    rows, channels, breadth = acc_ref.shape[1:]
    fill_edges(edges, near, far)
    sides = [edge_terms(edges, w_ref, side) for side in range(2)]
    for z in range(2):
        for y in range(rows):
            line = acc_ref[z, y]
            if y in (0, rows - 1):
                line = line + sides[0 if y == 0 else 1][z]
            out_ref[pl.ds(z * rows + y, channels, stride=2 * rows), :] = line


def unpack_kernel(mine, other, conv_ref, down_ref, sums_ref, *, scale):
    join(mine, other, sums_ref, owned_half())
    channels = conv_ref.shape[2]
    for a in range(3):
        for b in range(3):
            base = (a * 3 + b) * 3 * channels // 2
            conv_ref[a, b, :, 0 : 2 * channels] = sums_ref[base : base + channels].astype(F32) * scale
            rest = sums_ref[base + channels : base + 3 * channels // 2].astype(F32) * scale
            conv_ref[a, b, 0 : channels // 2, 2 * channels :] = rest[:, 0:channels]
            conv_ref[a, b, channels // 2 :, 2 * channels :] = rest[:, channels:]
    base = 9 * 3 * channels // 2
    height = down_ref.shape[2]
    for a in range(2):
        for b in range(2):
            at = base + (2 * a + b) * height
            down_ref[a, b] = sums_ref[at : at + height].astype(F32) * scale


def swap(cells, axis, low):
    count = lax.axis_size(axis)
    pairs = [(i % count, (i + 1) % count) for i in range(low, low + count, 2)]
    return lax.ppermute(cells, axis, pairs + [(b, a) for a, b in pairs])


def flip(cells, axis, bit):
    row = lax.axis_size("gy")
    mask = bit * row | 1 if axis == "gz" else bit | 1
    return lax.ppermute(cells, ("gz", "gy"), [(i, i ^ mask) for i in range(lax.axis_size("gz") * row)])


def tied(first, *others):
    found = lax.optimization_barrier((first, *others))
    return found[0], tuple(found[1:])


def swapped(near, far, axis):
    return swap(near, axis, 0), swap(far, axis, 1)


def body(features, conv_weight, down_weight, cotangent):
    channels, plane_count, row_count, breadth = features.shape
    out_channels = down_weight.shape[2]
    count = lax.axis_size("gz") * lax.axis_size("gy")
    grad_scale = 1.0 / math.sqrt(plane_count * row_count * breadth * count)
    turned = conv_weight.reshape(3, 3, channels, 3, channels)[::-1, ::-1, :, ::-1]
    weight_bwd = turned.transpose(0, 1, 4, 3, 2).reshape(3, 3, channels, 3 * channels)
    cot = cotangent.reshape(out_channels, -1)
    plane = ((row_count, channels, breadth), BF16)
    edge = ((plane_count + 2, channels, breadth), BF16)
    cols = ((plane_count, row_count + 2, 3 * channels, breadth), BF16)
    edge_cols = ((plane_count + 2, 2, 3 * channels, breadth), BF16)
    lines = (plane_count, row_count, channels, breadth)
    conv_flops = 2 * 27 * channels * channels * plane_count * row_count * breadth

    own = call(
        lines_kernel, [plane, plane], [((channels * plane_count * row_count, breadth), F32)], 0, (features,)
    )
    outside = swapped(*own, "gz")
    inner, acc, hidden_grad = call(
        inner_kernel, [cols, (lines, F32), (lines, F32)],
        [((out_channels, row_count // 2 * breadth), BF16)],
        2 * conv_flops // 3, (*own, conv_weight, down_weight, cot),
    )
    near, far, acc = lax.optimization_barrier((*outside, acc))
    outside = (near, far)
    beside = swapped(*call(edges_kernel, [edge, edge], [], 0, (*own, *outside)), "gy")
    outer, acc = call(
        outer_kernel, [cols, (lines, F32)], [], conv_flops // 3, (*outside, conv_weight, acc)
    )
    edges, near, far, hidden = call(
        gate_kernel, [edge_cols, plane, plane, (lines, BF16)], [], conv_flops // 10,
        (*beside, acc, hidden_grad, conv_weight),
    )
    gates = (near, far)

    used = 27 * channels * channels // 128 + 4 * out_channels
    rows = -(-used // 128) * 128
    keep, send = call(
        weight_grad_kernel, [((rows // 2, 128), F32), ((rows // 2, 128), BF16)], [((rows, 128), F32)],
        conv_flops, (inner, outer, edges, *gates, hidden, cot),
    )
    keep, gates = tied(keep, *gates)
    near, far = gates
    far_in = swap(far, "gz", 1)
    for level, (axis, bit) in enumerate((("gy", 2), ("gz", 2))):
        size = rows >> (level + 2)
        mine, got = keep, flip(send, *(("gy", 1), ("gy", 2))[level])
        keep, send = call(
            functools.partial(halve_kernel, axis=axis, bit=bit),
            [((size, 128), F32), ((size, 128), BF16)], [((2 * size, 128), F32)], 0, (mine, got),
        )
        if level == 0:
            keep, (hidden,) = tied(keep, hidden)
            (section_out,) = call(
                section_kernel, [((out_channels, cot.shape[1]), BF16)], [], conv_flops // 10,
                (hidden, down_weight),
            )
    keep, (near,) = tied(keep, near)
    near_in = swap(near, "gz", 0)
    shard = ((rows // 8, 128), BF16)
    (sums,) = call(add_kernel, [shard], [], 0, (keep, flip(send, "gz", 2)))
    (sums,) = call(add_kernel, [shard], [], 0, (sums, flip(sums, "gz", 1)))
    sums, outside = tied(sums, near_in, far_in)
    sends = call(edges_kernel, [edge, edge], [], 0, (*gates, *outside))
    beside = swapped(*sends, "gy")
    (acc,) = call(
        field_kernel, [(lines, F32)], [cols, cols], conv_flops, (*gates, *outside, weight_bwd)
    )
    wide = [("gy", 1 << k) for k in range(2, lax.axis_size("gy").bit_length() - 1)]
    wide += [("gz", 1 << k) for k in range(2, lax.axis_size("gz").bit_length() - 1)]
    for axis, bit in wide:
        (sums,) = call(add_kernel, [shard], [], 0, (sums, flip(sums, axis, bit)))
    sums, (section_out,) = tied(sums, section_out)
    (sums,) = call(
        functools.partial(join_kernel, axis="gz", bit=2), [((rows // 4, 128), BF16)], [], 0,
        (sums, flip(sums, "gz", 2)),
    )
    sums, (acc, *beside) = tied(sums, acc, *beside)
    (field,) = call(
        field_edges_kernel, [((channels * plane_count * row_count, breadth), F32)], [edge_cols],
        conv_flops // 10, (*beside, acc, weight_bwd),
    )
    (sums,) = call(
        functools.partial(join_kernel, axis="gy", bit=2), [((rows // 2, 128), BF16)], [], 0,
        (sums, flip(sums, "gy", 2)),
    )
    sums, (field,) = tied(sums, field)
    grad_conv, grad_down = call(
        functools.partial(unpack_kernel, scale=grad_scale),
        [(conv_weight.shape, F32), (down_weight.shape, F32)], [((rows, 128), BF16)], 0,
        (sums, flip(sums, "gy", 1)),
    )
    section_out = section_out.reshape(out_channels, plane_count // 2, -1)
    return (section_out, field.reshape(features.shape), grad_conv, grad_down)


def solution(mesh):
    return jax.shard_map(
        body,
        mesh=mesh,
        in_specs=(P(None, "gz", "gy", None), P(), P(), P(None, "gz", "gy")),
        out_specs=(P(None, "gz", "gy"), P(None, "gz", "gy", None), P(), P()),
        check_vma=False,
    )
```

```python
import functools
import math

import jax
import jax.numpy as jnp
from jax import lax
from jax.experimental import pallas as pl
from jax.experimental.pallas import tpu as pltpu
from jax.sharding import PartitionSpec as P

F32 = jnp.float32
BF16 = jnp.bfloat16
PARAMS = pltpu.CompilerParams(vmem_limit_bytes=24 * 1024 * 1024)


def call(kernel, outs, scratch, flops, operands):
    moved = sum(x.size * x.dtype.itemsize for x in operands)
    moved += sum(math.prod(s) * jnp.dtype(d).itemsize for s, d in outs)
    vmem = pl.BlockSpec(memory_space=pltpu.VMEM)
    return pl.pallas_call(
        kernel,
        out_shape=[jax.ShapeDtypeStruct(s, d) for s, d in outs],
        in_specs=[vmem] * len(operands),
        out_specs=[vmem] * len(outs),
        scratch_shapes=[pltpu.VMEM(s, d) for s, d in scratch],
        compiler_params=PARAMS,
        cost_estimate=pl.CostEstimate(flops=flops, bytes_accessed=moved, transcendentals=0),
    )(*operands)


def is_even(axis):
    return lax.rem(lax.axis_index(axis), 2) == 0


def choose(cond, yes, no):
    return jnp.where(jnp.broadcast_to(cond, yes.shape), yes, no)


def lines_kernel(f_ref, far_ref, near_ref, wide):
    channels, planes, rows, breadth = f_ref.shape
    wide[...] = f_ref[...].astype(F32).reshape(channels * planes * rows, breadth)
    even = is_even("gz")
    for y in range(rows):
        low, high = (
            wide[pl.ds(z * rows + y, channels, stride=planes * rows), :].astype(BF16) for z in range(2)
        )
        near_ref[y] = choose(even, high, low)
        far_ref[y] = choose(even, low, high)


def edges_kernel(near, far, near_in, far_in, near_ref, far_ref):
    rows = near.shape[0]
    even_z, even_y = is_even("gz"), is_even("gy")

    def put(p, one, other):
        first = choose(even_z, one[0], other[0])
        last = choose(even_z, one[rows - 1], other[rows - 1])
        near_ref[p] = choose(even_y, last, first)
        far_ref[p] = choose(even_y, first, last)

    put(0, far_in, near_in)
    put(1, far, near)
    put(2, near, far)
    put(3, near_in, far_in)


def put_columns(cols, p, q, line):
    channels = line.shape[0]
    wide = line.astype(F32)
    cols[p, q, 0:channels] = pltpu.roll(wide, 1, 1).astype(BF16)
    cols[p, q, channels : 2 * channels] = line
    cols[p, q, 2 * channels : 3 * channels] = pltpu.roll(wide, line.shape[1] - 1, 1).astype(BF16)


def fill_columns(cols, near, far):
    rows = near.shape[0]
    even = is_even("gz")

    def step(y, carry):
        put_columns(cols, 0, y + 1, choose(even, far[y], near[y]))
        put_columns(cols, 1, y + 1, choose(even, near[y], far[y]))
        return carry

    lax.fori_loop(0, rows, step, 0, unroll=2)
    for p in range(2):
        for q in (0, rows + 1):
            cols[p, q] = jnp.zeros(cols.shape[2:], BF16)


def fill_edges(cols, near, far):
    even = is_even("gy")
    for p in range(4):
        put_columns(cols, p, 0, choose(even, far[p], near[p]))
        put_columns(cols, p, 1, choose(even, near[p], far[p]))


def dot(lhs, rhs):
    return jnp.dot(lhs, rhs, preferred_element_type=F32)


def taps(w_ref, b, first, last):
    return jnp.concatenate([w_ref[a, b] for a in range(first, last)], axis=0)


def window(cols, p, q):
    return jnp.concatenate([cols[p, q], cols[p, q + 1]], axis=1)


def inner_terms(cols, w_ref, y):
    acc = None
    for b in range(3):
        for p in range(2):
            term = dot(taps(w_ref, b, p, p + 2), window(cols, p, y + b))
            acc = term if acc is None else acc + term
    half = acc.shape[0] // 2
    return acc[half:], acc[:half]


def outer_terms(cols, w_ref, y):
    lower = upper = None
    for b in range(3):
        low, high = dot(w_ref[0, b], window(cols, 0, y + b)), dot(w_ref[2, b], window(cols, 1, y + b))
        lower = low if lower is None else lower + low
        upper = high if upper is None else upper + high
    return lower, upper


def edge_terms(edges, w_ref, side):
    b = 2 * side
    half = w_ref.shape[2]
    acc = dot(taps(w_ref, b, 0, 2), edges[1, side]) + dot(taps(w_ref, b, 1, 3), edges[2, side])
    return acc[half:] + dot(w_ref[0, b], edges[0, side]), acc[:half] + dot(w_ref[2, b], edges[3, side])


def inner_kernel(near, far, w_ref, d_ref, cot_ref, cols, acc_ref, grad_ref, up):
    rows, channels, breadth = near.shape
    fill_columns(cols, near, far)
    source = lax.broadcasted_iota(jnp.int32, (breadth, 2 * breadth), 0)
    target = lax.broadcasted_iota(jnp.int32, (breadth, 2 * breadth), 1)
    spread = jnp.where(source == target // 2, 1.0, 0.0).astype(BF16)
    for pair in range(rows // 4):
        both = dot(cot_ref[:, pair * breadth : (pair + 1) * breadth], spread)
        up[:, 2 * pair * breadth : 2 * (pair + 1) * breadth] = both.astype(BF16)
    even = lax.broadcasted_iota(jnp.int32, (channels, breadth), 1) % 2 == 0
    for a in range(2):
        for b in range(2):
            terms = lax.dot_general(d_ref[a, b], up[...], (((0,), (0,)), ((), ())), preferred_element_type=F32)
            for t in range(rows // 2):
                part = terms[:, t * breadth : (t + 1) * breadth]
                grad_ref[a, 2 * t + b] = jnp.where(even, part[0:channels], part[channels:])

    def step(t, carry):
        y = 2 * t
        for z, lines in enumerate(inner_terms(cols, w_ref, y)):
            for b in range(2):
                acc_ref[z, y + b] = lines[:, b * breadth : (b + 1) * breadth]
        return carry

    lax.fori_loop(0, rows // 2, step, 0)


def outer_kernel(near, far, w_ref, acc_ref, cols, out_ref):
    rows, channels, breadth = near.shape
    fill_columns(cols, near, far)

    def step(t, carry):
        y = 2 * t
        for z, lines in enumerate(outer_terms(cols, w_ref, y)):
            for b in range(2):
                out_ref[z, y + b] = acc_ref[z, y + b] + lines[:, b * breadth : (b + 1) * breadth]
        return carry

    lax.fori_loop(0, rows // 2, step, 0)


def gate_kernel(near, far, acc_ref, grad_ref, w_ref, edges, near_ref, far_ref, h_ref):
    rows, channels, breadth = acc_ref.shape[1:]
    fill_edges(edges, near, far)
    sides = [edge_terms(edges, w_ref, side) for side in range(2)]
    even = is_even("gz")

    def gate(y, extra):
        found = []
        for z in range(2):
            preact = acc_ref[z, y] if extra is None else acc_ref[z, y] + extra[z]
            sig = 1.0 / (1.0 + jnp.exp(-preact))
            h_ref[z, y] = (preact * sig).astype(BF16)
            found.append((grad_ref[z, y] * sig * (1.0 + preact * (1.0 - sig))).astype(BF16))
        near_ref[y] = choose(even, found[1], found[0])
        far_ref[y] = choose(even, found[0], found[1])

    gate(0, sides[0])
    for y in range(1, rows - 1):
        gate(y, None)
    gate(rows - 1, sides[1])


def coarse_hidden(h_ref, a, b):
    rows, channels, breadth = h_ref.shape[1:]
    source = lax.broadcasted_iota(jnp.int32, (2 * breadth, 2 * breadth), 0)
    target = lax.broadcasted_iota(jnp.int32, (2 * breadth, 2 * breadth), 1)
    wanted = 2 * (target % breadth) + target // breadth
    pick = jnp.where(source == wanted, 1.0, 0.0).astype(BF16)
    pairs = []
    for pair in range(rows // 4):
        both = jnp.concatenate([h_ref[a, 4 * pair + b], h_ref[a, 4 * pair + 2 + b]], axis=1)
        pairs.append(dot(both, pick).astype(BF16))
    return jnp.concatenate(
        [jnp.concatenate([x[:, e * breadth : (e + 1) * breadth] for x in pairs], axis=1) for e in range(2)],
        axis=0,
    )


def section_kernel(h_ref, d_ref, out_ref):
    coarse = None
    for a in range(2):
        for b in range(2):
            term = dot(d_ref[a, b], coarse_hidden(h_ref, a, b))
            coarse = term if coarse is None else coarse + term
    out_ref[...] = coarse.astype(BF16)


def weight_grad_kernel(inner, outer, edges, near, far, h_ref, cot_ref, keep, send, packed):
    rows, channels, breadth = near.shape
    across = (((1,), (1,)), ((), ()))
    even = is_even("gz")
    low = [choose(even, far[y], near[y]) for y in range(rows)]
    high = [choose(even, near[y], far[y]) for y in range(rows)]
    gates = jnp.concatenate([jnp.concatenate(low, axis=1), jnp.concatenate(high, axis=1)], axis=0)

    def columns(p, q):
        if q in (0, rows + 1):
            return edges[p, 0 if q == 0 else 1]
        return inner[p - 1, q] if p in (1, 2) else outer[p // 3, q]

    lane = lax.broadcasted_iota(jnp.int32, (channels // 2, breadth), 1)
    for b in range(3):
        parts = []
        for p in range(4):
            across_rows = jnp.concatenate([columns(p, y + b) for y in range(rows)], axis=1)
            lhs = gates[0:channels] if p == 0 else gates[channels:] if p == 3 else gates
            parts.append(lax.dot_general(lhs, across_rows, across, preferred_element_type=F32))
        for a in range(3):
            low = parts[a][0:channels]
            high = parts[a + 1] if a == 2 else parts[a + 1][channels:]
            total = low + high
            base = (a * 3 + b) * 3 * channels // 2
            packed[base : base + channels] = total[:, 0:breadth]
            rest = jnp.concatenate([total[:, breadth:], total[:, breadth:]], axis=1)
            mix = jnp.where(lane < channels, rest[0 : channels // 2], rest[channels // 2 :])
            packed[base + channels : base + 3 * channels // 2] = mix
    base = 9 * 3 * channels // 2
    height = cot_ref.shape[0]
    for a in range(2):
        for b in range(2):
            down = lax.dot_general(cot_ref[...], coarse_hidden(h_ref, a, b), across, preferred_element_type=F32)
            at = base + (2 * a + b) * height
            packed[at : at + height] = down
    end = base + 4 * height
    if end < packed.shape[0]:
        packed[end:] = jnp.zeros((packed.shape[0] - end, packed.shape[1]), F32)
    split(packed, keep, send, owned_half())


def side_of(axis, bit):
    return lax.rem(lax.axis_index(axis) // bit, 2)


def owned_half():
    total = 0
    for axis in ("gz", "gy"):
        for k in range(lax.axis_size(axis).bit_length() - 1):
            total = total + side_of(axis, 1 << k)
    return lax.rem(total, 2)


def part(side, rows):
    return pl.ds(pl.multiple_of(side * rows, 16), rows)


def split(packed, keep, send, side):
    half = keep.shape[0]
    keep[...] = packed[part(side, half)]
    send[...] = packed[part(1 - side, half)].astype(BF16)


def halve_kernel(mine, other, keep, send, total, *, axis, bit):
    total[...] = mine[...] + other[...].astype(F32)
    split(total, keep, send, side_of(axis, bit))


def add_kernel(x, y, out):
    out[...] = (x[...].astype(F32) + y[...].astype(F32)).astype(BF16)


def join_kernel(mine, other, out, *, axis, bit):
    join(mine, other, out, side_of(axis, bit))


def join(mine, other, out, side):
    rows = mine.shape[0]
    out[part(side, rows)] = mine[...]
    out[part(1 - side, rows)] = other[...]


def field_kernel(near, far, near_in, far_in, w_ref, acc_ref, inner, outer):
    rows, channels, breadth = near.shape
    fill_columns(inner, near, far)
    fill_columns(outer, near_in, far_in)

    def step(t, carry):
        y = 2 * t
        own = inner_terms(inner, w_ref, y)
        rest = outer_terms(outer, w_ref, y)
        for z in range(2):
            total = own[z] + rest[z]
            for b in range(2):
                acc_ref[z, y + b] = total[:, b * breadth : (b + 1) * breadth]
        return carry

    lax.fori_loop(0, rows // 2, step, 0)


def field_edges_kernel(near, far, acc_ref, w_ref, out_ref, edges):
    rows, channels, breadth = acc_ref.shape[1:]
    fill_edges(edges, near, far)
    sides = [edge_terms(edges, w_ref, side) for side in range(2)]
    for z in range(2):
        for y in range(rows):
            line = acc_ref[z, y]
            if y in (0, rows - 1):
                line = line + sides[0 if y == 0 else 1][z]
            out_ref[pl.ds(z * rows + y, channels, stride=2 * rows), :] = line


def unpack_kernel(mine, other, conv_ref, down_ref, sums_ref, *, scale):
    join(mine, other, sums_ref, owned_half())
    channels = conv_ref.shape[2]
    for a in range(3):
        for b in range(3):
            base = (a * 3 + b) * 3 * channels // 2
            conv_ref[a, b, :, 0 : 2 * channels] = sums_ref[base : base + channels].astype(F32) * scale
            rest = sums_ref[base + channels : base + 3 * channels // 2].astype(F32) * scale
            conv_ref[a, b, 0 : channels // 2, 2 * channels :] = rest[:, 0:channels]
            conv_ref[a, b, channels // 2 :, 2 * channels :] = rest[:, channels:]
    base = 9 * 3 * channels // 2
    height = down_ref.shape[2]
    for a in range(2):
        for b in range(2):
            at = base + (2 * a + b) * height
            down_ref[a, b] = sums_ref[at : at + height].astype(F32) * scale


def swap(cells, axis, low):
    count = lax.axis_size(axis)
    pairs = [(i % count, (i + 1) % count) for i in range(low, low + count, 2)]
    return lax.ppermute(cells, axis, pairs + [(b, a) for a, b in pairs])


def flip(cells, axis, bit):
    row = lax.axis_size("gy")
    mask = bit * row | 1 if axis == "gz" else bit | 1
    return lax.ppermute(cells, ("gz", "gy"), [(i, i ^ mask) for i in range(lax.axis_size("gz") * row)])


def tied(first, *others):
    found = lax.optimization_barrier((first, *others))
    return found[0], tuple(found[1:])


def swapped(near, far, axis):
    far = swap(far, axis, 1)
    return swap(near, axis, 0), far


def body(features, conv_weight, down_weight, cotangent):
    channels, plane_count, row_count, breadth = features.shape
    out_channels = down_weight.shape[2]
    count = lax.axis_size("gz") * lax.axis_size("gy")
    grad_scale = 1.0 / math.sqrt(plane_count * row_count * breadth * count)
    turned = conv_weight.reshape(3, 3, channels, 3, channels)[::-1, ::-1, :, ::-1]
    weight_bwd = turned.transpose(0, 1, 4, 3, 2).reshape(3, 3, channels, 3 * channels)
    cot = cotangent.reshape(out_channels, -1)
    plane = ((row_count, channels, breadth), BF16)
    edge = ((plane_count + 2, channels, breadth), BF16)
    cols = ((plane_count, row_count + 2, 3 * channels, breadth), BF16)
    edge_cols = ((plane_count + 2, 2, 3 * channels, breadth), BF16)
    lines = (plane_count, row_count, channels, breadth)
    conv_flops = 2 * 27 * channels * channels * plane_count * row_count * breadth

    far, near = call(
        lines_kernel, [plane, plane], [((channels * plane_count * row_count, breadth), F32)], 0, (features,)
    )
    own = (near, far)
    outside = swapped(*own, "gz")
    inner, acc, hidden_grad = call(
        inner_kernel, [cols, (lines, F32), (lines, F32)],
        [((out_channels, row_count // 2 * breadth), BF16)],
        2 * conv_flops // 3, (*own, conv_weight, down_weight, cot),
    )
    acc, far, near = lax.optimization_barrier((acc, outside[1], outside[0]))
    outside = (near, far)
    beside = swapped(*call(edges_kernel, [edge, edge], [], 0, (*own, *outside)), "gy")
    outer, acc = call(
        outer_kernel, [cols, (lines, F32)], [], conv_flops // 3, (*outside, conv_weight, acc)
    )
    edges, near, far, hidden = call(
        gate_kernel, [edge_cols, plane, plane, (lines, BF16)], [], conv_flops // 10,
        (*beside, acc, hidden_grad, conv_weight),
    )
    gates = (near, far)

    used = 27 * channels * channels // 128 + 4 * out_channels
    rows = -(-used // 128) * 128
    keep, send = call(
        weight_grad_kernel, [((rows // 2, 128), F32), ((rows // 2, 128), BF16)], [((rows, 128), F32)],
        conv_flops, (inner, outer, edges, *gates, hidden, cot),
    )
    keep, gates = tied(keep, *gates)
    near, far = gates
    far_in = swap(far, "gz", 1)
    for level, (axis, bit) in enumerate((("gy", 2), ("gz", 2))):
        size = rows >> (level + 2)
        mine, got = keep, flip(send, *(("gy", 1), ("gy", 2))[level])
        keep, send = call(
            functools.partial(halve_kernel, axis=axis, bit=bit),
            [((size, 128), F32), ((size, 128), BF16)], [((2 * size, 128), F32)], 0, (mine, got),
        )
        if level == 0:
            keep, (hidden,) = tied(keep, hidden)
            (section_out,) = call(
                section_kernel, [((out_channels, cot.shape[1]), BF16)], [], conv_flops // 10,
                (hidden, down_weight),
            )
    keep, (near,) = tied(keep, near)
    near_in = swap(near, "gz", 0)
    shard = ((rows // 8, 128), BF16)
    (sums,) = call(add_kernel, [shard], [], 0, (keep, flip(send, "gz", 2)))
    (sums,) = call(add_kernel, [shard], [], 0, (sums, flip(sums, "gz", 1)))
    sums, outside = tied(sums, near_in, far_in)
    sends = call(edges_kernel, [edge, edge], [], 0, (*gates, *outside))
    beside = swapped(*sends, "gy")
    (acc,) = call(
        field_kernel, [(lines, F32)], [cols, cols], conv_flops, (*gates, *outside, weight_bwd)
    )
    wide = [("gy", 1 << k) for k in range(2, lax.axis_size("gy").bit_length() - 1)]
    wide += [("gz", 1 << k) for k in range(2, lax.axis_size("gz").bit_length() - 1)]
    for axis, bit in wide:
        (sums,) = call(add_kernel, [shard], [], 0, (sums, flip(sums, axis, bit)))
    sums, (section_out,) = tied(sums, section_out)
    (sums,) = call(
        functools.partial(join_kernel, axis="gz", bit=2), [((rows // 4, 128), BF16)], [], 0,
        (sums, flip(sums, "gz", 2)),
    )
    sums, (acc, *beside) = tied(sums, acc, *beside)
    (field,) = call(
        field_edges_kernel, [((channels * plane_count * row_count, breadth), F32)], [edge_cols],
        conv_flops // 10, (*beside, acc, weight_bwd),
    )
    (sums,) = call(
        functools.partial(join_kernel, axis="gy", bit=2), [((rows // 2, 128), BF16)], [], 0,
        (sums, flip(sums, "gy", 2)),
    )
    sums, (field,) = tied(sums, field)
    grad_conv, grad_down = call(
        functools.partial(unpack_kernel, scale=grad_scale),
        [(conv_weight.shape, F32), (down_weight.shape, F32)], [((rows, 128), BF16)], 0,
        (sums, flip(sums, "gy", 1)),
    )
    section_out = section_out.reshape(out_channels, plane_count // 2, -1)
    return (section_out, field.reshape(features.shape), grad_conv, grad_down)


def solution(mesh):
    return jax.shard_map(
        body,
        mesh=mesh,
        in_specs=(P(None, "gz", "gy", None), P(), P(), P(None, "gz", "gy")),
        out_specs=(P(None, "gz", "gy"), P(None, "gz", "gy", None), P(), P()),
        check_vma=False,
    )
```

```python
import functools
import math

import jax
import jax.numpy as jnp
from jax import lax
from jax.experimental import pallas as pl
from jax.experimental.pallas import tpu as pltpu
from jax.sharding import PartitionSpec as P

F32 = jnp.float32
BF16 = jnp.bfloat16
PARAMS = pltpu.CompilerParams(vmem_limit_bytes=24 * 1024 * 1024)


def call(kernel, outs, scratch, flops, operands):
    moved = sum(x.size * x.dtype.itemsize for x in operands)
    moved += sum(math.prod(s) * jnp.dtype(d).itemsize for s, d in outs)
    vmem = pl.BlockSpec(memory_space=pltpu.VMEM)
    return pl.pallas_call(
        kernel,
        out_shape=[jax.ShapeDtypeStruct(s, d) for s, d in outs],
        in_specs=[vmem] * len(operands),
        out_specs=[vmem] * len(outs),
        scratch_shapes=[pltpu.VMEM(s, d) for s, d in scratch],
        compiler_params=PARAMS,
        cost_estimate=pl.CostEstimate(flops=flops, bytes_accessed=moved, transcendentals=0),
    )(*operands)


def is_even(axis):
    return lax.rem(lax.axis_index(axis), 2) == 0


def choose(cond, yes, no):
    return jnp.where(jnp.broadcast_to(cond, yes.shape), yes, no)


def lines_kernel(f_ref, near_ref, far_ref, wide):
    channels, planes, rows, breadth = f_ref.shape
    wide[...] = f_ref[...].astype(F32).reshape(channels * planes * rows, breadth)
    even = is_even("gz")
    for y in range(rows):
        low, high = (
            wide[pl.ds(z * rows + y, channels, stride=planes * rows), :].astype(BF16) for z in range(2)
        )
        near_ref[y] = choose(even, high, low)
        far_ref[y] = choose(even, low, high)


def edges_kernel(near, far, near_in, far_in, near_ref, far_ref):
    rows = near.shape[0]
    even_z, even_y = is_even("gz"), is_even("gy")

    def put(p, one, other):
        first = choose(even_z, one[0], other[0])
        last = choose(even_z, one[rows - 1], other[rows - 1])
        near_ref[p] = choose(even_y, last, first)
        far_ref[p] = choose(even_y, first, last)

    put(0, far_in, near_in)
    put(1, far, near)
    put(2, near, far)
    put(3, near_in, far_in)


def put_columns(cols, p, q, line):
    channels = line.shape[0]
    wide = line.astype(F32)
    cols[p, q, 0:channels] = pltpu.roll(wide, 1, 1).astype(BF16)
    cols[p, q, channels : 2 * channels] = line
    cols[p, q, 2 * channels : 3 * channels] = pltpu.roll(wide, line.shape[1] - 1, 1).astype(BF16)


def fill_columns(cols, near, far):
    rows = near.shape[0]
    even = is_even("gz")

    def step(y, carry):
        put_columns(cols, 0, y + 1, choose(even, far[y], near[y]))
        put_columns(cols, 1, y + 1, choose(even, near[y], far[y]))
        return carry

    lax.fori_loop(0, rows, step, 0, unroll=2)
    for p in range(2):
        for q in (0, rows + 1):
            cols[p, q] = jnp.zeros(cols.shape[2:], BF16)


def fill_edges(cols, near, far):
    even = is_even("gy")
    for p in range(4):
        put_columns(cols, p, 0, choose(even, far[p], near[p]))
        put_columns(cols, p, 1, choose(even, near[p], far[p]))


def dot(lhs, rhs):
    return jnp.dot(lhs, rhs, preferred_element_type=F32)


def taps(w_ref, b, first, last):
    return jnp.concatenate([w_ref[a, b] for a in range(first, last)], axis=0)


def window(cols, p, q):
    return jnp.concatenate([cols[p, q], cols[p, q + 1]], axis=1)


def inner_terms(cols, w_ref, y):
    acc = None
    for b in range(3):
        for p in range(2):
            term = dot(taps(w_ref, b, p, p + 2), window(cols, p, y + b))
            acc = term if acc is None else acc + term
    half = acc.shape[0] // 2
    return acc[half:], acc[:half]


def outer_terms(cols, w_ref, y):
    lower = upper = None
    for b in range(3):
        low, high = dot(w_ref[0, b], window(cols, 0, y + b)), dot(w_ref[2, b], window(cols, 1, y + b))
        lower = low if lower is None else lower + low
        upper = high if upper is None else upper + high
    return lower, upper


def edge_terms(edges, w_ref, side):
    b = 2 * side
    half = w_ref.shape[2]
    acc = dot(taps(w_ref, b, 0, 2), edges[1, side]) + dot(taps(w_ref, b, 1, 3), edges[2, side])
    return acc[half:] + dot(w_ref[0, b], edges[0, side]), acc[:half] + dot(w_ref[2, b], edges[3, side])


def inner_kernel(near, far, w_ref, d_ref, cot_ref, cols, acc_ref, grad_ref, up):
    rows, channels, breadth = near.shape
    fill_columns(cols, near, far)
    source = lax.broadcasted_iota(jnp.int32, (breadth, 2 * breadth), 0)
    target = lax.broadcasted_iota(jnp.int32, (breadth, 2 * breadth), 1)
    spread = jnp.where(source == target // 2, 1.0, 0.0).astype(BF16)
    for pair in range(rows // 4):
        both = dot(cot_ref[:, pair * breadth : (pair + 1) * breadth], spread)
        up[:, 2 * pair * breadth : 2 * (pair + 1) * breadth] = both.astype(BF16)
    even = lax.broadcasted_iota(jnp.int32, (channels, breadth), 1) % 2 == 0
    for a in range(2):
        for b in range(2):
            terms = lax.dot_general(d_ref[a, b], up[...], (((0,), (0,)), ((), ())), preferred_element_type=F32)
            for t in range(rows // 2):
                part = terms[:, t * breadth : (t + 1) * breadth]
                grad_ref[a, 2 * t + b] = jnp.where(even, part[0:channels], part[channels:])

    def step(t, carry):
        y = 2 * t
        for z, lines in enumerate(inner_terms(cols, w_ref, y)):
            for b in range(2):
                acc_ref[z, y + b] = lines[:, b * breadth : (b + 1) * breadth]
        return carry

    lax.fori_loop(0, rows // 2, step, 0)


def outer_kernel(near, far, w_ref, acc_ref, cols, out_ref):
    rows, channels, breadth = near.shape
    fill_columns(cols, near, far)

    def step(t, carry):
        y = 2 * t
        for z, lines in enumerate(outer_terms(cols, w_ref, y)):
            for b in range(2):
                out_ref[z, y + b] = acc_ref[z, y + b] + lines[:, b * breadth : (b + 1) * breadth]
        return carry

    lax.fori_loop(0, rows // 2, step, 0)


def gate_kernel(near, far, acc_ref, grad_ref, w_ref, edges, near_ref, far_ref, h_ref):
    rows, channels, breadth = acc_ref.shape[1:]
    fill_edges(edges, near, far)
    sides = [edge_terms(edges, w_ref, side) for side in range(2)]
    even = is_even("gz")

    def gate(y, extra):
        found = []
        for z in range(2):
            preact = acc_ref[z, y] if extra is None else acc_ref[z, y] + extra[z]
            sig = 1.0 / (1.0 + jnp.exp(-preact))
            h_ref[z, y] = (preact * sig).astype(BF16)
            found.append((grad_ref[z, y] * sig * (1.0 + preact * (1.0 - sig))).astype(BF16))
        near_ref[y] = choose(even, found[1], found[0])
        far_ref[y] = choose(even, found[0], found[1])

    gate(0, sides[0])
    for y in range(1, rows - 1):
        gate(y, None)
    gate(rows - 1, sides[1])


def coarse_hidden(h_ref, a, b):
    rows, channels, breadth = h_ref.shape[1:]
    source = lax.broadcasted_iota(jnp.int32, (2 * breadth, 2 * breadth), 0)
    target = lax.broadcasted_iota(jnp.int32, (2 * breadth, 2 * breadth), 1)
    wanted = 2 * (target % breadth) + target // breadth
    pick = jnp.where(source == wanted, 1.0, 0.0).astype(BF16)
    pairs = []
    for pair in range(rows // 4):
        both = jnp.concatenate([h_ref[a, 4 * pair + b], h_ref[a, 4 * pair + 2 + b]], axis=1)
        pairs.append(dot(both, pick).astype(BF16))
    return jnp.concatenate(
        [jnp.concatenate([x[:, e * breadth : (e + 1) * breadth] for x in pairs], axis=1) for e in range(2)],
        axis=0,
    )


def section_kernel(h_ref, d_ref, out_ref):
    coarse = None
    for a in range(2):
        for b in range(2):
            term = dot(d_ref[a, b], coarse_hidden(h_ref, a, b))
            coarse = term if coarse is None else coarse + term
    out_ref[...] = coarse.astype(BF16)


def weight_grad_kernel(inner, outer, edges, near, far, h_ref, cot_ref, keep, send, packed):
    rows, channels, breadth = near.shape
    across = (((1,), (1,)), ((), ()))
    even = is_even("gz")
    low = [choose(even, far[y], near[y]) for y in range(rows)]
    high = [choose(even, near[y], far[y]) for y in range(rows)]
    gates = jnp.concatenate([jnp.concatenate(low, axis=1), jnp.concatenate(high, axis=1)], axis=0)

    def columns(p, q):
        if q in (0, rows + 1):
            return edges[p, 0 if q == 0 else 1]
        return inner[p - 1, q] if p in (1, 2) else outer[p // 3, q]

    lane = lax.broadcasted_iota(jnp.int32, (channels // 2, breadth), 1)
    for b in range(3):
        parts = []
        for p in range(4):
            across_rows = jnp.concatenate([columns(p, y + b) for y in range(rows)], axis=1)
            lhs = gates[0:channels] if p == 0 else gates[channels:] if p == 3 else gates
            parts.append(lax.dot_general(lhs, across_rows, across, preferred_element_type=F32))
        for a in range(3):
            low = parts[a][0:channels]
            high = parts[a + 1] if a == 2 else parts[a + 1][channels:]
            total = low + high
            base = (a * 3 + b) * 3 * channels // 2
            packed[base : base + channels] = total[:, 0:breadth]
            rest = jnp.concatenate([total[:, breadth:], total[:, breadth:]], axis=1)
            mix = jnp.where(lane < channels, rest[0 : channels // 2], rest[channels // 2 :])
            packed[base + channels : base + 3 * channels // 2] = mix
    base = 9 * 3 * channels // 2
    height = cot_ref.shape[0]
    for a in range(2):
        for b in range(2):
            down = lax.dot_general(cot_ref[...], coarse_hidden(h_ref, a, b), across, preferred_element_type=F32)
            at = base + (2 * a + b) * height
            packed[at : at + height] = down
    end = base + 4 * height
    if end < packed.shape[0]:
        packed[end:] = jnp.zeros((packed.shape[0] - end, packed.shape[1]), F32)
    split(packed, keep, send, owned_half())


def side_of(axis, bit):
    return lax.rem(lax.axis_index(axis) // bit, 2)


def owned_half():
    total = 0
    for axis in ("gz", "gy"):
        for k in range(lax.axis_size(axis).bit_length() - 1):
            total = total + side_of(axis, 1 << k)
    return lax.rem(total, 2)


def part(side, rows):
    return pl.ds(pl.multiple_of(side * rows, 16), rows)


def split(packed, keep, send, side):
    half = keep.shape[0]
    keep[...] = packed[part(side, half)]
    send[...] = packed[part(1 - side, half)].astype(BF16)


def halve_kernel(mine, other, keep, send, total, *, axis, bit):
    total[...] = mine[...] + other[...].astype(F32)
    split(total, keep, send, side_of(axis, bit))


def add_kernel(x, y, out):
    out[...] = (x[...].astype(F32) + y[...].astype(F32)).astype(BF16)


def join_kernel(mine, other, out, *, axis, bit):
    join(mine, other, out, side_of(axis, bit))


def join(mine, other, out, side):
    rows = mine.shape[0]
    out[part(side, rows)] = mine[...]
    out[part(1 - side, rows)] = other[...]


def field_kernel(near, far, near_in, far_in, w_ref, acc_ref, inner, outer):
    rows, channels, breadth = near.shape
    fill_columns(inner, near, far)
    fill_columns(outer, near_in, far_in)

    def step(t, carry):
        y = 2 * t
        own = inner_terms(inner, w_ref, y)
        rest = outer_terms(outer, w_ref, y)
        for z in range(2):
            total = own[z] + rest[z]
            for b in range(2):
                acc_ref[z, y + b] = total[:, b * breadth : (b + 1) * breadth]
        return carry

    lax.fori_loop(0, rows // 2, step, 0)


def field_edges_kernel(near, far, acc_ref, w_ref, out_ref, edges):
    rows, channels, breadth = acc_ref.shape[1:]
    fill_edges(edges, near, far)
    sides = [edge_terms(edges, w_ref, side) for side in range(2)]
    for z in range(2):
        for y in range(rows):
            line = acc_ref[z, y]
            if y in (0, rows - 1):
                line = line + sides[0 if y == 0 else 1][z]
            out_ref[pl.ds(z * rows + y, channels, stride=2 * rows), :] = line


def unpack_kernel(mine, other, conv_ref, down_ref, sums_ref, *, scale):
    join(mine, other, sums_ref, owned_half())
    channels = conv_ref.shape[2]
    for a in range(3):
        for b in range(3):
            base = (a * 3 + b) * 3 * channels // 2
            conv_ref[a, b, :, 0 : 2 * channels] = sums_ref[base : base + channels].astype(F32) * scale
            rest = sums_ref[base + channels : base + 3 * channels // 2].astype(F32) * scale
            conv_ref[a, b, 0 : channels // 2, 2 * channels :] = rest[:, 0:channels]
            conv_ref[a, b, channels // 2 :, 2 * channels :] = rest[:, channels:]
    base = 9 * 3 * channels // 2
    height = down_ref.shape[2]
    for a in range(2):
        for b in range(2):
            at = base + (2 * a + b) * height
            down_ref[a, b] = sums_ref[at : at + height].astype(F32) * scale


def swap(cells, axis, low):
    count = lax.axis_size(axis)
    pairs = [(i % count, (i + 1) % count) for i in range(low, low + count, 2)]
    return lax.ppermute(cells, axis, pairs + [(b, a) for a, b in pairs])


def flip(cells, axis, bit):
    row = lax.axis_size("gy")
    mask = bit * row | 1 if axis == "gz" else bit | 1
    return lax.ppermute(cells, ("gz", "gy"), [(i, i ^ mask) for i in range(lax.axis_size("gz") * row)])


def tied(first, *others):
    found = lax.optimization_barrier((first, *others))
    return found[0], tuple(found[1:])


def swapped(near, far, axis):
    return swap(near, axis, 0), swap(far, axis, 1)


def body(features, conv_weight, down_weight, cotangent):
    channels, plane_count, row_count, breadth = features.shape
    out_channels = down_weight.shape[2]
    count = lax.axis_size("gz") * lax.axis_size("gy")
    grad_scale = 1.0 / math.sqrt(plane_count * row_count * breadth * count)
    turned = conv_weight.reshape(3, 3, channels, 3, channels)[::-1, ::-1, :, ::-1]
    weight_bwd = turned.transpose(0, 1, 4, 3, 2).reshape(3, 3, channels, 3 * channels)
    cot = cotangent.reshape(out_channels, -1)
    plane = ((row_count, channels, breadth), BF16)
    edge = ((plane_count + 2, channels, breadth), BF16)
    cols = ((plane_count, row_count + 2, 3 * channels, breadth), BF16)
    edge_cols = ((plane_count + 2, 2, 3 * channels, breadth), BF16)
    lines = (plane_count, row_count, channels, breadth)
    conv_flops = 2 * 27 * channels * channels * plane_count * row_count * breadth

    own = call(
        lines_kernel, [plane, plane], [((channels * plane_count * row_count, breadth), F32)], 0, (features,)
    )
    outside = swapped(*own, "gz")
    inner, acc, hidden_grad = call(
        inner_kernel, [cols, (lines, F32), (lines, F32)],
        [((out_channels, row_count // 2 * breadth), BF16)],
        2 * conv_flops // 3, (*own, conv_weight, down_weight, cot),
    )
    near, far, acc = lax.optimization_barrier((*outside, acc))
    outside = (near, far)
    beside = swapped(*call(edges_kernel, [edge, edge], [], 0, (*own, *outside)), "gy")
    outer, acc = call(
        outer_kernel, [cols, (lines, F32)], [], conv_flops // 3, (*outside, conv_weight, acc)
    )
    edges, near, far, hidden = call(
        gate_kernel, [edge_cols, plane, plane, (lines, BF16)], [], conv_flops // 10,
        (*beside, acc, hidden_grad, conv_weight),
    )
    gates = (near, far)

    used = 27 * channels * channels // 128 + 4 * out_channels
    rows = -(-used // 128) * 128
    keep, send = call(
        weight_grad_kernel, [((rows // 2, 128), F32), ((rows // 2, 128), BF16)], [((rows, 128), F32)],
        conv_flops, (inner, outer, edges, *gates, hidden, cot),
    )
    keep, gates = tied(keep, *gates)
    near, far = gates
    far_in = swap(far, "gz", 1)
    for level, (axis, bit) in enumerate((("gy", 2), ("gz", 1))):
        size = rows >> (level + 2)
        mine, got = keep, flip(send, *(("gy", 1), ("gy", 2))[level])
        keep, send = call(
            functools.partial(halve_kernel, axis=axis, bit=bit),
            [((size, 128), F32), ((size, 128), BF16)], [((2 * size, 128), F32)], 0, (mine, got),
        )
        if level == 0:
            keep, (hidden,) = tied(keep, hidden)
            (section_out,) = call(
                section_kernel, [((out_channels, cot.shape[1]), BF16)], [], conv_flops // 10,
                (hidden, down_weight),
            )
    shard = ((rows // 8, 128), BF16)
    (sums,) = call(add_kernel, [shard], [], 0, (keep, flip(send, "gz", 1)))
    sums, (near, far_in) = tied(sums, near, far_in)
    outside = (swap(near, "gz", 0), far_in)
    sends = call(edges_kernel, [edge, edge], [], 0, (*gates, *outside))
    beside = swapped(*sends, "gy")
    (acc,) = call(
        field_kernel, [(lines, F32)], [cols, cols], conv_flops, (*gates, *outside, weight_bwd)
    )
    wide = [("gy", 1 << k) for k in range(2, lax.axis_size("gy").bit_length() - 1)]
    wide += [("gz", 1 << k) for k in range(1, lax.axis_size("gz").bit_length() - 1)]
    for axis, bit in wide:
        (sums,) = call(add_kernel, [shard], [], 0, (sums, flip(sums, axis, bit)))
    sums, (section_out,) = tied(sums, section_out)
    (sums,) = call(
        functools.partial(join_kernel, axis="gz", bit=1), [((rows // 4, 128), BF16)], [], 0,
        (sums, flip(sums, "gz", 1)),
    )
    sums, (acc, *beside) = tied(sums, acc, *beside)
    (field,) = call(
        field_edges_kernel, [((channels * plane_count * row_count, breadth), F32)], [edge_cols],
        conv_flops // 10, (*beside, acc, weight_bwd),
    )
    (sums,) = call(
        functools.partial(join_kernel, axis="gy", bit=2), [((rows // 2, 128), BF16)], [], 0,
        (sums, flip(sums, "gy", 2)),
    )
    sums, (field,) = tied(sums, field)
    grad_conv, grad_down = call(
        functools.partial(unpack_kernel, scale=grad_scale),
        [(conv_weight.shape, F32), (down_weight.shape, F32)], [((rows, 128), BF16)], 0,
        (sums, flip(sums, "gy", 1)),
    )
    section_out = section_out.reshape(out_channels, plane_count // 2, -1)
    return (section_out, field.reshape(features.shape), grad_conv, grad_down)


def solution(mesh):
    return jax.shard_map(
        body,
        mesh=mesh,
        in_specs=(P(None, "gz", "gy", None), P(), P(), P(None, "gz", "gy")),
        out_specs=(P(None, "gz", "gy"), P(None, "gz", "gy", None), P(), P()),
        check_vma=False,
    )
```

```python
import functools
import math

import jax
import jax.numpy as jnp
from jax import lax
from jax.experimental import pallas as pl
from jax.experimental.pallas import tpu as pltpu
from jax.sharding import PartitionSpec as P

F32 = jnp.float32
BF16 = jnp.bfloat16
PARAMS = pltpu.CompilerParams(vmem_limit_bytes=24 * 1024 * 1024)


def call(kernel, outs, scratch, flops, operands):
    moved = sum(x.size * x.dtype.itemsize for x in operands)
    moved += sum(math.prod(s) * jnp.dtype(d).itemsize for s, d in outs)
    vmem = pl.BlockSpec(memory_space=pltpu.VMEM)
    return pl.pallas_call(
        kernel,
        out_shape=[jax.ShapeDtypeStruct(s, d) for s, d in outs],
        in_specs=[vmem] * len(operands),
        out_specs=[vmem] * len(outs),
        scratch_shapes=[pltpu.VMEM(s, d) for s, d in scratch],
        compiler_params=PARAMS,
        cost_estimate=pl.CostEstimate(flops=flops, bytes_accessed=moved, transcendentals=0),
    )(*operands)


def is_even(axis):
    return lax.rem(lax.axis_index(axis), 2) == 0


def choose(cond, yes, no):
    return jnp.where(jnp.broadcast_to(cond, yes.shape), yes, no)


def lines_kernel(f_ref, near_ref, far_ref, wide):
    channels, planes, rows, breadth = f_ref.shape
    wide[...] = f_ref[...].astype(F32).reshape(channels * planes * rows, breadth)
    even = is_even("gz")
    for y in range(rows):
        low, high = (
            wide[pl.ds(z * rows + y, channels, stride=planes * rows), :].astype(BF16) for z in range(2)
        )
        near_ref[y] = choose(even, high, low)
        far_ref[y] = choose(even, low, high)


def edges_kernel(near, far, near_in, far_in, near_ref, far_ref):
    rows = near.shape[0]
    even_z, even_y = is_even("gz"), is_even("gy")

    def put(p, one, other):
        first = choose(even_z, one[0], other[0])
        last = choose(even_z, one[rows - 1], other[rows - 1])
        near_ref[p] = choose(even_y, last, first)
        far_ref[p] = choose(even_y, first, last)

    put(0, far_in, near_in)
    put(1, far, near)
    put(2, near, far)
    put(3, near_in, far_in)


def put_columns(cols, p, q, line):
    channels = line.shape[0]
    wide = line.astype(F32)
    cols[p, q, 0:channels] = pltpu.roll(wide, 1, 1).astype(BF16)
    cols[p, q, channels : 2 * channels] = line
    cols[p, q, 2 * channels : 3 * channels] = pltpu.roll(wide, line.shape[1] - 1, 1).astype(BF16)


def fill_columns(cols, near, far):
    rows = near.shape[0]
    even = is_even("gz")

    def step(y, carry):
        put_columns(cols, 0, y + 1, choose(even, far[y], near[y]))
        put_columns(cols, 1, y + 1, choose(even, near[y], far[y]))
        return carry

    lax.fori_loop(0, rows, step, 0, unroll=2)
    for p in range(2):
        for q in (0, rows + 1):
            cols[p, q] = jnp.zeros(cols.shape[2:], BF16)


def fill_edges(cols, near, far):
    even = is_even("gy")
    for p in range(4):
        put_columns(cols, p, 0, choose(even, far[p], near[p]))
        put_columns(cols, p, 1, choose(even, near[p], far[p]))


def dot(lhs, rhs):
    return jnp.dot(lhs, rhs, preferred_element_type=F32)


def taps(w_ref, b, first, last):
    return jnp.concatenate([w_ref[a, b] for a in range(first, last)], axis=0)


def window(cols, p, q):
    return jnp.concatenate([cols[p, q], cols[p, q + 1]], axis=1)


def inner_terms(cols, w_ref, y):
    acc = None
    for b in range(3):
        for p in range(2):
            term = dot(taps(w_ref, b, p, p + 2), window(cols, p, y + b))
            acc = term if acc is None else acc + term
    half = acc.shape[0] // 2
    return acc[half:], acc[:half]


def outer_terms(cols, w_ref, y):
    lower = upper = None
    for b in range(3):
        low, high = dot(w_ref[0, b], window(cols, 0, y + b)), dot(w_ref[2, b], window(cols, 1, y + b))
        lower = low if lower is None else lower + low
        upper = high if upper is None else upper + high
    return lower, upper


def edge_terms(edges, w_ref, side):
    b = 2 * side
    half = w_ref.shape[2]
    acc = dot(taps(w_ref, b, 0, 2), edges[1, side]) + dot(taps(w_ref, b, 1, 3), edges[2, side])
    return acc[half:] + dot(w_ref[0, b], edges[0, side]), acc[:half] + dot(w_ref[2, b], edges[3, side])


def inner_kernel(near, far, w_ref, d_ref, cot_ref, cols, acc_ref, grad_ref, up):
    rows, channels, breadth = near.shape
    fill_columns(cols, near, far)
    source = lax.broadcasted_iota(jnp.int32, (breadth, 2 * breadth), 0)
    target = lax.broadcasted_iota(jnp.int32, (breadth, 2 * breadth), 1)
    spread = jnp.where(source == target // 2, 1.0, 0.0).astype(BF16)
    for pair in range(rows // 4):
        both = dot(cot_ref[:, pair * breadth : (pair + 1) * breadth], spread)
        up[:, 2 * pair * breadth : 2 * (pair + 1) * breadth] = both.astype(BF16)
    even = lax.broadcasted_iota(jnp.int32, (channels, breadth), 1) % 2 == 0
    for a in range(2):
        for b in range(2):
            terms = lax.dot_general(d_ref[a, b], up[...], (((0,), (0,)), ((), ())), preferred_element_type=F32)
            for t in range(rows // 2):
                part = terms[:, t * breadth : (t + 1) * breadth]
                grad_ref[a, 2 * t + b] = jnp.where(even, part[0:channels], part[channels:])

    def step(t, carry):
        y = 2 * t
        for z, lines in enumerate(inner_terms(cols, w_ref, y)):
            for b in range(2):
                acc_ref[z, y + b] = lines[:, b * breadth : (b + 1) * breadth]
        return carry

    lax.fori_loop(0, rows // 2, step, 0)


def outer_kernel(near, far, w_ref, acc_ref, cols, out_ref):
    rows, channels, breadth = near.shape
    fill_columns(cols, near, far)

    def step(t, carry):
        y = 2 * t
        for z, lines in enumerate(outer_terms(cols, w_ref, y)):
            for b in range(2):
                out_ref[z, y + b] = acc_ref[z, y + b] + lines[:, b * breadth : (b + 1) * breadth]
        return carry

    lax.fori_loop(0, rows // 2, step, 0)


def gate_kernel(near, far, acc_ref, grad_ref, w_ref, edges, near_ref, far_ref, h_ref):
    rows, channels, breadth = acc_ref.shape[1:]
    fill_edges(edges, near, far)
    sides = [edge_terms(edges, w_ref, side) for side in range(2)]
    even = is_even("gz")

    def gate(y, extra):
        found = []
        for z in range(2):
            preact = acc_ref[z, y] if extra is None else acc_ref[z, y] + extra[z]
            sig = 1.0 / (1.0 + jnp.exp(-preact))
            h_ref[z, y] = (preact * sig).astype(BF16)
            found.append((grad_ref[z, y] * sig * (1.0 + preact * (1.0 - sig))).astype(BF16))
        near_ref[y] = choose(even, found[1], found[0])
        far_ref[y] = choose(even, found[0], found[1])

    gate(0, sides[0])
    for y in range(1, rows - 1):
        gate(y, None)
    gate(rows - 1, sides[1])


def coarse_hidden(h_ref, a, b):
    rows, channels, breadth = h_ref.shape[1:]
    source = lax.broadcasted_iota(jnp.int32, (2 * breadth, 2 * breadth), 0)
    target = lax.broadcasted_iota(jnp.int32, (2 * breadth, 2 * breadth), 1)
    wanted = 2 * (target % breadth) + target // breadth
    pick = jnp.where(source == wanted, 1.0, 0.0).astype(BF16)
    pairs = []
    for pair in range(rows // 4):
        both = jnp.concatenate([h_ref[a, 4 * pair + b], h_ref[a, 4 * pair + 2 + b]], axis=1)
        pairs.append(dot(both, pick).astype(BF16))
    return jnp.concatenate(
        [jnp.concatenate([x[:, e * breadth : (e + 1) * breadth] for x in pairs], axis=1) for e in range(2)],
        axis=0,
    )


def section_kernel(h_ref, d_ref, out_ref):
    coarse = None
    for a in range(2):
        for b in range(2):
            term = dot(d_ref[a, b], coarse_hidden(h_ref, a, b))
            coarse = term if coarse is None else coarse + term
    out_ref[...] = coarse.astype(BF16)


def weight_grad_kernel(inner, outer, edges, near, far, h_ref, cot_ref, keep, send, packed):
    rows, channels, breadth = near.shape
    across = (((1,), (1,)), ((), ()))
    even = is_even("gz")
    low = [choose(even, far[y], near[y]) for y in range(rows)]
    high = [choose(even, near[y], far[y]) for y in range(rows)]
    gates = jnp.concatenate([jnp.concatenate(low, axis=1), jnp.concatenate(high, axis=1)], axis=0)

    def columns(p, q):
        if q in (0, rows + 1):
            return edges[p, 0 if q == 0 else 1]
        return inner[p - 1, q] if p in (1, 2) else outer[p // 3, q]

    lane = lax.broadcasted_iota(jnp.int32, (channels // 2, breadth), 1)
    for b in range(3):
        parts = []
        for p in range(4):
            across_rows = jnp.concatenate([columns(p, y + b) for y in range(rows)], axis=1)
            lhs = gates[0:channels] if p == 0 else gates[channels:] if p == 3 else gates
            parts.append(lax.dot_general(lhs, across_rows, across, preferred_element_type=F32))
        for a in range(3):
            low = parts[a][0:channels]
            high = parts[a + 1] if a == 2 else parts[a + 1][channels:]
            total = low + high
            base = (a * 3 + b) * 3 * channels // 2
            packed[base : base + channels] = total[:, 0:breadth]
            rest = jnp.concatenate([total[:, breadth:], total[:, breadth:]], axis=1)
            mix = jnp.where(lane < channels, rest[0 : channels // 2], rest[channels // 2 :])
            packed[base + channels : base + 3 * channels // 2] = mix
    base = 9 * 3 * channels // 2
    height = cot_ref.shape[0]
    for a in range(2):
        for b in range(2):
            down = lax.dot_general(cot_ref[...], coarse_hidden(h_ref, a, b), across, preferred_element_type=F32)
            at = base + (2 * a + b) * height
            packed[at : at + height] = down
    end = base + 4 * height
    if end < packed.shape[0]:
        packed[end:] = jnp.zeros((packed.shape[0] - end, packed.shape[1]), F32)
    split(packed, keep, send, owned_half())


def side_of(axis, bit):
    return lax.rem(lax.axis_index(axis) // bit, 2)


def owned_half():
    total = 0
    for axis in ("gz", "gy"):
        for k in range(lax.axis_size(axis).bit_length() - 1):
            total = total + side_of(axis, 1 << k)
    return lax.rem(total, 2)


def part(side, rows):
    return pl.ds(pl.multiple_of(side * rows, 16), rows)


def split(packed, keep, send, side):
    half = keep.shape[0]
    keep[...] = packed[part(side, half)]
    send[...] = packed[part(1 - side, half)].astype(BF16)


def halve_kernel(mine, other, keep, send, total, *, axis, bit):
    total[...] = mine[...] + other[...].astype(F32)
    split(total, keep, send, side_of(axis, bit))


def add_kernel(x, y, out):
    out[...] = (x[...].astype(F32) + y[...].astype(F32)).astype(BF16)


def join_kernel(mine, other, out, *, axis, bit):
    join(mine, other, out, side_of(axis, bit))


def join(mine, other, out, side):
    rows = mine.shape[0]
    out[part(side, rows)] = mine[...]
    out[part(1 - side, rows)] = other[...]


def field_kernel(near, far, near_in, far_in, w_ref, acc_ref, inner, outer):
    rows, channels, breadth = near.shape
    fill_columns(inner, near, far)
    fill_columns(outer, near_in, far_in)

    def step(t, carry):
        y = 2 * t
        own = inner_terms(inner, w_ref, y)
        rest = outer_terms(outer, w_ref, y)
        for z in range(2):
            total = own[z] + rest[z]
            for b in range(2):
                acc_ref[z, y + b] = total[:, b * breadth : (b + 1) * breadth]
        return carry

    lax.fori_loop(0, rows // 2, step, 0)


def field_edges_kernel(near, far, acc_ref, w_ref, out_ref, edges):
    rows, channels, breadth = acc_ref.shape[1:]
    fill_edges(edges, near, far)
    sides = [edge_terms(edges, w_ref, side) for side in range(2)]
    for z in range(2):
        for y in range(rows):
            line = acc_ref[z, y]
            if y in (0, rows - 1):
                line = line + sides[0 if y == 0 else 1][z]
            out_ref[pl.ds(z * rows + y, channels, stride=2 * rows), :] = line


def unpack_kernel(mine, other, conv_ref, down_ref, sums_ref, *, scale):
    join(mine, other, sums_ref, owned_half())
    channels = conv_ref.shape[2]
    for a in range(3):
        for b in range(3):
            base = (a * 3 + b) * 3 * channels // 2
            conv_ref[a, b, :, 0 : 2 * channels] = sums_ref[base : base + channels].astype(F32) * scale
            rest = sums_ref[base + channels : base + 3 * channels // 2].astype(F32) * scale
            conv_ref[a, b, 0 : channels // 2, 2 * channels :] = rest[:, 0:channels]
            conv_ref[a, b, channels // 2 :, 2 * channels :] = rest[:, channels:]
    base = 9 * 3 * channels // 2
    height = down_ref.shape[2]
    for a in range(2):
        for b in range(2):
            at = base + (2 * a + b) * height
            down_ref[a, b] = sums_ref[at : at + height].astype(F32) * scale


def swap(cells, axis, low):
    count = lax.axis_size(axis)
    pairs = [(i % count, (i + 1) % count) for i in range(low, low + count, 2)]
    return lax.ppermute(cells, axis, pairs + [(b, a) for a, b in pairs])


def flip(cells, axis, bit):
    row = lax.axis_size("gy")
    mask = bit * row | 1 if axis == "gz" else bit | 1
    return lax.ppermute(cells, ("gz", "gy"), [(i, i ^ mask) for i in range(lax.axis_size("gz") * row)])


def tied(first, *others):
    found = lax.optimization_barrier((first, *others))
    return found[0], tuple(found[1:])


def swapped(near, far, axis):
    return swap(near, axis, 0), swap(far, axis, 1)


def body(features, conv_weight, down_weight, cotangent):
    channels, plane_count, row_count, breadth = features.shape
    out_channels = down_weight.shape[2]
    count = lax.axis_size("gz") * lax.axis_size("gy")
    grad_scale = 1.0 / math.sqrt(plane_count * row_count * breadth * count)
    turned = conv_weight.reshape(3, 3, channels, 3, channels)[::-1, ::-1, :, ::-1]
    weight_bwd = turned.transpose(0, 1, 4, 3, 2).reshape(3, 3, channels, 3 * channels)
    cot = cotangent.reshape(out_channels, -1)
    plane = ((row_count, channels, breadth), BF16)
    edge = ((plane_count + 2, channels, breadth), BF16)
    cols = ((plane_count, row_count + 2, 3 * channels, breadth), BF16)
    edge_cols = ((plane_count + 2, 2, 3 * channels, breadth), BF16)
    lines = (plane_count, row_count, channels, breadth)
    conv_flops = 2 * 27 * channels * channels * plane_count * row_count * breadth

    own = call(
        lines_kernel, [plane, plane], [((channels * plane_count * row_count, breadth), F32)], 0, (features,)
    )
    outside = swapped(*own, "gz")
    inner, acc, hidden_grad = call(
        inner_kernel, [cols, (lines, F32), (lines, F32)],
        [((out_channels, row_count // 2 * breadth), BF16)],
        2 * conv_flops // 3, (*own, conv_weight, down_weight, cot),
    )
    near, far, acc = lax.optimization_barrier((*outside, acc))
    outside = (near, far)
    beside = swapped(*call(edges_kernel, [edge, edge], [], 0, (*own, *outside)), "gy")
    outer, acc = call(
        outer_kernel, [cols, (lines, F32)], [], conv_flops // 3, (*outside, conv_weight, acc)
    )
    edges, near, far, hidden = call(
        gate_kernel, [edge_cols, plane, plane, (lines, BF16)], [], conv_flops // 10,
        (*beside, acc, hidden_grad, conv_weight),
    )
    gates = (near, far)

    used = 27 * channels * channels // 128 + 4 * out_channels
    rows = -(-used // 128) * 128
    keep, send = call(
        weight_grad_kernel, [((rows // 2, 128), F32), ((rows // 2, 128), BF16)], [((rows, 128), F32)],
        conv_flops, (inner, outer, edges, *gates, hidden, cot),
    )
    keep, gates = tied(keep, *gates)
    near, far = gates
    near_in = swap(near, "gz", 0)
    for level, (axis, bit) in enumerate((("gz", 2), ("gy", 2))):
        size = rows >> (level + 2)
        mine, got = keep, flip(send, *(("gy", 1), ("gz", 2))[level])
        keep, send = call(
            functools.partial(halve_kernel, axis=axis, bit=bit),
            [((size, 128), F32), ((size, 128), BF16)], [((2 * size, 128), F32)], 0, (mine, got),
        )
        if level == 0:
            keep, (far, hidden) = tied(keep, far, hidden)
            far_in = swap(far, "gz", 1)
            (section_out,) = call(
                section_kernel, [((out_channels, cot.shape[1]), BF16)], [], conv_flops // 10,
                (hidden, down_weight),
            )
    shard = ((rows // 8, 128), BF16)
    (sums,) = call(add_kernel, [shard], [], 0, (keep, flip(send, "gy", 2)))
    (sums,) = call(add_kernel, [shard], [], 0, (sums, flip(sums, "gz", 1)))
    sums, outside = tied(sums, near_in, far_in)
    sends = call(edges_kernel, [edge, edge], [], 0, (*gates, *outside))
    beside = swapped(*sends, "gy")
    (acc,) = call(
        field_kernel, [(lines, F32)], [cols, cols], conv_flops, (*gates, *outside, weight_bwd)
    )
    wide = [("gy", 1 << k) for k in range(2, lax.axis_size("gy").bit_length() - 1)]
    wide += [("gz", 1 << k) for k in range(2, lax.axis_size("gz").bit_length() - 1)]
    for axis, bit in wide:
        (sums,) = call(add_kernel, [shard], [], 0, (sums, flip(sums, axis, bit)))
    sums, (section_out,) = tied(sums, section_out)
    (sums,) = call(
        functools.partial(join_kernel, axis="gy", bit=2), [((rows // 4, 128), BF16)], [], 0,
        (sums, flip(sums, "gy", 2)),
    )
    sums, (acc, *beside) = tied(sums, acc, *beside)
    (field,) = call(
        field_edges_kernel, [((channels * plane_count * row_count, breadth), F32)], [edge_cols],
        conv_flops // 10, (*beside, acc, weight_bwd),
    )
    (sums,) = call(
        functools.partial(join_kernel, axis="gz", bit=2), [((rows // 2, 128), BF16)], [], 0,
        (sums, flip(sums, "gz", 2)),
    )
    sums, (field,) = tied(sums, field)
    grad_conv, grad_down = call(
        functools.partial(unpack_kernel, scale=grad_scale),
        [(conv_weight.shape, F32), (down_weight.shape, F32)], [((rows, 128), BF16)], 0,
        (sums, flip(sums, "gy", 1)),
    )
    section_out = section_out.reshape(out_channels, plane_count // 2, -1)
    return (section_out, field.reshape(features.shape), grad_conv, grad_down)


def solution(mesh):
    return jax.shard_map(
        body,
        mesh=mesh,
        in_specs=(P(None, "gz", "gy", None), P(), P(), P(None, "gz", "gy")),
        out_specs=(P(None, "gz", "gy"), P(None, "gz", "gy", None), P(), P()),
        check_vma=False,
    )
```

```python
import functools
import math

import jax
import jax.numpy as jnp
from jax import lax
from jax.experimental import pallas as pl
from jax.experimental.pallas import tpu as pltpu
from jax.sharding import PartitionSpec as P

F32 = jnp.float32
BF16 = jnp.bfloat16
PARAMS = pltpu.CompilerParams(vmem_limit_bytes=24 * 1024 * 1024)


def call(kernel, outs, scratch, flops, operands):
    moved = sum(x.size * x.dtype.itemsize for x in operands)
    moved += sum(math.prod(s) * jnp.dtype(d).itemsize for s, d in outs)
    vmem = pl.BlockSpec(memory_space=pltpu.VMEM)
    return pl.pallas_call(
        kernel,
        out_shape=[jax.ShapeDtypeStruct(s, d) for s, d in outs],
        in_specs=[vmem] * len(operands),
        out_specs=[vmem] * len(outs),
        scratch_shapes=[pltpu.VMEM(s, d) for s, d in scratch],
        compiler_params=PARAMS,
        cost_estimate=pl.CostEstimate(flops=flops, bytes_accessed=moved, transcendentals=0),
    )(*operands)


def is_even(axis):
    return lax.rem(lax.axis_index(axis), 2) == 0


def choose(cond, yes, no):
    return jnp.where(jnp.broadcast_to(cond, yes.shape), yes, no)


def lines_kernel(f_ref, near_ref, far_ref, wide):
    channels, planes, rows, breadth = f_ref.shape
    wide[...] = f_ref[...].astype(F32).reshape(channels * planes * rows, breadth)
    even = is_even("gz")
    for y in range(rows):
        low, high = (
            wide[pl.ds(z * rows + y, channels, stride=planes * rows), :].astype(BF16) for z in range(2)
        )
        near_ref[y] = choose(even, high, low)
        far_ref[y] = choose(even, low, high)


def edges_kernel(near, far, near_in, far_in, near_ref, far_ref):
    rows = near.shape[0]
    even_z, even_y = is_even("gz"), is_even("gy")

    def put(p, one, other):
        first = choose(even_z, one[0], other[0])
        last = choose(even_z, one[rows - 1], other[rows - 1])
        near_ref[p] = choose(even_y, last, first)
        far_ref[p] = choose(even_y, first, last)

    put(0, far_in, near_in)
    put(1, far, near)
    put(2, near, far)
    put(3, near_in, far_in)


def put_columns(cols, p, q, line):
    channels = line.shape[0]
    wide = line.astype(F32)
    cols[p, q, 0:channels] = pltpu.roll(wide, 1, 1).astype(BF16)
    cols[p, q, channels : 2 * channels] = line
    cols[p, q, 2 * channels : 3 * channels] = pltpu.roll(wide, line.shape[1] - 1, 1).astype(BF16)


def fill_columns(cols, near, far):
    rows = near.shape[0]
    even = is_even("gz")

    def step(y, carry):
        put_columns(cols, 0, y + 1, choose(even, far[y], near[y]))
        put_columns(cols, 1, y + 1, choose(even, near[y], far[y]))
        return carry

    lax.fori_loop(0, rows, step, 0, unroll=2)
    for p in range(2):
        for q in (0, rows + 1):
            cols[p, q] = jnp.zeros(cols.shape[2:], BF16)


def fill_edges(cols, near, far):
    even = is_even("gy")
    for p in range(4):
        put_columns(cols, p, 0, choose(even, far[p], near[p]))
        put_columns(cols, p, 1, choose(even, near[p], far[p]))


def dot(lhs, rhs):
    return jnp.dot(lhs, rhs, preferred_element_type=F32)


def taps(w_ref, b, first, last):
    return jnp.concatenate([w_ref[a, b] for a in range(first, last)], axis=0)


def window(cols, p, q):
    return jnp.concatenate([cols[p, q], cols[p, q + 1]], axis=1)


def inner_terms(cols, w_ref, y):
    acc = None
    for b in range(3):
        for p in range(2):
            term = dot(taps(w_ref, b, p, p + 2), window(cols, p, y + b))
            acc = term if acc is None else acc + term
    half = acc.shape[0] // 2
    return acc[half:], acc[:half]


def outer_terms(cols, w_ref, y):
    lower = upper = None
    for b in range(3):
        low, high = dot(w_ref[0, b], window(cols, 0, y + b)), dot(w_ref[2, b], window(cols, 1, y + b))
        lower = low if lower is None else lower + low
        upper = high if upper is None else upper + high
    return lower, upper


def edge_terms(edges, w_ref, side):
    b = 2 * side
    half = w_ref.shape[2]
    acc = dot(taps(w_ref, b, 0, 2), edges[1, side]) + dot(taps(w_ref, b, 1, 3), edges[2, side])
    return acc[half:] + dot(w_ref[0, b], edges[0, side]), acc[:half] + dot(w_ref[2, b], edges[3, side])


def inner_kernel(near, far, w_ref, d_ref, cot_ref, cols, acc_ref, grad_ref, up):
    rows, channels, breadth = near.shape
    fill_columns(cols, near, far)
    source = lax.broadcasted_iota(jnp.int32, (breadth, 2 * breadth), 0)
    target = lax.broadcasted_iota(jnp.int32, (breadth, 2 * breadth), 1)
    spread = jnp.where(source == target // 2, 1.0, 0.0).astype(BF16)
    for pair in range(rows // 4):
        both = dot(cot_ref[:, pair * breadth : (pair + 1) * breadth], spread)
        up[:, 2 * pair * breadth : 2 * (pair + 1) * breadth] = both.astype(BF16)
    even = lax.broadcasted_iota(jnp.int32, (channels, breadth), 1) % 2 == 0
    for a in range(2):
        for b in range(2):
            terms = lax.dot_general(d_ref[a, b], up[...], (((0,), (0,)), ((), ())), preferred_element_type=F32)
            for t in range(rows // 2):
                part = terms[:, t * breadth : (t + 1) * breadth]
                grad_ref[a, 2 * t + b] = jnp.where(even, part[0:channels], part[channels:])

    def step(t, carry):
        y = 2 * t
        for z, lines in enumerate(inner_terms(cols, w_ref, y)):
            for b in range(2):
                acc_ref[z, y + b] = lines[:, b * breadth : (b + 1) * breadth]
        return carry

    lax.fori_loop(0, rows // 2, step, 0)


def gated(preact, grad):
    sig = 1.0 / (1.0 + jnp.exp(-preact))
    return (preact * sig).astype(BF16), (grad * sig * (1.0 + preact * (1.0 - sig))).astype(BF16)


def outer_kernel(near, far, w_ref, acc_ref, grad_ref, cols, side_ref, near_ref, far_ref, h_ref):
    rows, channels, breadth = near.shape
    fill_columns(cols, near, far)
    even = is_even("gz")
    for y in range(0, rows, 2):
        outer = outer_terms(cols, w_ref, y)
        for b in range(2):
            found = []
            for z in range(2):
                preact = acc_ref[z, y + b] + outer[z][:, b * breadth : (b + 1) * breadth]
                if y + b in (0, rows - 1):
                    side_ref[z, b] = preact
                else:
                    h_ref[z, y + b], gate = gated(preact, grad_ref[z, y + b])
                    found.append(gate)
            if len(found) > 0:
                near_ref[y + b] = choose(even, found[1], found[0])
                far_ref[y + b] = choose(even, found[0], found[1])


def gate_kernel(near, far, side_ref, near_in, far_in, h_in, grad_ref, w_ref, edges, near_ref, far_ref, h_ref):
    rows = near_in.shape[0]
    fill_edges(edges, near, far)
    even = is_even("gz")
    for side, y in enumerate((0, rows - 1)):
        terms = edge_terms(edges, w_ref, side)
        found = []
        for z in range(2):
            h_ref[z, y], gate = gated(side_ref[z, side] + terms[z], grad_ref[z, y])
            found.append(gate)
        near_ref[y] = choose(even, found[1], found[0])
        far_ref[y] = choose(even, found[0], found[1])
    for y in range(1, rows - 1):
        near_ref[y] = near_in[y]
        far_ref[y] = far_in[y]
        for z in range(2):
            h_ref[z, y] = h_in[z, y]


def coarse_hidden(h_ref):
    rows, channels, breadth = h_ref.shape[1:]
    source = lax.broadcasted_iota(jnp.int32, (2 * breadth, 2 * breadth), 0)
    target = lax.broadcasted_iota(jnp.int32, (2 * breadth, 2 * breadth), 1)
    wanted = 2 * (target % breadth) + target // breadth
    pick = jnp.where(source == wanted, 1.0, 0.0).astype(BF16)
    pairs = rows // 4
    both = [
        jnp.concatenate([h_ref[a, 4 * pair + b], h_ref[a, 4 * pair + 2 + b]], axis=1)
        for a in range(2) for b in range(2) for pair in range(pairs)
    ]
    picked = dot(jnp.concatenate(both, axis=0), pick).astype(BF16)
    blocks = []
    for tap in range(4):
        parts = [picked[(tap * pairs + pair) * channels : (tap * pairs + pair + 1) * channels] for pair in range(pairs)]
        for e in range(2):
            blocks.append(jnp.concatenate([x[:, e * breadth : (e + 1) * breadth] for x in parts], axis=1))
    return jnp.concatenate(blocks, axis=0)


def section_kernel(h_ref, d_ref, out_ref):
    down = jnp.concatenate([d_ref[a, b] for a in range(2) for b in range(2)], axis=1)
    out_ref[...] = dot(down, coarse_hidden(h_ref)).astype(BF16)


def weight_grad_kernel(inner, outer, edges, near, far, h_ref, cot_ref, keep, send, packed):
    rows, channels, breadth = near.shape
    across = (((1,), (1,)), ((), ()))
    even = is_even("gz")
    low = [choose(even, far[y], near[y]) for y in range(rows)]
    high = [choose(even, near[y], far[y]) for y in range(rows)]
    nothing = jnp.zeros((channels, breadth), BF16)

    def shifted(lines):
        return jnp.concatenate(
            [jnp.concatenate([nothing] * b + lines + [nothing] * (2 - b), axis=1) for b in range(3)], axis=0
        )

    low, high = shifted(low), shifted(high)
    both = jnp.concatenate([low, high], axis=0)

    def columns(p, q):
        if q in (0, rows + 1):
            return edges[p, 0 if q == 0 else 1]
        return inner[p - 1, q] if p in (1, 2) else outer[p // 3, q]

    parts = []
    for p in range(4):
        lines = jnp.concatenate([columns(p, q) for q in range(rows + 2)], axis=1)
        lhs = low if p == 0 else high if p == 3 else both
        parts.append(lax.dot_general(lhs, lines, across, preferred_element_type=F32))
    lane = lax.broadcasted_iota(jnp.int32, (channels // 2, breadth), 1)
    for a in range(3):
        for b in range(3):
            at = b * channels + (0 if a == 2 else 3 * channels)
            total = parts[a][b * channels : (b + 1) * channels] + parts[a + 1][at : at + channels]
            base = (a * 3 + b) * 3 * channels // 2
            packed[base : base + channels] = total[:, 0:breadth]
            rest = jnp.concatenate([total[:, breadth:], total[:, breadth:]], axis=1)
            mix = jnp.where(lane < channels, rest[0 : channels // 2], rest[channels // 2 :])
            packed[base + channels : base + 3 * channels // 2] = mix
    base = 9 * 3 * channels // 2
    height = cot_ref.shape[0]
    down = lax.dot_general(cot_ref[...], coarse_hidden(h_ref), across, preferred_element_type=F32)
    for tap in range(4):
        packed[base + tap * height : base + (tap + 1) * height] = down[:, tap * breadth : (tap + 1) * breadth]
    end = base + 4 * height
    if end < packed.shape[0]:
        packed[end:] = jnp.zeros((packed.shape[0] - end, packed.shape[1]), F32)
    split(packed, keep, send, owned_half())


def side_of(axis, bit):
    return lax.rem(lax.axis_index(axis) // bit, 2)


def owned_half():
    total = 0
    for axis in ("gz", "gy"):
        for k in range(lax.axis_size(axis).bit_length() - 1):
            total = total + side_of(axis, 1 << k)
    return lax.rem(total, 2)


def part(side, rows):
    return pl.ds(pl.multiple_of(side * rows, 16), rows)


def split(packed, keep, send, side):
    half = keep.shape[0]
    keep[...] = packed[part(side, half)]
    send[...] = packed[part(1 - side, half)].astype(BF16)


def halve_kernel(mine, other, keep, send, total, *, axis, bit):
    total[...] = mine[...] + other[...].astype(F32)
    split(total, keep, send, side_of(axis, bit))


def add_kernel(x, y, out):
    out[...] = (x[...].astype(F32) + y[...].astype(F32)).astype(BF16)


def join_kernel(mine, other, out, *, axis, bit):
    join(mine, other, out, side_of(axis, bit))


def join(mine, other, out, side):
    rows = mine.shape[0]
    out[part(side, rows)] = mine[...]
    out[part(1 - side, rows)] = other[...]


def field_kernel(near, far, near_in, far_in, w_ref, acc_ref, inner, outer):
    rows, channels, breadth = near.shape
    fill_columns(inner, near, far)
    fill_columns(outer, near_in, far_in)

    def step(t, carry):
        y = 2 * t
        own = inner_terms(inner, w_ref, y)
        rest = outer_terms(outer, w_ref, y)
        for z in range(2):
            total = own[z] + rest[z]
            for b in range(2):
                acc_ref[z, y + b] = total[:, b * breadth : (b + 1) * breadth]
        return carry

    lax.fori_loop(0, rows // 2, step, 0)


def field_edges_kernel(near, far, acc_ref, w_ref, out_ref, edges):
    rows, channels, breadth = acc_ref.shape[1:]
    fill_edges(edges, near, far)
    sides = [edge_terms(edges, w_ref, side) for side in range(2)]
    for z in range(2):
        for y in range(rows):
            line = acc_ref[z, y]
            if y in (0, rows - 1):
                line = line + sides[0 if y == 0 else 1][z]
            out_ref[pl.ds(z * rows + y, channels, stride=2 * rows), :] = line


def unpack_kernel(mine, other, conv_ref, down_ref, sums_ref, *, scale):
    join(mine, other, sums_ref, owned_half())
    channels = conv_ref.shape[2]
    for a in range(3):
        for b in range(3):
            base = (a * 3 + b) * 3 * channels // 2
            conv_ref[a, b, :, 0 : 2 * channels] = sums_ref[base : base + channels].astype(F32) * scale
            rest = sums_ref[base + channels : base + 3 * channels // 2].astype(F32) * scale
            conv_ref[a, b, 0 : channels // 2, 2 * channels :] = rest[:, 0:channels]
            conv_ref[a, b, channels // 2 :, 2 * channels :] = rest[:, channels:]
    base = 9 * 3 * channels // 2
    height = down_ref.shape[2]
    for a in range(2):
        for b in range(2):
            at = base + (2 * a + b) * height
            down_ref[a, b] = sums_ref[at : at + height].astype(F32) * scale


def swap(cells, axis, low):
    count = lax.axis_size(axis)
    pairs = [(i % count, (i + 1) % count) for i in range(low, low + count, 2)]
    return lax.ppermute(cells, axis, pairs + [(b, a) for a, b in pairs])


def flip(cells, axis, bit):
    row = lax.axis_size("gy")
    mask = bit * row | 1 if axis == "gz" else bit | 1
    return lax.ppermute(cells, ("gz", "gy"), [(i, i ^ mask) for i in range(lax.axis_size("gz") * row)])


def tied(first, *others):
    found = lax.optimization_barrier((first, *others))
    return found[0], tuple(found[1:])


def swapped(near, far, axis):
    return swap(near, axis, 0), swap(far, axis, 1)


def body(features, conv_weight, down_weight, cotangent):
    channels, plane_count, row_count, breadth = features.shape
    out_channels = down_weight.shape[2]
    count = lax.axis_size("gz") * lax.axis_size("gy")
    grad_scale = 1.0 / math.sqrt(plane_count * row_count * breadth * count)
    turned = conv_weight.reshape(3, 3, channels, 3, channels)[::-1, ::-1, :, ::-1]
    weight_bwd = turned.transpose(0, 1, 4, 3, 2).reshape(3, 3, channels, 3 * channels)
    cot = cotangent.reshape(out_channels, -1)
    plane = ((row_count, channels, breadth), BF16)
    edge = ((plane_count + 2, channels, breadth), BF16)
    cols = ((plane_count, row_count + 2, 3 * channels, breadth), BF16)
    edge_cols = ((plane_count + 2, 2, 3 * channels, breadth), BF16)
    lines = (plane_count, row_count, channels, breadth)
    conv_flops = 2 * 27 * channels * channels * plane_count * row_count * breadth

    own = call(
        lines_kernel, [plane, plane], [((channels * plane_count * row_count, breadth), F32)], 0, (features,)
    )
    outside = swapped(*own, "gz")
    inner, acc, hidden_grad = call(
        inner_kernel, [cols, (lines, F32), (lines, F32)],
        [((out_channels, row_count // 2 * breadth), BF16)],
        2 * conv_flops // 3, (*own, conv_weight, down_weight, cot),
    )
    near, far, acc = lax.optimization_barrier((*outside, acc))
    outside = (near, far)
    beside = swapped(*call(edges_kernel, [edge, edge], [], 0, (*own, *outside)), "gy")
    outer, *inside = call(
        outer_kernel, [cols, ((plane_count, 2, channels, breadth), F32), plane, plane, (lines, BF16)], [],
        conv_flops // 3, (*outside, conv_weight, acc, hidden_grad),
    )
    edges, near, far, hidden = call(
        gate_kernel, [edge_cols, plane, plane, (lines, BF16)], [], conv_flops // 10,
        (*beside, *inside, hidden_grad, conv_weight),
    )
    gates = (near, far)

    used = 27 * channels * channels // 128 + 4 * out_channels
    rows = -(-used // 128) * 128
    keep, send = call(
        weight_grad_kernel, [((rows // 2, 128), F32), ((rows // 2, 128), BF16)], [((rows, 128), F32)],
        conv_flops, (inner, outer, edges, *gates, hidden, cot),
    )
    keep, gates = tied(keep, *gates)
    near, far = gates
    near_in = swap(near, "gz", 0)
    for level, (axis, bit) in enumerate((("gz", 2), ("gy", 2))):
        size = rows >> (level + 2)
        mine, got = keep, flip(send, *(("gy", 1), ("gz", 2))[level])
        keep, send = call(
            functools.partial(halve_kernel, axis=axis, bit=bit),
            [((size, 128), F32), ((size, 128), BF16)], [((2 * size, 128), F32)], 0, (mine, got),
        )
        if level == 0:
            keep, (far, hidden) = tied(keep, far, hidden)
            far_in = swap(far, "gz", 1)
            (section_out,) = call(
                section_kernel, [((out_channels, cot.shape[1]), BF16)], [], conv_flops // 10,
                (hidden, down_weight),
            )
    shard = ((rows // 8, 128), BF16)
    (sums,) = call(add_kernel, [shard], [], 0, (keep, flip(send, "gy", 2)))
    (sums,) = call(add_kernel, [shard], [], 0, (sums, flip(sums, "gz", 1)))
    sums, outside = tied(sums, near_in, far_in)
    sends = call(edges_kernel, [edge, edge], [], 0, (*gates, *outside))
    beside = swapped(*sends, "gy")
    (acc,) = call(
        field_kernel, [(lines, F32)], [cols, cols], conv_flops, (*gates, *outside, weight_bwd)
    )
    wide = [("gy", 1 << k) for k in range(2, lax.axis_size("gy").bit_length() - 1)]
    wide += [("gz", 1 << k) for k in range(2, lax.axis_size("gz").bit_length() - 1)]
    for axis, bit in wide:
        (sums,) = call(add_kernel, [shard], [], 0, (sums, flip(sums, axis, bit)))
    sums, (section_out,) = tied(sums, section_out)
    (sums,) = call(
        functools.partial(join_kernel, axis="gy", bit=2), [((rows // 4, 128), BF16)], [], 0,
        (sums, flip(sums, "gy", 2)),
    )
    sums, (acc, *beside) = tied(sums, acc, *beside)
    (field,) = call(
        field_edges_kernel, [((channels * plane_count * row_count, breadth), F32)], [edge_cols],
        conv_flops // 10, (*beside, acc, weight_bwd),
    )
    (sums,) = call(
        functools.partial(join_kernel, axis="gz", bit=2), [((rows // 2, 128), BF16)], [], 0,
        (sums, flip(sums, "gz", 2)),
    )
    sums, (field,) = tied(sums, field)
    grad_conv, grad_down = call(
        functools.partial(unpack_kernel, scale=grad_scale),
        [(conv_weight.shape, F32), (down_weight.shape, F32)], [((rows, 128), BF16)], 0,
        (sums, flip(sums, "gy", 1)),
    )
    section_out = section_out.reshape(out_channels, plane_count // 2, -1)
    return (section_out, field.reshape(features.shape), grad_conv, grad_down)


def solution(mesh):
    return jax.shard_map(
        body,
        mesh=mesh,
        in_specs=(P(None, "gz", "gy", None), P(), P(), P(None, "gz", "gy")),
        out_specs=(P(None, "gz", "gy"), P(None, "gz", "gy", None), P(), P()),
        check_vma=False,
    )
```

```python
import functools
import math

import jax
import jax.numpy as jnp
from jax import lax
from jax.experimental import pallas as pl
from jax.experimental.pallas import tpu as pltpu
from jax.sharding import PartitionSpec as P

F32 = jnp.float32
BF16 = jnp.bfloat16
PARAMS = pltpu.CompilerParams(vmem_limit_bytes=24 * 1024 * 1024)


def call(kernel, outs, scratch, flops, operands):
    moved = sum(x.size * x.dtype.itemsize for x in operands)
    moved += sum(math.prod(s) * jnp.dtype(d).itemsize for s, d in outs)
    vmem = pl.BlockSpec(memory_space=pltpu.VMEM)
    return pl.pallas_call(
        kernel,
        out_shape=[jax.ShapeDtypeStruct(s, d) for s, d in outs],
        in_specs=[vmem] * len(operands),
        out_specs=[vmem] * len(outs),
        scratch_shapes=[pltpu.VMEM(s, d) for s, d in scratch],
        compiler_params=PARAMS,
        cost_estimate=pl.CostEstimate(flops=flops, bytes_accessed=moved, transcendentals=0),
    )(*operands)


def is_even(axis):
    return lax.rem(lax.axis_index(axis), 2) == 0


def choose(cond, yes, no):
    return jnp.where(jnp.broadcast_to(cond, yes.shape), yes, no)


def lines_kernel(f_ref, near_ref, far_ref, near_row, far_row, wide):
    channels, planes, rows, breadth = f_ref.shape
    wide[...] = f_ref[...].astype(F32).reshape(channels * planes * rows, breadth)
    even = is_even("gz")
    ends = {}
    for y in range(rows):
        low, high = ends[y] = [
            wide[pl.ds(z * rows + y, channels, stride=planes * rows), :].astype(BF16) for z in range(2)
        ]
        near_ref[y] = choose(even, high, low)
        far_ref[y] = choose(even, low, high)
    even_y = is_even("gy")
    for z in range(2):
        near_row[z] = choose(even_y, ends[rows - 1][z], ends[0][z])
        far_row[z] = choose(even_y, ends[0][z], ends[rows - 1][z])


def outer_rows_kernel(near_in, far_in, near_ref, far_ref):
    rows = near_in.shape[0]
    even_z, even_y = is_even("gz"), is_even("gy")
    for p, (one, other) in enumerate(((far_in, near_in), (near_in, far_in))):
        first = choose(even_z, one[0], other[0])
        last = choose(even_z, one[rows - 1], other[rows - 1])
        near_ref[p] = choose(even_y, last, first)
        far_ref[p] = choose(even_y, first, last)


def edges_kernel(near, far, near_in, far_in, near_ref, far_ref):
    rows = near.shape[0]
    even_z, even_y = is_even("gz"), is_even("gy")

    def put(p, one, other):
        first = choose(even_z, one[0], other[0])
        last = choose(even_z, one[rows - 1], other[rows - 1])
        near_ref[p] = choose(even_y, last, first)
        far_ref[p] = choose(even_y, first, last)

    put(0, far_in, near_in)
    put(1, far, near)
    put(2, near, far)
    put(3, near_in, far_in)


def put_columns(cols, p, q, line):
    channels = line.shape[0]
    wide = line.astype(F32)
    cols[p, q, 0:channels] = pltpu.roll(wide, 1, 1).astype(BF16)
    cols[p, q, channels : 2 * channels] = line
    cols[p, q, 2 * channels : 3 * channels] = pltpu.roll(wide, line.shape[1] - 1, 1).astype(BF16)


def fill_columns(cols, near, far, near_row=None, far_row=None):
    rows = near.shape[0]
    even = is_even("gz")

    def step(y, carry):
        put_columns(cols, 0, y + 1, choose(even, far[y], near[y]))
        put_columns(cols, 1, y + 1, choose(even, near[y], far[y]))
        return carry

    lax.fori_loop(0, rows, step, 0, unroll=2)
    if near_row is not None:
        fill_rows(cols, near_row, far_row, 0, rows + 1)
        return
    for p in range(2):
        for q in (0, rows + 1):
            cols[p, q] = jnp.zeros(cols.shape[2:], BF16)


def fill_rows(cols, near, far, below, above):
    even = is_even("gy")
    for p in range(near.shape[0]):
        put_columns(cols, p, below, choose(even, far[p], near[p]))
        put_columns(cols, p, above, choose(even, near[p], far[p]))


def dot(lhs, rhs):
    return jnp.dot(lhs, rhs, preferred_element_type=F32)


def taps(w_ref, b, first, last):
    return jnp.concatenate([w_ref[a, b] for a in range(first, last)], axis=0)


def window(cols, p, q):
    return jnp.concatenate([cols[p, q], cols[p, q + 1]], axis=1)


def inner_terms(cols, w_ref, y):
    acc = None
    for b in range(3):
        for p in range(2):
            term = dot(taps(w_ref, b, p, p + 2), window(cols, p, y + b))
            acc = term if acc is None else acc + term
    half = acc.shape[0] // 2
    return acc[half:], acc[:half]


def outer_terms(cols, w_ref, y):
    lower = upper = None
    for b in range(3):
        low, high = dot(w_ref[0, b], window(cols, 0, y + b)), dot(w_ref[2, b], window(cols, 1, y + b))
        lower = low if lower is None else lower + low
        upper = high if upper is None else upper + high
    return lower, upper


def edge_terms(edges, w_ref, side):
    b = 2 * side
    half = w_ref.shape[2]
    acc = dot(taps(w_ref, b, 0, 2), edges[1, side]) + dot(taps(w_ref, b, 1, 3), edges[2, side])
    return acc[half:] + dot(w_ref[0, b], edges[0, side]), acc[:half] + dot(w_ref[2, b], edges[3, side])


def inner_kernel(near, far, near_row, far_row, w_ref, d_ref, cot_ref, cols, acc_ref, grad_ref, up):
    rows, channels, breadth = near.shape
    fill_columns(cols, near, far, near_row, far_row)
    source = lax.broadcasted_iota(jnp.int32, (breadth, 2 * breadth), 0)
    target = lax.broadcasted_iota(jnp.int32, (breadth, 2 * breadth), 1)
    spread = jnp.where(source == target // 2, 1.0, 0.0).astype(BF16)
    for pair in range(rows // 4):
        both = dot(cot_ref[:, pair * breadth : (pair + 1) * breadth], spread)
        up[:, 2 * pair * breadth : 2 * (pair + 1) * breadth] = both.astype(BF16)
    even = lax.broadcasted_iota(jnp.int32, (channels, breadth), 1) % 2 == 0
    for a in range(2):
        for b in range(2):
            terms = lax.dot_general(d_ref[a, b], up[...], (((0,), (0,)), ((), ())), preferred_element_type=F32)
            for t in range(rows // 2):
                part = terms[:, t * breadth : (t + 1) * breadth]
                grad_ref[a, 2 * t + b] = jnp.where(even, part[0:channels], part[channels:])

    def step(t, carry):
        y = 2 * t
        for z, lines in enumerate(inner_terms(cols, w_ref, y)):
            for b in range(2):
                acc_ref[z, y + b] = lines[:, b * breadth : (b + 1) * breadth]
        return carry

    lax.fori_loop(0, rows // 2, step, 0)


def gated(preact, grad):
    sig = 1.0 / (1.0 + jnp.exp(-preact))
    return (preact * sig).astype(BF16), (grad * sig * (1.0 + preact * (1.0 - sig))).astype(BF16)


def outer_kernel(near, far, w_ref, acc_ref, grad_ref, cols, side_ref, near_ref, far_ref, h_ref):
    rows, channels, breadth = near.shape
    fill_columns(cols, near, far)
    even = is_even("gz")
    for y in range(0, rows, 2):
        outer = outer_terms(cols, w_ref, y)
        for b in range(2):
            found = []
            for z in range(2):
                preact = acc_ref[z, y + b] + outer[z][:, b * breadth : (b + 1) * breadth]
                if y + b in (0, rows - 1):
                    side_ref[z, b] = preact
                else:
                    h_ref[z, y + b], gate = gated(preact, grad_ref[z, y + b])
                    found.append(gate)
            if len(found) > 0:
                near_ref[y + b] = choose(even, found[1], found[0])
                far_ref[y + b] = choose(even, found[0], found[1])


def gate_kernel(near, far, side_ref, near_in, far_in, h_in, grad_ref, w_ref, edges, near_ref, far_ref, h_ref):
    rows = near_in.shape[0]
    fill_rows(edges, near, far, 0, 1)
    even = is_even("gz")
    for side, y in enumerate((0, rows - 1)):
        terms = [dot(w_ref[2 * z, 2 * side], edges[z, side]) for z in range(2)]
        found = []
        for z in range(2):
            h_ref[z, y], gate = gated(side_ref[z, side] + terms[z], grad_ref[z, y])
            found.append(gate)
        near_ref[y] = choose(even, found[1], found[0])
        far_ref[y] = choose(even, found[0], found[1])
    for y in range(1, rows - 1):
        near_ref[y] = near_in[y]
        far_ref[y] = far_in[y]
        for z in range(2):
            h_ref[z, y] = h_in[z, y]


def coarse_hidden(h_ref):
    rows, channels, breadth = h_ref.shape[1:]
    source = lax.broadcasted_iota(jnp.int32, (2 * breadth, 2 * breadth), 0)
    target = lax.broadcasted_iota(jnp.int32, (2 * breadth, 2 * breadth), 1)
    wanted = 2 * (target % breadth) + target // breadth
    pick = jnp.where(source == wanted, 1.0, 0.0).astype(BF16)
    pairs = rows // 4
    both = [
        jnp.concatenate([h_ref[a, 4 * pair + b], h_ref[a, 4 * pair + 2 + b]], axis=1)
        for a in range(2) for b in range(2) for pair in range(pairs)
    ]
    picked = dot(jnp.concatenate(both, axis=0), pick).astype(BF16)
    blocks = []
    for tap in range(4):
        parts = [picked[(tap * pairs + pair) * channels : (tap * pairs + pair + 1) * channels] for pair in range(pairs)]
        for e in range(2):
            blocks.append(jnp.concatenate([x[:, e * breadth : (e + 1) * breadth] for x in parts], axis=1))
    return jnp.concatenate(blocks, axis=0)


def section_kernel(h_ref, d_ref, out_ref):
    down = jnp.concatenate([d_ref[a, b] for a in range(2) for b in range(2)], axis=1)
    out_ref[...] = dot(down, coarse_hidden(h_ref)).astype(BF16)


def weight_grad_kernel(inner, outer, edges, near, far, h_ref, cot_ref, keep, send, packed):
    rows, channels, breadth = near.shape
    across = (((1,), (1,)), ((), ()))
    even = is_even("gz")
    low = [choose(even, far[y], near[y]) for y in range(rows)]
    high = [choose(even, near[y], far[y]) for y in range(rows)]
    nothing = jnp.zeros((channels, breadth), BF16)

    def shifted(lines):
        return jnp.concatenate(
            [jnp.concatenate([nothing] * b + lines + [nothing] * (2 - b), axis=1) for b in range(3)], axis=0
        )

    low, high = shifted(low), shifted(high)
    both = jnp.concatenate([low, high], axis=0)

    def columns(p, q):
        if p in (1, 2):
            return inner[p - 1, q]
        return edges[p // 3, q // (rows + 1)] if q in (0, rows + 1) else outer[p // 3, q]

    parts = []
    for p in range(4):
        lines = jnp.concatenate([columns(p, q) for q in range(rows + 2)], axis=1)
        lhs = low if p == 0 else high if p == 3 else both
        parts.append(lax.dot_general(lhs, lines, across, preferred_element_type=F32))
    lane = lax.broadcasted_iota(jnp.int32, (channels // 2, breadth), 1)
    for a in range(3):
        for b in range(3):
            at = b * channels + (0 if a == 2 else 3 * channels)
            total = parts[a][b * channels : (b + 1) * channels] + parts[a + 1][at : at + channels]
            base = (a * 3 + b) * 3 * channels // 2
            packed[base : base + channels] = total[:, 0:breadth]
            rest = jnp.concatenate([total[:, breadth:], total[:, breadth:]], axis=1)
            mix = jnp.where(lane < channels, rest[0 : channels // 2], rest[channels // 2 :])
            packed[base + channels : base + 3 * channels // 2] = mix
    base = 9 * 3 * channels // 2
    height = cot_ref.shape[0]
    down = lax.dot_general(cot_ref[...], coarse_hidden(h_ref), across, preferred_element_type=F32)
    for tap in range(4):
        packed[base + tap * height : base + (tap + 1) * height] = down[:, tap * breadth : (tap + 1) * breadth]
    end = base + 4 * height
    if end < packed.shape[0]:
        packed[end:] = jnp.zeros((packed.shape[0] - end, packed.shape[1]), F32)
    split(packed, keep, send, owned_half())


def side_of(axis, bit):
    return lax.rem(lax.axis_index(axis) // bit, 2)


def owned_half():
    total = 0
    for axis in ("gz", "gy"):
        for k in range(lax.axis_size(axis).bit_length() - 1):
            total = total + side_of(axis, 1 << k)
    return lax.rem(total, 2)


def part(side, rows):
    return pl.ds(pl.multiple_of(side * rows, 16), rows)


def split(packed, keep, send, side):
    half = keep.shape[0]
    keep[...] = packed[part(side, half)]
    send[...] = packed[part(1 - side, half)].astype(BF16)


def halve_kernel(mine, other, keep, send, total, *, axis, bit):
    total[...] = mine[...] + other[...].astype(F32)
    split(total, keep, send, side_of(axis, bit))


def add_kernel(x, y, out):
    out[...] = (x[...].astype(F32) + y[...].astype(F32)).astype(BF16)


def join_kernel(mine, other, out, *, axis, bit):
    join(mine, other, out, side_of(axis, bit))


def join(mine, other, out, side):
    rows = mine.shape[0]
    out[part(side, rows)] = mine[...]
    out[part(1 - side, rows)] = other[...]


def field_kernel(near, far, near_in, far_in, w_ref, acc_ref, inner, outer):
    rows, channels, breadth = near.shape
    fill_columns(inner, near, far)
    fill_columns(outer, near_in, far_in)

    def step(t, carry):
        y = 2 * t
        own = inner_terms(inner, w_ref, y)
        rest = outer_terms(outer, w_ref, y)
        for z in range(2):
            total = own[z] + rest[z]
            for b in range(2):
                acc_ref[z, y + b] = total[:, b * breadth : (b + 1) * breadth]
        return carry

    lax.fori_loop(0, rows // 2, step, 0)


def field_edges_kernel(near, far, acc_ref, w_ref, out_ref, edges):
    rows, channels, breadth = acc_ref.shape[1:]
    fill_rows(edges, near, far, 0, 1)
    sides = [edge_terms(edges, w_ref, side) for side in range(2)]
    for z in range(2):
        for y in range(rows):
            line = acc_ref[z, y]
            if y in (0, rows - 1):
                line = line + sides[0 if y == 0 else 1][z]
            out_ref[pl.ds(z * rows + y, channels, stride=2 * rows), :] = line


def unpack_kernel(mine, other, conv_ref, down_ref, sums_ref, *, scale):
    join(mine, other, sums_ref, owned_half())
    channels = conv_ref.shape[2]
    for a in range(3):
        for b in range(3):
            base = (a * 3 + b) * 3 * channels // 2
            conv_ref[a, b, :, 0 : 2 * channels] = sums_ref[base : base + channels].astype(F32) * scale
            rest = sums_ref[base + channels : base + 3 * channels // 2].astype(F32) * scale
            conv_ref[a, b, 0 : channels // 2, 2 * channels :] = rest[:, 0:channels]
            conv_ref[a, b, channels // 2 :, 2 * channels :] = rest[:, channels:]
    base = 9 * 3 * channels // 2
    height = down_ref.shape[2]
    for a in range(2):
        for b in range(2):
            at = base + (2 * a + b) * height
            down_ref[a, b] = sums_ref[at : at + height].astype(F32) * scale


def swap(cells, axis, low):
    count = lax.axis_size(axis)
    pairs = [(i % count, (i + 1) % count) for i in range(low, low + count, 2)]
    return lax.ppermute(cells, axis, pairs + [(b, a) for a, b in pairs])


def flip(cells, axis, bit):
    row = lax.axis_size("gy")
    mask = bit * row | 1 if axis == "gz" else bit | 1
    return lax.ppermute(cells, ("gz", "gy"), [(i, i ^ mask) for i in range(lax.axis_size("gz") * row)])


def tied(first, *others):
    found = lax.optimization_barrier((first, *others))
    return found[0], tuple(found[1:])


def swapped(near, far, axis):
    return swap(near, axis, 0), swap(far, axis, 1)


def body(features, conv_weight, down_weight, cotangent):
    channels, plane_count, row_count, breadth = features.shape
    out_channels = down_weight.shape[2]
    count = lax.axis_size("gz") * lax.axis_size("gy")
    grad_scale = 1.0 / math.sqrt(plane_count * row_count * breadth * count)
    turned = conv_weight.reshape(3, 3, channels, 3, channels)[::-1, ::-1, :, ::-1]
    weight_bwd = turned.transpose(0, 1, 4, 3, 2).reshape(3, 3, channels, 3 * channels)
    cot = cotangent.reshape(out_channels, -1)
    plane = ((row_count, channels, breadth), BF16)
    edge = ((plane_count + 2, channels, breadth), BF16)
    cols = ((plane_count, row_count + 2, 3 * channels, breadth), BF16)
    edge_cols = ((plane_count + 2, 2, 3 * channels, breadth), BF16)
    lines = (plane_count, row_count, channels, breadth)
    conv_flops = 2 * 27 * channels * channels * plane_count * row_count * breadth

    pair = ((plane_count, channels, breadth), BF16)
    *own, near_row, far_row = call(
        lines_kernel, [plane, plane, pair, pair],
        [((channels * plane_count * row_count, breadth), F32)], 0, (features,),
    )
    outside = swapped(*own, "gz")
    beside = swapped(near_row, far_row, "gy")
    inner, acc, hidden_grad = call(
        inner_kernel, [cols, (lines, F32), (lines, F32)],
        [((out_channels, row_count // 2 * breadth), BF16)],
        2 * conv_flops // 3, (*own, *beside, conv_weight, down_weight, cot),
    )
    near, far, acc = lax.optimization_barrier((*outside, acc))
    outside = (near, far)
    beside = swapped(*call(outer_rows_kernel, [pair, pair], [], 0, outside), "gy")
    outer, *inside = call(
        outer_kernel, [cols, ((plane_count, 2, channels, breadth), F32), plane, plane, (lines, BF16)], [],
        conv_flops // 3, (*outside, conv_weight, acc, hidden_grad),
    )
    edges, near, far, hidden = call(
        gate_kernel, [((plane_count, 2, 3 * channels, breadth), BF16), plane, plane, (lines, BF16)], [], conv_flops // 10,
        (*beside, *inside, hidden_grad, conv_weight),
    )
    gates = (near, far)

    used = 27 * channels * channels // 128 + 4 * out_channels
    rows = -(-used // 128) * 128
    keep, send = call(
        weight_grad_kernel, [((rows // 2, 128), F32), ((rows // 2, 128), BF16)], [((rows, 128), F32)],
        conv_flops, (inner, outer, edges, *gates, hidden, cot),
    )
    keep, gates = tied(keep, *gates)
    near, far = gates
    near_in = swap(near, "gz", 0)
    for level, (axis, bit) in enumerate((("gz", 2), ("gy", 2))):
        size = rows >> (level + 2)
        mine, got = keep, flip(send, *(("gy", 1), ("gz", 2))[level])
        keep, send = call(
            functools.partial(halve_kernel, axis=axis, bit=bit),
            [((size, 128), F32), ((size, 128), BF16)], [((2 * size, 128), F32)], 0, (mine, got),
        )
        if level == 0:
            keep, (far, hidden) = tied(keep, far, hidden)
            far_in = swap(far, "gz", 1)
            (section_out,) = call(
                section_kernel, [((out_channels, cot.shape[1]), BF16)], [], conv_flops // 10,
                (hidden, down_weight),
            )
    shard = ((rows // 8, 128), BF16)
    (sums,) = call(add_kernel, [shard], [], 0, (keep, flip(send, "gy", 2)))
    (sums,) = call(add_kernel, [shard], [], 0, (sums, flip(sums, "gz", 1)))
    sums, outside = tied(sums, near_in, far_in)
    sends = call(edges_kernel, [edge, edge], [], 0, (*gates, *outside))
    beside = swapped(*sends, "gy")
    (acc,) = call(
        field_kernel, [(lines, F32)], [cols, cols], conv_flops, (*gates, *outside, weight_bwd)
    )
    wide = [("gy", 1 << k) for k in range(2, lax.axis_size("gy").bit_length() - 1)]
    wide += [("gz", 1 << k) for k in range(2, lax.axis_size("gz").bit_length() - 1)]
    for axis, bit in wide:
        (sums,) = call(add_kernel, [shard], [], 0, (sums, flip(sums, axis, bit)))
    sums, (section_out,) = tied(sums, section_out)
    (sums,) = call(
        functools.partial(join_kernel, axis="gy", bit=2), [((rows // 4, 128), BF16)], [], 0,
        (sums, flip(sums, "gy", 2)),
    )
    sums, (acc, *beside) = tied(sums, acc, *beside)
    (field,) = call(
        field_edges_kernel, [((channels * plane_count * row_count, breadth), F32)], [edge_cols],
        conv_flops // 10, (*beside, acc, weight_bwd),
    )
    (sums,) = call(
        functools.partial(join_kernel, axis="gz", bit=2), [((rows // 2, 128), BF16)], [], 0,
        (sums, flip(sums, "gz", 2)),
    )
    sums, (field,) = tied(sums, field)
    grad_conv, grad_down = call(
        functools.partial(unpack_kernel, scale=grad_scale),
        [(conv_weight.shape, F32), (down_weight.shape, F32)], [((rows, 128), BF16)], 0,
        (sums, flip(sums, "gy", 1)),
    )
    section_out = section_out.reshape(out_channels, plane_count // 2, -1)
    return (section_out, field.reshape(features.shape), grad_conv, grad_down)


def solution(mesh):
    return jax.shard_map(
        body,
        mesh=mesh,
        in_specs=(P(None, "gz", "gy", None), P(), P(), P(None, "gz", "gy")),
        out_specs=(P(None, "gz", "gy"), P(None, "gz", "gy", None), P(), P()),
        check_vma=False,
    )
```

```python
import functools
import math

import jax
import jax.numpy as jnp
from jax import lax
from jax.experimental import pallas as pl
from jax.experimental.pallas import tpu as pltpu
from jax.sharding import PartitionSpec as P

F32 = jnp.float32
BF16 = jnp.bfloat16
PARAMS = pltpu.CompilerParams(vmem_limit_bytes=24 * 1024 * 1024)


def call(kernel, outs, scratch, flops, operands):
    moved = sum(x.size * x.dtype.itemsize for x in operands)
    moved += sum(math.prod(s) * jnp.dtype(d).itemsize for s, d in outs)
    vmem = pl.BlockSpec(memory_space=pltpu.VMEM)
    return pl.pallas_call(
        kernel,
        out_shape=[jax.ShapeDtypeStruct(s, d) for s, d in outs],
        in_specs=[vmem] * len(operands),
        out_specs=[vmem] * len(outs),
        scratch_shapes=[pltpu.VMEM(s, d) for s, d in scratch],
        compiler_params=PARAMS,
        cost_estimate=pl.CostEstimate(flops=flops, bytes_accessed=moved, transcendentals=0),
    )(*operands)


def is_even(axis):
    return lax.rem(lax.axis_index(axis), 2) == 0


def choose(cond, yes, no):
    return jnp.where(jnp.broadcast_to(cond, yes.shape), yes, no)


def lines_kernel(f_ref, near_ref, far_ref, wide):
    channels, planes, rows, breadth = f_ref.shape
    wide[...] = f_ref[...].astype(F32).reshape(channels * planes * rows, breadth)
    even = is_even("gz")
    for y in range(rows):
        low, high = (
            wide[pl.ds(z * rows + y, channels, stride=planes * rows), :].astype(BF16) for z in range(2)
        )
        near_ref[y] = choose(even, high, low)
        far_ref[y] = choose(even, low, high)


def edges_kernel(near, far, near_in, far_in, near_ref, far_ref):
    rows = near.shape[0]
    even_z, even_y = is_even("gz"), is_even("gy")

    def put(p, one, other):
        first = choose(even_z, one[0], other[0])
        last = choose(even_z, one[rows - 1], other[rows - 1])
        near_ref[p] = choose(even_y, last, first)
        far_ref[p] = choose(even_y, first, last)

    put(0, far_in, near_in)
    put(1, far, near)
    put(2, near, far)
    put(3, near_in, far_in)


def put_columns(cols, p, q, line):
    channels = line.shape[0]
    wide = line.astype(F32)
    cols[p, q, 0:channels] = pltpu.roll(wide, 1, 1).astype(BF16)
    cols[p, q, channels : 2 * channels] = line
    cols[p, q, 2 * channels : 3 * channels] = pltpu.roll(wide, line.shape[1] - 1, 1).astype(BF16)


def fill_columns(cols, near, far):
    rows = near.shape[0]
    even = is_even("gz")

    def step(y, carry):
        put_columns(cols, 0, y + 1, choose(even, far[y], near[y]))
        put_columns(cols, 1, y + 1, choose(even, near[y], far[y]))
        return carry

    lax.fori_loop(0, rows, step, 0, unroll=2)
    for p in range(2):
        for q in (0, rows + 1):
            cols[p, q] = jnp.zeros(cols.shape[2:], BF16)


def fill_edges(cols, near, far):
    even = is_even("gy")
    for p in range(4):
        put_columns(cols, p, 0, choose(even, far[p], near[p]))
        put_columns(cols, p, 1, choose(even, near[p], far[p]))


def dot(lhs, rhs):
    return jnp.dot(lhs, rhs, preferred_element_type=F32)


def taps(w_ref, b, first, last):
    return jnp.concatenate([w_ref[a, b] for a in range(first, last)], axis=0)


def window(cols, p, q):
    return jnp.concatenate([cols[p, q], cols[p, q + 1]], axis=1)


def inner_terms(cols, w_ref, y):
    acc = None
    for b in range(3):
        for p in range(2):
            term = dot(taps(w_ref, b, p, p + 2), window(cols, p, y + b))
            acc = term if acc is None else acc + term
    half = acc.shape[0] // 2
    return acc[half:], acc[:half]


def outer_terms(cols, w_ref, y):
    lower = upper = None
    for b in range(3):
        low, high = dot(w_ref[0, b], window(cols, 0, y + b)), dot(w_ref[2, b], window(cols, 1, y + b))
        lower = low if lower is None else lower + low
        upper = high if upper is None else upper + high
    return lower, upper


def edge_terms(edges, w_ref, side):
    b = 2 * side
    half = w_ref.shape[2]
    acc = dot(taps(w_ref, b, 0, 2), edges[1, side]) + dot(taps(w_ref, b, 1, 3), edges[2, side])
    return acc[half:] + dot(w_ref[0, b], edges[0, side]), acc[:half] + dot(w_ref[2, b], edges[3, side])


def inner_kernel(near, far, w_ref, d_ref, cot_ref, cols, acc_ref, grad_ref, up):
    rows, channels, breadth = near.shape
    fill_columns(cols, near, far)
    source = lax.broadcasted_iota(jnp.int32, (breadth, 2 * breadth), 0)
    target = lax.broadcasted_iota(jnp.int32, (breadth, 2 * breadth), 1)
    spread = jnp.where(source == target // 2, 1.0, 0.0).astype(BF16)
    for pair in range(rows // 4):
        both = dot(cot_ref[:, pair * breadth : (pair + 1) * breadth], spread)
        up[:, 2 * pair * breadth : 2 * (pair + 1) * breadth] = both.astype(BF16)
    even = lax.broadcasted_iota(jnp.int32, (channels, breadth), 1) % 2 == 0
    for a in range(2):
        for b in range(2):
            terms = lax.dot_general(d_ref[a, b], up[...], (((0,), (0,)), ((), ())), preferred_element_type=F32)
            for t in range(rows // 2):
                part = terms[:, t * breadth : (t + 1) * breadth]
                grad_ref[a, 2 * t + b] = jnp.where(even, part[0:channels], part[channels:])

    def step(t, carry):
        y = 2 * t
        for z, lines in enumerate(inner_terms(cols, w_ref, y)):
            for b in range(2):
                acc_ref[z, y + b] = lines[:, b * breadth : (b + 1) * breadth]
        return carry

    lax.fori_loop(0, rows // 2, step, 0)


def gated(preact, grad):
    sig = 1.0 / (1.0 + jnp.exp(-preact))
    return (preact * sig).astype(BF16), (grad * sig * (1.0 + preact * (1.0 - sig))).astype(BF16)


def outer_kernel(near, far, w_ref, acc_ref, grad_ref, cols, side_ref, near_ref, far_ref, h_ref):
    rows, channels, breadth = near.shape
    fill_columns(cols, near, far)
    even = is_even("gz")
    for y in range(0, rows, 2):
        outer = outer_terms(cols, w_ref, y)
        for b in range(2):
            found = []
            for z in range(2):
                preact = acc_ref[z, y + b] + outer[z][:, b * breadth : (b + 1) * breadth]
                if y + b in (0, rows - 1):
                    side_ref[z, b] = preact
                else:
                    h_ref[z, y + b], gate = gated(preact, grad_ref[z, y + b])
                    found.append(gate)
            if len(found) > 0:
                near_ref[y + b] = choose(even, found[1], found[0])
                far_ref[y + b] = choose(even, found[0], found[1])


def gate_kernel(near, far, side_ref, near_in, far_in, h_in, grad_ref, w_ref, edges, near_ref, far_ref, h_ref):
    rows = near_in.shape[0]
    fill_edges(edges, near, far)
    even = is_even("gz")
    for side, y in enumerate((0, rows - 1)):
        terms = edge_terms(edges, w_ref, side)
        found = []
        for z in range(2):
            h_ref[z, y], gate = gated(side_ref[z, side] + terms[z], grad_ref[z, y])
            found.append(gate)
        near_ref[y] = choose(even, found[1], found[0])
        far_ref[y] = choose(even, found[0], found[1])
    for y in range(1, rows - 1):
        near_ref[y] = near_in[y]
        far_ref[y] = far_in[y]
        for z in range(2):
            h_ref[z, y] = h_in[z, y]


def coarse_hidden(h_ref):
    rows, channels, breadth = h_ref.shape[1:]
    source = lax.broadcasted_iota(jnp.int32, (2 * breadth, 2 * breadth), 0)
    target = lax.broadcasted_iota(jnp.int32, (2 * breadth, 2 * breadth), 1)
    wanted = 2 * (target % breadth) + target // breadth
    pick = jnp.where(source == wanted, 1.0, 0.0).astype(BF16)
    pairs = rows // 4
    both = [
        jnp.concatenate([h_ref[a, 4 * pair + b], h_ref[a, 4 * pair + 2 + b]], axis=1)
        for a in range(2) for b in range(2) for pair in range(pairs)
    ]
    picked = dot(jnp.concatenate(both, axis=0), pick).astype(BF16)
    blocks = []
    for tap in range(4):
        parts = [picked[(tap * pairs + pair) * channels : (tap * pairs + pair + 1) * channels] for pair in range(pairs)]
        for e in range(2):
            blocks.append(jnp.concatenate([x[:, e * breadth : (e + 1) * breadth] for x in parts], axis=1))
    return jnp.concatenate(blocks, axis=0)


def section_kernel(h_ref, d_ref, out_ref):
    down = jnp.concatenate([d_ref[a, b] for a in range(2) for b in range(2)], axis=1)
    out_ref[...] = dot(down, coarse_hidden(h_ref)).astype(BF16)


def weight_grad_kernel(inner, outer, edges, near, far, h_ref, cot_ref, keep, send, packed):
    rows, channels, breadth = near.shape
    across = (((1,), (1,)), ((), ()))
    even = is_even("gz")
    low = [choose(even, far[y], near[y]) for y in range(rows)]
    high = [choose(even, near[y], far[y]) for y in range(rows)]
    nothing = jnp.zeros((channels, breadth), BF16)

    def shifted(lines):
        return jnp.concatenate(
            [jnp.concatenate([nothing] * b + lines + [nothing] * (2 - b), axis=1) for b in range(3)], axis=0
        )

    low, high = shifted(low), shifted(high)
    both = jnp.concatenate([low, high], axis=0)

    def columns(p, q):
        if q in (0, rows + 1):
            return edges[p, 0 if q == 0 else 1]
        return inner[p - 1, q] if p in (1, 2) else outer[p // 3, q]

    parts = []
    for p in range(4):
        lines = jnp.concatenate([columns(p, q) for q in range(rows + 2)], axis=1)
        lhs = low if p == 0 else high if p == 3 else both
        parts.append(lax.dot_general(lhs, lines, across, preferred_element_type=F32))
    lane = lax.broadcasted_iota(jnp.int32, (channels // 2, breadth), 1)
    for a in range(3):
        for b in range(3):
            at = b * channels + (0 if a == 2 else 3 * channels)
            total = parts[a][b * channels : (b + 1) * channels] + parts[a + 1][at : at + channels]
            base = (a * 3 + b) * 3 * channels // 2
            packed[base : base + channels] = total[:, 0:breadth]
            rest = jnp.concatenate([total[:, breadth:], total[:, breadth:]], axis=1)
            mix = jnp.where(lane < channels, rest[0 : channels // 2], rest[channels // 2 :])
            packed[base + channels : base + 3 * channels // 2] = mix
    base = 9 * 3 * channels // 2
    height = cot_ref.shape[0]
    down = lax.dot_general(cot_ref[...], coarse_hidden(h_ref), across, preferred_element_type=F32)
    for tap in range(4):
        packed[base + tap * height : base + (tap + 1) * height] = down[:, tap * breadth : (tap + 1) * breadth]
    end = base + 4 * height
    if end < packed.shape[0]:
        packed[end:] = jnp.zeros((packed.shape[0] - end, packed.shape[1]), F32)
    split(packed, keep, send, owned_half())


def side_of(axis, bit):
    return lax.rem(lax.axis_index(axis) // bit, 2)


def owned_half():
    total = 0
    for axis in ("gz", "gy"):
        for k in range(lax.axis_size(axis).bit_length() - 1):
            total = total + side_of(axis, 1 << k)
    return lax.rem(total, 2)


def part(side, rows):
    return pl.ds(pl.multiple_of(side * rows, 16), rows)


def split(packed, keep, send, side):
    half = keep.shape[0]
    keep[...] = packed[part(side, half)]
    send[...] = packed[part(1 - side, half)].astype(BF16)


def halve_kernel(mine, other, keep, send, total, *, axis, bit):
    total[...] = mine[...] + other[...].astype(F32)
    split(total, keep, send, side_of(axis, bit))


def add_kernel(x, y, out):
    out[...] = (x[...].astype(F32) + y[...].astype(F32)).astype(BF16)


def join_kernel(mine, other, out, *, axis, bit):
    join(mine, other, out, side_of(axis, bit))


def join(mine, other, out, side):
    rows = mine.shape[0]
    out[part(side, rows)] = mine[...]
    out[part(1 - side, rows)] = other[...]


def field_kernel(near, far, near_in, far_in, w_ref, acc_ref, inner, outer):
    rows, channels, breadth = near.shape
    fill_columns(inner, near, far)
    fill_columns(outer, near_in, far_in)

    def step(t, carry):
        y = 2 * t
        own = inner_terms(inner, w_ref, y)
        rest = outer_terms(outer, w_ref, y)
        for z in range(2):
            total = own[z] + rest[z]
            for b in range(2):
                acc_ref[z, y + b] = total[:, b * breadth : (b + 1) * breadth]
        return carry

    lax.fori_loop(0, rows // 2, step, 0)


def field_edges_kernel(near, far, acc_ref, w_ref, out_ref, edges):
    rows, channels, breadth = acc_ref.shape[1:]
    fill_edges(edges, near, far)
    sides = [edge_terms(edges, w_ref, side) for side in range(2)]
    for z in range(2):
        for y in range(rows):
            line = acc_ref[z, y]
            if y in (0, rows - 1):
                line = line + sides[0 if y == 0 else 1][z]
            out_ref[pl.ds(z * rows + y, channels, stride=2 * rows), :] = line


def unpack_kernel(mine, other, conv_ref, down_ref, sums_ref, *, scale):
    join(mine, other, sums_ref, owned_half())
    channels = conv_ref.shape[2]
    for a in range(3):
        for b in range(3):
            base = (a * 3 + b) * 3 * channels // 2
            conv_ref[a, b, :, 0 : 2 * channels] = sums_ref[base : base + channels].astype(F32) * scale
            rest = sums_ref[base + channels : base + 3 * channels // 2].astype(F32) * scale
            conv_ref[a, b, 0 : channels // 2, 2 * channels :] = rest[:, 0:channels]
            conv_ref[a, b, channels // 2 :, 2 * channels :] = rest[:, channels:]
    base = 9 * 3 * channels // 2
    height = down_ref.shape[2]
    for a in range(2):
        for b in range(2):
            at = base + (2 * a + b) * height
            down_ref[a, b] = sums_ref[at : at + height].astype(F32) * scale


def swap(cells, axis, low):
    count = lax.axis_size(axis)
    pairs = [(i % count, (i + 1) % count) for i in range(low, low + count, 2)]
    return lax.ppermute(cells, axis, pairs + [(b, a) for a, b in pairs])


def flip(cells, axis, bit):
    row = lax.axis_size("gy")
    mask = bit * row | 1 if axis == "gz" else bit | 1
    return lax.ppermute(cells, ("gz", "gy"), [(i, i ^ mask) for i in range(lax.axis_size("gz") * row)])


def tied(first, *others):
    found = lax.optimization_barrier((first, *others))
    return found[0], tuple(found[1:])


def swapped(near, far, axis):
    return swap(near, axis, 0), swap(far, axis, 1)


def body(features, conv_weight, down_weight, cotangent):
    channels, plane_count, row_count, breadth = features.shape
    out_channels = down_weight.shape[2]
    count = lax.axis_size("gz") * lax.axis_size("gy")
    grad_scale = 1.0 / math.sqrt(plane_count * row_count * breadth * count)
    turned = conv_weight.reshape(3, 3, channels, 3, channels)[::-1, ::-1, :, ::-1]
    weight_bwd = turned.transpose(0, 1, 4, 3, 2).reshape(3, 3, channels, 3 * channels)
    cot = cotangent.reshape(out_channels, -1)
    plane = ((row_count, channels, breadth), BF16)
    edge = ((plane_count + 2, channels, breadth), BF16)
    cols = ((plane_count, row_count + 2, 3 * channels, breadth), BF16)
    edge_cols = ((plane_count + 2, 2, 3 * channels, breadth), BF16)
    lines = (plane_count, row_count, channels, breadth)
    conv_flops = 2 * 27 * channels * channels * plane_count * row_count * breadth

    own = call(
        lines_kernel, [plane, plane], [((channels * plane_count * row_count, breadth), F32)], 0, (features,)
    )
    outside = swapped(*own, "gz")
    inner, acc, hidden_grad = call(
        inner_kernel, [cols, (lines, F32), (lines, F32)],
        [((out_channels, row_count // 2 * breadth), BF16)],
        2 * conv_flops // 3, (*own, conv_weight, down_weight, cot),
    )
    near, far, acc, weight_bwd = lax.optimization_barrier((*outside, acc, weight_bwd))
    outside = (near, far)
    beside = swapped(*call(edges_kernel, [edge, edge], [], 0, (*own, *outside)), "gy")
    outer, *inside = call(
        outer_kernel, [cols, ((plane_count, 2, channels, breadth), F32), plane, plane, (lines, BF16)], [],
        conv_flops // 3, (*outside, conv_weight, acc, hidden_grad),
    )
    edges, near, far, hidden = call(
        gate_kernel, [edge_cols, plane, plane, (lines, BF16)], [], conv_flops // 10,
        (*beside, *inside, hidden_grad, conv_weight),
    )
    gates = (near, far)

    used = 27 * channels * channels // 128 + 4 * out_channels
    rows = -(-used // 128) * 128
    keep, send = call(
        weight_grad_kernel, [((rows // 2, 128), F32), ((rows // 2, 128), BF16)], [((rows, 128), F32)],
        conv_flops, (inner, outer, edges, *gates, hidden, cot),
    )
    keep, gates = tied(keep, *gates)
    near, far = gates
    near_in = swap(near, "gz", 0)
    for level, (axis, bit) in enumerate((("gz", 2), ("gy", 2))):
        size = rows >> (level + 2)
        mine, got = keep, flip(send, *(("gy", 1), ("gz", 2))[level])
        keep, send = call(
            functools.partial(halve_kernel, axis=axis, bit=bit),
            [((size, 128), F32), ((size, 128), BF16)], [((2 * size, 128), F32)], 0, (mine, got),
        )
        if level == 0:
            keep, (far, hidden) = tied(keep, far, hidden)
            far_in = swap(far, "gz", 1)
            (section_out,) = call(
                section_kernel, [((out_channels, cot.shape[1]), BF16)], [], conv_flops // 10,
                (hidden, down_weight),
            )
    shard = ((rows // 8, 128), BF16)
    (sums,) = call(add_kernel, [shard], [], 0, (keep, flip(send, "gy", 2)))
    (sums,) = call(add_kernel, [shard], [], 0, (sums, flip(sums, "gz", 1)))
    sums, outside = tied(sums, near_in, far_in)
    sends = call(edges_kernel, [edge, edge], [], 0, (*gates, *outside))
    beside = swapped(*sends, "gy")
    (acc,) = call(
        field_kernel, [(lines, F32)], [cols, cols], conv_flops, (*gates, *outside, weight_bwd)
    )
    wide = [("gy", 1 << k) for k in range(2, lax.axis_size("gy").bit_length() - 1)]
    wide += [("gz", 1 << k) for k in range(2, lax.axis_size("gz").bit_length() - 1)]
    for axis, bit in wide:
        (sums,) = call(add_kernel, [shard], [], 0, (sums, flip(sums, axis, bit)))
    sums, (section_out,) = tied(sums, section_out)
    (sums,) = call(
        functools.partial(join_kernel, axis="gy", bit=2), [((rows // 4, 128), BF16)], [], 0,
        (sums, flip(sums, "gy", 2)),
    )
    sums, (acc, *beside) = tied(sums, acc, *beside)
    (field,) = call(
        field_edges_kernel, [((channels * plane_count * row_count, breadth), F32)], [edge_cols],
        conv_flops // 10, (*beside, acc, weight_bwd),
    )
    (sums,) = call(
        functools.partial(join_kernel, axis="gz", bit=2), [((rows // 2, 128), BF16)], [], 0,
        (sums, flip(sums, "gz", 2)),
    )
    sums, (field,) = tied(sums, field)
    grad_conv, grad_down = call(
        functools.partial(unpack_kernel, scale=grad_scale),
        [(conv_weight.shape, F32), (down_weight.shape, F32)], [((rows, 128), BF16)], 0,
        (sums, flip(sums, "gy", 1)),
    )
    section_out = section_out.reshape(out_channels, plane_count // 2, -1)
    return (section_out, field.reshape(features.shape), grad_conv, grad_down)


def solution(mesh):
    return jax.shard_map(
        body,
        mesh=mesh,
        in_specs=(P(None, "gz", "gy", None), P(), P(), P(None, "gz", "gy")),
        out_specs=(P(None, "gz", "gy"), P(None, "gz", "gy", None), P(), P()),
        check_vma=False,
    )
```

```python
import functools
import math

import jax
import jax.numpy as jnp
from jax import lax
from jax.experimental import pallas as pl
from jax.experimental.pallas import tpu as pltpu
from jax.sharding import PartitionSpec as P

F32 = jnp.float32
BF16 = jnp.bfloat16
PARAMS = pltpu.CompilerParams(vmem_limit_bytes=24 * 1024 * 1024)


def call(kernel, outs, scratch, flops, operands):
    moved = sum(x.size * x.dtype.itemsize for x in operands)
    moved += sum(math.prod(s) * jnp.dtype(d).itemsize for s, d in outs)
    vmem = pl.BlockSpec(memory_space=pltpu.VMEM)
    return pl.pallas_call(
        kernel,
        out_shape=[jax.ShapeDtypeStruct(s, d) for s, d in outs],
        in_specs=[vmem] * len(operands),
        out_specs=[vmem] * len(outs),
        scratch_shapes=[pltpu.VMEM(s, d) for s, d in scratch],
        compiler_params=PARAMS,
        cost_estimate=pl.CostEstimate(flops=flops, bytes_accessed=moved, transcendentals=0),
    )(*operands)


def is_even(axis):
    return lax.rem(lax.axis_index(axis), 2) == 0


def choose(cond, yes, no):
    return jnp.where(jnp.broadcast_to(cond, yes.shape), yes, no)


def lines_kernel(f_ref, near_ref, far_ref, wide):
    channels, planes, rows, breadth = f_ref.shape
    wide[...] = f_ref[...].astype(F32).reshape(channels * planes * rows, breadth)
    even = is_even("gz")
    for y in range(rows):
        low, high = (
            wide[pl.ds(z * rows + y, channels, stride=planes * rows), :].astype(BF16) for z in range(2)
        )
        near_ref[y] = choose(even, high, low)
        far_ref[y] = choose(even, low, high)


def edges_kernel(near, far, near_in, far_in, near_ref, far_ref):
    rows = near.shape[0]
    even_z, even_y = is_even("gz"), is_even("gy")

    def put(p, one, other):
        first = choose(even_z, one[0], other[0])
        last = choose(even_z, one[rows - 1], other[rows - 1])
        near_ref[p] = choose(even_y, last, first)
        far_ref[p] = choose(even_y, first, last)

    put(0, far_in, near_in)
    put(1, far, near)
    put(2, near, far)
    put(3, near_in, far_in)


def put_columns(cols, p, q, line):
    channels = line.shape[0]
    wide = line.astype(F32)
    cols[p, q, 0:channels] = pltpu.roll(wide, 1, 1).astype(BF16)
    cols[p, q, channels : 2 * channels] = line
    cols[p, q, 2 * channels : 3 * channels] = pltpu.roll(wide, line.shape[1] - 1, 1).astype(BF16)


def fill_columns(cols, near, far):
    rows = near.shape[0]
    even = is_even("gz")

    def step(y, carry):
        put_columns(cols, 0, y + 1, choose(even, far[y], near[y]))
        put_columns(cols, 1, y + 1, choose(even, near[y], far[y]))
        return carry

    lax.fori_loop(0, rows, step, 0, unroll=2)
    for p in range(2):
        for q in (0, rows + 1):
            cols[p, q] = jnp.zeros(cols.shape[2:], BF16)


def fill_edges(cols, near, far):
    even = is_even("gy")
    for p in range(4):
        put_columns(cols, p, 0, choose(even, far[p], near[p]))
        put_columns(cols, p, 1, choose(even, near[p], far[p]))


def dot(lhs, rhs):
    return jnp.dot(lhs, rhs, preferred_element_type=F32)


def taps(w_ref, b, first, last):
    return jnp.concatenate([w_ref[a, b] for a in range(first, last)], axis=0)


def window(cols, p, q):
    return jnp.concatenate([cols[p, q], cols[p, q + 1]], axis=1)


def inner_terms(cols, w_ref, y):
    acc = None
    for b in range(3):
        for p in range(2):
            term = dot(taps(w_ref, b, p, p + 2), window(cols, p, y + b))
            acc = term if acc is None else acc + term
    half = acc.shape[0] // 2
    return acc[half:], acc[:half]


def outer_terms(cols, w_ref, y):
    lower = upper = None
    for b in range(3):
        low, high = dot(w_ref[0, b], window(cols, 0, y + b)), dot(w_ref[2, b], window(cols, 1, y + b))
        lower = low if lower is None else lower + low
        upper = high if upper is None else upper + high
    return lower, upper


def edge_terms(edges, w_ref, side):
    b = 2 * side
    half = w_ref.shape[2]
    acc = dot(taps(w_ref, b, 0, 2), edges[1, side]) + dot(taps(w_ref, b, 1, 3), edges[2, side])
    return acc[half:] + dot(w_ref[0, b], edges[0, side]), acc[:half] + dot(w_ref[2, b], edges[3, side])


def inner_kernel(near, far, w_ref, d_ref, cot_ref, cols, acc_ref, grad_ref, up):
    rows, channels, breadth = near.shape
    fill_columns(cols, near, far)
    source = lax.broadcasted_iota(jnp.int32, (breadth, 2 * breadth), 0)
    target = lax.broadcasted_iota(jnp.int32, (breadth, 2 * breadth), 1)
    spread = jnp.where(source == target // 2, 1.0, 0.0).astype(BF16)
    for pair in range(rows // 4):
        both = dot(cot_ref[:, pair * breadth : (pair + 1) * breadth], spread)
        up[:, 2 * pair * breadth : 2 * (pair + 1) * breadth] = both.astype(BF16)
    even = lax.broadcasted_iota(jnp.int32, (channels, breadth), 1) % 2 == 0
    for a in range(2):
        for b in range(2):
            terms = lax.dot_general(d_ref[a, b], up[...], (((0,), (0,)), ((), ())), preferred_element_type=F32)
            for t in range(rows // 2):
                part = terms[:, t * breadth : (t + 1) * breadth]
                grad_ref[a, 2 * t + b] = jnp.where(even, part[0:channels], part[channels:])

    def step(t, carry):
        y = 2 * t
        for z, lines in enumerate(inner_terms(cols, w_ref, y)):
            for b in range(2):
                acc_ref[z, y + b] = lines[:, b * breadth : (b + 1) * breadth]
        return carry

    lax.fori_loop(0, rows // 2, step, 0)


def gated(preact, grad):
    sig = 1.0 / (1.0 + jnp.exp(-preact))
    return (preact * sig).astype(BF16), (grad * sig * (1.0 + preact * (1.0 - sig))).astype(BF16)


def outer_kernel(near, far, w_ref, acc_ref, grad_ref, cols, side_ref, near_ref, far_ref, h_ref):
    rows, channels, breadth = near.shape
    fill_columns(cols, near, far)
    even = is_even("gz")
    for y in range(0, rows, 2):
        outer = outer_terms(cols, w_ref, y)
        for b in range(2):
            found = []
            for z in range(2):
                preact = acc_ref[z, y + b] + outer[z][:, b * breadth : (b + 1) * breadth]
                if y + b in (0, rows - 1):
                    side_ref[z, b] = preact
                else:
                    h_ref[z, y + b], gate = gated(preact, grad_ref[z, y + b])
                    found.append(gate)
            if len(found) > 0:
                near_ref[y + b] = choose(even, found[1], found[0])
                far_ref[y + b] = choose(even, found[0], found[1])


def gate_kernel(near, far, side_ref, near_in, far_in, h_in, grad_ref, w_ref, edges, near_ref, far_ref, h_ref):
    rows = near_in.shape[0]
    fill_edges(edges, near, far)
    even = is_even("gz")
    for side, y in enumerate((0, rows - 1)):
        terms = edge_terms(edges, w_ref, side)
        found = []
        for z in range(2):
            h_ref[z, y], gate = gated(side_ref[z, side] + terms[z], grad_ref[z, y])
            found.append(gate)
        near_ref[y] = choose(even, found[1], found[0])
        far_ref[y] = choose(even, found[0], found[1])
    for y in range(1, rows - 1):
        near_ref[y] = near_in[y]
        far_ref[y] = far_in[y]
        for z in range(2):
            h_ref[z, y] = h_in[z, y]


def coarse_hidden(h_ref):
    rows, channels, breadth = h_ref.shape[1:]
    source = lax.broadcasted_iota(jnp.int32, (2 * breadth, 2 * breadth), 0)
    target = lax.broadcasted_iota(jnp.int32, (2 * breadth, 2 * breadth), 1)
    wanted = 2 * (target % breadth) + target // breadth
    pick = jnp.where(source == wanted, 1.0, 0.0).astype(BF16)
    pairs = rows // 4
    both = [
        jnp.concatenate([h_ref[a, 4 * pair + b], h_ref[a, 4 * pair + 2 + b]], axis=1)
        for a in range(2) for b in range(2) for pair in range(pairs)
    ]
    picked = dot(jnp.concatenate(both, axis=0), pick).astype(BF16)
    blocks = []
    for tap in range(4):
        parts = [picked[(tap * pairs + pair) * channels : (tap * pairs + pair + 1) * channels] for pair in range(pairs)]
        for e in range(2):
            blocks.append(jnp.concatenate([x[:, e * breadth : (e + 1) * breadth] for x in parts], axis=1))
    return jnp.concatenate(blocks, axis=0)


def section_kernel(h_ref, d_ref, out_ref):
    down = jnp.concatenate([d_ref[a, b] for a in range(2) for b in range(2)], axis=1)
    out_ref[...] = dot(down, coarse_hidden(h_ref)).astype(BF16)


def weight_grad_kernel(inner, outer, edges, near, far, h_ref, cot_ref, keep, send, packed):
    rows, channels, breadth = near.shape
    across = (((1,), (1,)), ((), ()))
    even = is_even("gz")
    low = [choose(even, far[y], near[y]) for y in range(rows)]
    high = [choose(even, near[y], far[y]) for y in range(rows)]
    nothing = jnp.zeros((channels, breadth), BF16)

    def shifted(lines):
        return jnp.concatenate(
            [jnp.concatenate([nothing] * b + lines + [nothing] * (2 - b), axis=1) for b in range(3)], axis=0
        )

    low, high = shifted(low), shifted(high)
    both = jnp.concatenate([low, high], axis=0)

    def columns(p, q):
        if q in (0, rows + 1):
            return edges[p, 0 if q == 0 else 1]
        return inner[p - 1, q] if p in (1, 2) else outer[p // 3, q]

    parts = []
    for p in range(4):
        lines = jnp.concatenate([columns(p, q) for q in range(rows + 2)], axis=1)
        lhs = low if p == 0 else high if p == 3 else both
        parts.append(lax.dot_general(lhs, lines, across, preferred_element_type=F32))
    lane = lax.broadcasted_iota(jnp.int32, (channels // 2, breadth), 1)
    for a in range(3):
        for b in range(3):
            at = b * channels + (0 if a == 2 else 3 * channels)
            total = parts[a][b * channels : (b + 1) * channels] + parts[a + 1][at : at + channels]
            base = (a * 3 + b) * 3 * channels // 2
            packed[base : base + channels] = total[:, 0:breadth]
            rest = jnp.concatenate([total[:, breadth:], total[:, breadth:]], axis=1)
            mix = jnp.where(lane < channels, rest[0 : channels // 2], rest[channels // 2 :])
            packed[base + channels : base + 3 * channels // 2] = mix
    base = 9 * 3 * channels // 2
    height = cot_ref.shape[0]
    down = lax.dot_general(cot_ref[...], coarse_hidden(h_ref), across, preferred_element_type=F32)
    for tap in range(4):
        packed[base + tap * height : base + (tap + 1) * height] = down[:, tap * breadth : (tap + 1) * breadth]
    end = base + 4 * height
    if end < packed.shape[0]:
        packed[end:] = jnp.zeros((packed.shape[0] - end, packed.shape[1]), F32)
    split(packed, keep, send, owned_half())


def side_of(axis, bit):
    return lax.rem(lax.axis_index(axis) // bit, 2)


def owned_half():
    total = 0
    for axis in ("gz", "gy"):
        for k in range(lax.axis_size(axis).bit_length() - 1):
            total = total + side_of(axis, 1 << k)
    return lax.rem(total, 2)


def part(side, rows):
    return pl.ds(pl.multiple_of(side * rows, 16), rows)


def split(packed, keep, send, side):
    half = keep.shape[0]
    keep[...] = packed[part(side, half)]
    send[...] = packed[part(1 - side, half)].astype(BF16)


def halve_kernel(mine, other, keep, send, total, *, axis, bit):
    total[...] = mine[...] + other[...].astype(F32)
    split(total, keep, send, side_of(axis, bit))


def add_kernel(x, y, out):
    out[...] = (x[...].astype(F32) + y[...].astype(F32)).astype(BF16)


def join_kernel(mine, other, out, *, axis, bit):
    join(mine, other, out, side_of(axis, bit))


def join(mine, other, out, side):
    rows = mine.shape[0]
    out[part(side, rows)] = mine[...]
    out[part(1 - side, rows)] = other[...]


def field_kernel(near, far, near_in, far_in, w_ref, acc_ref, inner, outer):
    rows, channels, breadth = near.shape
    fill_columns(inner, near, far)
    fill_columns(outer, near_in, far_in)

    def step(t, carry):
        y = 2 * t
        own = inner_terms(inner, w_ref, y)
        rest = outer_terms(outer, w_ref, y)
        for z in range(2):
            total = own[z] + rest[z]
            for b in range(2):
                acc_ref[z, y + b] = total[:, b * breadth : (b + 1) * breadth]
        return carry

    lax.fori_loop(0, rows // 2, step, 0)


def field_edges_kernel(near, far, acc_ref, w_ref, out_ref, edges):
    rows, channels, breadth = acc_ref.shape[1:]
    fill_edges(edges, near, far)
    sides = [edge_terms(edges, w_ref, side) for side in range(2)]
    for z in range(2):
        for y in range(rows):
            line = acc_ref[z, y]
            if y in (0, rows - 1):
                line = line + sides[0 if y == 0 else 1][z]
            out_ref[pl.ds(z * rows + y, channels, stride=2 * rows), :] = line


def unpack_kernel(mine, other, conv_ref, down_ref, sums_ref, *, scale):
    join(mine, other, sums_ref, owned_half())
    channels = conv_ref.shape[2]
    for a in range(3):
        for b in range(3):
            base = (a * 3 + b) * 3 * channels // 2
            conv_ref[a, b, :, 0 : 2 * channels] = sums_ref[base : base + channels].astype(F32) * scale
            rest = sums_ref[base + channels : base + 3 * channels // 2].astype(F32) * scale
            conv_ref[a, b, 0 : channels // 2, 2 * channels :] = rest[:, 0:channels]
            conv_ref[a, b, channels // 2 :, 2 * channels :] = rest[:, channels:]
    base = 9 * 3 * channels // 2
    height = down_ref.shape[2]
    for a in range(2):
        for b in range(2):
            at = base + (2 * a + b) * height
            down_ref[a, b] = sums_ref[at : at + height].astype(F32) * scale


def swap(cells, axis, low):
    count = lax.axis_size(axis)
    pairs = [(i % count, (i + 1) % count) for i in range(low, low + count, 2)]
    return lax.ppermute(cells, axis, pairs + [(b, a) for a, b in pairs])


def flip(cells, axis, bit):
    row = lax.axis_size("gy")
    mask = bit * row | 1 if axis == "gz" else bit | 1
    return lax.ppermute(cells, ("gz", "gy"), [(i, i ^ mask) for i in range(lax.axis_size("gz") * row)])


def tied(first, *others):
    found = lax.optimization_barrier((first, *others))
    return found[0], tuple(found[1:])


def swapped(near, far, axis):
    return swap(near, axis, 0), swap(far, axis, 1)


def body(features, conv_weight, down_weight, cotangent):
    channels, plane_count, row_count, breadth = features.shape
    out_channels = down_weight.shape[2]
    count = lax.axis_size("gz") * lax.axis_size("gy")
    grad_scale = 1.0 / math.sqrt(plane_count * row_count * breadth * count)
    turned = conv_weight.reshape(3, 3, channels, 3, channels)[::-1, ::-1, :, ::-1]
    weight_bwd = turned.transpose(0, 1, 4, 3, 2).reshape(3, 3, channels, 3 * channels)
    cot = cotangent.reshape(out_channels, -1)
    plane = ((row_count, channels, breadth), BF16)
    edge = ((plane_count + 2, channels, breadth), BF16)
    cols = ((plane_count, row_count + 2, 3 * channels, breadth), BF16)
    edge_cols = ((plane_count + 2, 2, 3 * channels, breadth), BF16)
    lines = (plane_count, row_count, channels, breadth)
    conv_flops = 2 * 27 * channels * channels * plane_count * row_count * breadth

    own = call(
        lines_kernel, [plane, plane], [((channels * plane_count * row_count, breadth), F32)], 0, (features,)
    )
    outside = swapped(*own, "gz")
    inner, acc, hidden_grad = call(
        inner_kernel, [cols, (lines, F32), (lines, F32)],
        [((out_channels, row_count // 2 * breadth), BF16)],
        2 * conv_flops // 3, (*own, conv_weight, down_weight, cot),
    )
    near, far, acc, weight_bwd = lax.optimization_barrier((*outside, acc, weight_bwd))
    outside = (near, far)
    beside = swapped(*call(edges_kernel, [edge, edge], [], 0, (*own, *outside)), "gy")
    far, near = lax.optimization_barrier((beside[1], beside[0]))
    beside = (near, far)
    outer, *inside = call(
        outer_kernel, [cols, ((plane_count, 2, channels, breadth), F32), plane, plane, (lines, BF16)], [],
        conv_flops // 3, (*outside, conv_weight, acc, hidden_grad),
    )
    edges, near, far, hidden = call(
        gate_kernel, [edge_cols, plane, plane, (lines, BF16)], [], conv_flops // 10,
        (*beside, *inside, hidden_grad, conv_weight),
    )
    gates = (near, far)

    used = 27 * channels * channels // 128 + 4 * out_channels
    rows = -(-used // 128) * 128
    keep, send = call(
        weight_grad_kernel, [((rows // 2, 128), F32), ((rows // 2, 128), BF16)], [((rows, 128), F32)],
        conv_flops, (inner, outer, edges, *gates, hidden, cot),
    )
    keep, gates = tied(keep, *gates)
    near, far = gates
    near_in = swap(near, "gz", 0)
    for level, (axis, bit) in enumerate((("gz", 2), ("gy", 2))):
        size = rows >> (level + 2)
        mine, got = keep, flip(send, *(("gy", 1), ("gz", 2))[level])
        keep, send = call(
            functools.partial(halve_kernel, axis=axis, bit=bit),
            [((size, 128), F32), ((size, 128), BF16)], [((2 * size, 128), F32)], 0, (mine, got),
        )
        if level == 0:
            keep, (far, hidden) = tied(keep, far, hidden)
            far_in = swap(far, "gz", 1)
            (section_out,) = call(
                section_kernel, [((out_channels, cot.shape[1]), BF16)], [], conv_flops // 10,
                (hidden, down_weight),
            )
    shard = ((rows // 8, 128), BF16)
    (sums,) = call(add_kernel, [shard], [], 0, (keep, flip(send, "gy", 2)))
    (sums,) = call(add_kernel, [shard], [], 0, (sums, flip(sums, "gz", 1)))
    sums, outside = tied(sums, near_in, far_in)
    sends = call(edges_kernel, [edge, edge], [], 0, (*gates, *outside))
    beside = swapped(*sends, "gy")
    (acc,) = call(
        field_kernel, [(lines, F32)], [cols, cols], conv_flops, (*gates, *outside, weight_bwd)
    )
    wide = [("gy", 1 << k) for k in range(2, lax.axis_size("gy").bit_length() - 1)]
    wide += [("gz", 1 << k) for k in range(2, lax.axis_size("gz").bit_length() - 1)]
    for axis, bit in wide:
        (sums,) = call(add_kernel, [shard], [], 0, (sums, flip(sums, axis, bit)))
    sums, (section_out,) = tied(sums, section_out)
    (sums,) = call(
        functools.partial(join_kernel, axis="gy", bit=2), [((rows // 4, 128), BF16)], [], 0,
        (sums, flip(sums, "gy", 2)),
    )
    sums, (acc, *beside) = tied(sums, acc, *beside)
    (field,) = call(
        field_edges_kernel, [((channels * plane_count * row_count, breadth), F32)], [edge_cols],
        conv_flops // 10, (*beside, acc, weight_bwd),
    )
    (sums,) = call(
        functools.partial(join_kernel, axis="gz", bit=2), [((rows // 2, 128), BF16)], [], 0,
        (sums, flip(sums, "gz", 2)),
    )
    sums, (field,) = tied(sums, field)
    grad_conv, grad_down = call(
        functools.partial(unpack_kernel, scale=grad_scale),
        [(conv_weight.shape, F32), (down_weight.shape, F32)], [((rows, 128), BF16)], 0,
        (sums, flip(sums, "gy", 1)),
    )
    section_out = section_out.reshape(out_channels, plane_count // 2, -1)
    return (section_out, field.reshape(features.shape), grad_conv, grad_down)


def solution(mesh):
    return jax.shard_map(
        body,
        mesh=mesh,
        in_specs=(P(None, "gz", "gy", None), P(), P(), P(None, "gz", "gy")),
        out_specs=(P(None, "gz", "gy"), P(None, "gz", "gy", None), P(), P()),
        check_vma=False,
    )
```

```python
import functools
import math

import jax
import jax.numpy as jnp
from jax import lax
from jax.experimental import pallas as pl
from jax.experimental.pallas import tpu as pltpu
from jax.sharding import PartitionSpec as P

F32 = jnp.float32
BF16 = jnp.bfloat16
PARAMS = pltpu.CompilerParams(vmem_limit_bytes=24 * 1024 * 1024)


def call(kernel, outs, scratch, flops, operands):
    moved = sum(x.size * x.dtype.itemsize for x in operands)
    moved += sum(math.prod(s) * jnp.dtype(d).itemsize for s, d in outs)
    vmem = pl.BlockSpec(memory_space=pltpu.VMEM)
    return pl.pallas_call(
        kernel,
        out_shape=[jax.ShapeDtypeStruct(s, d) for s, d in outs],
        in_specs=[vmem] * len(operands),
        out_specs=[vmem] * len(outs),
        scratch_shapes=[pltpu.VMEM(s, d) for s, d in scratch],
        compiler_params=PARAMS,
        cost_estimate=pl.CostEstimate(flops=flops, bytes_accessed=moved, transcendentals=0),
    )(*operands)


def is_even(axis):
    return lax.rem(lax.axis_index(axis), 2) == 0


def choose(cond, yes, no):
    return jnp.where(jnp.broadcast_to(cond, yes.shape), yes, no)


def lines_kernel(f_ref, near_ref, far_ref, near_row, far_row, wide):
    channels, planes, rows, breadth = f_ref.shape
    wide[...] = f_ref[...].astype(F32).reshape(channels * planes * rows, breadth)
    even = is_even("gz")
    ends = {}
    for y in range(rows):
        low, high = ends[y] = [
            wide[pl.ds(z * rows + y, channels, stride=planes * rows), :].astype(BF16) for z in range(2)
        ]
        near_ref[y] = choose(even, high, low)
        far_ref[y] = choose(even, low, high)
    even_y = is_even("gy")
    for z in range(2):
        near_row[z] = choose(even_y, ends[rows - 1][z], ends[0][z])
        far_row[z] = choose(even_y, ends[0][z], ends[rows - 1][z])


def copy_kernel(x, out):
    out[...] = x[...]


def outer_rows_kernel(near_in, far_in, near_ref, far_ref):
    rows = near_in.shape[0]
    even_z, even_y = is_even("gz"), is_even("gy")
    for p, (one, other) in enumerate(((far_in, near_in), (near_in, far_in))):
        first = choose(even_z, one[0], other[0])
        last = choose(even_z, one[rows - 1], other[rows - 1])
        near_ref[p] = choose(even_y, last, first)
        far_ref[p] = choose(even_y, first, last)


def edges_kernel(near, far, near_in, far_in, near_ref, far_ref):
    rows = near.shape[0]
    even_z, even_y = is_even("gz"), is_even("gy")

    def put(p, one, other):
        first = choose(even_z, one[0], other[0])
        last = choose(even_z, one[rows - 1], other[rows - 1])
        near_ref[p] = choose(even_y, last, first)
        far_ref[p] = choose(even_y, first, last)

    put(0, far_in, near_in)
    put(1, far, near)
    put(2, near, far)
    put(3, near_in, far_in)


def put_columns(cols, p, q, line):
    channels = line.shape[0]
    wide = line.astype(F32)
    cols[p, q, 0:channels] = pltpu.roll(wide, 1, 1).astype(BF16)
    cols[p, q, channels : 2 * channels] = line
    cols[p, q, 2 * channels : 3 * channels] = pltpu.roll(wide, line.shape[1] - 1, 1).astype(BF16)


def fill_columns(cols, near, far, near_row=None, far_row=None):
    rows = near.shape[0]
    even = is_even("gz")

    def step(y, carry):
        put_columns(cols, 0, y + 1, choose(even, far[y], near[y]))
        put_columns(cols, 1, y + 1, choose(even, near[y], far[y]))
        return carry

    lax.fori_loop(0, rows, step, 0, unroll=2)
    if near_row is not None:
        fill_rows(cols, near_row, far_row, 0, rows + 1)
        return
    for p in range(2):
        for q in (0, rows + 1):
            cols[p, q] = jnp.zeros(cols.shape[2:], BF16)


def fill_rows(cols, near, far, below, above):
    even = is_even("gy")
    for p in range(near.shape[0]):
        put_columns(cols, p, below, choose(even, far[p], near[p]))
        put_columns(cols, p, above, choose(even, near[p], far[p]))


def dot(lhs, rhs):
    return jnp.dot(lhs, rhs, preferred_element_type=F32)


def taps(w_ref, b, first, last):
    return jnp.concatenate([w_ref[a, b] for a in range(first, last)], axis=0)


def window(cols, p, q):
    return jnp.concatenate([cols[p, q], cols[p, q + 1]], axis=1)


def inner_terms(cols, w_ref, y):
    acc = None
    for b in range(3):
        for p in range(2):
            term = dot(taps(w_ref, b, p, p + 2), window(cols, p, y + b))
            acc = term if acc is None else acc + term
    half = acc.shape[0] // 2
    return acc[half:], acc[:half]


def outer_terms(cols, w_ref, y):
    lower = upper = None
    for b in range(3):
        low, high = dot(w_ref[0, b], window(cols, 0, y + b)), dot(w_ref[2, b], window(cols, 1, y + b))
        lower = low if lower is None else lower + low
        upper = high if upper is None else upper + high
    return lower, upper


def edge_terms(edges, w_ref, side):
    b = 2 * side
    half = w_ref.shape[2]
    acc = dot(taps(w_ref, b, 0, 2), edges[1, side]) + dot(taps(w_ref, b, 1, 3), edges[2, side])
    return acc[half:] + dot(w_ref[0, b], edges[0, side]), acc[:half] + dot(w_ref[2, b], edges[3, side])


def inner_kernel(near, far, near_row, far_row, w_ref, d_ref, cot_ref, cols, acc_ref, grad_ref, up):
    rows, channels, breadth = near.shape
    fill_columns(cols, near, far, near_row, far_row)
    source = lax.broadcasted_iota(jnp.int32, (breadth, 2 * breadth), 0)
    target = lax.broadcasted_iota(jnp.int32, (breadth, 2 * breadth), 1)
    spread = jnp.where(source == target // 2, 1.0, 0.0).astype(BF16)
    for pair in range(rows // 4):
        both = dot(cot_ref[:, pair * breadth : (pair + 1) * breadth], spread)
        up[:, 2 * pair * breadth : 2 * (pair + 1) * breadth] = both.astype(BF16)
    even = lax.broadcasted_iota(jnp.int32, (channels, breadth), 1) % 2 == 0
    for a in range(2):
        for b in range(2):
            terms = lax.dot_general(d_ref[a, b], up[...], (((0,), (0,)), ((), ())), preferred_element_type=F32)
            for t in range(rows // 2):
                part = terms[:, t * breadth : (t + 1) * breadth]
                grad_ref[a, 2 * t + b] = jnp.where(even, part[0:channels], part[channels:])

    def step(t, carry):
        y = 2 * t
        for z, lines in enumerate(inner_terms(cols, w_ref, y)):
            for b in range(2):
                acc_ref[z, y + b] = lines[:, b * breadth : (b + 1) * breadth]
        return carry

    lax.fori_loop(0, rows // 2, step, 0)


def gated(preact, grad):
    sig = 1.0 / (1.0 + jnp.exp(-preact))
    return (preact * sig).astype(BF16), (grad * sig * (1.0 + preact * (1.0 - sig))).astype(BF16)


def outer_kernel(near, far, w_ref, acc_ref, grad_ref, cols, side_ref, near_ref, far_ref, h_ref):
    rows, channels, breadth = near.shape
    fill_columns(cols, near, far)
    even = is_even("gz")
    for y in range(0, rows, 2):
        outer = outer_terms(cols, w_ref, y)
        for b in range(2):
            found = []
            for z in range(2):
                preact = acc_ref[z, y + b] + outer[z][:, b * breadth : (b + 1) * breadth]
                if y + b in (0, rows - 1):
                    side_ref[z, b] = preact
                else:
                    h_ref[z, y + b], gate = gated(preact, grad_ref[z, y + b])
                    found.append(gate)
            if len(found) > 0:
                near_ref[y + b] = choose(even, found[1], found[0])
                far_ref[y + b] = choose(even, found[0], found[1])


def gate_kernel(near, far, side_ref, near_in, far_in, h_in, grad_ref, w_ref, edges, near_ref, far_ref, h_ref):
    rows = near_in.shape[0]
    fill_rows(edges, near, far, 0, 1)
    even = is_even("gz")
    for side, y in enumerate((0, rows - 1)):
        terms = [dot(w_ref[2 * z, 2 * side], edges[z, side]) for z in range(2)]
        found = []
        for z in range(2):
            h_ref[z, y], gate = gated(side_ref[z, side] + terms[z], grad_ref[z, y])
            found.append(gate)
        near_ref[y] = choose(even, found[1], found[0])
        far_ref[y] = choose(even, found[0], found[1])
    for y in range(1, rows - 1):
        near_ref[y] = near_in[y]
        far_ref[y] = far_in[y]
        for z in range(2):
            h_ref[z, y] = h_in[z, y]


def coarse_hidden(h_ref):
    rows, channels, breadth = h_ref.shape[1:]
    source = lax.broadcasted_iota(jnp.int32, (2 * breadth, 2 * breadth), 0)
    target = lax.broadcasted_iota(jnp.int32, (2 * breadth, 2 * breadth), 1)
    wanted = 2 * (target % breadth) + target // breadth
    pick = jnp.where(source == wanted, 1.0, 0.0).astype(BF16)
    pairs = rows // 4
    both = [
        jnp.concatenate([h_ref[a, 4 * pair + b], h_ref[a, 4 * pair + 2 + b]], axis=1)
        for a in range(2) for b in range(2) for pair in range(pairs)
    ]
    picked = dot(jnp.concatenate(both, axis=0), pick).astype(BF16)
    blocks = []
    for tap in range(4):
        parts = [picked[(tap * pairs + pair) * channels : (tap * pairs + pair + 1) * channels] for pair in range(pairs)]
        for e in range(2):
            blocks.append(jnp.concatenate([x[:, e * breadth : (e + 1) * breadth] for x in parts], axis=1))
    return jnp.concatenate(blocks, axis=0)


def section_kernel(h_ref, d_ref, out_ref):
    down = jnp.concatenate([d_ref[a, b] for a in range(2) for b in range(2)], axis=1)
    out_ref[...] = dot(down, coarse_hidden(h_ref)).astype(BF16)


def weight_grad_kernel(inner, outer, edges, near, far, h_ref, cot_ref, keep, send, packed):
    rows, channels, breadth = near.shape
    across = (((1,), (1,)), ((), ()))
    even = is_even("gz")
    low = [choose(even, far[y], near[y]) for y in range(rows)]
    high = [choose(even, near[y], far[y]) for y in range(rows)]
    nothing = jnp.zeros((channels, breadth), BF16)

    def shifted(lines):
        return jnp.concatenate(
            [jnp.concatenate([nothing] * b + lines + [nothing] * (2 - b), axis=1) for b in range(3)], axis=0
        )

    low, high = shifted(low), shifted(high)
    both = jnp.concatenate([low, high], axis=0)

    def columns(p, q):
        if p in (1, 2):
            return inner[p - 1, q]
        return edges[p // 3, q // (rows + 1)] if q in (0, rows + 1) else outer[p // 3, q]

    parts = []
    for p in range(4):
        lines = jnp.concatenate([columns(p, q) for q in range(rows + 2)], axis=1)
        lhs = low if p == 0 else high if p == 3 else both
        parts.append(lax.dot_general(lhs, lines, across, preferred_element_type=F32))
    lane = lax.broadcasted_iota(jnp.int32, (channels // 2, breadth), 1)
    for a in range(3):
        for b in range(3):
            at = b * channels + (0 if a == 2 else 3 * channels)
            total = parts[a][b * channels : (b + 1) * channels] + parts[a + 1][at : at + channels]
            base = (a * 3 + b) * 3 * channels // 2
            packed[base : base + channels] = total[:, 0:breadth]
            rest = jnp.concatenate([total[:, breadth:], total[:, breadth:]], axis=1)
            mix = jnp.where(lane < channels, rest[0 : channels // 2], rest[channels // 2 :])
            packed[base + channels : base + 3 * channels // 2] = mix
    base = 9 * 3 * channels // 2
    height = cot_ref.shape[0]
    down = lax.dot_general(cot_ref[...], coarse_hidden(h_ref), across, preferred_element_type=F32)
    for tap in range(4):
        packed[base + tap * height : base + (tap + 1) * height] = down[:, tap * breadth : (tap + 1) * breadth]
    end = base + 4 * height
    if end < packed.shape[0]:
        packed[end:] = jnp.zeros((packed.shape[0] - end, packed.shape[1]), F32)
    split(packed, keep, send, owned_half())


def side_of(axis, bit):
    return lax.rem(lax.axis_index(axis) // bit, 2)


def owned_half():
    total = 0
    for axis in ("gz", "gy"):
        for k in range(lax.axis_size(axis).bit_length() - 1):
            total = total + side_of(axis, 1 << k)
    return lax.rem(total, 2)


def part(side, rows):
    return pl.ds(pl.multiple_of(side * rows, 16), rows)


def split(packed, keep, send, side):
    half = keep.shape[0]
    keep[...] = packed[part(side, half)]
    send[...] = packed[part(1 - side, half)].astype(BF16)


def halve_kernel(mine, other, keep, send, total, *, axis, bit):
    total[...] = mine[...] + other[...].astype(F32)
    split(total, keep, send, side_of(axis, bit))


def add_kernel(x, y, out):
    out[...] = (x[...].astype(F32) + y[...].astype(F32)).astype(BF16)


def join_kernel(mine, other, out, *, axis, bit):
    join(mine, other, out, side_of(axis, bit))


def join(mine, other, out, side):
    rows = mine.shape[0]
    out[part(side, rows)] = mine[...]
    out[part(1 - side, rows)] = other[...]


def field_kernel(near, far, near_in, far_in, w_ref, acc_ref, inner, outer):
    rows, channels, breadth = near.shape
    fill_columns(inner, near, far)
    fill_columns(outer, near_in, far_in)

    def step(t, carry):
        y = 2 * t
        own = inner_terms(inner, w_ref, y)
        rest = outer_terms(outer, w_ref, y)
        for z in range(2):
            total = own[z] + rest[z]
            for b in range(2):
                acc_ref[z, y + b] = total[:, b * breadth : (b + 1) * breadth]
        return carry

    lax.fori_loop(0, rows // 2, step, 0)


def field_edges_kernel(near, far, acc_ref, w_ref, out_ref, edges):
    rows, channels, breadth = acc_ref.shape[1:]
    fill_rows(edges, near, far, 0, 1)
    sides = [edge_terms(edges, w_ref, side) for side in range(2)]
    for z in range(2):
        for y in range(rows):
            line = acc_ref[z, y]
            if y in (0, rows - 1):
                line = line + sides[0 if y == 0 else 1][z]
            out_ref[pl.ds(z * rows + y, channels, stride=2 * rows), :] = line


def unpack_kernel(mine, other, conv_ref, down_ref, sums_ref, *, scale):
    join(mine, other, sums_ref, owned_half())
    channels = conv_ref.shape[2]
    for a in range(3):
        for b in range(3):
            base = (a * 3 + b) * 3 * channels // 2
            conv_ref[a, b, :, 0 : 2 * channels] = sums_ref[base : base + channels].astype(F32) * scale
            rest = sums_ref[base + channels : base + 3 * channels // 2].astype(F32) * scale
            conv_ref[a, b, 0 : channels // 2, 2 * channels :] = rest[:, 0:channels]
            conv_ref[a, b, channels // 2 :, 2 * channels :] = rest[:, channels:]
    base = 9 * 3 * channels // 2
    height = down_ref.shape[2]
    for a in range(2):
        for b in range(2):
            at = base + (2 * a + b) * height
            down_ref[a, b] = sums_ref[at : at + height].astype(F32) * scale


def swap(cells, axis, low):
    count = lax.axis_size(axis)
    pairs = [(i % count, (i + 1) % count) for i in range(low, low + count, 2)]
    return lax.ppermute(cells, axis, pairs + [(b, a) for a, b in pairs])


def flip(cells, axis, bit):
    row = lax.axis_size("gy")
    mask = bit * row | 1 if axis == "gz" else bit | 1
    return lax.ppermute(cells, ("gz", "gy"), [(i, i ^ mask) for i in range(lax.axis_size("gz") * row)])


def tied(first, *others):
    found = lax.optimization_barrier((first, *others))
    return found[0], tuple(found[1:])


def swapped(near, far, axis):
    return swap(near, axis, 0), swap(far, axis, 1)


def body(features, conv_weight, down_weight, cotangent):
    channels, plane_count, row_count, breadth = features.shape
    out_channels = down_weight.shape[2]
    count = lax.axis_size("gz") * lax.axis_size("gy")
    grad_scale = 1.0 / math.sqrt(plane_count * row_count * breadth * count)
    (conv_weight,) = call(copy_kernel, [(conv_weight.shape, BF16)], [], 0, (conv_weight,))
    turned = conv_weight.reshape(3, 3, channels, 3, channels)[::-1, ::-1, :, ::-1]
    weight_bwd = turned.transpose(0, 1, 4, 3, 2).reshape(3, 3, channels, 3 * channels)
    cot = cotangent.reshape(out_channels, -1)
    plane = ((row_count, channels, breadth), BF16)
    edge = ((plane_count + 2, channels, breadth), BF16)
    cols = ((plane_count, row_count + 2, 3 * channels, breadth), BF16)
    edge_cols = ((plane_count + 2, 2, 3 * channels, breadth), BF16)
    lines = (plane_count, row_count, channels, breadth)
    conv_flops = 2 * 27 * channels * channels * plane_count * row_count * breadth

    pair = ((plane_count, channels, breadth), BF16)
    *own, near_row, far_row = call(
        lines_kernel, [plane, plane, pair, pair],
        [((channels * plane_count * row_count, breadth), F32)], 0, (features,),
    )
    outside = swapped(*own, "gz")
    beside = swapped(near_row, far_row, "gy")
    inner, acc, hidden_grad = call(
        inner_kernel, [cols, (lines, F32), (lines, F32)],
        [((out_channels, row_count // 2 * breadth), BF16)],
        2 * conv_flops // 3, (*own, *beside, conv_weight, down_weight, cot),
    )
    near, far, acc = lax.optimization_barrier((*outside, acc))
    outside = (near, far)
    beside = swapped(*call(outer_rows_kernel, [pair, pair], [], 0, outside), "gy")
    far, near = lax.optimization_barrier((beside[1], beside[0]))
    beside = (near, far)
    outer, *inside = call(
        outer_kernel, [cols, ((plane_count, 2, channels, breadth), F32), plane, plane, (lines, BF16)], [],
        conv_flops // 3, (*outside, conv_weight, acc, hidden_grad),
    )
    edges, near, far, hidden = call(
        gate_kernel, [((plane_count, 2, 3 * channels, breadth), BF16), plane, plane, (lines, BF16)], [], conv_flops // 10,
        (*beside, *inside, hidden_grad, conv_weight),
    )
    gates = (near, far)

    used = 27 * channels * channels // 128 + 4 * out_channels
    rows = -(-used // 128) * 128
    keep, send = call(
        weight_grad_kernel, [((rows // 2, 128), F32), ((rows // 2, 128), BF16)], [((rows, 128), F32)],
        conv_flops, (inner, outer, edges, *gates, hidden, cot),
    )
    keep, gates = tied(keep, *gates)
    near, far = gates
    near_in = swap(near, "gz", 0)
    for level, (axis, bit) in enumerate((("gz", 2), ("gy", 2))):
        size = rows >> (level + 2)
        mine, got = keep, flip(send, *(("gy", 1), ("gz", 2))[level])
        keep, send = call(
            functools.partial(halve_kernel, axis=axis, bit=bit),
            [((size, 128), F32), ((size, 128), BF16)], [((2 * size, 128), F32)], 0, (mine, got),
        )
        if level == 0:
            keep, (far, hidden) = tied(keep, far, hidden)
            far_in = swap(far, "gz", 1)
            (section_out,) = call(
                section_kernel, [((out_channels, cot.shape[1]), BF16)], [], conv_flops // 10,
                (hidden, down_weight),
            )
    shard = ((rows // 8, 128), BF16)
    (sums,) = call(add_kernel, [shard], [], 0, (keep, flip(send, "gy", 2)))
    (sums,) = call(add_kernel, [shard], [], 0, (sums, flip(sums, "gz", 1)))
    sums, outside = tied(sums, near_in, far_in)
    sends = call(edges_kernel, [edge, edge], [], 0, (*gates, *outside))
    beside = swapped(*sends, "gy")
    (acc,) = call(
        field_kernel, [(lines, F32)], [cols, cols], conv_flops, (*gates, *outside, weight_bwd)
    )
    wide = [("gy", 1 << k) for k in range(2, lax.axis_size("gy").bit_length() - 1)]
    wide += [("gz", 1 << k) for k in range(2, lax.axis_size("gz").bit_length() - 1)]
    for axis, bit in wide:
        (sums,) = call(add_kernel, [shard], [], 0, (sums, flip(sums, axis, bit)))
    sums, (section_out,) = tied(sums, section_out)
    (sums,) = call(
        functools.partial(join_kernel, axis="gy", bit=2), [((rows // 4, 128), BF16)], [], 0,
        (sums, flip(sums, "gy", 2)),
    )
    sums, (acc, *beside) = tied(sums, acc, *beside)
    (field,) = call(
        field_edges_kernel, [((channels * plane_count * row_count, breadth), F32)], [edge_cols],
        conv_flops // 10, (*beside, acc, weight_bwd),
    )
    (sums,) = call(
        functools.partial(join_kernel, axis="gz", bit=2), [((rows // 2, 128), BF16)], [], 0,
        (sums, flip(sums, "gz", 2)),
    )
    sums, (field,) = tied(sums, field)
    grad_conv, grad_down = call(
        functools.partial(unpack_kernel, scale=grad_scale),
        [(conv_weight.shape, F32), (down_weight.shape, F32)], [((rows, 128), BF16)], 0,
        (sums, flip(sums, "gy", 1)),
    )
    section_out = section_out.reshape(out_channels, plane_count // 2, -1)
    return (section_out, field.reshape(features.shape), grad_conv, grad_down)


def solution(mesh):
    return jax.shard_map(
        body,
        mesh=mesh,
        in_specs=(P(None, "gz", "gy", None), P(), P(), P(None, "gz", "gy")),
        out_specs=(P(None, "gz", "gy"), P(None, "gz", "gy", None), P(), P()),
        check_vma=False,
    )
```

```python
import functools
import math

import jax
import jax.numpy as jnp
from jax import lax
from jax.experimental import pallas as pl
from jax.experimental.pallas import tpu as pltpu
from jax.sharding import PartitionSpec as P

F32 = jnp.float32
BF16 = jnp.bfloat16
PARAMS = pltpu.CompilerParams(vmem_limit_bytes=24 * 1024 * 1024)


def call(kernel, outs, scratch, flops, operands):
    moved = sum(x.size * x.dtype.itemsize for x in operands)
    moved += sum(math.prod(s) * jnp.dtype(d).itemsize for s, d in outs)
    vmem = pl.BlockSpec(memory_space=pltpu.VMEM)
    return pl.pallas_call(
        kernel,
        out_shape=[jax.ShapeDtypeStruct(s, d) for s, d in outs],
        in_specs=[vmem] * len(operands),
        out_specs=[vmem] * len(outs),
        scratch_shapes=[pltpu.VMEM(s, d) for s, d in scratch],
        compiler_params=PARAMS,
        cost_estimate=pl.CostEstimate(flops=flops, bytes_accessed=moved, transcendentals=0),
    )(*operands)


def is_even(axis):
    return lax.rem(lax.axis_index(axis), 2) == 0


def choose(cond, yes, no):
    return jnp.where(jnp.broadcast_to(cond, yes.shape), yes, no)


def lines_kernel(f_ref, near_ref, far_ref, near_row, far_row, wide):
    channels, planes, rows, breadth = f_ref.shape
    wide[...] = f_ref[...].astype(F32).reshape(channels * planes * rows, breadth)
    even = is_even("gz")
    ends = {}
    for y in range(rows):
        low, high = ends[y] = [
            wide[pl.ds(z * rows + y, channels, stride=planes * rows), :].astype(BF16) for z in range(2)
        ]
        near_ref[y] = choose(even, high, low)
        far_ref[y] = choose(even, low, high)
    even_y = is_even("gy")
    for z in range(2):
        near_row[z] = choose(even_y, ends[rows - 1][z], ends[0][z])
        far_row[z] = choose(even_y, ends[0][z], ends[rows - 1][z])


def copy_kernel(x, out):
    out[...] = x[...]


def outer_rows_kernel(near_in, far_in, near_ref, far_ref):
    rows = near_in.shape[0]
    even_z, even_y = is_even("gz"), is_even("gy")
    for p, (one, other) in enumerate(((far_in, near_in), (near_in, far_in))):
        first = choose(even_z, one[0], other[0])
        last = choose(even_z, one[rows - 1], other[rows - 1])
        near_ref[p] = choose(even_y, last, first)
        far_ref[p] = choose(even_y, first, last)


def edges_kernel(near, far, near_in, far_in, near_ref, far_ref):
    rows = near.shape[0]
    even_z, even_y = is_even("gz"), is_even("gy")

    def put(p, one, other):
        first = choose(even_z, one[0], other[0])
        last = choose(even_z, one[rows - 1], other[rows - 1])
        near_ref[p] = choose(even_y, last, first)
        far_ref[p] = choose(even_y, first, last)

    put(0, far_in, near_in)
    put(1, far, near)
    put(2, near, far)
    put(3, near_in, far_in)


def put_columns(cols, p, q, line):
    channels = line.shape[0]
    wide = line.astype(F32)
    cols[p, q, 0:channels] = pltpu.roll(wide, 1, 1).astype(BF16)
    cols[p, q, channels : 2 * channels] = line
    cols[p, q, 2 * channels : 3 * channels] = pltpu.roll(wide, line.shape[1] - 1, 1).astype(BF16)


def fill_columns(cols, near, far):
    rows = near.shape[0]
    even = is_even("gz")

    def step(y, carry):
        put_columns(cols, 0, y + 1, choose(even, far[y], near[y]))
        put_columns(cols, 1, y + 1, choose(even, near[y], far[y]))
        return carry

    lax.fori_loop(0, rows, step, 0, unroll=2)
    for p in range(2):
        for q in (0, rows + 1):
            cols[p, q] = jnp.zeros(cols.shape[2:], BF16)


def fill_rows(cols, near, far):
    even = is_even("gy")
    for p in range(near.shape[0]):
        put_columns(cols, p, 0, choose(even, far[p], near[p]))
        put_columns(cols, p, 1, choose(even, near[p], far[p]))


def dot(lhs, rhs):
    return jnp.dot(lhs, rhs, preferred_element_type=F32)


def taps(w_ref, b, first, last):
    return jnp.concatenate([w_ref[a, b] for a in range(first, last)], axis=0)


def window(cols, p, q):
    return jnp.concatenate([cols[p, q], cols[p, q + 1]], axis=1)


def inner_terms(cols, w_ref, y):
    acc = None
    for b in range(3):
        for p in range(2):
            term = dot(taps(w_ref, b, p, p + 2), window(cols, p, y + b))
            acc = term if acc is None else acc + term
    half = acc.shape[0] // 2
    return acc[half:], acc[:half]


def outer_terms(cols, w_ref, y):
    lower = upper = None
    for b in range(3):
        low, high = dot(w_ref[0, b], window(cols, 0, y + b)), dot(w_ref[2, b], window(cols, 1, y + b))
        lower = low if lower is None else lower + low
        upper = high if upper is None else upper + high
    return lower, upper


def edge_terms(edges, w_ref, side):
    b = 2 * side
    half = w_ref.shape[2]
    acc = dot(taps(w_ref, b, 0, 2), edges[1, side]) + dot(taps(w_ref, b, 1, 3), edges[2, side])
    return acc[half:] + dot(w_ref[0, b], edges[0, side]), acc[:half] + dot(w_ref[2, b], edges[3, side])


def inner_kernel(near, far, w_ref, d_ref, cot_ref, cols, acc_ref, grad_ref, up):
    rows, channels, breadth = near.shape
    fill_columns(cols, near, far)
    source = lax.broadcasted_iota(jnp.int32, (breadth, 2 * breadth), 0)
    target = lax.broadcasted_iota(jnp.int32, (breadth, 2 * breadth), 1)
    spread = jnp.where(source == target // 2, 1.0, 0.0).astype(BF16)
    for pair in range(rows // 4):
        both = dot(cot_ref[:, pair * breadth : (pair + 1) * breadth], spread)
        up[:, 2 * pair * breadth : 2 * (pair + 1) * breadth] = both.astype(BF16)
    even = lax.broadcasted_iota(jnp.int32, (channels, breadth), 1) % 2 == 0
    for a in range(2):
        for b in range(2):
            terms = lax.dot_general(d_ref[a, b], up[...], (((0,), (0,)), ((), ())), preferred_element_type=F32)
            for t in range(rows // 2):
                part = terms[:, t * breadth : (t + 1) * breadth]
                grad_ref[a, 2 * t + b] = jnp.where(even, part[0:channels], part[channels:])

    def step(t, carry):
        y = 2 * t
        for z, lines in enumerate(inner_terms(cols, w_ref, y)):
            for b in range(2):
                acc_ref[z, y + b] = lines[:, b * breadth : (b + 1) * breadth]
        return carry

    lax.fori_loop(0, rows // 2, step, 0)


def gated(preact, grad):
    sig = 1.0 / (1.0 + jnp.exp(-preact))
    return (preact * sig).astype(BF16), (grad * sig * (1.0 + preact * (1.0 - sig))).astype(BF16)


def outer_kernel(
    near, far, near_row, far_row, w_ref, acc_ref, grad_ref, cols, edges, side_ref, near_ref, far_ref, h_ref
):
    rows, channels, breadth = near.shape
    fill_columns(cols, near, far)
    fill_rows(edges, near_row, far_row)
    beside = []
    for side in range(2):
        terms = dot(taps(w_ref, 2 * side, 0, 2), edges[0, side]) + dot(taps(w_ref, 2 * side, 1, 3), edges[1, side])
        beside.append((terms[channels:], terms[:channels]))
    even = is_even("gz")
    for y in range(0, rows, 2):
        outer = outer_terms(cols, w_ref, y)
        for b in range(2):
            found = []
            for z in range(2):
                preact = acc_ref[z, y + b] + outer[z][:, b * breadth : (b + 1) * breadth]
                if y + b in (0, rows - 1):
                    side_ref[z, b] = preact + beside[b][z]
                else:
                    h_ref[z, y + b], gate = gated(preact, grad_ref[z, y + b])
                    found.append(gate)
            if len(found) > 0:
                near_ref[y + b] = choose(even, found[1], found[0])
                far_ref[y + b] = choose(even, found[0], found[1])


def gate_kernel(near, far, side_ref, near_in, far_in, h_in, grad_ref, w_ref, edges, near_ref, far_ref, h_ref):
    rows = near_in.shape[0]
    fill_rows(edges, near, far)
    even = is_even("gz")
    for side, y in enumerate((0, rows - 1)):
        terms = [dot(w_ref[2 * z, 2 * side], edges[z, side]) for z in range(2)]
        found = []
        for z in range(2):
            h_ref[z, y], gate = gated(side_ref[z, side] + terms[z], grad_ref[z, y])
            found.append(gate)
        near_ref[y] = choose(even, found[1], found[0])
        far_ref[y] = choose(even, found[0], found[1])
    for y in range(1, rows - 1):
        near_ref[y] = near_in[y]
        far_ref[y] = far_in[y]
        for z in range(2):
            h_ref[z, y] = h_in[z, y]


def coarse_hidden(h_ref):
    rows, channels, breadth = h_ref.shape[1:]
    source = lax.broadcasted_iota(jnp.int32, (2 * breadth, 2 * breadth), 0)
    target = lax.broadcasted_iota(jnp.int32, (2 * breadth, 2 * breadth), 1)
    wanted = 2 * (target % breadth) + target // breadth
    pick = jnp.where(source == wanted, 1.0, 0.0).astype(BF16)
    pairs = rows // 4
    both = [
        jnp.concatenate([h_ref[a, 4 * pair + b], h_ref[a, 4 * pair + 2 + b]], axis=1)
        for a in range(2) for b in range(2) for pair in range(pairs)
    ]
    picked = dot(jnp.concatenate(both, axis=0), pick).astype(BF16)
    blocks = []
    for tap in range(4):
        parts = [picked[(tap * pairs + pair) * channels : (tap * pairs + pair + 1) * channels] for pair in range(pairs)]
        for e in range(2):
            blocks.append(jnp.concatenate([x[:, e * breadth : (e + 1) * breadth] for x in parts], axis=1))
    return jnp.concatenate(blocks, axis=0)


def section_kernel(h_ref, d_ref, out_ref):
    down = jnp.concatenate([d_ref[a, b] for a in range(2) for b in range(2)], axis=1)
    out_ref[...] = dot(down, coarse_hidden(h_ref)).astype(BF16)


def weight_grad_kernel(inner, outer, own_edges, edges, near, far, h_ref, cot_ref, keep, send, packed):
    rows, channels, breadth = near.shape
    across = (((1,), (1,)), ((), ()))
    even = is_even("gz")
    low = [choose(even, far[y], near[y]) for y in range(rows)]
    high = [choose(even, near[y], far[y]) for y in range(rows)]
    nothing = jnp.zeros((channels, breadth), BF16)

    def shifted(lines):
        return jnp.concatenate(
            [jnp.concatenate([nothing] * b + lines + [nothing] * (2 - b), axis=1) for b in range(3)], axis=0
        )

    low, high = shifted(low), shifted(high)
    both = jnp.concatenate([low, high], axis=0)

    def columns(p, q):
        planes, rows_beside, at = (inner, own_edges, p - 1) if p in (1, 2) else (outer, edges, p // 3)
        return rows_beside[at, q // (rows + 1)] if q in (0, rows + 1) else planes[at, q]

    parts = []
    for p in range(4):
        lines = jnp.concatenate([columns(p, q) for q in range(rows + 2)], axis=1)
        lhs = low if p == 0 else high if p == 3 else both
        parts.append(lax.dot_general(lhs, lines, across, preferred_element_type=F32))
    lane = lax.broadcasted_iota(jnp.int32, (channels // 2, breadth), 1)
    for a in range(3):
        for b in range(3):
            at = b * channels + (0 if a == 2 else 3 * channels)
            total = parts[a][b * channels : (b + 1) * channels] + parts[a + 1][at : at + channels]
            base = (a * 3 + b) * 3 * channels // 2
            packed[base : base + channels] = total[:, 0:breadth]
            rest = jnp.concatenate([total[:, breadth:], total[:, breadth:]], axis=1)
            mix = jnp.where(lane < channels, rest[0 : channels // 2], rest[channels // 2 :])
            packed[base + channels : base + 3 * channels // 2] = mix
    base = 9 * 3 * channels // 2
    height = cot_ref.shape[0]
    down = lax.dot_general(cot_ref[...], coarse_hidden(h_ref), across, preferred_element_type=F32)
    for tap in range(4):
        packed[base + tap * height : base + (tap + 1) * height] = down[:, tap * breadth : (tap + 1) * breadth]
    end = base + 4 * height
    if end < packed.shape[0]:
        packed[end:] = jnp.zeros((packed.shape[0] - end, packed.shape[1]), F32)
    split(packed, keep, send, owned_half())


def side_of(axis, bit):
    return lax.rem(lax.axis_index(axis) // bit, 2)


def owned_half():
    total = 0
    for axis in ("gz", "gy"):
        for k in range(lax.axis_size(axis).bit_length() - 1):
            total = total + side_of(axis, 1 << k)
    return lax.rem(total, 2)


def part(side, rows):
    return pl.ds(pl.multiple_of(side * rows, 16), rows)


def split(packed, keep, send, side):
    half = keep.shape[0]
    keep[...] = packed[part(side, half)]
    send[...] = packed[part(1 - side, half)].astype(BF16)


def halve_kernel(mine, other, keep, send, total, *, axis, bit):
    total[...] = mine[...] + other[...].astype(F32)
    split(total, keep, send, side_of(axis, bit))


def add_kernel(x, y, out):
    out[...] = (x[...].astype(F32) + y[...].astype(F32)).astype(BF16)


def join_kernel(mine, other, out, *, axis, bit):
    join(mine, other, out, side_of(axis, bit))


def join(mine, other, out, side):
    rows = mine.shape[0]
    out[part(side, rows)] = mine[...]
    out[part(1 - side, rows)] = other[...]


def field_kernel(near, far, near_in, far_in, w_ref, acc_ref, inner, outer):
    rows, channels, breadth = near.shape
    fill_columns(inner, near, far)
    fill_columns(outer, near_in, far_in)

    def step(t, carry):
        y = 2 * t
        own = inner_terms(inner, w_ref, y)
        rest = outer_terms(outer, w_ref, y)
        for z in range(2):
            total = own[z] + rest[z]
            for b in range(2):
                acc_ref[z, y + b] = total[:, b * breadth : (b + 1) * breadth]
        return carry

    lax.fori_loop(0, rows // 2, step, 0)


def field_edges_kernel(near, far, acc_ref, w_ref, out_ref, edges):
    rows, channels, breadth = acc_ref.shape[1:]
    fill_rows(edges, near, far)
    sides = [edge_terms(edges, w_ref, side) for side in range(2)]
    for z in range(2):
        for y in range(rows):
            line = acc_ref[z, y]
            if y in (0, rows - 1):
                line = line + sides[0 if y == 0 else 1][z]
            out_ref[pl.ds(z * rows + y, channels, stride=2 * rows), :] = line


def unpack_kernel(mine, other, conv_ref, down_ref, sums_ref, *, scale):
    join(mine, other, sums_ref, owned_half())
    channels = conv_ref.shape[2]
    for a in range(3):
        for b in range(3):
            base = (a * 3 + b) * 3 * channels // 2
            conv_ref[a, b, :, 0 : 2 * channels] = sums_ref[base : base + channels].astype(F32) * scale
            rest = sums_ref[base + channels : base + 3 * channels // 2].astype(F32) * scale
            conv_ref[a, b, 0 : channels // 2, 2 * channels :] = rest[:, 0:channels]
            conv_ref[a, b, channels // 2 :, 2 * channels :] = rest[:, channels:]
    base = 9 * 3 * channels // 2
    height = down_ref.shape[2]
    for a in range(2):
        for b in range(2):
            at = base + (2 * a + b) * height
            down_ref[a, b] = sums_ref[at : at + height].astype(F32) * scale


def swap(cells, axis, low):
    count = lax.axis_size(axis)
    pairs = [(i % count, (i + 1) % count) for i in range(low, low + count, 2)]
    return lax.ppermute(cells, axis, pairs + [(b, a) for a, b in pairs])


def flip(cells, axis, bit):
    row = lax.axis_size("gy")
    mask = bit * row | 1 if axis == "gz" else bit | 1
    return lax.ppermute(cells, ("gz", "gy"), [(i, i ^ mask) for i in range(lax.axis_size("gz") * row)])


def tied(first, *others):
    found = lax.optimization_barrier((first, *others))
    return found[0], tuple(found[1:])


def swapped(near, far, axis):
    return swap(near, axis, 0), swap(far, axis, 1)


def body(features, conv_weight, down_weight, cotangent):
    channels, plane_count, row_count, breadth = features.shape
    out_channels = down_weight.shape[2]
    count = lax.axis_size("gz") * lax.axis_size("gy")
    grad_scale = 1.0 / math.sqrt(plane_count * row_count * breadth * count)
    (conv_weight,) = call(copy_kernel, [(conv_weight.shape, BF16)], [], 0, (conv_weight,))
    turned = conv_weight.reshape(3, 3, channels, 3, channels)[::-1, ::-1, :, ::-1]
    weight_bwd = turned.transpose(0, 1, 4, 3, 2).reshape(3, 3, channels, 3 * channels)
    cot = cotangent.reshape(out_channels, -1)
    plane = ((row_count, channels, breadth), BF16)
    edge = ((plane_count + 2, channels, breadth), BF16)
    cols = ((plane_count, row_count + 2, 3 * channels, breadth), BF16)
    edge_cols = ((plane_count + 2, 2, 3 * channels, breadth), BF16)
    lines = (plane_count, row_count, channels, breadth)
    conv_flops = 2 * 27 * channels * channels * plane_count * row_count * breadth

    pair = ((plane_count, channels, breadth), BF16)
    *own, near_row, far_row = call(
        lines_kernel, [plane, plane, pair, pair],
        [((channels * plane_count * row_count, breadth), F32)], 0, (features,),
    )
    outside = swapped(*own, "gz")
    beside = swapped(near_row, far_row, "gy")
    inner, acc, hidden_grad = call(
        inner_kernel, [cols, (lines, F32), (lines, F32)],
        [((out_channels, row_count // 2 * breadth), BF16)],
        2 * conv_flops // 3, (*own, conv_weight, down_weight, cot),
    )
    near, far, near_row, far_row, acc = lax.optimization_barrier((*outside, *beside, acc))
    outside, own_rows = (near, far), (near_row, far_row)
    beside = swapped(*call(outer_rows_kernel, [pair, pair], [], 0, outside), "gy")
    far, near = lax.optimization_barrier((beside[1], beside[0]))
    beside = (near, far)
    rows_cols = ((plane_count, 2, 3 * channels, breadth), BF16)
    outer, own_edges, *inside = call(
        outer_kernel,
        [cols, rows_cols, ((plane_count, 2, channels, breadth), F32), plane, plane, (lines, BF16)], [],
        conv_flops // 3, (*outside, *own_rows, conv_weight, acc, hidden_grad),
    )
    edges, near, far, hidden = call(
        gate_kernel, [rows_cols, plane, plane, (lines, BF16)], [], conv_flops // 10,
        (*beside, *inside, hidden_grad, conv_weight),
    )
    gates = (near, far)

    used = 27 * channels * channels // 128 + 4 * out_channels
    rows = -(-used // 128) * 128
    keep, send = call(
        weight_grad_kernel, [((rows // 2, 128), F32), ((rows // 2, 128), BF16)], [((rows, 128), F32)],
        conv_flops, (inner, outer, own_edges, edges, *gates, hidden, cot),
    )
    keep, gates = tied(keep, *gates)
    near, far = gates
    near_in = swap(near, "gz", 0)
    for level, (axis, bit) in enumerate((("gz", 2), ("gy", 2))):
        size = rows >> (level + 2)
        mine, got = keep, flip(send, *(("gy", 1), ("gz", 2))[level])
        keep, send = call(
            functools.partial(halve_kernel, axis=axis, bit=bit),
            [((size, 128), F32), ((size, 128), BF16)], [((2 * size, 128), F32)], 0, (mine, got),
        )
        if level == 0:
            keep, (far, hidden) = tied(keep, far, hidden)
            far_in = swap(far, "gz", 1)
            (section_out,) = call(
                section_kernel, [((out_channels, cot.shape[1]), BF16)], [], conv_flops // 10,
                (hidden, down_weight),
            )
    shard = ((rows // 8, 128), BF16)
    (sums,) = call(add_kernel, [shard], [], 0, (keep, flip(send, "gy", 2)))
    (sums,) = call(add_kernel, [shard], [], 0, (sums, flip(sums, "gz", 1)))
    sums, outside = tied(sums, near_in, far_in)
    sends = call(edges_kernel, [edge, edge], [], 0, (*gates, *outside))
    beside = swapped(*sends, "gy")
    (acc,) = call(
        field_kernel, [(lines, F32)], [cols, cols], conv_flops, (*gates, *outside, weight_bwd)
    )
    wide = [("gy", 1 << k) for k in range(2, lax.axis_size("gy").bit_length() - 1)]
    wide += [("gz", 1 << k) for k in range(2, lax.axis_size("gz").bit_length() - 1)]
    for axis, bit in wide:
        (sums,) = call(add_kernel, [shard], [], 0, (sums, flip(sums, axis, bit)))
    sums, (section_out,) = tied(sums, section_out)
    (sums,) = call(
        functools.partial(join_kernel, axis="gy", bit=2), [((rows // 4, 128), BF16)], [], 0,
        (sums, flip(sums, "gy", 2)),
    )
    sums, (acc, *beside) = tied(sums, acc, *beside)
    (field,) = call(
        field_edges_kernel, [((channels * plane_count * row_count, breadth), F32)], [edge_cols],
        conv_flops // 10, (*beside, acc, weight_bwd),
    )
    (sums,) = call(
        functools.partial(join_kernel, axis="gz", bit=2), [((rows // 2, 128), BF16)], [], 0,
        (sums, flip(sums, "gz", 2)),
    )
    sums, (field,) = tied(sums, field)
    grad_conv, grad_down = call(
        functools.partial(unpack_kernel, scale=grad_scale),
        [(conv_weight.shape, F32), (down_weight.shape, F32)], [((rows, 128), BF16)], 0,
        (sums, flip(sums, "gy", 1)),
    )
    section_out = section_out.reshape(out_channels, plane_count // 2, -1)
    return (section_out, field.reshape(features.shape), grad_conv, grad_down)


def solution(mesh):
    return jax.shard_map(
        body,
        mesh=mesh,
        in_specs=(P(None, "gz", "gy", None), P(), P(), P(None, "gz", "gy")),
        out_specs=(P(None, "gz", "gy"), P(None, "gz", "gy", None), P(), P()),
        check_vma=False,
    )
```

```python
import functools
import math

import jax
import jax.numpy as jnp
from jax import lax
from jax.experimental import pallas as pl
from jax.experimental.pallas import tpu as pltpu
from jax.sharding import PartitionSpec as P

F32 = jnp.float32
BF16 = jnp.bfloat16
PARAMS = pltpu.CompilerParams(vmem_limit_bytes=24 * 1024 * 1024)


def call(kernel, outs, scratch, flops, operands):
    moved = sum(x.size * x.dtype.itemsize for x in operands)
    moved += sum(math.prod(s) * jnp.dtype(d).itemsize for s, d in outs)
    vmem = pl.BlockSpec(memory_space=pltpu.VMEM)
    return pl.pallas_call(
        kernel,
        out_shape=[jax.ShapeDtypeStruct(s, d) for s, d in outs],
        in_specs=[vmem] * len(operands),
        out_specs=[vmem] * len(outs),
        scratch_shapes=[pltpu.VMEM(s, d) for s, d in scratch],
        compiler_params=PARAMS,
        cost_estimate=pl.CostEstimate(flops=flops, bytes_accessed=moved, transcendentals=0),
    )(*operands)


def is_even(axis):
    return lax.rem(lax.axis_index(axis), 2) == 0


def choose(cond, yes, no):
    return jnp.where(jnp.broadcast_to(cond, yes.shape), yes, no)


def lines_kernel(f_ref, near_ref, far_ref, near_row, far_row, wide):
    channels, planes, rows, breadth = f_ref.shape
    wide[...] = f_ref[...].astype(F32).reshape(channels * planes * rows, breadth)
    even = is_even("gz")
    ends = {}
    for y in range(rows):
        low, high = ends[y] = [
            wide[pl.ds(z * rows + y, channels, stride=planes * rows), :].astype(BF16) for z in range(2)
        ]
        near_ref[y] = choose(even, high, low)
        far_ref[y] = choose(even, low, high)
    even_y = is_even("gy")
    for z in range(2):
        near_row[z] = choose(even_y, ends[rows - 1][z], ends[0][z])
        far_row[z] = choose(even_y, ends[0][z], ends[rows - 1][z])


def fetch_kernel(*refs):
    *both, sems = refs
    count = len(both) // 2
    copies = [pltpu.make_async_copy(both[k], both[count + k], sems.at[k]) for k in range(count)]
    for copy in copies:
        copy.start()
    for copy in copies:
        copy.wait()


def fetch(*operands):
    return pl.pallas_call(
        fetch_kernel,
        out_shape=[jax.ShapeDtypeStruct(x.shape, x.dtype) for x in operands],
        in_specs=[pl.BlockSpec(memory_space=pltpu.HBM)] * len(operands),
        out_specs=[pl.BlockSpec(memory_space=pltpu.VMEM)] * len(operands),
        scratch_shapes=[pltpu.SemaphoreType.DMA((len(operands),))],
        compiler_params=PARAMS,
        cost_estimate=pl.CostEstimate(flops=0, bytes_accessed=2 * sum(x.size * 2 for x in operands), transcendentals=0),
    )(*operands)


def outer_rows_kernel(near_in, far_in, near_ref, far_ref):
    rows = near_in.shape[0]
    even_z, even_y = is_even("gz"), is_even("gy")
    for p, (one, other) in enumerate(((far_in, near_in), (near_in, far_in))):
        first = choose(even_z, one[0], other[0])
        last = choose(even_z, one[rows - 1], other[rows - 1])
        near_ref[p] = choose(even_y, last, first)
        far_ref[p] = choose(even_y, first, last)


def edges_kernel(near, far, near_in, far_in, near_ref, far_ref):
    rows = near.shape[0]
    even_z, even_y = is_even("gz"), is_even("gy")

    def put(p, one, other):
        first = choose(even_z, one[0], other[0])
        last = choose(even_z, one[rows - 1], other[rows - 1])
        near_ref[p] = choose(even_y, last, first)
        far_ref[p] = choose(even_y, first, last)

    put(0, far_in, near_in)
    put(1, far, near)
    put(2, near, far)
    put(3, near_in, far_in)


def put_columns(cols, p, q, line):
    channels = line.shape[0]
    wide = line.astype(F32)
    cols[p, q, 0:channels] = pltpu.roll(wide, 1, 1).astype(BF16)
    cols[p, q, channels : 2 * channels] = line
    cols[p, q, 2 * channels : 3 * channels] = pltpu.roll(wide, line.shape[1] - 1, 1).astype(BF16)


def fill_columns(cols, near, far):
    rows = near.shape[0]
    even = is_even("gz")

    def step(y, carry):
        put_columns(cols, 0, y + 1, choose(even, far[y], near[y]))
        put_columns(cols, 1, y + 1, choose(even, near[y], far[y]))
        return carry

    lax.fori_loop(0, rows, step, 0, unroll=2)
    for p in range(2):
        for q in (0, rows + 1):
            cols[p, q] = jnp.zeros(cols.shape[2:], BF16)


def fill_rows(cols, near, far):
    even = is_even("gy")
    for p in range(near.shape[0]):
        put_columns(cols, p, 0, choose(even, far[p], near[p]))
        put_columns(cols, p, 1, choose(even, near[p], far[p]))


def dot(lhs, rhs):
    return jnp.dot(lhs, rhs, preferred_element_type=F32)


def taps(w_ref, b, first, last):
    return jnp.concatenate([w_ref[a, b] for a in range(first, last)], axis=0)


def window(cols, p, q):
    return jnp.concatenate([cols[p, q], cols[p, q + 1]], axis=1)


def inner_terms(cols, w_ref, y):
    acc = None
    for b in range(3):
        for p in range(2):
            term = dot(taps(w_ref, b, p, p + 2), window(cols, p, y + b))
            acc = term if acc is None else acc + term
    half = acc.shape[0] // 2
    return acc[half:], acc[:half]


def outer_terms(cols, w_ref, y):
    lower = upper = None
    for b in range(3):
        low, high = dot(w_ref[0, b], window(cols, 0, y + b)), dot(w_ref[2, b], window(cols, 1, y + b))
        lower = low if lower is None else lower + low
        upper = high if upper is None else upper + high
    return lower, upper


def edge_terms(edges, w_ref, side):
    b = 2 * side
    half = w_ref.shape[2]
    acc = dot(taps(w_ref, b, 0, 2), edges[1, side]) + dot(taps(w_ref, b, 1, 3), edges[2, side])
    return acc[half:] + dot(w_ref[0, b], edges[0, side]), acc[:half] + dot(w_ref[2, b], edges[3, side])


def inner_kernel(near, far, w_ref, d_ref, cot_ref, cols, acc_ref, grad_ref, up):
    rows, channels, breadth = near.shape
    fill_columns(cols, near, far)
    source = lax.broadcasted_iota(jnp.int32, (breadth, 2 * breadth), 0)
    target = lax.broadcasted_iota(jnp.int32, (breadth, 2 * breadth), 1)
    spread = jnp.where(source == target // 2, 1.0, 0.0).astype(BF16)
    for pair in range(rows // 4):
        both = dot(cot_ref[:, pair * breadth : (pair + 1) * breadth], spread)
        up[:, 2 * pair * breadth : 2 * (pair + 1) * breadth] = both.astype(BF16)
    even = lax.broadcasted_iota(jnp.int32, (channels, breadth), 1) % 2 == 0
    for a in range(2):
        for b in range(2):
            terms = lax.dot_general(d_ref[a, b], up[...], (((0,), (0,)), ((), ())), preferred_element_type=F32)
            for t in range(rows // 2):
                part = terms[:, t * breadth : (t + 1) * breadth]
                grad_ref[a, 2 * t + b] = jnp.where(even, part[0:channels], part[channels:])

    def step(t, carry):
        y = 2 * t
        for z, lines in enumerate(inner_terms(cols, w_ref, y)):
            for b in range(2):
                acc_ref[z, y + b] = lines[:, b * breadth : (b + 1) * breadth]
        return carry

    lax.fori_loop(0, rows // 2, step, 0)


def gated(preact, grad):
    sig = 1.0 / (1.0 + jnp.exp(-preact))
    return (preact * sig).astype(BF16), (grad * sig * (1.0 + preact * (1.0 - sig))).astype(BF16)


def outer_kernel(
    near, far, near_row, far_row, w_ref, acc_ref, grad_ref, cols, edges, side_ref, near_ref, far_ref, h_ref
):
    rows, channels, breadth = near.shape
    fill_columns(cols, near, far)
    fill_rows(edges, near_row, far_row)
    beside = []
    for side in range(2):
        terms = dot(taps(w_ref, 2 * side, 0, 2), edges[0, side]) + dot(taps(w_ref, 2 * side, 1, 3), edges[1, side])
        beside.append((terms[channels:], terms[:channels]))
    even = is_even("gz")
    for y in range(0, rows, 2):
        outer = outer_terms(cols, w_ref, y)
        for b in range(2):
            found = []
            for z in range(2):
                preact = acc_ref[z, y + b] + outer[z][:, b * breadth : (b + 1) * breadth]
                if y + b in (0, rows - 1):
                    side_ref[z, b] = preact + beside[b][z]
                else:
                    h_ref[z, y + b], gate = gated(preact, grad_ref[z, y + b])
                    found.append(gate)
            if len(found) > 0:
                near_ref[y + b] = choose(even, found[1], found[0])
                far_ref[y + b] = choose(even, found[0], found[1])


def gate_kernel(near, far, side_ref, near_in, far_in, h_in, grad_ref, w_ref, edges, near_ref, far_ref, h_ref):
    rows = near_in.shape[0]
    fill_rows(edges, near, far)
    even = is_even("gz")
    for side, y in enumerate((0, rows - 1)):
        terms = [dot(w_ref[2 * z, 2 * side], edges[z, side]) for z in range(2)]
        found = []
        for z in range(2):
            h_ref[z, y], gate = gated(side_ref[z, side] + terms[z], grad_ref[z, y])
            found.append(gate)
        near_ref[y] = choose(even, found[1], found[0])
        far_ref[y] = choose(even, found[0], found[1])
    for y in range(1, rows - 1):
        near_ref[y] = near_in[y]
        far_ref[y] = far_in[y]
        for z in range(2):
            h_ref[z, y] = h_in[z, y]


def coarse_hidden(h_ref):
    rows, channels, breadth = h_ref.shape[1:]
    source = lax.broadcasted_iota(jnp.int32, (2 * breadth, 2 * breadth), 0)
    target = lax.broadcasted_iota(jnp.int32, (2 * breadth, 2 * breadth), 1)
    wanted = 2 * (target % breadth) + target // breadth
    pick = jnp.where(source == wanted, 1.0, 0.0).astype(BF16)
    pairs = rows // 4
    both = [
        jnp.concatenate([h_ref[a, 4 * pair + b], h_ref[a, 4 * pair + 2 + b]], axis=1)
        for a in range(2) for b in range(2) for pair in range(pairs)
    ]
    picked = dot(jnp.concatenate(both, axis=0), pick).astype(BF16)
    blocks = []
    for tap in range(4):
        parts = [picked[(tap * pairs + pair) * channels : (tap * pairs + pair + 1) * channels] for pair in range(pairs)]
        for e in range(2):
            blocks.append(jnp.concatenate([x[:, e * breadth : (e + 1) * breadth] for x in parts], axis=1))
    return jnp.concatenate(blocks, axis=0)


def section_kernel(h_ref, d_ref, out_ref):
    down = jnp.concatenate([d_ref[a, b] for a in range(2) for b in range(2)], axis=1)
    out_ref[...] = dot(down, coarse_hidden(h_ref)).astype(BF16)


def weight_grad_kernel(inner, outer, own_edges, edges, near, far, h_ref, cot_ref, keep, send, packed):
    rows, channels, breadth = near.shape
    across = (((1,), (1,)), ((), ()))
    even = is_even("gz")
    low = [choose(even, far[y], near[y]) for y in range(rows)]
    high = [choose(even, near[y], far[y]) for y in range(rows)]
    nothing = jnp.zeros((channels, breadth), BF16)

    def shifted(lines):
        return jnp.concatenate(
            [jnp.concatenate([nothing] * b + lines + [nothing] * (2 - b), axis=1) for b in range(3)], axis=0
        )

    low, high = shifted(low), shifted(high)
    both = jnp.concatenate([low, high], axis=0)

    def columns(p, q):
        planes, rows_beside, at = (inner, own_edges, p - 1) if p in (1, 2) else (outer, edges, p // 3)
        return rows_beside[at, q // (rows + 1)] if q in (0, rows + 1) else planes[at, q]

    parts = []
    for p in range(4):
        lines = jnp.concatenate([columns(p, q) for q in range(rows + 2)], axis=1)
        lhs = low if p == 0 else high if p == 3 else both
        parts.append(lax.dot_general(lhs, lines, across, preferred_element_type=F32))
    lane = lax.broadcasted_iota(jnp.int32, (channels // 2, breadth), 1)
    for a in range(3):
        for b in range(3):
            at = b * channels + (0 if a == 2 else 3 * channels)
            total = parts[a][b * channels : (b + 1) * channels] + parts[a + 1][at : at + channels]
            base = (a * 3 + b) * 3 * channels // 2
            packed[base : base + channels] = total[:, 0:breadth]
            rest = jnp.concatenate([total[:, breadth:], total[:, breadth:]], axis=1)
            mix = jnp.where(lane < channels, rest[0 : channels // 2], rest[channels // 2 :])
            packed[base + channels : base + 3 * channels // 2] = mix
    base = 9 * 3 * channels // 2
    height = cot_ref.shape[0]
    down = lax.dot_general(cot_ref[...], coarse_hidden(h_ref), across, preferred_element_type=F32)
    for tap in range(4):
        packed[base + tap * height : base + (tap + 1) * height] = down[:, tap * breadth : (tap + 1) * breadth]
    end = base + 4 * height
    if end < packed.shape[0]:
        packed[end:] = jnp.zeros((packed.shape[0] - end, packed.shape[1]), F32)
    split(packed, keep, send, owned_half())


def side_of(axis, bit):
    return lax.rem(lax.axis_index(axis) // bit, 2)


def owned_half():
    total = 0
    for axis in ("gz", "gy"):
        for k in range(lax.axis_size(axis).bit_length() - 1):
            total = total + side_of(axis, 1 << k)
    return lax.rem(total, 2)


def part(side, rows):
    return pl.ds(pl.multiple_of(side * rows, 16), rows)


def split(packed, keep, send, side):
    half = keep.shape[0]
    keep[...] = packed[part(side, half)]
    send[...] = packed[part(1 - side, half)].astype(BF16)


def halve_kernel(mine, other, keep, send, total, *, axis, bit):
    total[...] = mine[...] + other[...].astype(F32)
    split(total, keep, send, side_of(axis, bit))


def add_kernel(x, y, out):
    out[...] = (x[...].astype(F32) + y[...].astype(F32)).astype(BF16)


def join_kernel(mine, other, out, *, axis, bit):
    join(mine, other, out, side_of(axis, bit))


def join(mine, other, out, side):
    rows = mine.shape[0]
    out[part(side, rows)] = mine[...]
    out[part(1 - side, rows)] = other[...]


def field_kernel(near, far, near_in, far_in, w_ref, acc_ref, inner, outer):
    rows, channels, breadth = near.shape
    fill_columns(inner, near, far)
    fill_columns(outer, near_in, far_in)

    def step(t, carry):
        y = 2 * t
        own = inner_terms(inner, w_ref, y)
        rest = outer_terms(outer, w_ref, y)
        for z in range(2):
            total = own[z] + rest[z]
            for b in range(2):
                acc_ref[z, y + b] = total[:, b * breadth : (b + 1) * breadth]
        return carry

    lax.fori_loop(0, rows // 2, step, 0)


def field_edges_kernel(near, far, acc_ref, w_ref, out_ref, edges):
    rows, channels, breadth = acc_ref.shape[1:]
    fill_rows(edges, near, far)
    sides = [edge_terms(edges, w_ref, side) for side in range(2)]
    for z in range(2):
        for y in range(rows):
            line = acc_ref[z, y]
            if y in (0, rows - 1):
                line = line + sides[0 if y == 0 else 1][z]
            out_ref[pl.ds(z * rows + y, channels, stride=2 * rows), :] = line


def unpack_kernel(mine, other, conv_ref, down_ref, sums_ref, *, scale):
    join(mine, other, sums_ref, owned_half())
    channels = conv_ref.shape[2]
    for a in range(3):
        for b in range(3):
            base = (a * 3 + b) * 3 * channels // 2
            conv_ref[a, b, :, 0 : 2 * channels] = sums_ref[base : base + channels].astype(F32) * scale
            rest = sums_ref[base + channels : base + 3 * channels // 2].astype(F32) * scale
            conv_ref[a, b, 0 : channels // 2, 2 * channels :] = rest[:, 0:channels]
            conv_ref[a, b, channels // 2 :, 2 * channels :] = rest[:, channels:]
    base = 9 * 3 * channels // 2
    height = down_ref.shape[2]
    for a in range(2):
        for b in range(2):
            at = base + (2 * a + b) * height
            down_ref[a, b] = sums_ref[at : at + height].astype(F32) * scale


def swap(cells, axis, low):
    count = lax.axis_size(axis)
    pairs = [(i % count, (i + 1) % count) for i in range(low, low + count, 2)]
    return lax.ppermute(cells, axis, pairs + [(b, a) for a, b in pairs])


def flip(cells, axis, bit):
    row = lax.axis_size("gy")
    mask = bit * row | 1 if axis == "gz" else bit | 1
    return lax.ppermute(cells, ("gz", "gy"), [(i, i ^ mask) for i in range(lax.axis_size("gz") * row)])


def tied(first, *others):
    found = lax.optimization_barrier((first, *others))
    return found[0], tuple(found[1:])


def swapped(near, far, axis):
    return swap(near, axis, 0), swap(far, axis, 1)


def body(features, conv_weight, down_weight, cotangent):
    channels, plane_count, row_count, breadth = features.shape
    out_channels = down_weight.shape[2]
    count = lax.axis_size("gz") * lax.axis_size("gy")
    grad_scale = 1.0 / math.sqrt(plane_count * row_count * breadth * count)
    cot = cotangent.reshape(out_channels, -1)
    conv_weight, down_weight, cot = fetch(conv_weight, down_weight, cot)
    turned = conv_weight.reshape(3, 3, channels, 3, channels)[::-1, ::-1, :, ::-1]
    weight_bwd = turned.transpose(0, 1, 4, 3, 2).reshape(3, 3, channels, 3 * channels)
    plane = ((row_count, channels, breadth), BF16)
    edge = ((plane_count + 2, channels, breadth), BF16)
    cols = ((plane_count, row_count + 2, 3 * channels, breadth), BF16)
    edge_cols = ((plane_count + 2, 2, 3 * channels, breadth), BF16)
    lines = (plane_count, row_count, channels, breadth)
    conv_flops = 2 * 27 * channels * channels * plane_count * row_count * breadth

    pair = ((plane_count, channels, breadth), BF16)
    *own, near_row, far_row = call(
        lines_kernel, [plane, plane, pair, pair],
        [((channels * plane_count * row_count, breadth), F32)], 0, (features,),
    )
    outside = swapped(*own, "gz")
    beside = swapped(near_row, far_row, "gy")
    inner, acc, hidden_grad = call(
        inner_kernel, [cols, (lines, F32), (lines, F32)],
        [((out_channels, row_count // 2 * breadth), BF16)],
        2 * conv_flops // 3, (*own, conv_weight, down_weight, cot),
    )
    near, far, near_row, far_row, acc = lax.optimization_barrier((*outside, *beside, acc))
    outside, own_rows = (near, far), (near_row, far_row)
    beside = swapped(*call(outer_rows_kernel, [pair, pair], [], 0, outside), "gy")
    far, near = lax.optimization_barrier((beside[1], beside[0]))
    beside = (near, far)
    rows_cols = ((plane_count, 2, 3 * channels, breadth), BF16)
    outer, own_edges, *inside = call(
        outer_kernel,
        [cols, rows_cols, ((plane_count, 2, channels, breadth), F32), plane, plane, (lines, BF16)], [],
        conv_flops // 3, (*outside, *own_rows, conv_weight, acc, hidden_grad),
    )
    edges, near, far, hidden = call(
        gate_kernel, [rows_cols, plane, plane, (lines, BF16)], [], conv_flops // 10,
        (*beside, *inside, hidden_grad, conv_weight),
    )
    gates = (near, far)

    used = 27 * channels * channels // 128 + 4 * out_channels
    rows = -(-used // 128) * 128
    keep, send = call(
        weight_grad_kernel, [((rows // 2, 128), F32), ((rows // 2, 128), BF16)], [((rows, 128), F32)],
        conv_flops, (inner, outer, own_edges, edges, *gates, hidden, cot),
    )
    keep, gates = tied(keep, *gates)
    near, far = gates
    near_in = swap(near, "gz", 0)
    for level, (axis, bit) in enumerate((("gz", 2), ("gy", 2))):
        size = rows >> (level + 2)
        mine, got = keep, flip(send, *(("gy", 1), ("gz", 2))[level])
        keep, send = call(
            functools.partial(halve_kernel, axis=axis, bit=bit),
            [((size, 128), F32), ((size, 128), BF16)], [((2 * size, 128), F32)], 0, (mine, got),
        )
        if level == 0:
            keep, (far, hidden) = tied(keep, far, hidden)
            far_in = swap(far, "gz", 1)
            (section_out,) = call(
                section_kernel, [((out_channels, cot.shape[1]), BF16)], [], conv_flops // 10,
                (hidden, down_weight),
            )
    shard = ((rows // 8, 128), BF16)
    (sums,) = call(add_kernel, [shard], [], 0, (keep, flip(send, "gy", 2)))
    (sums,) = call(add_kernel, [shard], [], 0, (sums, flip(sums, "gz", 1)))
    sums, outside = tied(sums, near_in, far_in)
    sends = call(edges_kernel, [edge, edge], [], 0, (*gates, *outside))
    beside = swapped(*sends, "gy")
    (acc,) = call(
        field_kernel, [(lines, F32)], [cols, cols], conv_flops, (*gates, *outside, weight_bwd)
    )
    wide = [("gy", 1 << k) for k in range(2, lax.axis_size("gy").bit_length() - 1)]
    wide += [("gz", 1 << k) for k in range(2, lax.axis_size("gz").bit_length() - 1)]
    for axis, bit in wide:
        (sums,) = call(add_kernel, [shard], [], 0, (sums, flip(sums, axis, bit)))
    sums, (section_out,) = tied(sums, section_out)
    (sums,) = call(
        functools.partial(join_kernel, axis="gy", bit=2), [((rows // 4, 128), BF16)], [], 0,
        (sums, flip(sums, "gy", 2)),
    )
    sums, (acc, *beside) = tied(sums, acc, *beside)
    (field,) = call(
        field_edges_kernel, [((channels * plane_count * row_count, breadth), F32)], [edge_cols],
        conv_flops // 10, (*beside, acc, weight_bwd),
    )
    (sums,) = call(
        functools.partial(join_kernel, axis="gz", bit=2), [((rows // 2, 128), BF16)], [], 0,
        (sums, flip(sums, "gz", 2)),
    )
    sums, (field,) = tied(sums, field)
    grad_conv, grad_down = call(
        functools.partial(unpack_kernel, scale=grad_scale),
        [(conv_weight.shape, F32), (down_weight.shape, F32)], [((rows, 128), BF16)], 0,
        (sums, flip(sums, "gy", 1)),
    )
    section_out = section_out.reshape(out_channels, plane_count // 2, -1)
    return (section_out, field.reshape(features.shape), grad_conv, grad_down)


def solution(mesh):
    return jax.shard_map(
        body,
        mesh=mesh,
        in_specs=(P(None, "gz", "gy", None), P(), P(), P(None, "gz", "gy")),
        out_specs=(P(None, "gz", "gy"), P(None, "gz", "gy", None), P(), P()),
        check_vma=False,
    )
```

```python
import functools
import math

import jax
import jax.numpy as jnp
from jax import lax
from jax.experimental import pallas as pl
from jax.experimental.pallas import tpu as pltpu
from jax.sharding import PartitionSpec as P

F32 = jnp.float32
BF16 = jnp.bfloat16
PARAMS = pltpu.CompilerParams(vmem_limit_bytes=24 * 1024 * 1024)


def call(kernel, outs, scratch, flops, operands):
    moved = sum(x.size * x.dtype.itemsize for x in operands)
    moved += sum(math.prod(s) * jnp.dtype(d).itemsize for s, d in outs)
    vmem = pl.BlockSpec(memory_space=pltpu.VMEM)
    return pl.pallas_call(
        kernel,
        out_shape=[jax.ShapeDtypeStruct(s, d) for s, d in outs],
        in_specs=[vmem] * len(operands),
        out_specs=[vmem] * len(outs),
        scratch_shapes=[pltpu.VMEM(s, d) for s, d in scratch],
        compiler_params=PARAMS,
        cost_estimate=pl.CostEstimate(flops=flops, bytes_accessed=moved, transcendentals=0),
    )(*operands)


def is_even(axis):
    return lax.rem(lax.axis_index(axis), 2) == 0


def choose(cond, yes, no):
    return jnp.where(jnp.broadcast_to(cond, yes.shape), yes, no)


def lines_kernel(f_ref, near_ref, far_ref, near_row, far_row, wide):
    channels, planes, rows, breadth = f_ref.shape
    wide[...] = f_ref[...].astype(F32).reshape(channels * planes * rows, breadth)
    even = is_even("gz")
    ends = {}
    for y in range(rows):
        low, high = ends[y] = [
            wide[pl.ds(z * rows + y, channels, stride=planes * rows), :].astype(BF16) for z in range(2)
        ]
        near_ref[y] = choose(even, high, low)
        far_ref[y] = choose(even, low, high)
    even_y = is_even("gy")
    for z in range(2):
        near_row[z] = choose(even_y, ends[rows - 1][z], ends[0][z])
        far_row[z] = choose(even_y, ends[0][z], ends[rows - 1][z])


def fetch_kernel(*refs):
    *both, sems = refs
    count = len(both) // 2
    copies = [pltpu.make_async_copy(both[k], both[count + k], sems.at[k]) for k in range(count)]
    for copy in copies:
        copy.start()
    for copy in copies:
        copy.wait()


def fetch(*operands):
    return pl.pallas_call(
        fetch_kernel,
        out_shape=[jax.ShapeDtypeStruct(x.shape, x.dtype) for x in operands],
        in_specs=[pl.BlockSpec(memory_space=pltpu.HBM)] * len(operands),
        out_specs=[pl.BlockSpec(memory_space=pltpu.VMEM)] * len(operands),
        scratch_shapes=[pltpu.SemaphoreType.DMA((len(operands),))],
        compiler_params=PARAMS,
        cost_estimate=pl.CostEstimate(flops=0, bytes_accessed=2 * sum(x.size * 2 for x in operands), transcendentals=0),
    )(*operands)


def outer_rows_kernel(near_in, far_in, near_ref, far_ref):
    rows = near_in.shape[0]
    even_z, even_y = is_even("gz"), is_even("gy")
    for p, (one, other) in enumerate(((far_in, near_in), (near_in, far_in))):
        first = choose(even_z, one[0], other[0])
        last = choose(even_z, one[rows - 1], other[rows - 1])
        near_ref[p] = choose(even_y, last, first)
        far_ref[p] = choose(even_y, first, last)


def edges_kernel(near, far, near_in, far_in, near_ref, far_ref):
    rows = near.shape[0]
    even_z, even_y = is_even("gz"), is_even("gy")

    def put(p, one, other):
        first = choose(even_z, one[0], other[0])
        last = choose(even_z, one[rows - 1], other[rows - 1])
        near_ref[p] = choose(even_y, last, first)
        far_ref[p] = choose(even_y, first, last)

    put(0, far_in, near_in)
    put(1, far, near)
    put(2, near, far)
    put(3, near_in, far_in)


def put_columns(cols, p, q, line):
    channels = line.shape[0]
    wide = line.astype(F32)
    cols[p, q, 0:channels] = pltpu.roll(wide, 1, 1).astype(BF16)
    cols[p, q, channels : 2 * channels] = line
    cols[p, q, 2 * channels : 3 * channels] = pltpu.roll(wide, line.shape[1] - 1, 1).astype(BF16)


def fill_columns(cols, near, far):
    rows = near.shape[0]
    even = is_even("gz")

    def step(y, carry):
        put_columns(cols, 0, y + 1, choose(even, far[y], near[y]))
        put_columns(cols, 1, y + 1, choose(even, near[y], far[y]))
        return carry

    lax.fori_loop(0, rows, step, 0, unroll=2)
    for p in range(2):
        for q in (0, rows + 1):
            cols[p, q] = jnp.zeros(cols.shape[2:], BF16)


def fill_rows(cols, near, far):
    even = is_even("gy")
    for p in range(near.shape[0]):
        put_columns(cols, p, 0, choose(even, far[p], near[p]))
        put_columns(cols, p, 1, choose(even, near[p], far[p]))


def dot(lhs, rhs):
    return jnp.dot(lhs, rhs, preferred_element_type=F32)


def taps(w_ref, b, first, last):
    return jnp.concatenate([w_ref[a, b] for a in range(first, last)], axis=0)


def window(cols, p, q):
    return jnp.concatenate([cols[p, q], cols[p, q + 1]], axis=1)


def add_terms(acc, w_ref, inner, outer=None):
    channels, breadth = acc.shape[2:]
    acc[...] = jnp.zeros(acc.shape, F32)
    stacks = [jnp.concatenate([taps(w_ref, b, p, p + 2) for b in range(3)], axis=0) for p in range(2)]
    if outer is not None:
        low, high = (jnp.concatenate([w_ref[a, b] for b in range(3)], axis=0) for a in (0, 2))

    def step(t, carry):
        q = 2 * t
        own = dot(stacks[0], window(inner, 0, q)) + dot(stacks[1], window(inner, 1, q))
        if outer is not None:
            rest = [dot(low, window(outer, 0, q)), dot(high, window(outer, 1, q))]
        for b in range(3):
            for z in range(2):
                at = (2 * b + 1 - z) * channels
                block = own[at : at + channels]
                if outer is not None:
                    block = block + rest[z][b * channels : (b + 1) * channels]
                for row in range(2):
                    acc[z, q + row - b + 2] += block[:, row * breadth : (row + 1) * breadth]
        return carry

    lax.fori_loop(0, inner.shape[1] // 2, step, 0)


def outer_terms(cols, w_ref, y):
    lower = upper = None
    for b in range(3):
        low, high = dot(w_ref[0, b], window(cols, 0, y + b)), dot(w_ref[2, b], window(cols, 1, y + b))
        lower = low if lower is None else lower + low
        upper = high if upper is None else upper + high
    return lower, upper


def edge_terms(edges, w_ref, side):
    b = 2 * side
    half = w_ref.shape[2]
    acc = dot(taps(w_ref, b, 0, 2), edges[1, side]) + dot(taps(w_ref, b, 1, 3), edges[2, side])
    return acc[half:] + dot(w_ref[0, b], edges[0, side]), acc[:half] + dot(w_ref[2, b], edges[3, side])


def inner_kernel(near, far, w_ref, d_ref, cot_ref, cols, acc_ref, grad_ref, up):
    rows, channels, breadth = near.shape
    fill_columns(cols, near, far)
    source = lax.broadcasted_iota(jnp.int32, (breadth, 2 * breadth), 0)
    target = lax.broadcasted_iota(jnp.int32, (breadth, 2 * breadth), 1)
    spread = jnp.where(source == target // 2, 1.0, 0.0).astype(BF16)
    for pair in range(rows // 4):
        both = dot(cot_ref[:, pair * breadth : (pair + 1) * breadth], spread)
        up[:, 2 * pair * breadth : 2 * (pair + 1) * breadth] = both.astype(BF16)
    even = lax.broadcasted_iota(jnp.int32, (channels, breadth), 1) % 2 == 0
    for a in range(2):
        for b in range(2):
            terms = lax.dot_general(d_ref[a, b], up[...], (((0,), (0,)), ((), ())), preferred_element_type=F32)
            for t in range(rows // 2):
                part = terms[:, t * breadth : (t + 1) * breadth]
                grad_ref[a, 2 * t + b] = jnp.where(even, part[0:channels], part[channels:])
    add_terms(acc_ref, w_ref, cols)


def gated(preact, grad):
    sig = 1.0 / (1.0 + jnp.exp(-preact))
    return (preact * sig).astype(BF16), (grad * sig * (1.0 + preact * (1.0 - sig))).astype(BF16)


def outer_kernel(
    near, far, near_row, far_row, w_ref, acc_ref, grad_ref, cols, edges, side_ref, near_ref, far_ref, h_ref
):
    rows, channels, breadth = near.shape
    fill_columns(cols, near, far)
    fill_rows(edges, near_row, far_row)
    beside = []
    for side in range(2):
        terms = dot(taps(w_ref, 2 * side, 0, 2), edges[0, side]) + dot(taps(w_ref, 2 * side, 1, 3), edges[1, side])
        beside.append((terms[channels:], terms[:channels]))
    even = is_even("gz")
    for y in range(0, rows, 2):
        outer = outer_terms(cols, w_ref, y)
        for b in range(2):
            found = []
            for z in range(2):
                preact = acc_ref[z, y + b + 2] + outer[z][:, b * breadth : (b + 1) * breadth]
                if y + b in (0, rows - 1):
                    side_ref[z, b] = preact + beside[b][z]
                else:
                    h_ref[z, y + b], gate = gated(preact, grad_ref[z, y + b])
                    found.append(gate)
            if len(found) > 0:
                near_ref[y + b] = choose(even, found[1], found[0])
                far_ref[y + b] = choose(even, found[0], found[1])


def gate_kernel(near, far, side_ref, near_in, far_in, h_in, grad_ref, w_ref, edges, near_ref, far_ref, h_ref):
    rows = near_in.shape[0]
    fill_rows(edges, near, far)
    even = is_even("gz")
    for side, y in enumerate((0, rows - 1)):
        terms = [dot(w_ref[2 * z, 2 * side], edges[z, side]) for z in range(2)]
        found = []
        for z in range(2):
            h_ref[z, y], gate = gated(side_ref[z, side] + terms[z], grad_ref[z, y])
            found.append(gate)
        near_ref[y] = choose(even, found[1], found[0])
        far_ref[y] = choose(even, found[0], found[1])
    for y in range(1, rows - 1):
        near_ref[y] = near_in[y]
        far_ref[y] = far_in[y]
        for z in range(2):
            h_ref[z, y] = h_in[z, y]


def coarse_hidden(h_ref):
    rows, channels, breadth = h_ref.shape[1:]
    source = lax.broadcasted_iota(jnp.int32, (2 * breadth, 2 * breadth), 0)
    target = lax.broadcasted_iota(jnp.int32, (2 * breadth, 2 * breadth), 1)
    wanted = 2 * (target % breadth) + target // breadth
    pick = jnp.where(source == wanted, 1.0, 0.0).astype(BF16)
    pairs = rows // 4
    both = [
        jnp.concatenate([h_ref[a, 4 * pair + b], h_ref[a, 4 * pair + 2 + b]], axis=1)
        for a in range(2) for b in range(2) for pair in range(pairs)
    ]
    picked = dot(jnp.concatenate(both, axis=0), pick).astype(BF16)
    blocks = []
    for tap in range(4):
        parts = [picked[(tap * pairs + pair) * channels : (tap * pairs + pair + 1) * channels] for pair in range(pairs)]
        for e in range(2):
            blocks.append(jnp.concatenate([x[:, e * breadth : (e + 1) * breadth] for x in parts], axis=1))
    return jnp.concatenate(blocks, axis=0)


def section_kernel(h_ref, d_ref, out_ref):
    down = jnp.concatenate([d_ref[a, b] for a in range(2) for b in range(2)], axis=1)
    out_ref[...] = dot(down, coarse_hidden(h_ref)).astype(BF16)


def weight_grad_kernel(inner, outer, own_edges, edges, near, far, h_ref, cot_ref, keep, send, packed):
    rows, channels, breadth = near.shape
    across = (((1,), (1,)), ((), ()))
    even = is_even("gz")
    low = [choose(even, far[y], near[y]) for y in range(rows)]
    high = [choose(even, near[y], far[y]) for y in range(rows)]
    nothing = jnp.zeros((channels, breadth), BF16)

    def shifted(lines):
        return jnp.concatenate(
            [jnp.concatenate([nothing] * b + lines + [nothing] * (2 - b), axis=1) for b in range(3)], axis=0
        )

    low, high = shifted(low), shifted(high)
    both = jnp.concatenate([low, high], axis=0)

    def columns(p, q):
        planes, rows_beside, at = (inner, own_edges, p - 1) if p in (1, 2) else (outer, edges, p // 3)
        return rows_beside[at, q // (rows + 1)] if q in (0, rows + 1) else planes[at, q]

    parts = []
    for p in range(4):
        lines = jnp.concatenate([columns(p, q) for q in range(rows + 2)], axis=1)
        lhs = low if p == 0 else high if p == 3 else both
        parts.append(lax.dot_general(lhs, lines, across, preferred_element_type=F32))
    lane = lax.broadcasted_iota(jnp.int32, (channels // 2, breadth), 1)
    for a in range(3):
        for b in range(3):
            at = b * channels + (0 if a == 2 else 3 * channels)
            total = parts[a][b * channels : (b + 1) * channels] + parts[a + 1][at : at + channels]
            base = (a * 3 + b) * 3 * channels // 2
            packed[base : base + channels] = total[:, 0:breadth]
            rest = jnp.concatenate([total[:, breadth:], total[:, breadth:]], axis=1)
            mix = jnp.where(lane < channels, rest[0 : channels // 2], rest[channels // 2 :])
            packed[base + channels : base + 3 * channels // 2] = mix
    base = 9 * 3 * channels // 2
    height = cot_ref.shape[0]
    down = lax.dot_general(cot_ref[...], coarse_hidden(h_ref), across, preferred_element_type=F32)
    for tap in range(4):
        packed[base + tap * height : base + (tap + 1) * height] = down[:, tap * breadth : (tap + 1) * breadth]
    end = base + 4 * height
    if end < packed.shape[0]:
        packed[end:] = jnp.zeros((packed.shape[0] - end, packed.shape[1]), F32)
    split(packed, keep, send, owned_half())


def side_of(axis, bit):
    return lax.rem(lax.axis_index(axis) // bit, 2)


def owned_half():
    total = 0
    for axis in ("gz", "gy"):
        for k in range(lax.axis_size(axis).bit_length() - 1):
            total = total + side_of(axis, 1 << k)
    return lax.rem(total, 2)


def part(side, rows):
    return pl.ds(pl.multiple_of(side * rows, 16), rows)


def split(packed, keep, send, side):
    half = keep.shape[0]
    keep[...] = packed[part(side, half)]
    send[...] = packed[part(1 - side, half)].astype(BF16)


def halve_kernel(mine, other, keep, send, total, *, axis, bit):
    total[...] = mine[...] + other[...].astype(F32)
    split(total, keep, send, side_of(axis, bit))


def add_kernel(x, y, out):
    out[...] = (x[...].astype(F32) + y[...].astype(F32)).astype(BF16)


def join_kernel(mine, other, out, *, axis, bit):
    join(mine, other, out, side_of(axis, bit))


def join(mine, other, out, side):
    rows = mine.shape[0]
    out[part(side, rows)] = mine[...]
    out[part(1 - side, rows)] = other[...]


def field_kernel(near, far, near_in, far_in, w_ref, acc_ref, inner, outer):
    fill_columns(inner, near, far)
    fill_columns(outer, near_in, far_in)
    add_terms(acc_ref, w_ref, inner, outer)


def field_edges_kernel(near, far, acc_ref, w_ref, out_ref, edges):
    channels = acc_ref.shape[2]
    rows = acc_ref.shape[1] - 4
    fill_rows(edges, near, far)
    sides = [edge_terms(edges, w_ref, side) for side in range(2)]
    for z in range(2):
        for y in range(rows):
            line = acc_ref[z, y + 2]
            if y in (0, rows - 1):
                line = line + sides[0 if y == 0 else 1][z]
            out_ref[pl.ds(z * rows + y, channels, stride=2 * rows), :] = line


def unpack_kernel(mine, other, conv_ref, down_ref, sums_ref, *, scale):
    join(mine, other, sums_ref, owned_half())
    channels = conv_ref.shape[2]
    for a in range(3):
        for b in range(3):
            base = (a * 3 + b) * 3 * channels // 2
            conv_ref[a, b, :, 0 : 2 * channels] = sums_ref[base : base + channels].astype(F32) * scale
            rest = sums_ref[base + channels : base + 3 * channels // 2].astype(F32) * scale
            conv_ref[a, b, 0 : channels // 2, 2 * channels :] = rest[:, 0:channels]
            conv_ref[a, b, channels // 2 :, 2 * channels :] = rest[:, channels:]
    base = 9 * 3 * channels // 2
    height = down_ref.shape[2]
    for a in range(2):
        for b in range(2):
            at = base + (2 * a + b) * height
            down_ref[a, b] = sums_ref[at : at + height].astype(F32) * scale


def swap(cells, axis, low):
    count = lax.axis_size(axis)
    pairs = [(i % count, (i + 1) % count) for i in range(low, low + count, 2)]
    return lax.ppermute(cells, axis, pairs + [(b, a) for a, b in pairs])


def flip(cells, axis, bit):
    row = lax.axis_size("gy")
    mask = bit * row | 1 if axis == "gz" else bit | 1
    return lax.ppermute(cells, ("gz", "gy"), [(i, i ^ mask) for i in range(lax.axis_size("gz") * row)])


def tied(first, *others):
    found = lax.optimization_barrier((first, *others))
    return found[0], tuple(found[1:])


def swapped(near, far, axis):
    return swap(near, axis, 0), swap(far, axis, 1)


def body(features, conv_weight, down_weight, cotangent):
    channels, plane_count, row_count, breadth = features.shape
    out_channels = down_weight.shape[2]
    count = lax.axis_size("gz") * lax.axis_size("gy")
    grad_scale = 1.0 / math.sqrt(plane_count * row_count * breadth * count)
    cot = cotangent.reshape(out_channels, -1)
    conv_weight, down_weight, cot = fetch(conv_weight, down_weight, cot)
    turned = conv_weight.reshape(3, 3, channels, 3, channels)[::-1, ::-1, :, ::-1]
    weight_bwd = turned.transpose(0, 1, 4, 3, 2).reshape(3, 3, channels, 3 * channels)
    plane = ((row_count, channels, breadth), BF16)
    edge = ((plane_count + 2, channels, breadth), BF16)
    cols = ((plane_count, row_count + 2, 3 * channels, breadth), BF16)
    edge_cols = ((plane_count + 2, 2, 3 * channels, breadth), BF16)
    lines = (plane_count, row_count, channels, breadth)
    sums_of = (plane_count, row_count + 4, channels, breadth)
    conv_flops = 2 * 27 * channels * channels * plane_count * row_count * breadth

    pair = ((plane_count, channels, breadth), BF16)
    *own, near_row, far_row = call(
        lines_kernel, [plane, plane, pair, pair],
        [((channels * plane_count * row_count, breadth), F32)], 0, (features,),
    )
    outside = swapped(*own, "gz")
    beside = swapped(near_row, far_row, "gy")
    inner, acc, hidden_grad = call(
        inner_kernel, [cols, (sums_of, F32), (lines, F32)],
        [((out_channels, row_count // 2 * breadth), BF16)],
        2 * conv_flops // 3, (*own, conv_weight, down_weight, cot),
    )
    near, far, near_row, far_row, acc = lax.optimization_barrier((*outside, *beside, acc))
    outside, own_rows = (near, far), (near_row, far_row)
    beside = swapped(*call(outer_rows_kernel, [pair, pair], [], 0, outside), "gy")
    far, near, weight_bwd = lax.optimization_barrier((beside[1], beside[0], weight_bwd))
    beside = (near, far)
    rows_cols = ((plane_count, 2, 3 * channels, breadth), BF16)
    outer, own_edges, *inside = call(
        outer_kernel,
        [cols, rows_cols, ((plane_count, 2, channels, breadth), F32), plane, plane, (lines, BF16)], [],
        conv_flops // 3, (*outside, *own_rows, conv_weight, acc, hidden_grad),
    )
    edges, near, far, hidden = call(
        gate_kernel, [rows_cols, plane, plane, (lines, BF16)], [], conv_flops // 10,
        (*beside, *inside, hidden_grad, conv_weight),
    )
    gates = (near, far)

    used = 27 * channels * channels // 128 + 4 * out_channels
    rows = -(-used // 128) * 128
    keep, send = call(
        weight_grad_kernel, [((rows // 2, 128), F32), ((rows // 2, 128), BF16)], [((rows, 128), F32)],
        conv_flops, (inner, outer, own_edges, edges, *gates, hidden, cot),
    )
    keep, gates = tied(keep, *gates)
    near, far = gates
    near_in = swap(near, "gz", 0)
    for level, (axis, bit) in enumerate((("gz", 2), ("gy", 2))):
        size = rows >> (level + 2)
        mine, got = keep, flip(send, *(("gy", 1), ("gz", 2))[level])
        keep, send = call(
            functools.partial(halve_kernel, axis=axis, bit=bit),
            [((size, 128), F32), ((size, 128), BF16)], [((2 * size, 128), F32)], 0, (mine, got),
        )
        if level == 0:
            keep, (far, hidden) = tied(keep, far, hidden)
            far_in = swap(far, "gz", 1)
            (section_out,) = call(
                section_kernel, [((out_channels, cot.shape[1]), BF16)], [], conv_flops // 10,
                (hidden, down_weight),
            )
    shard = ((rows // 8, 128), BF16)
    (sums,) = call(add_kernel, [shard], [], 0, (keep, flip(send, "gy", 2)))
    (sums,) = call(add_kernel, [shard], [], 0, (sums, flip(sums, "gz", 1)))
    sums, outside = tied(sums, near_in, far_in)
    sends = call(edges_kernel, [edge, edge], [], 0, (*gates, *outside))
    beside = swapped(*sends, "gy")
    (acc,) = call(
        field_kernel, [(sums_of, F32)], [cols, cols], conv_flops, (*gates, *outside, weight_bwd)
    )
    wide = [("gy", 1 << k) for k in range(2, lax.axis_size("gy").bit_length() - 1)]
    wide += [("gz", 1 << k) for k in range(2, lax.axis_size("gz").bit_length() - 1)]
    for axis, bit in wide:
        (sums,) = call(add_kernel, [shard], [], 0, (sums, flip(sums, axis, bit)))
    sums, (section_out,) = tied(sums, section_out)
    (sums,) = call(
        functools.partial(join_kernel, axis="gy", bit=2), [((rows // 4, 128), BF16)], [], 0,
        (sums, flip(sums, "gy", 2)),
    )
    sums, (acc, *beside) = tied(sums, acc, *beside)
    (field,) = call(
        field_edges_kernel, [((channels * plane_count * row_count, breadth), F32)], [edge_cols],
        conv_flops // 10, (*beside, acc, weight_bwd),
    )
    (sums,) = call(
        functools.partial(join_kernel, axis="gz", bit=2), [((rows // 2, 128), BF16)], [], 0,
        (sums, flip(sums, "gz", 2)),
    )
    sums, (field,) = tied(sums, field)
    grad_conv, grad_down = call(
        functools.partial(unpack_kernel, scale=grad_scale),
        [(conv_weight.shape, F32), (down_weight.shape, F32)], [((rows, 128), BF16)], 0,
        (sums, flip(sums, "gy", 1)),
    )
    section_out = section_out.reshape(out_channels, plane_count // 2, -1)
    return (section_out, field.reshape(features.shape), grad_conv, grad_down)


def solution(mesh):
    return jax.shard_map(
        body,
        mesh=mesh,
        in_specs=(P(None, "gz", "gy", None), P(), P(), P(None, "gz", "gy")),
        out_specs=(P(None, "gz", "gy"), P(None, "gz", "gy", None), P(), P()),
        check_vma=False,
    )
```

```python
import functools
import math

import jax
import jax.numpy as jnp
from jax import lax
from jax.experimental import pallas as pl
from jax.experimental.pallas import tpu as pltpu
from jax.sharding import PartitionSpec as P

F32 = jnp.float32
BF16 = jnp.bfloat16
PARAMS = pltpu.CompilerParams(vmem_limit_bytes=24 * 1024 * 1024)


def call(kernel, outs, scratch, flops, operands):
    moved = sum(x.size * x.dtype.itemsize for x in operands)
    moved += sum(math.prod(s) * jnp.dtype(d).itemsize for s, d in outs)
    vmem = pl.BlockSpec(memory_space=pltpu.VMEM)
    return pl.pallas_call(
        kernel,
        out_shape=[jax.ShapeDtypeStruct(s, d) for s, d in outs],
        in_specs=[vmem] * len(operands),
        out_specs=[vmem] * len(outs),
        scratch_shapes=[pltpu.VMEM(s, d) for s, d in scratch],
        compiler_params=PARAMS,
        cost_estimate=pl.CostEstimate(flops=flops, bytes_accessed=moved, transcendentals=0),
    )(*operands)


def is_even(axis):
    return lax.rem(lax.axis_index(axis), 2) == 0


def choose(cond, yes, no):
    return jnp.where(jnp.broadcast_to(cond, yes.shape), yes, no)


def lines_kernel(f_ref, near_ref, far_ref, near_row, far_row, wide):
    channels, planes, rows, breadth = f_ref.shape
    wide[...] = f_ref[...].astype(F32).reshape(channels * planes * rows, breadth)
    even = is_even("gz")
    ends = {}
    for y in range(rows):
        low, high = ends[y] = [
            wide[pl.ds(z * rows + y, channels, stride=planes * rows), :].astype(BF16) for z in range(2)
        ]
        near_ref[y] = choose(even, high, low)
        far_ref[y] = choose(even, low, high)
    even_y = is_even("gy")
    for z in range(2):
        near_row[z] = choose(even_y, ends[rows - 1][z], ends[0][z])
        far_row[z] = choose(even_y, ends[0][z], ends[rows - 1][z])


def turn_kernel(w_ref, out):
    channels = w_ref.shape[2]
    for a in range(3):
        for b in range(3):
            turned = w_ref[a, b].astype(F32).T
            blocks = [turned[(2 - e) * channels : (3 - e) * channels] for e in range(3)]
            out[2 - a, 2 - b] = jnp.concatenate(blocks, axis=1).astype(BF16)


def fetch_kernel(*refs):
    *both, sems = refs
    count = len(both) // 2
    copies = [pltpu.make_async_copy(both[k], both[count + k], sems.at[k]) for k in range(count)]
    for copy in copies:
        copy.start()
    for copy in copies:
        copy.wait()


def fetch(*operands):
    return pl.pallas_call(
        fetch_kernel,
        out_shape=[jax.ShapeDtypeStruct(x.shape, x.dtype) for x in operands],
        in_specs=[pl.BlockSpec(memory_space=pltpu.HBM)] * len(operands),
        out_specs=[pl.BlockSpec(memory_space=pltpu.VMEM)] * len(operands),
        scratch_shapes=[pltpu.SemaphoreType.DMA((len(operands),))],
        compiler_params=PARAMS,
        cost_estimate=pl.CostEstimate(flops=0, bytes_accessed=2 * sum(x.size * 2 for x in operands), transcendentals=0),
    )(*operands)


def outer_rows_kernel(near_in, far_in, near_ref, far_ref):
    rows = near_in.shape[0]
    even_z, even_y = is_even("gz"), is_even("gy")
    for p, (one, other) in enumerate(((far_in, near_in), (near_in, far_in))):
        first = choose(even_z, one[0], other[0])
        last = choose(even_z, one[rows - 1], other[rows - 1])
        near_ref[p] = choose(even_y, last, first)
        far_ref[p] = choose(even_y, first, last)


def edges_kernel(near, far, near_in, far_in, near_ref, far_ref):
    rows = near.shape[0]
    even_z, even_y = is_even("gz"), is_even("gy")

    def put(p, one, other):
        first = choose(even_z, one[0], other[0])
        last = choose(even_z, one[rows - 1], other[rows - 1])
        near_ref[p] = choose(even_y, last, first)
        far_ref[p] = choose(even_y, first, last)

    put(0, far_in, near_in)
    put(1, far, near)
    put(2, near, far)
    put(3, near_in, far_in)


def put_columns(cols, p, q, line):
    channels = line.shape[0]
    wide = line.astype(F32)
    cols[p, q, 0:channels] = pltpu.roll(wide, 1, 1).astype(BF16)
    cols[p, q, channels : 2 * channels] = line
    cols[p, q, 2 * channels : 3 * channels] = pltpu.roll(wide, line.shape[1] - 1, 1).astype(BF16)


def fill_columns(cols, near, far):
    rows = near.shape[0]
    even = is_even("gz")

    def step(y, carry):
        put_columns(cols, 0, y + 1, choose(even, far[y], near[y]))
        put_columns(cols, 1, y + 1, choose(even, near[y], far[y]))
        return carry

    lax.fori_loop(0, rows, step, 0, unroll=2)
    for p in range(2):
        for q in (0, rows + 1):
            cols[p, q] = jnp.zeros(cols.shape[2:], BF16)


def fill_rows(cols, near, far):
    even = is_even("gy")
    for p in range(near.shape[0]):
        put_columns(cols, p, 0, choose(even, far[p], near[p]))
        put_columns(cols, p, 1, choose(even, near[p], far[p]))


def dot(lhs, rhs):
    return jnp.dot(lhs, rhs, preferred_element_type=F32)


def taps(w_ref, b, first, last):
    return jnp.concatenate([w_ref[a, b] for a in range(first, last)], axis=0)


def window(cols, p, q):
    return jnp.concatenate([cols[p, q], cols[p, q + 1]], axis=1)


def inner_terms(cols, w_ref, y):
    acc = None
    for b in range(3):
        for p in range(2):
            term = dot(taps(w_ref, b, p, p + 2), window(cols, p, y + b))
            acc = term if acc is None else acc + term
    half = acc.shape[0] // 2
    return acc[half:], acc[:half]


def outer_terms(cols, w_ref, y):
    lower = upper = None
    for b in range(3):
        low, high = dot(w_ref[0, b], window(cols, 0, y + b)), dot(w_ref[2, b], window(cols, 1, y + b))
        lower = low if lower is None else lower + low
        upper = high if upper is None else upper + high
    return lower, upper


def edge_terms(edges, w_ref, side):
    b = 2 * side
    half = w_ref.shape[2]
    acc = dot(taps(w_ref, b, 0, 2), edges[1, side]) + dot(taps(w_ref, b, 1, 3), edges[2, side])
    return acc[half:] + dot(w_ref[0, b], edges[0, side]), acc[:half] + dot(w_ref[2, b], edges[3, side])


def inner_kernel(near, far, w_ref, d_ref, cot_ref, cols, acc_ref, grad_ref, up):
    rows, channels, breadth = near.shape
    fill_columns(cols, near, far)
    source = lax.broadcasted_iota(jnp.int32, (breadth, 2 * breadth), 0)
    target = lax.broadcasted_iota(jnp.int32, (breadth, 2 * breadth), 1)
    spread = jnp.where(source == target // 2, 1.0, 0.0).astype(BF16)
    for pair in range(rows // 4):
        both = dot(cot_ref[:, pair * breadth : (pair + 1) * breadth], spread)
        up[:, 2 * pair * breadth : 2 * (pair + 1) * breadth] = both.astype(BF16)
    even = lax.broadcasted_iota(jnp.int32, (channels, breadth), 1) % 2 == 0
    for a in range(2):
        for b in range(2):
            terms = lax.dot_general(d_ref[a, b], up[...], (((0,), (0,)), ((), ())), preferred_element_type=F32)
            for t in range(rows // 2):
                part = terms[:, t * breadth : (t + 1) * breadth]
                grad_ref[a, 2 * t + b] = jnp.where(even, part[0:channels], part[channels:])

    def step(t, carry):
        y = 2 * t
        for z, lines in enumerate(inner_terms(cols, w_ref, y)):
            for b in range(2):
                acc_ref[z, y + b] = lines[:, b * breadth : (b + 1) * breadth]
        return carry

    lax.fori_loop(0, rows // 2, step, 0)


def gated(preact, grad):
    sig = 1.0 / (1.0 + jnp.exp(-preact))
    return (preact * sig).astype(BF16), (grad * sig * (1.0 + preact * (1.0 - sig))).astype(BF16)


def outer_kernel(
    near, far, near_row, far_row, w_ref, acc_ref, grad_ref, cols, edges, side_ref, near_ref, far_ref, h_ref
):
    rows, channels, breadth = near.shape
    fill_columns(cols, near, far)
    fill_rows(edges, near_row, far_row)
    beside = []
    for side in range(2):
        terms = dot(taps(w_ref, 2 * side, 0, 2), edges[0, side]) + dot(taps(w_ref, 2 * side, 1, 3), edges[1, side])
        beside.append((terms[channels:], terms[:channels]))
    even = is_even("gz")
    for y in range(0, rows, 2):
        outer = outer_terms(cols, w_ref, y)
        for b in range(2):
            found = []
            for z in range(2):
                preact = acc_ref[z, y + b] + outer[z][:, b * breadth : (b + 1) * breadth]
                if y + b in (0, rows - 1):
                    side_ref[z, b] = preact + beside[b][z]
                else:
                    h_ref[z, y + b], gate = gated(preact, grad_ref[z, y + b])
                    found.append(gate)
            if len(found) > 0:
                near_ref[y + b] = choose(even, found[1], found[0])
                far_ref[y + b] = choose(even, found[0], found[1])


def gate_kernel(near, far, side_ref, near_in, far_in, h_in, grad_ref, w_ref, edges, near_ref, far_ref, h_ref):
    rows = near_in.shape[0]
    fill_rows(edges, near, far)
    even = is_even("gz")
    for side, y in enumerate((0, rows - 1)):
        terms = [dot(w_ref[2 * z, 2 * side], edges[z, side]) for z in range(2)]
        found = []
        for z in range(2):
            h_ref[z, y], gate = gated(side_ref[z, side] + terms[z], grad_ref[z, y])
            found.append(gate)
        near_ref[y] = choose(even, found[1], found[0])
        far_ref[y] = choose(even, found[0], found[1])
    for y in range(1, rows - 1):
        near_ref[y] = near_in[y]
        far_ref[y] = far_in[y]
        for z in range(2):
            h_ref[z, y] = h_in[z, y]


def coarse_hidden(h_ref):
    rows, channels, breadth = h_ref.shape[1:]
    source = lax.broadcasted_iota(jnp.int32, (2 * breadth, 2 * breadth), 0)
    target = lax.broadcasted_iota(jnp.int32, (2 * breadth, 2 * breadth), 1)
    wanted = 2 * (target % breadth) + target // breadth
    pick = jnp.where(source == wanted, 1.0, 0.0).astype(BF16)
    pairs = rows // 4
    both = [
        jnp.concatenate([h_ref[a, 4 * pair + b], h_ref[a, 4 * pair + 2 + b]], axis=1)
        for a in range(2) for b in range(2) for pair in range(pairs)
    ]
    picked = dot(jnp.concatenate(both, axis=0), pick).astype(BF16)
    blocks = []
    for tap in range(4):
        parts = [picked[(tap * pairs + pair) * channels : (tap * pairs + pair + 1) * channels] for pair in range(pairs)]
        for e in range(2):
            blocks.append(jnp.concatenate([x[:, e * breadth : (e + 1) * breadth] for x in parts], axis=1))
    return jnp.concatenate(blocks, axis=0)


def section_kernel(h_ref, d_ref, out_ref):
    down = jnp.concatenate([d_ref[a, b] for a in range(2) for b in range(2)], axis=1)
    out_ref[...] = dot(down, coarse_hidden(h_ref)).astype(BF16)


def weight_grad_kernel(inner, outer, own_edges, edges, near, far, h_ref, cot_ref, keep, send, packed):
    rows, channels, breadth = near.shape
    across = (((1,), (1,)), ((), ()))
    even = is_even("gz")
    low = [choose(even, far[y], near[y]) for y in range(rows)]
    high = [choose(even, near[y], far[y]) for y in range(rows)]
    nothing = jnp.zeros((channels, breadth), BF16)

    def shifted(lines):
        return jnp.concatenate(
            [jnp.concatenate([nothing] * b + lines + [nothing] * (2 - b), axis=1) for b in range(3)], axis=0
        )

    low, high = shifted(low), shifted(high)
    both = jnp.concatenate([low, high], axis=0)

    def columns(p, q):
        planes, rows_beside, at = (inner, own_edges, p - 1) if p in (1, 2) else (outer, edges, p // 3)
        return rows_beside[at, q // (rows + 1)] if q in (0, rows + 1) else planes[at, q]

    parts = []
    for p in range(4):
        lines = jnp.concatenate([columns(p, q) for q in range(rows + 2)], axis=1)
        lhs = low if p == 0 else high if p == 3 else both
        parts.append(lax.dot_general(lhs, lines, across, preferred_element_type=F32))
    lane = lax.broadcasted_iota(jnp.int32, (channels // 2, breadth), 1)
    for a in range(3):
        for b in range(3):
            at = b * channels + (0 if a == 2 else 3 * channels)
            total = parts[a][b * channels : (b + 1) * channels] + parts[a + 1][at : at + channels]
            base = (a * 3 + b) * 3 * channels // 2
            packed[base : base + channels] = total[:, 0:breadth]
            rest = jnp.concatenate([total[:, breadth:], total[:, breadth:]], axis=1)
            mix = jnp.where(lane < channels, rest[0 : channels // 2], rest[channels // 2 :])
            packed[base + channels : base + 3 * channels // 2] = mix
    base = 9 * 3 * channels // 2
    height = cot_ref.shape[0]
    down = lax.dot_general(cot_ref[...], coarse_hidden(h_ref), across, preferred_element_type=F32)
    for tap in range(4):
        packed[base + tap * height : base + (tap + 1) * height] = down[:, tap * breadth : (tap + 1) * breadth]
    end = base + 4 * height
    if end < packed.shape[0]:
        packed[end:] = jnp.zeros((packed.shape[0] - end, packed.shape[1]), F32)
    split(packed, keep, send, owned_half())


def side_of(axis, bit):
    return lax.rem(lax.axis_index(axis) // bit, 2)


def owned_half():
    total = 0
    for axis in ("gz", "gy"):
        for k in range(lax.axis_size(axis).bit_length() - 1):
            total = total + side_of(axis, 1 << k)
    return lax.rem(total, 2)


def part(side, rows):
    return pl.ds(pl.multiple_of(side * rows, 16), rows)


def split(packed, keep, send, side):
    half = keep.shape[0]
    keep[...] = packed[part(side, half)]
    send[...] = packed[part(1 - side, half)].astype(BF16)


def halve_kernel(mine, other, keep, send, total, *, axis, bit):
    total[...] = mine[...] + other[...].astype(F32)
    split(total, keep, send, side_of(axis, bit))


def add_kernel(x, y, out):
    out[...] = (x[...].astype(F32) + y[...].astype(F32)).astype(BF16)


def join_kernel(mine, other, out, *, axis, bit):
    join(mine, other, out, side_of(axis, bit))


def join(mine, other, out, side):
    rows = mine.shape[0]
    out[part(side, rows)] = mine[...]
    out[part(1 - side, rows)] = other[...]


def field_kernel(near, far, near_in, far_in, w_ref, acc_ref, inner, outer):
    rows, channels, breadth = near.shape
    fill_columns(inner, near, far)
    fill_columns(outer, near_in, far_in)

    def step(t, carry):
        y = 2 * t
        own = inner_terms(inner, w_ref, y)
        rest = outer_terms(outer, w_ref, y)
        for z in range(2):
            total = own[z] + rest[z]
            for b in range(2):
                acc_ref[z, y + b] = total[:, b * breadth : (b + 1) * breadth]
        return carry

    lax.fori_loop(0, rows // 2, step, 0)


def field_edges_kernel(near, far, acc_ref, w_ref, out_ref, edges):
    rows, channels, breadth = acc_ref.shape[1:]
    fill_rows(edges, near, far)
    sides = [edge_terms(edges, w_ref, side) for side in range(2)]
    for z in range(2):
        for y in range(rows):
            line = acc_ref[z, y]
            if y in (0, rows - 1):
                line = line + sides[0 if y == 0 else 1][z]
            out_ref[pl.ds(z * rows + y, channels, stride=2 * rows), :] = line


def unpack_kernel(mine, other, conv_ref, down_ref, sums_ref, *, scale):
    join(mine, other, sums_ref, owned_half())
    channels = conv_ref.shape[2]
    for a in range(3):
        for b in range(3):
            base = (a * 3 + b) * 3 * channels // 2
            conv_ref[a, b, :, 0 : 2 * channels] = sums_ref[base : base + channels].astype(F32) * scale
            rest = sums_ref[base + channels : base + 3 * channels // 2].astype(F32) * scale
            conv_ref[a, b, 0 : channels // 2, 2 * channels :] = rest[:, 0:channels]
            conv_ref[a, b, channels // 2 :, 2 * channels :] = rest[:, channels:]
    base = 9 * 3 * channels // 2
    height = down_ref.shape[2]
    for a in range(2):
        for b in range(2):
            at = base + (2 * a + b) * height
            down_ref[a, b] = sums_ref[at : at + height].astype(F32) * scale


def swap(cells, axis, low):
    count = lax.axis_size(axis)
    pairs = [(i % count, (i + 1) % count) for i in range(low, low + count, 2)]
    return lax.ppermute(cells, axis, pairs + [(b, a) for a, b in pairs])


def flip(cells, axis, bit):
    row = lax.axis_size("gy")
    mask = bit * row | 1 if axis == "gz" else bit | 1
    return lax.ppermute(cells, ("gz", "gy"), [(i, i ^ mask) for i in range(lax.axis_size("gz") * row)])


def tied(first, *others):
    found = lax.optimization_barrier((first, *others))
    return found[0], tuple(found[1:])


def swapped(near, far, axis):
    return swap(near, axis, 0), swap(far, axis, 1)


def body(features, conv_weight, down_weight, cotangent):
    channels, plane_count, row_count, breadth = features.shape
    out_channels = down_weight.shape[2]
    count = lax.axis_size("gz") * lax.axis_size("gy")
    grad_scale = 1.0 / math.sqrt(plane_count * row_count * breadth * count)
    cot = cotangent.reshape(out_channels, -1)
    conv_weight, down_weight, cot = fetch(conv_weight, down_weight, cot)
    (weight_bwd,) = call(turn_kernel, [(conv_weight.shape, BF16)], [], 0, (conv_weight,))
    plane = ((row_count, channels, breadth), BF16)
    edge = ((plane_count + 2, channels, breadth), BF16)
    cols = ((plane_count, row_count + 2, 3 * channels, breadth), BF16)
    edge_cols = ((plane_count + 2, 2, 3 * channels, breadth), BF16)
    lines = (plane_count, row_count, channels, breadth)
    conv_flops = 2 * 27 * channels * channels * plane_count * row_count * breadth

    pair = ((plane_count, channels, breadth), BF16)
    *own, near_row, far_row = call(
        lines_kernel, [plane, plane, pair, pair],
        [((channels * plane_count * row_count, breadth), F32)], 0, (features,),
    )
    outside = swapped(*own, "gz")
    beside = swapped(near_row, far_row, "gy")
    inner, acc, hidden_grad = call(
        inner_kernel, [cols, (lines, F32), (lines, F32)],
        [((out_channels, row_count // 2 * breadth), BF16)],
        2 * conv_flops // 3, (*own, conv_weight, down_weight, cot),
    )
    near, far, near_row, far_row, acc = lax.optimization_barrier((*outside, *beside, acc))
    outside, own_rows = (near, far), (near_row, far_row)
    beside = swapped(*call(outer_rows_kernel, [pair, pair], [], 0, outside), "gy")
    far, near = lax.optimization_barrier((beside[1], beside[0]))
    beside = (near, far)
    rows_cols = ((plane_count, 2, 3 * channels, breadth), BF16)
    outer, own_edges, *inside = call(
        outer_kernel,
        [cols, rows_cols, ((plane_count, 2, channels, breadth), F32), plane, plane, (lines, BF16)], [],
        conv_flops // 3, (*outside, *own_rows, conv_weight, acc, hidden_grad),
    )
    edges, near, far, hidden = call(
        gate_kernel, [rows_cols, plane, plane, (lines, BF16)], [], conv_flops // 10,
        (*beside, *inside, hidden_grad, conv_weight),
    )
    gates = (near, far)

    used = 27 * channels * channels // 128 + 4 * out_channels
    rows = -(-used // 128) * 128
    keep, send = call(
        weight_grad_kernel, [((rows // 2, 128), F32), ((rows // 2, 128), BF16)], [((rows, 128), F32)],
        conv_flops, (inner, outer, own_edges, edges, *gates, hidden, cot),
    )
    keep, gates = tied(keep, *gates)
    near, far = gates
    near_in = swap(near, "gz", 0)
    for level, (axis, bit) in enumerate((("gz", 2), ("gy", 2))):
        size = rows >> (level + 2)
        mine, got = keep, flip(send, *(("gy", 1), ("gz", 2))[level])
        keep, send = call(
            functools.partial(halve_kernel, axis=axis, bit=bit),
            [((size, 128), F32), ((size, 128), BF16)], [((2 * size, 128), F32)], 0, (mine, got),
        )
        if level == 0:
            keep, (far, hidden) = tied(keep, far, hidden)
            far_in = swap(far, "gz", 1)
            (section_out,) = call(
                section_kernel, [((out_channels, cot.shape[1]), BF16)], [], conv_flops // 10,
                (hidden, down_weight),
            )
    shard = ((rows // 8, 128), BF16)
    (sums,) = call(add_kernel, [shard], [], 0, (keep, flip(send, "gy", 2)))
    (sums,) = call(add_kernel, [shard], [], 0, (sums, flip(sums, "gz", 1)))
    sums, outside = tied(sums, near_in, far_in)
    sends = call(edges_kernel, [edge, edge], [], 0, (*gates, *outside))
    beside = swapped(*sends, "gy")
    (acc,) = call(
        field_kernel, [(lines, F32)], [cols, cols], conv_flops, (*gates, *outside, weight_bwd)
    )
    wide = [("gy", 1 << k) for k in range(2, lax.axis_size("gy").bit_length() - 1)]
    wide += [("gz", 1 << k) for k in range(2, lax.axis_size("gz").bit_length() - 1)]
    for axis, bit in wide:
        (sums,) = call(add_kernel, [shard], [], 0, (sums, flip(sums, axis, bit)))
    sums, (section_out,) = tied(sums, section_out)
    (sums,) = call(
        functools.partial(join_kernel, axis="gy", bit=2), [((rows // 4, 128), BF16)], [], 0,
        (sums, flip(sums, "gy", 2)),
    )
    sums, (acc, *beside) = tied(sums, acc, *beside)
    (field,) = call(
        field_edges_kernel, [((channels * plane_count * row_count, breadth), F32)], [edge_cols],
        conv_flops // 10, (*beside, acc, weight_bwd),
    )
    (sums,) = call(
        functools.partial(join_kernel, axis="gz", bit=2), [((rows // 2, 128), BF16)], [], 0,
        (sums, flip(sums, "gz", 2)),
    )
    sums, (field,) = tied(sums, field)
    grad_conv, grad_down = call(
        functools.partial(unpack_kernel, scale=grad_scale),
        [(conv_weight.shape, F32), (down_weight.shape, F32)], [((rows, 128), BF16)], 0,
        (sums, flip(sums, "gy", 1)),
    )
    section_out = section_out.reshape(out_channels, plane_count // 2, -1)
    return (section_out, field.reshape(features.shape), grad_conv, grad_down)


def solution(mesh):
    return jax.shard_map(
        body,
        mesh=mesh,
        in_specs=(P(None, "gz", "gy", None), P(), P(), P(None, "gz", "gy")),
        out_specs=(P(None, "gz", "gy"), P(None, "gz", "gy", None), P(), P()),
        check_vma=False,
    )
```

```python
import functools
import math

import jax
import jax.numpy as jnp
from jax import lax
from jax.experimental import pallas as pl
from jax.experimental.pallas import tpu as pltpu
from jax.sharding import PartitionSpec as P

F32 = jnp.float32
BF16 = jnp.bfloat16
PARAMS = pltpu.CompilerParams(vmem_limit_bytes=24 * 1024 * 1024)


def call(kernel, outs, scratch, flops, operands):
    moved = sum(x.size * x.dtype.itemsize for x in operands)
    moved += sum(math.prod(s) * jnp.dtype(d).itemsize for s, d in outs)
    vmem = pl.BlockSpec(memory_space=pltpu.VMEM)
    return pl.pallas_call(
        kernel,
        out_shape=[jax.ShapeDtypeStruct(s, d) for s, d in outs],
        in_specs=[vmem] * len(operands),
        out_specs=[vmem] * len(outs),
        scratch_shapes=[pltpu.VMEM(s, d) for s, d in scratch],
        compiler_params=PARAMS,
        cost_estimate=pl.CostEstimate(flops=flops, bytes_accessed=moved, transcendentals=0),
    )(*operands)


def is_even(axis):
    return lax.rem(lax.axis_index(axis), 2) == 0


def choose(cond, yes, no):
    return jnp.where(jnp.broadcast_to(cond, yes.shape), yes, no)


def lines_kernel(f_ref, near_ref, far_ref, near_row, far_row, wide):
    channels, planes, rows, breadth = f_ref.shape
    wide[...] = f_ref[...].astype(F32).reshape(channels * planes * rows, breadth)
    even = is_even("gz")
    ends = {}
    for y in range(rows):
        low, high = ends[y] = [
            wide[pl.ds(z * rows + y, channels, stride=planes * rows), :].astype(BF16) for z in range(2)
        ]
        near_ref[y] = choose(even, high, low)
        far_ref[y] = choose(even, low, high)
    even_y = is_even("gy")
    for z in range(2):
        near_row[z] = choose(even_y, ends[rows - 1][z], ends[0][z])
        far_row[z] = choose(even_y, ends[0][z], ends[rows - 1][z])


def turn_kernel(w_ref, out):
    channels = w_ref.shape[2]
    for a in range(3):
        for b in range(3):
            turned = w_ref[a, b].astype(F32).T
            blocks = [turned[(2 - e) * channels : (3 - e) * channels] for e in range(3)]
            out[2 - a, 2 - b] = jnp.concatenate(blocks, axis=1).astype(BF16)


def fetch_kernel(*refs):
    *both, sems = refs
    count = len(both) // 2
    copies = [pltpu.make_async_copy(both[k], both[count + k], sems.at[k]) for k in range(count)]
    for copy in copies:
        copy.start()
    for copy in copies:
        copy.wait()


def fetch(*operands):
    return pl.pallas_call(
        fetch_kernel,
        out_shape=[jax.ShapeDtypeStruct(x.shape, x.dtype) for x in operands],
        in_specs=[pl.BlockSpec(memory_space=pltpu.HBM)] * len(operands),
        out_specs=[pl.BlockSpec(memory_space=pltpu.VMEM)] * len(operands),
        scratch_shapes=[pltpu.SemaphoreType.DMA((len(operands),))],
        compiler_params=PARAMS,
        cost_estimate=pl.CostEstimate(flops=0, bytes_accessed=2 * sum(x.size * 2 for x in operands), transcendentals=0),
    )(*operands)


def outer_rows_kernel(near_in, far_in, near_ref, far_ref):
    rows = near_in.shape[0]
    even_z, even_y = is_even("gz"), is_even("gy")
    for p, (one, other) in enumerate(((far_in, near_in), (near_in, far_in))):
        first = choose(even_z, one[0], other[0])
        last = choose(even_z, one[rows - 1], other[rows - 1])
        near_ref[p] = choose(even_y, last, first)
        far_ref[p] = choose(even_y, first, last)


def edges_kernel(near, far, near_in, far_in, near_ref, far_ref):
    rows = near.shape[0]
    even_z, even_y = is_even("gz"), is_even("gy")

    def put(p, one, other):
        first = choose(even_z, one[0], other[0])
        last = choose(even_z, one[rows - 1], other[rows - 1])
        near_ref[p] = choose(even_y, last, first)
        far_ref[p] = choose(even_y, first, last)

    put(0, far_in, near_in)
    put(1, far, near)
    put(2, near, far)
    put(3, near_in, far_in)


def put_columns(cols, p, q, line):
    channels = line.shape[0]
    wide = line.astype(F32)
    cols[p, q, 0:channels] = pltpu.roll(wide, 1, 1).astype(BF16)
    cols[p, q, channels : 2 * channels] = line
    cols[p, q, 2 * channels : 3 * channels] = pltpu.roll(wide, line.shape[1] - 1, 1).astype(BF16)


def fill_columns(cols, near, far):
    rows = near.shape[0]
    even = is_even("gz")

    def step(y, carry):
        put_columns(cols, 0, y + 1, choose(even, far[y], near[y]))
        put_columns(cols, 1, y + 1, choose(even, near[y], far[y]))
        return carry

    lax.fori_loop(0, rows, step, 0, unroll=2)
    for p in range(2):
        for q in (0, rows + 1):
            cols[p, q] = jnp.zeros(cols.shape[2:], BF16)


def fill_rows(cols, near, far):
    even = is_even("gy")
    for p in range(near.shape[0]):
        put_columns(cols, p, 0, choose(even, far[p], near[p]))
        put_columns(cols, p, 1, choose(even, near[p], far[p]))


def dot(lhs, rhs):
    return jnp.dot(lhs, rhs, preferred_element_type=F32)


def taps(w_ref, b, first, last):
    return jnp.concatenate([w_ref[a, b] for a in range(first, last)], axis=0)


def window(cols, p, q):
    return jnp.concatenate([cols[p, q], cols[p, q + 1]], axis=1)


def inner_terms(cols, w_ref, y):
    acc = None
    for b in range(3):
        for p in range(2):
            term = dot(taps(w_ref, b, p, p + 2), window(cols, p, y + b))
            acc = term if acc is None else acc + term
    half = acc.shape[0] // 2
    return acc[half:], acc[:half]


def outer_terms(cols, w_ref, y):
    lower = upper = None
    for b in range(3):
        low, high = dot(w_ref[0, b], window(cols, 0, y + b)), dot(w_ref[2, b], window(cols, 1, y + b))
        lower = low if lower is None else lower + low
        upper = high if upper is None else upper + high
    return lower, upper


def edge_terms(edges, w_ref, side):
    b = 2 * side
    half = w_ref.shape[2]
    acc = dot(taps(w_ref, b, 0, 2), edges[1, side]) + dot(taps(w_ref, b, 1, 3), edges[2, side])
    return acc[half:] + dot(w_ref[0, b], edges[0, side]), acc[:half] + dot(w_ref[2, b], edges[3, side])


def inner_kernel(near, far, w_ref, d_ref, cot_ref, cols, acc_ref, grad_ref, up):
    rows, channels, breadth = near.shape
    fill_columns(cols, near, far)
    source = lax.broadcasted_iota(jnp.int32, (breadth, 2 * breadth), 0)
    target = lax.broadcasted_iota(jnp.int32, (breadth, 2 * breadth), 1)
    spread = jnp.where(source == target // 2, 1.0, 0.0).astype(BF16)
    for pair in range(rows // 4):
        both = dot(cot_ref[:, pair * breadth : (pair + 1) * breadth], spread)
        up[:, 2 * pair * breadth : 2 * (pair + 1) * breadth] = both.astype(BF16)
    even = lax.broadcasted_iota(jnp.int32, (channels, breadth), 1) % 2 == 0
    for a in range(2):
        for b in range(2):
            terms = lax.dot_general(d_ref[a, b], up[...], (((0,), (0,)), ((), ())), preferred_element_type=F32)
            for t in range(rows // 2):
                part = terms[:, t * breadth : (t + 1) * breadth]
                grad_ref[a, 2 * t + b] = jnp.where(even, part[0:channels], part[channels:])

    def step(t, carry):
        y = 2 * t
        for z, lines in enumerate(inner_terms(cols, w_ref, y)):
            for b in range(2):
                acc_ref[z, y + b] = lines[:, b * breadth : (b + 1) * breadth]
        return carry

    lax.fori_loop(0, rows // 2, step, 0)


def gated(preact, grad):
    sig = 1.0 / (1.0 + jnp.exp(-preact))
    return (preact * sig).astype(BF16), (grad * sig * (1.0 + preact * (1.0 - sig))).astype(BF16)


def outer_kernel(
    near, far, near_row, far_row, w_ref, acc_ref, grad_ref, cols, edges, side_ref, near_ref, far_ref, h_ref
):
    rows, channels, breadth = near.shape
    fill_columns(cols, near, far)
    fill_rows(edges, near_row, far_row)
    beside = []
    for side in range(2):
        terms = dot(taps(w_ref, 2 * side, 0, 2), edges[0, side]) + dot(taps(w_ref, 2 * side, 1, 3), edges[1, side])
        beside.append((terms[channels:], terms[:channels]))
    even = is_even("gz")
    for y in range(0, rows, 2):
        outer = outer_terms(cols, w_ref, y)
        for b in range(2):
            found = []
            for z in range(2):
                preact = acc_ref[z, y + b] + outer[z][:, b * breadth : (b + 1) * breadth]
                if y + b in (0, rows - 1):
                    side_ref[z, b] = preact + beside[b][z]
                else:
                    h_ref[z, y + b], gate = gated(preact, grad_ref[z, y + b])
                    found.append(gate)
            if len(found) > 0:
                near_ref[y + b] = choose(even, found[1], found[0])
                far_ref[y + b] = choose(even, found[0], found[1])


def gate_kernel(near, far, side_ref, near_in, far_in, h_in, grad_ref, w_ref, edges, near_ref, far_ref, h_ref):
    rows = near_in.shape[0]
    fill_rows(edges, near, far)
    even = is_even("gz")
    for side, y in enumerate((0, rows - 1)):
        terms = [dot(w_ref[2 * z, 2 * side], edges[z, side]) for z in range(2)]
        found = []
        for z in range(2):
            h_ref[z, y], gate = gated(side_ref[z, side] + terms[z], grad_ref[z, y])
            found.append(gate)
        near_ref[y] = choose(even, found[1], found[0])
        far_ref[y] = choose(even, found[0], found[1])
    for y in range(1, rows - 1):
        near_ref[y] = near_in[y]
        far_ref[y] = far_in[y]
        for z in range(2):
            h_ref[z, y] = h_in[z, y]


def coarse_hidden(h_ref):
    rows, channels, breadth = h_ref.shape[1:]
    source = lax.broadcasted_iota(jnp.int32, (2 * breadth, 2 * breadth), 0)
    target = lax.broadcasted_iota(jnp.int32, (2 * breadth, 2 * breadth), 1)
    wanted = 2 * (target % breadth) + target // breadth
    pick = jnp.where(source == wanted, 1.0, 0.0).astype(BF16)
    pairs = rows // 4
    both = [
        jnp.concatenate([h_ref[a, 4 * pair + b], h_ref[a, 4 * pair + 2 + b]], axis=1)
        for a in range(2) for b in range(2) for pair in range(pairs)
    ]
    picked = dot(jnp.concatenate(both, axis=0), pick).astype(BF16)
    blocks = []
    for tap in range(4):
        parts = [picked[(tap * pairs + pair) * channels : (tap * pairs + pair + 1) * channels] for pair in range(pairs)]
        for e in range(2):
            blocks.append(jnp.concatenate([x[:, e * breadth : (e + 1) * breadth] for x in parts], axis=1))
    return jnp.concatenate(blocks, axis=0)


def section_kernel(h_ref, d_ref, out_ref):
    down = jnp.concatenate([d_ref[a, b] for a in range(2) for b in range(2)], axis=1)
    out_ref[...] = dot(down, coarse_hidden(h_ref)).astype(BF16)


def weight_grad_kernel(inner, outer, own_edges, edges, near, far, h_ref, cot_ref, keep, send, packed):
    rows, channels, breadth = near.shape
    across = (((1,), (1,)), ((), ()))
    even = is_even("gz")
    low = [choose(even, far[y], near[y]) for y in range(rows)]
    high = [choose(even, near[y], far[y]) for y in range(rows)]
    nothing = jnp.zeros((channels, breadth), BF16)

    def shifted(lines):
        return jnp.concatenate(
            [jnp.concatenate([nothing] * b + lines + [nothing] * (2 - b), axis=1) for b in range(3)], axis=0
        )

    low, high = shifted(low), shifted(high)
    both = jnp.concatenate([low, high], axis=0)

    def columns(p, q):
        planes, rows_beside, at = (inner, own_edges, p - 1) if p in (1, 2) else (outer, edges, p // 3)
        return rows_beside[at, q // (rows + 1)] if q in (0, rows + 1) else planes[at, q]

    parts = []
    for p in range(4):
        lines = jnp.concatenate([columns(p, q) for q in range(rows + 2)], axis=1)
        lhs = low if p == 0 else high if p == 3 else both
        parts.append(lax.dot_general(lhs, lines, across, preferred_element_type=F32))
    lane = lax.broadcasted_iota(jnp.int32, (channels // 2, breadth), 1)
    for a in range(3):
        for b in range(3):
            at = b * channels + (0 if a == 2 else 3 * channels)
            total = parts[a][b * channels : (b + 1) * channels] + parts[a + 1][at : at + channels]
            base = (a * 3 + b) * 3 * channels // 2
            packed[base : base + channels] = total[:, 0:breadth]
            rest = jnp.concatenate([total[:, breadth:], total[:, breadth:]], axis=1)
            mix = jnp.where(lane < channels, rest[0 : channels // 2], rest[channels // 2 :])
            packed[base + channels : base + 3 * channels // 2] = mix
    base = 9 * 3 * channels // 2
    height = cot_ref.shape[0]
    down = lax.dot_general(cot_ref[...], coarse_hidden(h_ref), across, preferred_element_type=F32)
    for tap in range(4):
        packed[base + tap * height : base + (tap + 1) * height] = down[:, tap * breadth : (tap + 1) * breadth]
    end = base + 4 * height
    if end < packed.shape[0]:
        packed[end:] = jnp.zeros((packed.shape[0] - end, packed.shape[1]), F32)
    split(packed, keep, send, owned_half())


def side_of(axis, bit):
    return lax.rem(lax.axis_index(axis) // bit, 2)


def owned_half():
    total = 0
    for axis in ("gz", "gy"):
        for k in range(lax.axis_size(axis).bit_length() - 1):
            total = total + side_of(axis, 1 << k)
    return lax.rem(total, 2)


def part(side, rows):
    return pl.ds(pl.multiple_of(side * rows, 16), rows)


def split(packed, keep, send, side):
    half = keep.shape[0]
    keep[...] = packed[part(side, half)]
    send[...] = packed[part(1 - side, half)].astype(BF16)


def halve_kernel(mine, other, keep, send, total, *, axis, bit):
    total[...] = mine[...] + other[...].astype(F32)
    split(total, keep, send, side_of(axis, bit))


def add_kernel(x, y, out):
    out[...] = (x[...].astype(F32) + y[...].astype(F32)).astype(BF16)


def join_kernel(mine, other, out, *, axis, bit):
    join(mine, other, out, side_of(axis, bit))


def join(mine, other, out, side):
    rows = mine.shape[0]
    out[part(side, rows)] = mine[...]
    out[part(1 - side, rows)] = other[...]


def field_kernel(near, far, near_in, far_in, w_ref, acc_ref, inner, outer):
    rows, channels, breadth = near.shape
    fill_columns(inner, near, far)
    fill_columns(outer, near_in, far_in)

    def step(t, carry):
        y = 2 * t
        own = inner_terms(inner, w_ref, y)
        rest = outer_terms(outer, w_ref, y)
        for z in range(2):
            total = own[z] + rest[z]
            for b in range(2):
                acc_ref[z, y + b] = total[:, b * breadth : (b + 1) * breadth]
        return carry

    lax.fori_loop(0, rows // 2, step, 0)


def field_edges_kernel(near, far, acc_ref, w_ref, out_ref, edges):
    rows, channels, breadth = acc_ref.shape[1:]
    fill_rows(edges, near, far)
    sides = [edge_terms(edges, w_ref, side) for side in range(2)]
    for z in range(2):
        for y in range(rows):
            line = acc_ref[z, y]
            if y in (0, rows - 1):
                line = line + sides[0 if y == 0 else 1][z]
            out_ref[pl.ds(z * rows + y, channels, stride=2 * rows), :] = line


def unpack_kernel(mine, other, conv_ref, down_ref, sums_ref, *, scale):
    join(mine, other, sums_ref, owned_half())
    channels = conv_ref.shape[2]
    for a in range(3):
        for b in range(3):
            base = (a * 3 + b) * 3 * channels // 2
            conv_ref[a, b, :, 0 : 2 * channels] = sums_ref[base : base + channels].astype(F32) * scale
            rest = sums_ref[base + channels : base + 3 * channels // 2].astype(F32) * scale
            conv_ref[a, b, 0 : channels // 2, 2 * channels :] = rest[:, 0:channels]
            conv_ref[a, b, channels // 2 :, 2 * channels :] = rest[:, channels:]
    base = 9 * 3 * channels // 2
    height = down_ref.shape[2]
    for a in range(2):
        for b in range(2):
            at = base + (2 * a + b) * height
            down_ref[a, b] = sums_ref[at : at + height].astype(F32) * scale


def swap(cells, axis, low):
    count = lax.axis_size(axis)
    pairs = [(i % count, (i + 1) % count) for i in range(low, low + count, 2)]
    return lax.ppermute(cells, axis, pairs + [(b, a) for a, b in pairs])


def flip(cells, axis, bit):
    row = lax.axis_size("gy")
    mask = bit * row | 1 if axis == "gz" else bit | 1
    return lax.ppermute(cells, ("gz", "gy"), [(i, i ^ mask) for i in range(lax.axis_size("gz") * row)])


def tied(first, *others):
    found = lax.optimization_barrier((first, *others))
    return found[0], tuple(found[1:])


def swapped(near, far, axis):
    return swap(near, axis, 0), swap(far, axis, 1)


def body(features, conv_weight, down_weight, cotangent):
    channels, plane_count, row_count, breadth = features.shape
    out_channels = down_weight.shape[2]
    count = lax.axis_size("gz") * lax.axis_size("gy")
    grad_scale = 1.0 / math.sqrt(plane_count * row_count * breadth * count)
    cot = cotangent.reshape(out_channels, -1)
    conv_weight, down_weight, cot = fetch(conv_weight, down_weight, cot)
    (weight_bwd,) = call(turn_kernel, [(conv_weight.shape, BF16)], [], 0, (conv_weight,))
    plane = ((row_count, channels, breadth), BF16)
    edge = ((plane_count + 2, channels, breadth), BF16)
    cols = ((plane_count, row_count + 2, 3 * channels, breadth), BF16)
    edge_cols = ((plane_count + 2, 2, 3 * channels, breadth), BF16)
    lines = (plane_count, row_count, channels, breadth)
    conv_flops = 2 * 27 * channels * channels * plane_count * row_count * breadth

    pair = ((plane_count, channels, breadth), BF16)
    *own, near_row, far_row = call(
        lines_kernel, [plane, plane, pair, pair],
        [((channels * plane_count * row_count, breadth), F32)], 0, (features,),
    )
    outside = swapped(*own, "gz")
    beside = swapped(near_row, far_row, "gy")
    inner, acc, hidden_grad = call(
        inner_kernel, [cols, (lines, F32), (lines, F32)],
        [((out_channels, row_count // 2 * breadth), BF16)],
        2 * conv_flops // 3, (*own, conv_weight, down_weight, cot),
    )
    near, far, near_row, far_row, acc = lax.optimization_barrier((*outside, *beside, acc))
    outside, own_rows = (near, far), (near_row, far_row)
    beside = swapped(*call(outer_rows_kernel, [pair, pair], [], 0, outside), "gy")
    far, near = lax.optimization_barrier((beside[1], beside[0]))
    beside = (near, far)
    rows_cols = ((plane_count, 2, 3 * channels, breadth), BF16)
    outer, own_edges, *inside = call(
        outer_kernel,
        [cols, rows_cols, ((plane_count, 2, channels, breadth), F32), plane, plane, (lines, BF16)], [],
        conv_flops // 3, (*outside, *own_rows, conv_weight, acc, hidden_grad),
    )
    edges, near, far, hidden = call(
        gate_kernel, [rows_cols, plane, plane, (lines, BF16)], [], conv_flops // 10,
        (*beside, *inside, hidden_grad, conv_weight),
    )
    gates = (near, far)

    used = 27 * channels * channels // 128 + 4 * out_channels
    rows = -(-used // 128) * 128
    keep, send = call(
        weight_grad_kernel, [((rows // 2, 128), F32), ((rows // 2, 128), BF16)], [((rows, 128), F32)],
        conv_flops, (inner, outer, own_edges, edges, *gates, hidden, cot),
    )
    keep, gates = tied(keep, *gates)
    near, far = gates
    near_in = swap(near, "gz", 0)
    for level, (axis, bit) in enumerate((("gz", 2), ("gy", 2))):
        size = rows >> (level + 2)
        mine, got = keep, flip(send, *(("gy", 1), ("gz", 2))[level])
        keep, send = call(
            functools.partial(halve_kernel, axis=axis, bit=bit),
            [((size, 128), F32), ((size, 128), BF16)], [((2 * size, 128), F32)], 0, (mine, got),
        )
        if level == 0:
            keep, (far, hidden) = tied(keep, far, hidden)
            far_in = swap(far, "gz", 1)
            (section_out,) = call(
                section_kernel, [((out_channels, cot.shape[1]), BF16)], [], conv_flops // 10,
                (hidden, down_weight),
            )
    shard = ((rows // 8, 128), BF16)
    (sums,) = call(add_kernel, [shard], [], 0, (keep, flip(send, "gy", 2)))
    (sums,) = call(add_kernel, [shard], [], 0, (sums, flip(sums, "gz", 1)))
    sums, (near_in, far_in, weight_bwd) = tied(sums, near_in, far_in, weight_bwd)
    outside = (near_in, far_in)
    sends = call(edges_kernel, [edge, edge], [], 0, (*gates, *outside))
    beside = swapped(*sends, "gy")
    (acc,) = call(
        field_kernel, [(lines, F32)], [cols, cols], conv_flops, (*gates, *outside, weight_bwd)
    )
    wide = [("gy", 1 << k) for k in range(2, lax.axis_size("gy").bit_length() - 1)]
    wide += [("gz", 1 << k) for k in range(2, lax.axis_size("gz").bit_length() - 1)]
    for axis, bit in wide:
        (sums,) = call(add_kernel, [shard], [], 0, (sums, flip(sums, axis, bit)))
    sums, (section_out,) = tied(sums, section_out)
    (sums,) = call(
        functools.partial(join_kernel, axis="gy", bit=2), [((rows // 4, 128), BF16)], [], 0,
        (sums, flip(sums, "gy", 2)),
    )
    sums, (acc, *beside) = tied(sums, acc, *beside)
    (field,) = call(
        field_edges_kernel, [((channels * plane_count * row_count, breadth), F32)], [edge_cols],
        conv_flops // 10, (*beside, acc, weight_bwd),
    )
    (sums,) = call(
        functools.partial(join_kernel, axis="gz", bit=2), [((rows // 2, 128), BF16)], [], 0,
        (sums, flip(sums, "gz", 2)),
    )
    sums, (field,) = tied(sums, field)
    grad_conv, grad_down = call(
        functools.partial(unpack_kernel, scale=grad_scale),
        [(conv_weight.shape, F32), (down_weight.shape, F32)], [((rows, 128), BF16)], 0,
        (sums, flip(sums, "gy", 1)),
    )
    section_out = section_out.reshape(out_channels, plane_count // 2, -1)
    return (section_out, field.reshape(features.shape), grad_conv, grad_down)


def solution(mesh):
    return jax.shard_map(
        body,
        mesh=mesh,
        in_specs=(P(None, "gz", "gy", None), P(), P(), P(None, "gz", "gy")),
        out_specs=(P(None, "gz", "gy"), P(None, "gz", "gy", None), P(), P()),
        check_vma=False,
    )
```

```python
import functools
import math

import jax
import jax.numpy as jnp
from jax import lax
from jax.experimental import pallas as pl
from jax.experimental.pallas import tpu as pltpu
from jax.sharding import PartitionSpec as P

F32 = jnp.float32
BF16 = jnp.bfloat16
PARAMS = pltpu.CompilerParams(vmem_limit_bytes=24 * 1024 * 1024)


def call(kernel, outs, scratch, flops, operands):
    moved = sum(x.size * x.dtype.itemsize for x in operands)
    moved += sum(math.prod(s) * jnp.dtype(d).itemsize for s, d in outs)
    vmem = pl.BlockSpec(memory_space=pltpu.VMEM)
    return pl.pallas_call(
        kernel,
        out_shape=[jax.ShapeDtypeStruct(s, d) for s, d in outs],
        in_specs=[vmem] * len(operands),
        out_specs=[vmem] * len(outs),
        scratch_shapes=[pltpu.VMEM(s, d) for s, d in scratch],
        compiler_params=PARAMS,
        cost_estimate=pl.CostEstimate(flops=flops, bytes_accessed=moved, transcendentals=0),
    )(*operands)


def is_even(axis):
    return lax.rem(lax.axis_index(axis), 2) == 0


def choose(cond, yes, no):
    return jnp.where(jnp.broadcast_to(cond, yes.shape), yes, no)


def lines_kernel(f_ref, near_ref, far_ref, near_row, far_row, wide):
    channels, planes, rows, breadth = f_ref.shape
    wide[...] = f_ref[...].astype(F32).reshape(channels * planes * rows, breadth)
    even = is_even("gz")
    ends = {}
    for y in range(rows):
        low, high = ends[y] = [
            wide[pl.ds(z * rows + y, channels, stride=planes * rows), :].astype(BF16) for z in range(2)
        ]
        near_ref[y] = choose(even, high, low)
        far_ref[y] = choose(even, low, high)
    even_y = is_even("gy")
    for z in range(2):
        near_row[z] = choose(even_y, ends[rows - 1][z], ends[0][z])
        far_row[z] = choose(even_y, ends[0][z], ends[rows - 1][z])


def turn_kernel(w_ref, out):
    channels = w_ref.shape[2]
    for a in range(3):
        for b in range(3):
            turned = w_ref[a, b].astype(F32).T
            blocks = [turned[(2 - e) * channels : (3 - e) * channels] for e in range(3)]
            out[2 - a, 2 - b] = jnp.concatenate(blocks, axis=1).astype(BF16)


def fetch_kernel(*refs):
    *both, sems = refs
    count = len(both) // 2
    copies = [pltpu.make_async_copy(both[k], both[count + k], sems.at[k]) for k in range(count)]
    for copy in copies:
        copy.start()
    for copy in copies:
        copy.wait()


def fetch(*operands):
    return pl.pallas_call(
        fetch_kernel,
        out_shape=[jax.ShapeDtypeStruct(x.shape, x.dtype) for x in operands],
        in_specs=[pl.BlockSpec(memory_space=pltpu.HBM)] * len(operands),
        out_specs=[pl.BlockSpec(memory_space=pltpu.VMEM)] * len(operands),
        scratch_shapes=[pltpu.SemaphoreType.DMA((len(operands),))],
        compiler_params=PARAMS,
        cost_estimate=pl.CostEstimate(flops=0, bytes_accessed=2 * sum(x.size * 2 for x in operands), transcendentals=0),
    )(*operands)


def outer_rows_kernel(near_in, far_in, near_ref, far_ref):
    rows = near_in.shape[0]
    even_z, even_y = is_even("gz"), is_even("gy")
    for p, (one, other) in enumerate(((far_in, near_in), (near_in, far_in))):
        first = choose(even_z, one[0], other[0])
        last = choose(even_z, one[rows - 1], other[rows - 1])
        near_ref[p] = choose(even_y, last, first)
        far_ref[p] = choose(even_y, first, last)


def edges_kernel(near, far, near_in, far_in, near_ref, far_ref):
    rows = near.shape[0]
    even_z, even_y = is_even("gz"), is_even("gy")

    def put(p, one, other):
        first = choose(even_z, one[0], other[0])
        last = choose(even_z, one[rows - 1], other[rows - 1])
        near_ref[p] = choose(even_y, last, first)
        far_ref[p] = choose(even_y, first, last)

    put(0, far_in, near_in)
    put(1, far, near)
    put(2, near, far)
    put(3, near_in, far_in)


def put_columns(cols, p, q, line):
    channels = line.shape[0]
    wide = line.astype(F32)
    cols[p, q, 0:channels] = pltpu.roll(wide, 1, 1).astype(BF16)
    cols[p, q, channels : 2 * channels] = line
    cols[p, q, 2 * channels : 3 * channels] = pltpu.roll(wide, line.shape[1] - 1, 1).astype(BF16)


def fill_columns(cols, near, far):
    rows = near.shape[0]
    even = is_even("gz")

    def step(y, carry):
        put_columns(cols, 0, y + 1, choose(even, far[y], near[y]))
        put_columns(cols, 1, y + 1, choose(even, near[y], far[y]))
        return carry

    lax.fori_loop(0, rows, step, 0, unroll=2)
    for p in range(2):
        for q in (0, rows + 1):
            cols[p, q] = jnp.zeros(cols.shape[2:], BF16)


def fill_rows(cols, near, far):
    even = is_even("gy")
    for p in range(near.shape[0]):
        put_columns(cols, p, 0, choose(even, far[p], near[p]))
        put_columns(cols, p, 1, choose(even, near[p], far[p]))


def dot(lhs, rhs):
    return jnp.dot(lhs, rhs, preferred_element_type=F32)


def taps(w_ref, b, first, last):
    return jnp.concatenate([w_ref[a, b] for a in range(first, last)], axis=0)


def window(cols, p, q):
    return jnp.concatenate([cols[p, q], cols[p, q + 1]], axis=1)


def inner_terms(cols, w_ref, y):
    acc = None
    for b in range(3):
        for p in range(2):
            term = dot(taps(w_ref, b, p, p + 2), window(cols, p, y + b))
            acc = term if acc is None else acc + term
    half = acc.shape[0] // 2
    return acc[half:], acc[:half]


def outer_terms(cols, w_ref, y):
    lower = upper = None
    for b in range(3):
        low, high = dot(w_ref[0, b], window(cols, 0, y + b)), dot(w_ref[2, b], window(cols, 1, y + b))
        lower = low if lower is None else lower + low
        upper = high if upper is None else upper + high
    return lower, upper


def edge_terms(edges, w_ref, side):
    b = 2 * side
    half = w_ref.shape[2]
    acc = dot(taps(w_ref, b, 0, 2), edges[1, side]) + dot(taps(w_ref, b, 1, 3), edges[2, side])
    return acc[half:] + dot(w_ref[0, b], edges[0, side]), acc[:half] + dot(w_ref[2, b], edges[3, side])


def inner_kernel(near, far, w_ref, d_ref, cot_ref, cols, acc_ref, grad_ref, up):
    rows, channels, breadth = near.shape
    fill_columns(cols, near, far)
    source = lax.broadcasted_iota(jnp.int32, (breadth, 2 * breadth), 0)
    target = lax.broadcasted_iota(jnp.int32, (breadth, 2 * breadth), 1)
    spread = jnp.where(source == target // 2, 1.0, 0.0).astype(BF16)
    for pair in range(rows // 4):
        both = dot(cot_ref[:, pair * breadth : (pair + 1) * breadth], spread)
        up[:, 2 * pair * breadth : 2 * (pair + 1) * breadth] = both.astype(BF16)
    even = lax.broadcasted_iota(jnp.int32, (channels, breadth), 1) % 2 == 0
    for a in range(2):
        for b in range(2):
            terms = lax.dot_general(d_ref[a, b], up[...], (((0,), (0,)), ((), ())), preferred_element_type=F32)
            for t in range(rows // 2):
                part = terms[:, t * breadth : (t + 1) * breadth]
                grad_ref[a, 2 * t + b] = jnp.where(even, part[0:channels], part[channels:])

    def step(t, carry):
        y = 2 * t
        for z, lines in enumerate(inner_terms(cols, w_ref, y)):
            for b in range(2):
                acc_ref[z, y + b] = lines[:, b * breadth : (b + 1) * breadth]
        return carry

    lax.fori_loop(0, rows // 2, step, 0)


def gated(preact, grad):
    sig = 1.0 / (1.0 + jnp.exp(-preact))
    return (preact * sig).astype(BF16), (grad * sig * (1.0 + preact * (1.0 - sig))).astype(BF16)


def outer_kernel(
    near, far, near_row, far_row, w_ref, acc_ref, grad_ref, cols, edges, side_ref, near_ref, far_ref, h_ref
):
    rows, channels, breadth = near.shape
    fill_columns(cols, near, far)
    fill_rows(edges, near_row, far_row)
    beside = []
    for side in range(2):
        terms = dot(taps(w_ref, 2 * side, 0, 2), edges[0, side]) + dot(taps(w_ref, 2 * side, 1, 3), edges[1, side])
        beside.append((terms[channels:], terms[:channels]))
    even = is_even("gz")
    for y in range(0, rows, 2):
        outer = outer_terms(cols, w_ref, y)
        for b in range(2):
            found = []
            for z in range(2):
                preact = acc_ref[z, y + b] + outer[z][:, b * breadth : (b + 1) * breadth]
                if y + b in (0, rows - 1):
                    side_ref[z, b] = preact + beside[b][z]
                else:
                    h_ref[z, y + b], gate = gated(preact, grad_ref[z, y + b])
                    found.append(gate)
            if len(found) > 0:
                near_ref[y + b] = choose(even, found[1], found[0])
                far_ref[y + b] = choose(even, found[0], found[1])


def gate_kernel(near, far, side_ref, near_in, far_in, h_in, grad_ref, w_ref, edges, near_ref, far_ref, h_ref):
    rows = near_in.shape[0]
    fill_rows(edges, near, far)
    even = is_even("gz")
    for side, y in enumerate((0, rows - 1)):
        terms = [dot(w_ref[2 * z, 2 * side], edges[z, side]) for z in range(2)]
        found = []
        for z in range(2):
            h_ref[z, y], gate = gated(side_ref[z, side] + terms[z], grad_ref[z, y])
            found.append(gate)
        near_ref[y] = choose(even, found[1], found[0])
        far_ref[y] = choose(even, found[0], found[1])
    for y in range(1, rows - 1):
        near_ref[y] = near_in[y]
        far_ref[y] = far_in[y]
        for z in range(2):
            h_ref[z, y] = h_in[z, y]


def tap_row(tap, rows, channels):
    size = 3 * channels // 2
    return tap * size if tap < 7 else 7 * size + 8 * channels + (tap - 7) * size


def coarse_hidden(h_ref):
    rows, channels, breadth = h_ref.shape[1:]
    source = lax.broadcasted_iota(jnp.int32, (2 * breadth, 2 * breadth), 0)
    target = lax.broadcasted_iota(jnp.int32, (2 * breadth, 2 * breadth), 1)
    wanted = 2 * (target % breadth) + target // breadth
    pick = jnp.where(source == wanted, 1.0, 0.0).astype(BF16)
    pairs = rows // 4
    both = [
        jnp.concatenate([h_ref[a, 4 * pair + b], h_ref[a, 4 * pair + 2 + b]], axis=1)
        for a in range(2) for b in range(2) for pair in range(pairs)
    ]
    picked = dot(jnp.concatenate(both, axis=0), pick).astype(BF16)
    blocks = []
    for tap in range(4):
        parts = [picked[(tap * pairs + pair) * channels : (tap * pairs + pair + 1) * channels] for pair in range(pairs)]
        for e in range(2):
            blocks.append(jnp.concatenate([x[:, e * breadth : (e + 1) * breadth] for x in parts], axis=1))
    return jnp.concatenate(blocks, axis=0)


def section_kernel(h_ref, d_ref, out_ref):
    down = jnp.concatenate([d_ref[a, b] for a in range(2) for b in range(2)], axis=1)
    out_ref[...] = dot(down, coarse_hidden(h_ref)).astype(BF16)


def weight_grad_kernel(inner, outer, own_edges, edges, near, far, h_ref, cot_ref, keep, send, packed):
    rows, channels, breadth = near.shape
    across = (((1,), (1,)), ((), ()))
    even = is_even("gz")
    low = [choose(even, far[y], near[y]) for y in range(rows)]
    high = [choose(even, near[y], far[y]) for y in range(rows)]
    nothing = jnp.zeros((channels, breadth), BF16)

    def shifted(lines):
        return jnp.concatenate(
            [jnp.concatenate([nothing] * b + lines + [nothing] * (2 - b), axis=1) for b in range(3)], axis=0
        )

    low, high = shifted(low), shifted(high)
    both = jnp.concatenate([low, high], axis=0)

    def columns(p, q):
        planes, rows_beside, at = (inner, own_edges, p - 1) if p in (1, 2) else (outer, edges, p // 3)
        return rows_beside[at, q // (rows + 1)] if q in (0, rows + 1) else planes[at, q]

    parts = []
    for p in range(4):
        lines = jnp.concatenate([columns(p, q) for q in range(rows + 2)], axis=1)
        lhs = low if p == 0 else high if p == 3 else both
        parts.append(lax.dot_general(lhs, lines, across, preferred_element_type=F32))
    lane = lax.broadcasted_iota(jnp.int32, (channels // 2, breadth), 1)
    for a in range(3):
        for b in range(3):
            at = b * channels + (0 if a == 2 else 3 * channels)
            total = parts[a][b * channels : (b + 1) * channels] + parts[a + 1][at : at + channels]
            base = tap_row(a * 3 + b, packed.shape[0], channels)
            packed[base : base + channels] = total[:, 0:breadth]
            rest = jnp.concatenate([total[:, breadth:], total[:, breadth:]], axis=1)
            mix = jnp.where(lane < channels, rest[0 : channels // 2], rest[channels // 2 :])
            packed[base + channels : base + 3 * channels // 2] = mix
    height = cot_ref.shape[0]
    down = lax.dot_general(cot_ref[...], coarse_hidden(h_ref), across, preferred_element_type=F32)
    base = 7 * 3 * channels // 2
    for tap in range(4):
        packed[base + tap * height : base + (tap + 1) * height] = down[:, tap * breadth : (tap + 1) * breadth]
    end = base + 4 * height + 2 * 3 * channels // 2
    if end < packed.shape[0]:
        packed[end:] = jnp.zeros((packed.shape[0] - end, packed.shape[1]), F32)
    split(packed, keep, send, owned_half())


def side_of(axis, bit):
    return lax.rem(lax.axis_index(axis) // bit, 2)


def owned_half():
    total = 0
    for axis in ("gz", "gy"):
        for k in range(lax.axis_size(axis).bit_length() - 1):
            total = total + side_of(axis, 1 << k)
    return lax.rem(total, 2)


def part(side, rows):
    return pl.ds(pl.multiple_of(side * rows, 16), rows)


def split(packed, keep, send, side):
    half = keep.shape[0]
    keep[...] = packed[part(side, half)]
    send[...] = packed[part(1 - side, half)].astype(BF16)


def halve_kernel(mine, other, keep, send, total, *, axis, bit):
    total[...] = mine[...] + other[...].astype(F32)
    split(total, keep, send, side_of(axis, bit))


def add_kernel(x, y, out):
    out[...] = (x[...].astype(F32) + y[...].astype(F32)).astype(BF16)


def join_kernel(mine, other, out, *, axis, bit):
    join(mine, other, out, side_of(axis, bit))


def join(mine, other, out, side):
    rows = mine.shape[0]
    out[part(side, rows)] = mine[...]
    out[part(1 - side, rows)] = other[...]


def field_kernel(near, far, near_in, far_in, w_ref, acc_ref, inner, outer):
    rows, channels, breadth = near.shape
    fill_columns(inner, near, far)
    fill_columns(outer, near_in, far_in)

    def step(t, carry):
        y = 2 * t
        own = inner_terms(inner, w_ref, y)
        rest = outer_terms(outer, w_ref, y)
        for z in range(2):
            total = own[z] + rest[z]
            for b in range(2):
                acc_ref[z, y + b] = total[:, b * breadth : (b + 1) * breadth]
        return carry

    lax.fori_loop(0, rows // 2, step, 0)


def field_edges_kernel(near, far, acc_ref, w_ref, out_ref, edges):
    rows, channels, breadth = acc_ref.shape[1:]
    fill_rows(edges, near, far)
    sides = [edge_terms(edges, w_ref, side) for side in range(2)]
    for z in range(2):
        for y in range(rows):
            line = acc_ref[z, y]
            if y in (0, rows - 1):
                line = line + sides[0 if y == 0 else 1][z]
            out_ref[pl.ds(z * rows + y, channels, stride=2 * rows), :] = line


def write_half(half, sums, conv_out, down_out, conv, down, sems, scale):
    channels, height = conv.shape[2], down.shape[2]
    size, rows = 3 * channels // 2, sums.shape[0]
    for tap in range(7) if half == 0 else range(7, 9):
        base = tap_row(tap, 2 * rows, channels) - half * rows
        a, b = divmod(tap, 3)
        conv[a, b, :, 0 : 2 * channels] = sums[base : base + channels].astype(F32) * scale
        rest = sums[base + channels : base + size].astype(F32) * scale
        conv[a, b, 0 : channels // 2, 2 * channels :] = rest[:, 0:channels]
        conv[a, b, channels // 2 :, 2 * channels :] = rest[:, channels:]
    first = rows - 7 * size
    if half == 0:
        down[0, 0, 0:first] = sums[7 * size :].astype(F32) * scale
        spans = [(conv, conv_out, (pl.ds(0, 2),)), (conv, conv_out, (2, 0)), (down, down_out, (0, 0, pl.ds(0, first)))]
    else:
        down[0, 0, first:] = sums[0 : height - first].astype(F32) * scale
        for tap in range(1, 4):
            at = tap * height - first
            down[tap // 2, tap % 2] = sums[at : at + height].astype(F32) * scale
        spans = [
            (conv, conv_out, (2, pl.ds(1, 2))), (down, down_out, (0, 0, pl.ds(first, height - first))),
            (down, down_out, (0, 1)), (down, down_out, (1,)),
        ]
    copies = [pltpu.make_async_copy(x.at[at], y.at[at], sems.at[k]) for k, (x, y, at) in enumerate(spans)]
    for copy in copies:
        copy.start()
    for copy in copies:
        copy.wait()


def write_kernel(sums, *refs, own, scale):
    conv_out, down_out, conv, down, sems = refs[-5:]
    half = owned_half() if own else 1 - owned_half()

    @pl.when(half == 0)
    def _():
        write_half(0, sums, conv_out, down_out, conv, down, sems, scale)

    @pl.when(half == 1)
    def _():
        write_half(1, sums, conv_out, down_out, conv, down, sems, scale)


def write(sums, shapes, scale, outs=()):
    return pl.pallas_call(
        functools.partial(write_kernel, own=len(outs) == 0, scale=scale),
        out_shape=[jax.ShapeDtypeStruct(shape, F32) for shape in shapes],
        in_specs=[pl.BlockSpec(memory_space=pltpu.VMEM)] + [pl.BlockSpec(memory_space=pltpu.HBM)] * len(outs),
        out_specs=[pl.BlockSpec(memory_space=pltpu.HBM)] * 2,
        scratch_shapes=[pltpu.VMEM(shape, F32) for shape in shapes] + [pltpu.SemaphoreType.DMA((4,))],
        input_output_aliases={1 + k: k for k in range(len(outs))},
        compiler_params=PARAMS,
    )(sums, *outs)


def swap(cells, axis, low):
    count = lax.axis_size(axis)
    pairs = [(i % count, (i + 1) % count) for i in range(low, low + count, 2)]
    return lax.ppermute(cells, axis, pairs + [(b, a) for a, b in pairs])


def flip(cells, axis, bit):
    row = lax.axis_size("gy")
    mask = bit * row | 1 if axis == "gz" else bit | 1
    return lax.ppermute(cells, ("gz", "gy"), [(i, i ^ mask) for i in range(lax.axis_size("gz") * row)])


def tied(first, *others):
    found = lax.optimization_barrier((first, *others))
    return found[0], tuple(found[1:])


def swapped(near, far, axis):
    return swap(near, axis, 0), swap(far, axis, 1)


def body(features, conv_weight, down_weight, cotangent):
    channels, plane_count, row_count, breadth = features.shape
    out_channels = down_weight.shape[2]
    count = lax.axis_size("gz") * lax.axis_size("gy")
    grad_scale = 1.0 / math.sqrt(plane_count * row_count * breadth * count)
    cot = cotangent.reshape(out_channels, -1)
    conv_weight, down_weight, cot = fetch(conv_weight, down_weight, cot)
    (weight_bwd,) = call(turn_kernel, [(conv_weight.shape, BF16)], [], 0, (conv_weight,))
    plane = ((row_count, channels, breadth), BF16)
    edge = ((plane_count + 2, channels, breadth), BF16)
    cols = ((plane_count, row_count + 2, 3 * channels, breadth), BF16)
    edge_cols = ((plane_count + 2, 2, 3 * channels, breadth), BF16)
    lines = (plane_count, row_count, channels, breadth)
    conv_flops = 2 * 27 * channels * channels * plane_count * row_count * breadth

    pair = ((plane_count, channels, breadth), BF16)
    *own, near_row, far_row = call(
        lines_kernel, [plane, plane, pair, pair],
        [((channels * plane_count * row_count, breadth), F32)], 0, (features,),
    )
    outside = swapped(*own, "gz")
    beside = swapped(near_row, far_row, "gy")
    inner, acc, hidden_grad = call(
        inner_kernel, [cols, (lines, F32), (lines, F32)],
        [((out_channels, row_count // 2 * breadth), BF16)],
        2 * conv_flops // 3, (*own, conv_weight, down_weight, cot),
    )
    near, far, near_row, far_row, acc = lax.optimization_barrier((*outside, *beside, acc))
    outside, own_rows = (near, far), (near_row, far_row)
    beside = swapped(*call(outer_rows_kernel, [pair, pair], [], 0, outside), "gy")
    far, near = lax.optimization_barrier((beside[1], beside[0]))
    beside = (near, far)
    rows_cols = ((plane_count, 2, 3 * channels, breadth), BF16)
    outer, own_edges, *inside = call(
        outer_kernel,
        [cols, rows_cols, ((plane_count, 2, channels, breadth), F32), plane, plane, (lines, BF16)], [],
        conv_flops // 3, (*outside, *own_rows, conv_weight, acc, hidden_grad),
    )
    edges, near, far, hidden = call(
        gate_kernel, [rows_cols, plane, plane, (lines, BF16)], [], conv_flops // 10,
        (*beside, *inside, hidden_grad, conv_weight),
    )
    gates = (near, far)

    used = 27 * channels * channels // 128 + 4 * out_channels
    rows = -(-used // 128) * 128
    keep, send = call(
        weight_grad_kernel, [((rows // 2, 128), F32), ((rows // 2, 128), BF16)], [((rows, 128), F32)],
        conv_flops, (inner, outer, own_edges, edges, *gates, hidden, cot),
    )
    keep, gates = tied(keep, *gates)
    near, far = gates
    near_in = swap(near, "gz", 0)
    for level, (axis, bit) in enumerate((("gz", 2), ("gy", 2))):
        size = rows >> (level + 2)
        mine, got = keep, flip(send, *(("gy", 1), ("gz", 2))[level])
        keep, send = call(
            functools.partial(halve_kernel, axis=axis, bit=bit),
            [((size, 128), F32), ((size, 128), BF16)], [((2 * size, 128), F32)], 0, (mine, got),
        )
        if level == 0:
            keep, (far, hidden) = tied(keep, far, hidden)
            far_in = swap(far, "gz", 1)
            (section_out,) = call(
                section_kernel, [((out_channels, cot.shape[1]), BF16)], [], conv_flops // 10,
                (hidden, down_weight),
            )
    shard = ((rows // 8, 128), BF16)
    (sums,) = call(add_kernel, [shard], [], 0, (keep, flip(send, "gy", 2)))
    (sums,) = call(add_kernel, [shard], [], 0, (sums, flip(sums, "gz", 1)))
    sums, outside = tied(sums, near_in, far_in)
    sends = call(edges_kernel, [edge, edge], [], 0, (*gates, *outside))
    beside = swapped(*sends, "gy")
    (acc,) = call(
        field_kernel, [(lines, F32)], [cols, cols], conv_flops, (*gates, *outside, weight_bwd)
    )
    wide = [("gy", 1 << k) for k in range(2, lax.axis_size("gy").bit_length() - 1)]
    wide += [("gz", 1 << k) for k in range(2, lax.axis_size("gz").bit_length() - 1)]
    for axis, bit in wide:
        (sums,) = call(add_kernel, [shard], [], 0, (sums, flip(sums, axis, bit)))
    sums, (section_out,) = tied(sums, section_out)
    (sums,) = call(
        functools.partial(join_kernel, axis="gy", bit=2), [((rows // 4, 128), BF16)], [], 0,
        (sums, flip(sums, "gy", 2)),
    )
    sums, (acc, *beside) = tied(sums, acc, *beside)
    (field,) = call(
        field_edges_kernel, [((channels * plane_count * row_count, breadth), F32)], [edge_cols],
        conv_flops // 10, (*beside, acc, weight_bwd),
    )
    (sums,) = call(
        functools.partial(join_kernel, axis="gz", bit=2), [((rows // 2, 128), BF16)], [], 0,
        (sums, flip(sums, "gz", 2)),
    )
    sums, (field,) = tied(sums, field)
    shapes = (conv_weight.shape, down_weight.shape)
    other = flip(sums, "gy", 1)
    grad_conv, grad_down = write(other, shapes, grad_scale, write(sums, shapes, grad_scale))
    section_out = section_out.reshape(out_channels, plane_count // 2, -1)
    return (section_out, field.reshape(features.shape), grad_conv, grad_down)


def solution(mesh):
    return jax.shard_map(
        body,
        mesh=mesh,
        in_specs=(P(None, "gz", "gy", None), P(), P(), P(None, "gz", "gy")),
        out_specs=(P(None, "gz", "gy"), P(None, "gz", "gy", None), P(), P()),
        check_vma=False,
    )
```

```python
import functools
import math

import jax
import jax.numpy as jnp
from jax import lax
from jax.experimental import pallas as pl
from jax.experimental.pallas import tpu as pltpu
from jax.sharding import PartitionSpec as P

F32 = jnp.float32
BF16 = jnp.bfloat16
PARAMS = pltpu.CompilerParams(vmem_limit_bytes=24 * 1024 * 1024)


def call(kernel, outs, scratch, flops, operands):
    moved = sum(x.size * x.dtype.itemsize for x in operands)
    moved += sum(math.prod(s) * jnp.dtype(d).itemsize for s, d in outs)
    vmem = pl.BlockSpec(memory_space=pltpu.VMEM)
    return pl.pallas_call(
        kernel,
        out_shape=[jax.ShapeDtypeStruct(s, d) for s, d in outs],
        in_specs=[vmem] * len(operands),
        out_specs=[vmem] * len(outs),
        scratch_shapes=[pltpu.VMEM(s, d) for s, d in scratch],
        compiler_params=PARAMS,
        cost_estimate=pl.CostEstimate(flops=flops, bytes_accessed=moved, transcendentals=0),
    )(*operands)


def is_even(axis):
    return lax.rem(lax.axis_index(axis), 2) == 0


def choose(cond, yes, no):
    return jnp.where(jnp.broadcast_to(cond, yes.shape), yes, no)


def lines_kernel(f_ref, near_ref, far_ref, near_row, far_row, wide):
    channels, planes, rows, breadth = f_ref.shape
    wide[...] = f_ref[...].astype(F32).reshape(channels * planes * rows, breadth)
    even = is_even("gz")
    ends = {}
    for y in range(rows):
        low, high = ends[y] = [
            wide[pl.ds(z * rows + y, channels, stride=planes * rows), :].astype(BF16) for z in range(2)
        ]
        near_ref[y] = choose(even, high, low)
        far_ref[y] = choose(even, low, high)
    even_y = is_even("gy")
    for z in range(2):
        near_row[z] = choose(even_y, ends[rows - 1][z], ends[0][z])
        far_row[z] = choose(even_y, ends[0][z], ends[rows - 1][z])


def turn_kernel(w_ref, out):
    channels = w_ref.shape[2]
    for a in range(3):
        for b in range(3):
            turned = w_ref[a, b].astype(F32).T
            blocks = [turned[(2 - e) * channels : (3 - e) * channels] for e in range(3)]
            out[2 - a, 2 - b] = jnp.concatenate(blocks, axis=1).astype(BF16)


def fetch_kernel(*refs):
    *both, sems = refs
    count = len(both) // 2
    copies = [pltpu.make_async_copy(both[k], both[count + k], sems.at[k]) for k in range(count)]
    for copy in copies:
        copy.start()
    for copy in copies:
        copy.wait()


def fetch(*operands):
    return pl.pallas_call(
        fetch_kernel,
        out_shape=[jax.ShapeDtypeStruct(x.shape, x.dtype) for x in operands],
        in_specs=[pl.BlockSpec(memory_space=pltpu.HBM)] * len(operands),
        out_specs=[pl.BlockSpec(memory_space=pltpu.VMEM)] * len(operands),
        scratch_shapes=[pltpu.SemaphoreType.DMA((len(operands),))],
        compiler_params=PARAMS,
        cost_estimate=pl.CostEstimate(flops=0, bytes_accessed=2 * sum(x.size * 2 for x in operands), transcendentals=0),
    )(*operands)


def outer_rows_kernel(near_in, far_in, near_ref, far_ref):
    rows = near_in.shape[0]
    even_z, even_y = is_even("gz"), is_even("gy")
    for p, (one, other) in enumerate(((far_in, near_in), (near_in, far_in))):
        first = choose(even_z, one[0], other[0])
        last = choose(even_z, one[rows - 1], other[rows - 1])
        near_ref[p] = choose(even_y, last, first)
        far_ref[p] = choose(even_y, first, last)


def edges_kernel(near, far, near_in, far_in, near_ref, far_ref):
    rows = near.shape[0]
    even_z, even_y = is_even("gz"), is_even("gy")

    def put(p, one, other):
        first = choose(even_z, one[0], other[0])
        last = choose(even_z, one[rows - 1], other[rows - 1])
        near_ref[p] = choose(even_y, last, first)
        far_ref[p] = choose(even_y, first, last)

    put(0, far_in, near_in)
    put(1, far, near)
    put(2, near, far)
    put(3, near_in, far_in)


def put_columns(cols, p, q, line):
    channels = line.shape[0]
    wide = line.astype(F32)
    cols[p, q, 0:channels] = pltpu.roll(wide, 1, 1).astype(BF16)
    cols[p, q, channels : 2 * channels] = line
    cols[p, q, 2 * channels : 3 * channels] = pltpu.roll(wide, line.shape[1] - 1, 1).astype(BF16)


def fill_columns(cols, near, far):
    rows = near.shape[0]
    even = is_even("gz")

    def step(y, carry):
        put_columns(cols, 0, y + 1, choose(even, far[y], near[y]))
        put_columns(cols, 1, y + 1, choose(even, near[y], far[y]))
        return carry

    lax.fori_loop(0, rows, step, 0, unroll=2)
    for p in range(2):
        for q in (0, rows + 1):
            cols[p, q] = jnp.zeros(cols.shape[2:], BF16)


def fill_rows(cols, near, far):
    even = is_even("gy")
    for p in range(near.shape[0]):
        put_columns(cols, p, 0, choose(even, far[p], near[p]))
        put_columns(cols, p, 1, choose(even, near[p], far[p]))


def dot(lhs, rhs):
    return jnp.dot(lhs, rhs, preferred_element_type=F32)


def taps(w_ref, b, first, last):
    return jnp.concatenate([w_ref[a, b] for a in range(first, last)], axis=0)


def window(cols, p, q):
    return jnp.concatenate([cols[p, q], cols[p, q + 1]], axis=1)


def inner_terms(cols, w_ref, y):
    acc = None
    for b in range(3):
        for p in range(2):
            term = dot(taps(w_ref, b, p, p + 2), window(cols, p, y + b))
            acc = term if acc is None else acc + term
    half = acc.shape[0] // 2
    return acc[half:], acc[:half]


def outer_terms(cols, w_ref, y):
    lower = upper = None
    for b in range(3):
        low, high = dot(w_ref[0, b], window(cols, 0, y + b)), dot(w_ref[2, b], window(cols, 1, y + b))
        lower = low if lower is None else lower + low
        upper = high if upper is None else upper + high
    return lower, upper


def edge_terms(edges, w_ref, side):
    b = 2 * side
    half = w_ref.shape[2]
    acc = dot(taps(w_ref, b, 0, 2), edges[1, side]) + dot(taps(w_ref, b, 1, 3), edges[2, side])
    return acc[half:] + dot(w_ref[0, b], edges[0, side]), acc[:half] + dot(w_ref[2, b], edges[3, side])


def inner_kernel(near, far, w_ref, d_ref, cot_ref, cols, acc_ref, grad_ref, up):
    rows, channels, breadth = near.shape
    fill_columns(cols, near, far)
    source = lax.broadcasted_iota(jnp.int32, (breadth, 2 * breadth), 0)
    target = lax.broadcasted_iota(jnp.int32, (breadth, 2 * breadth), 1)
    spread = jnp.where(source == target // 2, 1.0, 0.0).astype(BF16)
    for pair in range(rows // 4):
        both = dot(cot_ref[:, pair * breadth : (pair + 1) * breadth], spread)
        up[:, 2 * pair * breadth : 2 * (pair + 1) * breadth] = both.astype(BF16)
    even = lax.broadcasted_iota(jnp.int32, (channels, breadth), 1) % 2 == 0
    for a in range(2):
        for b in range(2):
            terms = lax.dot_general(d_ref[a, b], up[...], (((0,), (0,)), ((), ())), preferred_element_type=F32)
            for t in range(rows // 2):
                part = terms[:, t * breadth : (t + 1) * breadth]
                grad_ref[a, 2 * t + b] = jnp.where(even, part[0:channels], part[channels:])

    def step(t, carry):
        y = 2 * t
        for z, lines in enumerate(inner_terms(cols, w_ref, y)):
            for b in range(2):
                acc_ref[z, y + b] = lines[:, b * breadth : (b + 1) * breadth]
        return carry

    lax.fori_loop(0, rows // 2, step, 0)


def gated(preact, grad):
    sig = 1.0 / (1.0 + jnp.exp(-preact))
    return (preact * sig).astype(BF16), (grad * sig * (1.0 + preact * (1.0 - sig))).astype(BF16)


def outer_kernel(
    near, far, near_row, far_row, w_ref, acc_ref, grad_ref, cols, edges, side_ref, near_ref, far_ref, h_ref
):
    rows, channels, breadth = near.shape
    fill_columns(cols, near, far)
    fill_rows(edges, near_row, far_row)
    beside = []
    for side in range(2):
        terms = dot(taps(w_ref, 2 * side, 0, 2), edges[0, side]) + dot(taps(w_ref, 2 * side, 1, 3), edges[1, side])
        beside.append((terms[channels:], terms[:channels]))
    even = is_even("gz")
    for y in range(0, rows, 2):
        outer = outer_terms(cols, w_ref, y)
        for b in range(2):
            found = []
            for z in range(2):
                preact = acc_ref[z, y + b] + outer[z][:, b * breadth : (b + 1) * breadth]
                if y + b in (0, rows - 1):
                    side_ref[z, b] = preact + beside[b][z]
                else:
                    h_ref[z, y + b], gate = gated(preact, grad_ref[z, y + b])
                    found.append(gate)
            if len(found) > 0:
                near_ref[y + b] = choose(even, found[1], found[0])
                far_ref[y + b] = choose(even, found[0], found[1])


def gate_kernel(near, far, side_ref, near_in, far_in, h_in, grad_ref, w_ref, edges, near_ref, far_ref, h_ref):
    rows = near_in.shape[0]
    fill_rows(edges, near, far)
    even = is_even("gz")
    for side, y in enumerate((0, rows - 1)):
        terms = [dot(w_ref[2 * z, 2 * side], edges[z, side]) for z in range(2)]
        found = []
        for z in range(2):
            h_ref[z, y], gate = gated(side_ref[z, side] + terms[z], grad_ref[z, y])
            found.append(gate)
        near_ref[y] = choose(even, found[1], found[0])
        far_ref[y] = choose(even, found[0], found[1])
    for y in range(1, rows - 1):
        near_ref[y] = near_in[y]
        far_ref[y] = far_in[y]
        for z in range(2):
            h_ref[z, y] = h_in[z, y]


def tap_row(tap, rows, channels):
    size = 3 * channels // 2
    return tap * size if tap < 7 else 7 * size + 8 * channels + (tap - 7) * size


def coarse_hidden(h_ref):
    rows, channels, breadth = h_ref.shape[1:]
    source = lax.broadcasted_iota(jnp.int32, (2 * breadth, 2 * breadth), 0)
    target = lax.broadcasted_iota(jnp.int32, (2 * breadth, 2 * breadth), 1)
    wanted = 2 * (target % breadth) + target // breadth
    pick = jnp.where(source == wanted, 1.0, 0.0).astype(BF16)
    pairs = rows // 4
    both = [
        jnp.concatenate([h_ref[a, 4 * pair + b], h_ref[a, 4 * pair + 2 + b]], axis=1)
        for a in range(2) for b in range(2) for pair in range(pairs)
    ]
    picked = dot(jnp.concatenate(both, axis=0), pick).astype(BF16)
    blocks = []
    for tap in range(4):
        parts = [picked[(tap * pairs + pair) * channels : (tap * pairs + pair + 1) * channels] for pair in range(pairs)]
        for e in range(2):
            blocks.append(jnp.concatenate([x[:, e * breadth : (e + 1) * breadth] for x in parts], axis=1))
    return jnp.concatenate(blocks, axis=0)


def section_kernel(h_ref, d_ref, out_ref):
    down = jnp.concatenate([d_ref[a, b] for a in range(2) for b in range(2)], axis=1)
    out_ref[...] = dot(down, coarse_hidden(h_ref)).astype(BF16)


def weight_grad_kernel(inner, outer, own_edges, edges, near, far, h_ref, cot_ref, keep, send, packed):
    rows, channels, breadth = near.shape
    across = (((1,), (1,)), ((), ()))
    even = is_even("gz")
    low = [choose(even, far[y], near[y]) for y in range(rows)]
    high = [choose(even, near[y], far[y]) for y in range(rows)]
    nothing = jnp.zeros((channels, breadth), BF16)

    def shifted(lines):
        return jnp.concatenate(
            [jnp.concatenate([nothing] * b + lines + [nothing] * (2 - b), axis=1) for b in range(3)], axis=0
        )

    low, high = shifted(low), shifted(high)
    both = jnp.concatenate([low, high], axis=0)

    def columns(p, q):
        planes, rows_beside, at = (inner, own_edges, p - 1) if p in (1, 2) else (outer, edges, p // 3)
        return rows_beside[at, q // (rows + 1)] if q in (0, rows + 1) else planes[at, q]

    parts = []
    for p in range(4):
        lines = jnp.concatenate([columns(p, q) for q in range(rows + 2)], axis=1)
        lhs = low if p == 0 else high if p == 3 else both
        parts.append(lax.dot_general(lhs, lines, across, preferred_element_type=F32))
    lane = lax.broadcasted_iota(jnp.int32, (channels // 2, breadth), 1)
    for a in range(3):
        for b in range(3):
            at = b * channels + (0 if a == 2 else 3 * channels)
            total = parts[a][b * channels : (b + 1) * channels] + parts[a + 1][at : at + channels]
            base = tap_row(a * 3 + b, packed.shape[0], channels)
            packed[base : base + channels] = total[:, 0:breadth]
            rest = jnp.concatenate([total[:, breadth:], total[:, breadth:]], axis=1)
            mix = jnp.where(lane < channels, rest[0 : channels // 2], rest[channels // 2 :])
            packed[base + channels : base + 3 * channels // 2] = mix
    height = cot_ref.shape[0]
    down = lax.dot_general(cot_ref[...], coarse_hidden(h_ref), across, preferred_element_type=F32)
    base = 7 * 3 * channels // 2
    for tap in range(4):
        packed[base + tap * height : base + (tap + 1) * height] = down[:, tap * breadth : (tap + 1) * breadth]
    end = base + 4 * height + 2 * 3 * channels // 2
    if end < packed.shape[0]:
        packed[end:] = jnp.zeros((packed.shape[0] - end, packed.shape[1]), F32)
    split(packed, keep, send, owned_half())


def side_of(axis, bit):
    return lax.rem(lax.axis_index(axis) // bit, 2)


def owned_half():
    total = 0
    for axis in ("gz", "gy"):
        for k in range(lax.axis_size(axis).bit_length() - 1):
            total = total + side_of(axis, 1 << k)
    return lax.rem(total, 2)


def part(side, rows):
    return pl.ds(pl.multiple_of(side * rows, 16), rows)


def split(packed, keep, send, side):
    half = keep.shape[0]
    keep[...] = packed[part(side, half)]
    send[...] = packed[part(1 - side, half)].astype(BF16)


def halve_kernel(mine, other, keep, send, total, *, axis, bit):
    total[...] = mine[...] + other[...].astype(F32)
    split(total, keep, send, side_of(axis, bit))


def add_kernel(x, y, out):
    out[...] = (x[...].astype(F32) + y[...].astype(F32)).astype(BF16)


def join_kernel(mine, other, out, *, axis, bit):
    join(mine, other, out, side_of(axis, bit))


def join(mine, other, out, side):
    rows = mine.shape[0]
    out[part(side, rows)] = mine[...]
    out[part(1 - side, rows)] = other[...]


def field_kernel(near, far, near_in, far_in, w_ref, acc_ref, inner, outer):
    rows, channels, breadth = near.shape
    fill_columns(inner, near, far)
    fill_columns(outer, near_in, far_in)

    def step(t, carry):
        y = 2 * t
        own = inner_terms(inner, w_ref, y)
        rest = outer_terms(outer, w_ref, y)
        for z in range(2):
            total = own[z] + rest[z]
            for b in range(2):
                acc_ref[z, y + b] = total[:, b * breadth : (b + 1) * breadth]
        return carry

    lax.fori_loop(0, rows // 2, step, 0)


def field_edges_kernel(near, far, acc_ref, w_ref, out_ref, edges):
    rows, channels, breadth = acc_ref.shape[1:]
    fill_rows(edges, near, far)
    sides = [edge_terms(edges, w_ref, side) for side in range(2)]
    for z in range(2):
        for y in range(rows):
            line = acc_ref[z, y]
            if y in (0, rows - 1):
                line = line + sides[0 if y == 0 else 1][z]
            out_ref[pl.ds(z * rows + y, channels, stride=2 * rows), :] = line


def write_half(half, sums, conv_out, down_out, conv, down, sems, scale):
    channels, height = conv.shape[2], down.shape[2]
    size, rows = 3 * channels // 2, sums.shape[0]
    copies = []

    def send(staged, out, at):
        copies.append(pltpu.make_async_copy(staged.at[at], out.at[at], sems.at[len(copies)]))
        copies[-1].start()

    for tap in range(7) if half == 0 else range(7, 9):
        base = tap_row(tap, 2 * rows, channels) - half * rows
        a, b = divmod(tap, 3)
        conv[a, b, :, 0 : 2 * channels] = sums[base : base + channels].astype(F32) * scale
        rest = sums[base + channels : base + size].astype(F32) * scale
        conv[a, b, 0 : channels // 2, 2 * channels :] = rest[:, 0:channels]
        conv[a, b, channels // 2 :, 2 * channels :] = rest[:, channels:]
        if tap in (2, 5):
            send(conv, conv_out, (a,))
    send(conv, conv_out, (2, 0) if half == 0 else (2, pl.ds(1, 2)))
    first = rows - 7 * size
    if half == 0:
        down[0, 0, 0:first] = sums[7 * size :].astype(F32) * scale
        send(down, down_out, (0, 0, pl.ds(0, first)))
    else:
        down[0, 0, first:] = sums[0 : height - first].astype(F32) * scale
        send(down, down_out, (0, 0, pl.ds(first, height - first)))
        for tap in range(1, 4):
            at = tap * height - first
            down[tap // 2, tap % 2] = sums[at : at + height].astype(F32) * scale
            if tap in (1, 3):
                send(down, down_out, (0, 1) if tap == 1 else (1,))
    for copy in copies:
        copy.wait()


def write_kernel(sums, *refs, own, scale):
    conv_out, down_out, conv, down, sems = refs[-5:]
    half = owned_half() if own else 1 - owned_half()

    @pl.when(half == 0)
    def _():
        write_half(0, sums, conv_out, down_out, conv, down, sems, scale)

    @pl.when(half == 1)
    def _():
        write_half(1, sums, conv_out, down_out, conv, down, sems, scale)


def write(sums, shapes, scale, outs=()):
    return pl.pallas_call(
        functools.partial(write_kernel, own=len(outs) == 0, scale=scale),
        out_shape=[jax.ShapeDtypeStruct(shape, F32) for shape in shapes],
        in_specs=[pl.BlockSpec(memory_space=pltpu.VMEM)] + [pl.BlockSpec(memory_space=pltpu.HBM)] * len(outs),
        out_specs=[pl.BlockSpec(memory_space=pltpu.HBM)] * 2,
        scratch_shapes=[pltpu.VMEM(shape, F32) for shape in shapes] + [pltpu.SemaphoreType.DMA((4,))],
        input_output_aliases={1 + k: k for k in range(len(outs))},
        compiler_params=PARAMS,
    )(sums, *outs)


def swap(cells, axis, low):
    count = lax.axis_size(axis)
    pairs = [(i % count, (i + 1) % count) for i in range(low, low + count, 2)]
    return lax.ppermute(cells, axis, pairs + [(b, a) for a, b in pairs])


def flip(cells, axis, bit):
    row = lax.axis_size("gy")
    mask = bit * row | 1 if axis == "gz" else bit | 1
    return lax.ppermute(cells, ("gz", "gy"), [(i, i ^ mask) for i in range(lax.axis_size("gz") * row)])


def tied(first, *others):
    found = lax.optimization_barrier((first, *others))
    return found[0], tuple(found[1:])


def swapped(near, far, axis):
    return swap(near, axis, 0), swap(far, axis, 1)


def body(features, conv_weight, down_weight, cotangent):
    channels, plane_count, row_count, breadth = features.shape
    out_channels = down_weight.shape[2]
    count = lax.axis_size("gz") * lax.axis_size("gy")
    grad_scale = 1.0 / math.sqrt(plane_count * row_count * breadth * count)
    cot = cotangent.reshape(out_channels, -1)
    conv_weight, down_weight, cot = fetch(conv_weight, down_weight, cot)
    (weight_bwd,) = call(turn_kernel, [(conv_weight.shape, BF16)], [], 0, (conv_weight,))
    plane = ((row_count, channels, breadth), BF16)
    edge = ((plane_count + 2, channels, breadth), BF16)
    cols = ((plane_count, row_count + 2, 3 * channels, breadth), BF16)
    edge_cols = ((plane_count + 2, 2, 3 * channels, breadth), BF16)
    lines = (plane_count, row_count, channels, breadth)
    conv_flops = 2 * 27 * channels * channels * plane_count * row_count * breadth

    pair = ((plane_count, channels, breadth), BF16)
    *own, near_row, far_row = call(
        lines_kernel, [plane, plane, pair, pair],
        [((channels * plane_count * row_count, breadth), F32)], 0, (features,),
    )
    outside = swapped(*own, "gz")
    beside = swapped(near_row, far_row, "gy")
    inner, acc, hidden_grad = call(
        inner_kernel, [cols, (lines, F32), (lines, F32)],
        [((out_channels, row_count // 2 * breadth), BF16)],
        2 * conv_flops // 3, (*own, conv_weight, down_weight, cot),
    )
    near, far, near_row, far_row, acc = lax.optimization_barrier((*outside, *beside, acc))
    outside, own_rows = (near, far), (near_row, far_row)
    beside = swapped(*call(outer_rows_kernel, [pair, pair], [], 0, outside), "gy")
    far, near = lax.optimization_barrier((beside[1], beside[0]))
    beside = (near, far)
    rows_cols = ((plane_count, 2, 3 * channels, breadth), BF16)
    outer, own_edges, *inside = call(
        outer_kernel,
        [cols, rows_cols, ((plane_count, 2, channels, breadth), F32), plane, plane, (lines, BF16)], [],
        conv_flops // 3, (*outside, *own_rows, conv_weight, acc, hidden_grad),
    )
    edges, near, far, hidden = call(
        gate_kernel, [rows_cols, plane, plane, (lines, BF16)], [], conv_flops // 10,
        (*beside, *inside, hidden_grad, conv_weight),
    )
    gates = (near, far)

    used = 27 * channels * channels // 128 + 4 * out_channels
    rows = -(-used // 128) * 128
    keep, send = call(
        weight_grad_kernel, [((rows // 2, 128), F32), ((rows // 2, 128), BF16)], [((rows, 128), F32)],
        conv_flops, (inner, outer, own_edges, edges, *gates, hidden, cot),
    )
    keep, gates = tied(keep, *gates)
    near, far = gates
    near_in = swap(near, "gz", 0)
    for level, (axis, bit) in enumerate((("gz", 2), ("gy", 2))):
        size = rows >> (level + 2)
        mine, got = keep, flip(send, *(("gy", 1), ("gz", 2))[level])
        keep, send = call(
            functools.partial(halve_kernel, axis=axis, bit=bit),
            [((size, 128), F32), ((size, 128), BF16)], [((2 * size, 128), F32)], 0, (mine, got),
        )
        if level == 0:
            keep, (far, hidden) = tied(keep, far, hidden)
            far_in = swap(far, "gz", 1)
            (section_out,) = call(
                section_kernel, [((out_channels, cot.shape[1]), BF16)], [], conv_flops // 10,
                (hidden, down_weight),
            )
    shard = ((rows // 8, 128), BF16)
    (sums,) = call(add_kernel, [shard], [], 0, (keep, flip(send, "gy", 2)))
    (sums,) = call(add_kernel, [shard], [], 0, (sums, flip(sums, "gz", 1)))
    sums, outside = tied(sums, near_in, far_in)
    sends = call(edges_kernel, [edge, edge], [], 0, (*gates, *outside))
    beside = swapped(*sends, "gy")
    (acc,) = call(
        field_kernel, [(lines, F32)], [cols, cols], conv_flops, (*gates, *outside, weight_bwd)
    )
    wide = [("gy", 1 << k) for k in range(2, lax.axis_size("gy").bit_length() - 1)]
    wide += [("gz", 1 << k) for k in range(2, lax.axis_size("gz").bit_length() - 1)]
    for axis, bit in wide:
        (sums,) = call(add_kernel, [shard], [], 0, (sums, flip(sums, axis, bit)))
    sums, (section_out,) = tied(sums, section_out)
    (sums,) = call(
        functools.partial(join_kernel, axis="gy", bit=2), [((rows // 4, 128), BF16)], [], 0,
        (sums, flip(sums, "gy", 2)),
    )
    sums, (acc, *beside) = tied(sums, acc, *beside)
    (field,) = call(
        field_edges_kernel, [((channels * plane_count * row_count, breadth), F32)], [edge_cols],
        conv_flops // 10, (*beside, acc, weight_bwd),
    )
    (sums,) = call(
        functools.partial(join_kernel, axis="gz", bit=2), [((rows // 2, 128), BF16)], [], 0,
        (sums, flip(sums, "gz", 2)),
    )
    sums, (field,) = tied(sums, field)
    shapes = (conv_weight.shape, down_weight.shape)
    other = flip(sums, "gy", 1)
    grad_conv, grad_down = write(other, shapes, grad_scale, write(sums, shapes, grad_scale))
    section_out = section_out.reshape(out_channels, plane_count // 2, -1)
    return (section_out, field.reshape(features.shape), grad_conv, grad_down)


def solution(mesh):
    return jax.shard_map(
        body,
        mesh=mesh,
        in_specs=(P(None, "gz", "gy", None), P(), P(), P(None, "gz", "gy")),
        out_specs=(P(None, "gz", "gy"), P(None, "gz", "gy", None), P(), P()),
        check_vma=False,
    )
```

```python
import functools
import math

import jax
import jax.numpy as jnp
from jax import lax
from jax.experimental import pallas as pl
from jax.experimental.pallas import tpu as pltpu
from jax.sharding import PartitionSpec as P

F32 = jnp.float32
BF16 = jnp.bfloat16
PARAMS = pltpu.CompilerParams(vmem_limit_bytes=24 * 1024 * 1024)


def call(kernel, outs, scratch, flops, operands):
    moved = sum(x.size * x.dtype.itemsize for x in operands)
    moved += sum(math.prod(s) * jnp.dtype(d).itemsize for s, d in outs)
    vmem = pl.BlockSpec(memory_space=pltpu.VMEM)
    return pl.pallas_call(
        kernel,
        out_shape=[jax.ShapeDtypeStruct(s, d) for s, d in outs],
        in_specs=[vmem] * len(operands),
        out_specs=[vmem] * len(outs),
        scratch_shapes=[pltpu.VMEM(s, d) for s, d in scratch],
        compiler_params=PARAMS,
        cost_estimate=pl.CostEstimate(flops=flops, bytes_accessed=moved, transcendentals=0),
    )(*operands)


def is_even(axis):
    return lax.rem(lax.axis_index(axis), 2) == 0


def choose(cond, yes, no):
    return jnp.where(jnp.broadcast_to(cond, yes.shape), yes, no)


def lines_kernel(f_ref, near_ref, far_ref, near_row, far_row, wide):
    channels, planes, rows, breadth = f_ref.shape
    wide[...] = f_ref[...].astype(F32).reshape(channels * planes * rows, breadth)
    even = is_even("gz")
    ends = {}
    for y in range(rows):
        low, high = ends[y] = [
            wide[pl.ds(z * rows + y, channels, stride=planes * rows), :].astype(BF16) for z in range(2)
        ]
        near_ref[y] = choose(even, high, low)
        far_ref[y] = choose(even, low, high)
    even_y = is_even("gy")
    for z in range(2):
        near_row[z] = choose(even_y, ends[rows - 1][z], ends[0][z])
        far_row[z] = choose(even_y, ends[0][z], ends[rows - 1][z])


def turn_kernel(w_ref, out):
    channels = w_ref.shape[2]
    for a in range(3):
        for b in range(3):
            turned = w_ref[a, b].astype(F32).T
            blocks = [turned[(2 - e) * channels : (3 - e) * channels] for e in range(3)]
            out[2 - a, 2 - b] = jnp.concatenate(blocks, axis=1).astype(BF16)


def fetch_kernel(*refs):
    *both, sems = refs
    count = len(both) // 2
    copies = [pltpu.make_async_copy(both[k], both[count + k], sems.at[k]) for k in range(count)]
    for copy in copies:
        copy.start()
    for copy in copies:
        copy.wait()


def fetch(*operands):
    return pl.pallas_call(
        fetch_kernel,
        out_shape=[jax.ShapeDtypeStruct(x.shape, x.dtype) for x in operands],
        in_specs=[pl.BlockSpec(memory_space=pltpu.HBM)] * len(operands),
        out_specs=[pl.BlockSpec(memory_space=pltpu.VMEM)] * len(operands),
        scratch_shapes=[pltpu.SemaphoreType.DMA((len(operands),))],
        compiler_params=PARAMS,
        cost_estimate=pl.CostEstimate(flops=0, bytes_accessed=2 * sum(x.size * 2 for x in operands), transcendentals=0),
    )(*operands)


def outer_rows_kernel(near_in, far_in, near_ref, far_ref):
    rows = near_in.shape[0]
    even_z, even_y = is_even("gz"), is_even("gy")
    for p, (one, other) in enumerate(((far_in, near_in), (near_in, far_in))):
        first = choose(even_z, one[0], other[0])
        last = choose(even_z, one[rows - 1], other[rows - 1])
        near_ref[p] = choose(even_y, last, first)
        far_ref[p] = choose(even_y, first, last)


def edges_kernel(near, far, near_in, far_in, near_ref, far_ref):
    rows = near.shape[0]
    even_z, even_y = is_even("gz"), is_even("gy")

    def put(p, one, other):
        first = choose(even_z, one[0], other[0])
        last = choose(even_z, one[rows - 1], other[rows - 1])
        near_ref[p] = choose(even_y, last, first)
        far_ref[p] = choose(even_y, first, last)

    put(0, far_in, near_in)
    put(1, far, near)
    put(2, near, far)
    put(3, near_in, far_in)


def put_columns(cols, p, q, line):
    channels = line.shape[0]
    wide = line.astype(F32)
    cols[p, q, 0:channels] = pltpu.roll(wide, 1, 1).astype(BF16)
    cols[p, q, channels : 2 * channels] = line
    cols[p, q, 2 * channels : 3 * channels] = pltpu.roll(wide, line.shape[1] - 1, 1).astype(BF16)


def fill_columns(cols, near, far):
    rows = near.shape[0]
    even = is_even("gz")

    def step(y, carry):
        put_columns(cols, 0, y + 1, choose(even, far[y], near[y]))
        put_columns(cols, 1, y + 1, choose(even, near[y], far[y]))
        return carry

    lax.fori_loop(0, rows, step, 0, unroll=2)
    for p in range(2):
        for q in (0, rows + 1):
            cols[p, q] = jnp.zeros(cols.shape[2:], BF16)


def fill_rows(cols, near, far):
    even = is_even("gy")
    for p in range(near.shape[0]):
        put_columns(cols, p, 0, choose(even, far[p], near[p]))
        put_columns(cols, p, 1, choose(even, near[p], far[p]))


def dot(lhs, rhs):
    return jnp.dot(lhs, rhs, preferred_element_type=F32)


def taps(w_ref, b, first, last):
    return jnp.concatenate([w_ref[a, b] for a in range(first, last)], axis=0)


def window(cols, p, q):
    return jnp.concatenate([cols[p, q], cols[p, q + 1]], axis=1)


def inner_terms(cols, w_ref, y):
    acc = None
    for b in range(3):
        for p in range(2):
            term = dot(taps(w_ref, b, p, p + 2), window(cols, p, y + b))
            acc = term if acc is None else acc + term
    half = acc.shape[0] // 2
    return acc[half:], acc[:half]


def outer_terms(cols, w_ref, y):
    lower = upper = None
    for b in range(3):
        low, high = dot(w_ref[0, b], window(cols, 0, y + b)), dot(w_ref[2, b], window(cols, 1, y + b))
        lower = low if lower is None else lower + low
        upper = high if upper is None else upper + high
    return lower, upper


def edge_terms(edges, w_ref, side):
    b = 2 * side
    half = w_ref.shape[2]
    acc = dot(taps(w_ref, b, 0, 2), edges[1, side]) + dot(taps(w_ref, b, 1, 3), edges[2, side])
    return acc[half:] + dot(w_ref[0, b], edges[0, side]), acc[:half] + dot(w_ref[2, b], edges[3, side])


def inner_kernel(near, far, w_ref, d_ref, cot_ref, cols, acc_ref, grad_ref, up):
    rows, channels, breadth = near.shape
    fill_columns(cols, near, far)
    source = lax.broadcasted_iota(jnp.int32, (breadth, 2 * breadth), 0)
    target = lax.broadcasted_iota(jnp.int32, (breadth, 2 * breadth), 1)
    spread = jnp.where(source == target // 2, 1.0, 0.0).astype(BF16)
    for pair in range(rows // 4):
        both = dot(cot_ref[:, pair * breadth : (pair + 1) * breadth], spread)
        up[:, 2 * pair * breadth : 2 * (pair + 1) * breadth] = both.astype(BF16)
    even = lax.broadcasted_iota(jnp.int32, (channels, breadth), 1) % 2 == 0
    for a in range(2):
        for b in range(2):
            terms = lax.dot_general(d_ref[a, b], up[...], (((0,), (0,)), ((), ())), preferred_element_type=F32)
            for t in range(rows // 2):
                part = terms[:, t * breadth : (t + 1) * breadth]
                grad_ref[a, 2 * t + b] = jnp.where(even, part[0:channels], part[channels:])

    def step(t, carry):
        y = 2 * t
        for z, lines in enumerate(inner_terms(cols, w_ref, y)):
            for b in range(2):
                acc_ref[z, y + b] = lines[:, b * breadth : (b + 1) * breadth]
        return carry

    lax.fori_loop(0, rows // 2, step, 0)


def gated(preact, grad):
    sig = 1.0 / (1.0 + jnp.exp(-preact))
    return (preact * sig).astype(BF16), (grad * sig * (1.0 + preact * (1.0 - sig))).astype(BF16)


def outer_kernel(
    near, far, near_row, far_row, w_ref, acc_ref, grad_ref, cols, edges, side_ref, near_ref, far_ref, h_ref
):
    rows, channels, breadth = near.shape
    fill_columns(cols, near, far)
    fill_rows(edges, near_row, far_row)
    beside = []
    for side in range(2):
        terms = dot(taps(w_ref, 2 * side, 0, 2), edges[0, side]) + dot(taps(w_ref, 2 * side, 1, 3), edges[1, side])
        beside.append((terms[channels:], terms[:channels]))
    even = is_even("gz")
    for y in range(0, rows, 2):
        outer = outer_terms(cols, w_ref, y)
        for b in range(2):
            found = []
            for z in range(2):
                preact = acc_ref[z, y + b] + outer[z][:, b * breadth : (b + 1) * breadth]
                if y + b in (0, rows - 1):
                    side_ref[z, b] = preact + beside[b][z]
                else:
                    h_ref[z, y + b], gate = gated(preact, grad_ref[z, y + b])
                    found.append(gate)
            if len(found) > 0:
                near_ref[y + b] = choose(even, found[1], found[0])
                far_ref[y + b] = choose(even, found[0], found[1])


def gate_kernel(near, far, side_ref, near_in, far_in, h_in, grad_ref, w_ref, edges, near_ref, far_ref, h_ref):
    rows = near_in.shape[0]
    fill_rows(edges, near, far)
    even = is_even("gz")
    for side, y in enumerate((0, rows - 1)):
        terms = [dot(w_ref[2 * z, 2 * side], edges[z, side]) for z in range(2)]
        found = []
        for z in range(2):
            h_ref[z, y], gate = gated(side_ref[z, side] + terms[z], grad_ref[z, y])
            found.append(gate)
        near_ref[y] = choose(even, found[1], found[0])
        far_ref[y] = choose(even, found[0], found[1])
    for y in range(1, rows - 1):
        near_ref[y] = near_in[y]
        far_ref[y] = far_in[y]
        for z in range(2):
            h_ref[z, y] = h_in[z, y]


def coarse_hidden(h_ref):
    rows, channels, breadth = h_ref.shape[1:]
    source = lax.broadcasted_iota(jnp.int32, (2 * breadth, 2 * breadth), 0)
    target = lax.broadcasted_iota(jnp.int32, (2 * breadth, 2 * breadth), 1)
    wanted = 2 * (target % breadth) + target // breadth
    pick = jnp.where(source == wanted, 1.0, 0.0).astype(BF16)
    pairs = rows // 4
    both = [
        jnp.concatenate([h_ref[a, 4 * pair + b], h_ref[a, 4 * pair + 2 + b]], axis=1)
        for a in range(2) for b in range(2) for pair in range(pairs)
    ]
    picked = dot(jnp.concatenate(both, axis=0), pick).astype(BF16)
    blocks = []
    for tap in range(4):
        parts = [picked[(tap * pairs + pair) * channels : (tap * pairs + pair + 1) * channels] for pair in range(pairs)]
        for e in range(2):
            blocks.append(jnp.concatenate([x[:, e * breadth : (e + 1) * breadth] for x in parts], axis=1))
    return jnp.concatenate(blocks, axis=0)


def section_kernel(h_ref, d_ref, out_ref):
    down = jnp.concatenate([d_ref[a, b] for a in range(2) for b in range(2)], axis=1)
    out_ref[...] = dot(down, coarse_hidden(h_ref)).astype(BF16)


def weight_grad_kernel(inner, outer, own_edges, edges, near, far, h_ref, cot_ref, keep, send, packed):
    rows, channels, breadth = near.shape
    across = (((1,), (1,)), ((), ()))
    even = is_even("gz")
    low = [choose(even, far[y], near[y]) for y in range(rows)]
    high = [choose(even, near[y], far[y]) for y in range(rows)]
    nothing = jnp.zeros((channels, breadth), BF16)

    def shifted(lines):
        return jnp.concatenate(
            [jnp.concatenate([nothing] * b + lines + [nothing] * (2 - b), axis=1) for b in range(3)], axis=0
        )

    low, high = shifted(low), shifted(high)
    both = jnp.concatenate([low, high], axis=0)

    def columns(p, q):
        planes, rows_beside, at = (inner, own_edges, p - 1) if p in (1, 2) else (outer, edges, p // 3)
        return rows_beside[at, q // (rows + 1)] if q in (0, rows + 1) else planes[at, q]

    parts = []
    for p in range(4):
        lines = jnp.concatenate([columns(p, q) for q in range(rows + 2)], axis=1)
        lhs = low if p == 0 else high if p == 3 else both
        parts.append(lax.dot_general(lhs, lines, across, preferred_element_type=F32))
    lane = lax.broadcasted_iota(jnp.int32, (channels // 2, breadth), 1)
    for a in range(3):
        for b in range(3):
            at = b * channels + (0 if a == 2 else 3 * channels)
            total = parts[a][b * channels : (b + 1) * channels] + parts[a + 1][at : at + channels]
            base = (a * 3 + b) * 3 * channels // 2
            packed[base : base + channels] = total[:, 0:breadth]
            rest = jnp.concatenate([total[:, breadth:], total[:, breadth:]], axis=1)
            mix = jnp.where(lane < channels, rest[0 : channels // 2], rest[channels // 2 :])
            packed[base + channels : base + 3 * channels // 2] = mix
    base = 9 * 3 * channels // 2
    height = cot_ref.shape[0]
    down = lax.dot_general(cot_ref[...], coarse_hidden(h_ref), across, preferred_element_type=F32)
    for tap in range(4):
        packed[base + tap * height : base + (tap + 1) * height] = down[:, tap * breadth : (tap + 1) * breadth]
    end = base + 4 * height
    if end < packed.shape[0]:
        packed[end:] = jnp.zeros((packed.shape[0] - end, packed.shape[1]), F32)
    split(packed, keep, send, owned_half())


def side_of(axis, bit):
    return lax.rem(lax.axis_index(axis) // bit, 2)


def owned_half():
    total = 0
    for axis in ("gz", "gy"):
        for k in range(lax.axis_size(axis).bit_length() - 1):
            total = total + side_of(axis, 1 << k)
    return lax.rem(total, 2)


def part(side, rows):
    return pl.ds(pl.multiple_of(side * rows, 16), rows)


def split(packed, keep, send, side):
    half = keep.shape[0]
    keep[...] = packed[part(side, half)]
    send[...] = packed[part(1 - side, half)].astype(BF16)


def halve_kernel(mine, other, keep, send, total, *, axis, bit):
    total[...] = mine[...] + other[...].astype(F32)
    split(total, keep, send, side_of(axis, bit))


def add_kernel(x, y, out):
    out[...] = (x[...].astype(F32) + y[...].astype(F32)).astype(BF16)


def join_kernel(mine, other, out, *, axis, bit):
    join(mine, other, out, side_of(axis, bit))


def join(mine, other, out, side):
    rows = mine.shape[0]
    out[part(side, rows)] = mine[...]
    out[part(1 - side, rows)] = other[...]


def field_kernel(near, far, near_in, far_in, w_ref, acc_ref, inner, outer):
    rows, channels, breadth = near.shape
    fill_columns(inner, near, far)
    fill_columns(outer, near_in, far_in)

    def step(t, carry):
        y = 2 * t
        own = inner_terms(inner, w_ref, y)
        rest = outer_terms(outer, w_ref, y)
        for z in range(2):
            total = own[z] + rest[z]
            for b in range(2):
                acc_ref[z, y + b] = total[:, b * breadth : (b + 1) * breadth]
        return carry

    lax.fori_loop(0, rows // 2, step, 0)


def field_edges_kernel(near, far, acc_ref, w_ref, out_ref, edges):
    rows, channels, breadth = acc_ref.shape[1:]
    fill_rows(edges, near, far)
    sides = [edge_terms(edges, w_ref, side) for side in range(2)]
    for z in range(2):
        for y in range(rows):
            line = acc_ref[z, y]
            if y in (0, rows - 1):
                line = line + sides[0 if y == 0 else 1][z]
            out_ref[pl.ds(z * rows + y, channels, stride=2 * rows), :] = line


def unpack_kernel(mine, other, conv_ref, down_ref, sums_ref, *, scale):
    join(mine, other, sums_ref, owned_half())
    channels = conv_ref.shape[2]
    for a in range(3):
        for b in range(3):
            base = (a * 3 + b) * 3 * channels // 2
            conv_ref[a, b, :, 0 : 2 * channels] = sums_ref[base : base + channels].astype(F32) * scale
            rest = sums_ref[base + channels : base + 3 * channels // 2].astype(F32) * scale
            conv_ref[a, b, 0 : channels // 2, 2 * channels :] = rest[:, 0:channels]
            conv_ref[a, b, channels // 2 :, 2 * channels :] = rest[:, channels:]
    base = 9 * 3 * channels // 2
    height = down_ref.shape[2]
    for a in range(2):
        for b in range(2):
            at = base + (2 * a + b) * height
            down_ref[a, b] = sums_ref[at : at + height].astype(F32) * scale


def swap(cells, axis, low):
    count = lax.axis_size(axis)
    pairs = [(i % count, (i + 1) % count) for i in range(low, low + count, 2)]
    return lax.ppermute(cells, axis, pairs + [(b, a) for a, b in pairs])


def flip(cells, axis, bit):
    row = lax.axis_size("gy")
    mask = bit * row | 1 if axis == "gz" else bit | 1
    return lax.ppermute(cells, ("gz", "gy"), [(i, i ^ mask) for i in range(lax.axis_size("gz") * row)])


def tied(first, *others):
    found = lax.optimization_barrier((first, *others))
    return found[0], tuple(found[1:])


def swapped(near, far, axis):
    return swap(near, axis, 0), swap(far, axis, 1)


def body(features, conv_weight, down_weight, cotangent):
    channels, plane_count, row_count, breadth = features.shape
    out_channels = down_weight.shape[2]
    count = lax.axis_size("gz") * lax.axis_size("gy")
    grad_scale = 1.0 / math.sqrt(plane_count * row_count * breadth * count)
    cot = cotangent.reshape(out_channels, -1)
    conv_weight, down_weight, cot = fetch(conv_weight, down_weight, cot)
    (weight_bwd,) = call(turn_kernel, [(conv_weight.shape, BF16)], [], 0, (conv_weight,))
    plane = ((row_count, channels, breadth), BF16)
    edge = ((plane_count + 2, channels, breadth), BF16)
    cols = ((plane_count, row_count + 2, 3 * channels, breadth), BF16)
    edge_cols = ((plane_count + 2, 2, 3 * channels, breadth), BF16)
    lines = (plane_count, row_count, channels, breadth)
    conv_flops = 2 * 27 * channels * channels * plane_count * row_count * breadth

    pair = ((plane_count, channels, breadth), BF16)
    *own, near_row, far_row = call(
        lines_kernel, [plane, plane, pair, pair],
        [((channels * plane_count * row_count, breadth), F32)], 0, (features,),
    )
    outside = swapped(*own, "gz")
    beside = swapped(near_row, far_row, "gy")
    inner, acc, hidden_grad = call(
        inner_kernel, [cols, (lines, F32), (lines, F32)],
        [((out_channels, row_count // 2 * breadth), BF16)],
        2 * conv_flops // 3, (*own, conv_weight, down_weight, cot),
    )
    near, far, near_row, far_row, acc = lax.optimization_barrier((*outside, *beside, acc))
    outside, own_rows = (near, far), (near_row, far_row)
    beside = swapped(*call(outer_rows_kernel, [pair, pair], [], 0, outside), "gy")
    far, near = lax.optimization_barrier((beside[1], beside[0]))
    beside = (near, far)
    rows_cols = ((plane_count, 2, 3 * channels, breadth), BF16)
    outer, own_edges, *inside = call(
        outer_kernel,
        [cols, rows_cols, ((plane_count, 2, channels, breadth), F32), plane, plane, (lines, BF16)], [],
        conv_flops // 3, (*outside, *own_rows, conv_weight, acc, hidden_grad),
    )
    edges, near, far, hidden = call(
        gate_kernel, [rows_cols, plane, plane, (lines, BF16)], [], conv_flops // 10,
        (*beside, *inside, hidden_grad, conv_weight),
    )
    gates = (near, far)

    used = 27 * channels * channels // 128 + 4 * out_channels
    rows = -(-used // 128) * 128
    keep, send = call(
        weight_grad_kernel, [((rows // 2, 128), F32), ((rows // 2, 128), BF16)], [((rows, 128), F32)],
        conv_flops, (inner, outer, own_edges, edges, *gates, hidden, cot),
    )
    keep, gates = tied(keep, *gates)
    near, far = gates
    near_in = swap(near, "gz", 0)
    for level, (axis, bit) in enumerate((("gz", 2), ("gy", 2))):
        size = rows >> (level + 2)
        mine, got = keep, flip(send, *(("gy", 1), ("gz", 2))[level])
        keep, send = call(
            functools.partial(halve_kernel, axis=axis, bit=bit),
            [((size, 128), F32), ((size, 128), BF16)], [((2 * size, 128), F32)], 0, (mine, got),
        )
        if level == 0:
            keep, (far, hidden) = tied(keep, far, hidden)
            far_in = swap(far, "gz", 1)
            (section_out,) = call(
                section_kernel, [((out_channels, cot.shape[1]), BF16)], [], conv_flops // 10,
                (hidden, down_weight),
            )
    shard = ((rows // 8, 128), BF16)
    (sums,) = call(add_kernel, [shard], [], 0, (keep, flip(send, "gy", 2)))
    (sums,) = call(add_kernel, [shard], [], 0, (sums, flip(sums, "gz", 1)))
    sums, (near_in, far_in, section_out) = tied(sums, near_in, far_in, section_out)
    outside = (near_in, far_in)
    sends = call(edges_kernel, [edge, edge], [], 0, (*gates, *outside))
    beside = swapped(*sends, "gy")
    (acc,) = call(
        field_kernel, [(lines, F32)], [cols, cols], conv_flops, (*gates, *outside, weight_bwd)
    )
    wide = [("gy", 1 << k) for k in range(2, lax.axis_size("gy").bit_length() - 1)]
    wide += [("gz", 1 << k) for k in range(2, lax.axis_size("gz").bit_length() - 1)]
    for axis, bit in wide:
        (sums,) = call(add_kernel, [shard], [], 0, (sums, flip(sums, axis, bit)))
    (sums,) = call(
        functools.partial(join_kernel, axis="gy", bit=2), [((rows // 4, 128), BF16)], [], 0,
        (sums, flip(sums, "gy", 2)),
    )
    sums, (acc, *beside) = tied(sums, acc, *beside)
    (field,) = call(
        field_edges_kernel, [((channels * plane_count * row_count, breadth), F32)], [edge_cols],
        conv_flops // 10, (*beside, acc, weight_bwd),
    )
    (sums,) = call(
        functools.partial(join_kernel, axis="gz", bit=2), [((rows // 2, 128), BF16)], [], 0,
        (sums, flip(sums, "gz", 2)),
    )
    sums, (field,) = tied(sums, field)
    grad_conv, grad_down = call(
        functools.partial(unpack_kernel, scale=grad_scale),
        [(conv_weight.shape, F32), (down_weight.shape, F32)], [((rows, 128), BF16)], 0,
        (sums, flip(sums, "gy", 1)),
    )
    section_out = section_out.reshape(out_channels, plane_count // 2, -1)
    return (section_out, field.reshape(features.shape), grad_conv, grad_down)


def solution(mesh):
    return jax.shard_map(
        body,
        mesh=mesh,
        in_specs=(P(None, "gz", "gy", None), P(), P(), P(None, "gz", "gy")),
        out_specs=(P(None, "gz", "gy"), P(None, "gz", "gy", None), P(), P()),
        check_vma=False,
    )
```
